32 devices in a mesh: gx: 4 (over y, x), gy: 8 (over z, core).
Axes of the slice: x: 2, y: 2, z: 4, core: 2. Of those that a mesh axis runs over, the one named last changes fastest.
Arguments:
- fluid_state: float32 [4, 32, 64, 512], P(None, None, 'gy', 'gx'), may hold values from -6 to 6
- particle_pos: float32 [3, 262144], P(None, ('gx', 'gy')), may hold values from -6 to 6
- particle_motion: float32 [6, 262144], P(None, ('gx', 'gy')), may hold values from -6 to 6
- particle_radius: float32 [262144], P(('gx', 'gy')), may hold values from 0.5 to 1
- particle_temp: float32 [262144], P(('gx', 'gy')), may hold values from -6 to 6
- particle_cell: int32 [262144], P(('gx', 'gy')), may hold values from 0 to 32767
- particle_box: int32 [262144, 1], P(('gx', 'gy')), may hold values from 0 to 31; in each aligned block of 8192 rows (0 to 8191, 8192 to 16383, ...) at most 512 rows name the same one
- box_owner: int32 [32], replicated, may hold values from 0 to 31, each once
- contact_mask: int32 [4096, 128, 128], P(('gx', 'gy')), may hold values 0 or 1
Outputs:
- fluid_next: float32 [4, 32, 64, 512], P(None, None, 'gy', 'gx')
- void_fraction: float32 [32, 64, 512], P(None, 'gy', 'gx')
- particle_next: float32 [7, 262144], P(None, ('gx', 'gy'))
The draws below stay inside these ranges and needn't reach their ends.
Inputs may be any that keep to these rules, and one draw needn't show every extreme that they name: `particle_box`: among the 8192 rows of one device no box is named by more than 512 rows, a bound that some block reaches. `box_owner`: A permutation of the devices.
All inputs are finite; a program needn't handle non-finite values. No bound on the sum of `contact_mask` on one device may be relied on, other than what follows from the above.
Results may differ from the reference program's by a relative error of at most 0.0003.
Values sent between devices are 32-bit elements; how exact they have to be, the bound alone decides.
No kernel may reach another device: no remote copies, remote signals or barrier semaphores. Data moves between devices by JAX's collectives and lax.ppermute only.
A program may use at most 64 MiB of HBM per device.

```python
import math
import jax
import jax.numpy as jnp
import numpy as np
from jax import lax

CX = 128
CY = 8
NZ = 32
P_DEV = 8192
BLOCK = 128
C = 512
NX = 512
NY = 64
NPART = 262144
NBLK = 4096
CELLS_DEV = 32768
N_GX = 4
N_GY = 8
DEVICES = 32


def touch_ends(values, key, smallest, high):
    extent = values.shape
    spot = [jax.random.randint(jax.random.fold_in(key, axis), (), 0, extent[axis]) for axis in range(len(extent))]
    values = values.at[tuple(spot)].set(smallest)
    longest = extent.index(max(extent))
    spot[longest] = (spot[longest] + 1) % extent[longest]
    return values.at[tuple(spot)].set(high)


def steps_of(rng, shape, cuts, low, largest):
    def one(dim, blocks):
        steps = jax.random.uniform(jax.random.fold_in(jax.random.fold_in(rng, 6), dim), (blocks,), jnp.float32, low / len(cuts), largest / len(cuts))
        return jnp.repeat(jnp.exp(steps), shape[dim] // blocks).reshape((-1,) + (1,) * (len(shape) - dim - 1))

    gain = one(*cuts[0])
    for cut in cuts[1:]:
        gain = gain * one(*cut)
    return gain


def assign_block(rng, own, number, rows, number_of, top, most, skew):
    sequence = jax.random.permutation(rng, number_of)
    packed, usual = load_shares(number_of, rows * top, most, skew, True), load_shares(number_of, rows * top, most, skew, False)
    places = jnp.arange(number_of)

    def named(sizes, offset_by):
        used = int((sizes > 0).sum())
        fixed = max(1, used // 4)
        passed = fixed + (places - fixed + offset_by * (used - fixed)) % max(1, number_of - fixed)
        return jnp.zeros((number_of,), jnp.int32).at[sequence[jnp.where(places < fixed, places, passed)]].set(jnp.asarray(sizes, jnp.int32))

    sizes = jnp.where(number % 4 == 0, named(packed, number // 4), named(usual, number - number // 4 - 1))
    mixed = jax.random.permutation(jax.random.fold_in(own, 3), number_of)
    donor, taker = mixed[0:number_of // 2 * 2:2], mixed[1:number_of // 2 * 2:2]
    slack = jnp.minimum(sizes[donor] - 1, most - sizes[taker]) // 2
    slack = jnp.where((donor == sequence[0]) | (taker == sequence[0]) | (sizes[taker] == 0), 0, jnp.maximum(slack, 0))
    passed = jax.random.randint(jax.random.fold_in(own, 4), (number_of // 2,), 0, 1 << 20) % (slack + 1)
    sizes = sizes.at[donor].add(-passed).at[taker].add(passed)
    labels = jnp.searchsorted(jnp.cumsum(sizes), jnp.arange(rows * top), side="right").astype(jnp.int32)
    grid = labels.reshape(top, rows).T
    grid = grid[jax.random.permutation(jax.random.fold_in(own, 1), rows)]
    offset_by = jax.random.randint(jax.random.fold_in(own, 2), (rows, 1), 0, top)
    return jnp.take_along_axis(grid, (jnp.arange(top)[None, :] + offset_by) % top, axis=1)


def load_shares(number_of, total, bound, lean, full):
    loads = [(1 << 20) // math.isqrt(standing ** lean) + 1 for standing in range(1, number_of + 1)]
    largest = bound if full else min(bound, max(-(-total // number_of), total * loads[0] // sum(loads)))
    least = 1 if total - largest >= number_of - 1 else 0
    counts, rest = [largest] + [least] * (number_of - 1), total - largest - least * (number_of - 1)
    while rest > 0:
        free = [i for i in range(1, number_of) if counts[i] < largest] or [i for i in range(1, number_of) if counts[i] < bound]
        whole, remaining = sum([loads[i] for i in free]), rest
        for i in free:
            more = min(bound - counts[i], max(1, remaining * loads[i] // whole), rest)
            counts[i] = counts[i] + more
            rest = rest - more
    return np.array(counts)


def centred(key, extent, scale, most, cuts=(), kind=jnp.bfloat16):
    factor_of = steps_of(key, extent, cuts, -0.22, 0.18) if cuts else 1.0
    values = jax.random.normal(key, extent, jnp.float32) * scale * factor_of
    return jnp.minimum(jnp.maximum(values, -most), most).astype(kind)


def setup_inputs(seed: int = 0) -> dict:
    key_of = jax.random.split(jax.random.key(seed), 10)
    fluid_state = centred(key_of[0], (4, NZ, NY, NX), 1.0, 6.0, ((2, 8), (3, 4)), jnp.float32)
    particle_pos = centred(key_of[1], (3, NPART), 1.0, 6.0, ((1, 32),), jnp.float32)
    particle_motion = centred(key_of[2], (6, NPART), 1.0, 6.0, ((1, 32),), jnp.float32)
    particle_radius = jnp.clip(0.5 + 0.5 * jax.random.uniform(key_of[3], (NPART,), jnp.float32) ** steps_of(key_of[3], (NPART,), ((0, 32),), -0.2, 0.2), 0.5, 1.0)
    particle_temp = centred(key_of[4], (NPART,), 1.0, 6.0, ((0, 32),), jnp.float32)
    particle_cell = touch_ends(jax.random.randint(key_of[5], (NPART,), 0, CELLS_DEV), jax.random.fold_in(key_of[5], 1), 0, CELLS_DEV - 1).astype(jnp.int32)
    particle_box_keys = jax.random.split(jax.random.fold_in(key_of[6], 1), NPART // P_DEV)
    particle_box_turns = jax.random.permutation(jax.random.fold_in(key_of[6], 3), NPART // P_DEV)
    particle_box = jax.vmap(lambda own, number: assign_block(jax.random.fold_in(key_of[6], 2), own, number, P_DEV, DEVICES, 1, C, 1))(particle_box_keys, particle_box_turns).reshape((NPART, 1))
    box_owner = jax.random.permutation(key_of[7], DEVICES).astype(jnp.int32)
    contact_mask = touch_ends((jax.random.randint(key_of[8], (NBLK, BLOCK, BLOCK), 0, 8) < 1).astype(jnp.int32), jax.random.fold_in(key_of[8], 1), 0, 1)
    return dict(fluid_state=fluid_state, particle_pos=particle_pos, particle_motion=particle_motion, particle_radius=particle_radius, particle_temp=particle_temp, particle_cell=particle_cell, particle_box=particle_box, box_owner=box_owner, contact_mask=contact_mask)


TIME_STEP = 0.1
STIFFNESS = 0.5
DAMPING_RATE = 0.2
ROTATION_DRAG = 0.1
DRAG_COEFF = 4.0
CONDUCTION = 0.3
HEAT_TRANSFER = 4.0
GRAVITY = 0.3
COUPLING = 4.0
CENTRE_WEIGHT = 0.25
SIDE_WEIGHT = 0.125


def smooth(field):
    padded = jnp.pad(field, ((0, 0), (1, 1), (1, 1), (1, 1)))
    interior = padded[:, 1:-1, 1:-1, 1:-1]
    beside_all = padded[:, 2:, 1:-1, 1:-1] + padded[:, :-2, 1:-1, 1:-1]
    beside_all = beside_all + padded[:, 1:-1, 2:, 1:-1] + padded[:, 1:-1, :-2, 1:-1]
    beside_all = beside_all + padded[:, 1:-1, 1:-1, 2:] + padded[:, 1:-1, 1:-1, :-2]
    return CENTRE_WEIGHT * interior + SIDE_WEIGHT * beside_all


def contact(arrived, mask_blocks):
    position = arrived[0:3]
    velocity = arrived[3:6]
    angular = arrived[6:9]
    fluid_vel = arrived[9:12]
    radius = arrived[12]
    solid_temp = arrived[13]
    gas_temp = arrived[14]
    occupied = (radius > 0.0).astype(jnp.float32)
    pair_mask = mask_blocks.astype(jnp.float32) * occupied[:, :, None] * occupied[:, None, :]
    distance = jnp.zeros(pair_mask.shape, jnp.float32)
    for component in range(3):
        offset = position[component][:, :, None] - position[component][:, None, :]
        distance = distance + offset * offset
    reach_sq = (radius[:, :, None] + radius[:, None, :]) ** 2 + 1.0
    weight = pair_mask * jnp.exp(-distance / reach_sq)
    weight_sum = jnp.sum(weight, axis=2)
    stacked = jnp.concatenate([position, velocity, angular, solid_temp[None]], axis=0)
    mixed = jnp.einsum("bij,cbj->cbi", weight, stacked, precision=lax.Precision.HIGHEST)
    spring = position * weight_sum - mixed[0:3]
    damping = velocity * weight_sum - mixed[3:6]
    drag_force = DRAG_COEFF / (radius * radius + 0.25) * (fluid_vel - velocity)
    upward = jnp.array([0.0, 0.0, 1.0], jnp.float32)[:, None, None]
    velocity_next = velocity + TIME_STEP * (STIFFNESS * spring - DAMPING_RATE * damping + drag_force) - TIME_STEP * GRAVITY * upward
    angular_next = angular - TIME_STEP * ROTATION_DRAG * (angular * weight_sum + mixed[6:9])
    temp_next = solid_temp + TIME_STEP * (CONDUCTION * (mixed[9] - solid_temp * weight_sum) + HEAT_TRANSFER * (gas_temp - solid_temp))
    return jnp.concatenate([velocity_next, angular_next, drag_force, temp_next[None]], axis=0)


def reference(fluid_state, particle_pos, particle_motion, particle_radius, particle_temp, particle_cell, particle_box, box_owner, contact_mask):
    devices = N_GX * N_GY
    peer_slots = 2 * P_DEV // devices
    particle_ids = jnp.arange(NPART, dtype=jnp.int32)
    home_dev = particle_ids // P_DEV
    owner_dev = box_owner[particle_box[:, 0]].astype(jnp.int32)
    group_key = (home_dev * devices + owner_dev).astype(jnp.int32)
    sort_order = jnp.argsort(group_key, stable=True).astype(jnp.int32)
    group_counts = jnp.zeros((devices * devices,), jnp.int32).at[group_key].add(1)
    group_starts = jnp.cumsum(group_counts).astype(jnp.int32) - group_counts
    rank_sorted = particle_ids - group_starts[group_key[sort_order]]
    slot_rank = jnp.zeros((NPART,), jnp.int32).at[sort_order].set(rank_sorted)
    target = owner_dev * (2 * P_DEV) + home_dev * peer_slots + slot_rank
    cell_z = particle_cell // (CY * CX)
    cell_y = (particle_cell // CX) % CY
    cell_x = particle_cell % CX
    global_y = (home_dev % N_GY) * CY + cell_y
    global_x = (home_dev // N_GY) * CX + cell_x
    filtered = smooth(fluid_state)
    at_particle = filtered[:, cell_z, global_y, global_x]
    payload = jnp.concatenate([particle_pos, particle_motion, at_particle[0:3], particle_radius[None], particle_temp[None], at_particle[3:4]], axis=0)
    buffer = jnp.zeros((15, 2 * NPART), jnp.float32).at[:, target].set(payload)
    per_block = 2 * P_DEV // BLOCK
    blocks = buffer.reshape(15, devices, per_block, BLOCK).transpose(1, 0, 2, 3)
    mask_blocks = contact_mask.reshape(devices, per_block, BLOCK, BLOCK)

    def contact_pair(pieces):
        return contact(pieces[0], pieces[1])

    result = lax.map(contact_pair, (blocks, mask_blocks))
    result = result.transpose(1, 0, 2, 3).reshape(10, 2 * NPART)
    returned = result[:, target]
    particle_next = jnp.concatenate([returned[0:6], returned[9:10]], axis=0)
    volume = particle_radius ** 3
    deposit_terms = jnp.concatenate([volume[None], -volume[None] * returned[6:9], (volume * (returned[9] - at_particle[3]))[None]], axis=0)
    deposits = jnp.zeros((5, NZ, NY, NX), jnp.float32).at[:, cell_z, global_y, global_x].add(deposit_terms)
    spread = smooth(deposits)
    crowding = 1.0 + COUPLING * spread[0]
    void_fraction = 1.0 / crowding
    fluid_next = jnp.concatenate([fluid_state[0:3] + TIME_STEP * COUPLING * spread[1:4] * crowding, fluid_state[3:4] + TIME_STEP * COUPLING * spread[4:5] * crowding], axis=0)
    return fluid_next, void_fraction, particle_next
```

```python
import functools

import jax
import jax.numpy as jnp
from jax import lax
from jax.experimental import pallas as pl
from jax.experimental.pallas import tpu as pltpu
from jax.sharding import PartitionSpec as P

BLOCK = 128
TIME_STEP = 0.1
STIFFNESS = 0.5
DAMPING_RATE = 0.2
ROTATION_DRAG = 0.1
DRAG_COEFF = 4.0
CONDUCTION = 0.3
HEAT_TRANSFER = 4.0
GRAVITY = 0.3
COUPLING = 4.0
CENTRE_WEIGHT = 0.25
SIDE_WEIGHT = 0.125

F32 = jnp.float32
BF16 = jnp.bfloat16
VMEM = pltpu.VMEM
NT = (((1,), (1,)), ((), ()))
NN = (((1,), (0,)), ((), ()))


def split(value):
    high = value.astype(BF16)
    return high, (value - high.astype(F32)).astype(BF16)


def hot(count, row):
    places = lax.broadcasted_iota(jnp.int32, (count, row.shape[1]), 0)
    return jnp.where(places == row, 1.0, 0.0).astype(BF16)


def rank_hot(ranks, slots):
    places = lax.broadcasted_iota(jnp.int32, (slots, ranks.shape[1]), 0)
    return jnp.where(places == ranks, 1.0, 0.0).astype(BF16)


def place_kernel(
    owner_ref, box_ref, pos_ref, motion_ref, radius_ref, temp_ref,
    out_ref, rank_ref, box_of, first_acc, second_acc, *, chunk
):
    devices, rows, _ = out_ref.shape
    layers = rows // 12
    slots = layers * BLOCK
    particles = box_ref.shape[1]

    def invert(b, _):
        box_of[owner_ref[b]] = b
        return 0

    lax.fori_loop(0, devices, invert, 0)
    first_acc[...] = jnp.zeros_like(first_acc)
    second_acc[...] = jnp.zeros_like(second_acc)
    sub = 256
    above = (
        lax.broadcasted_iota(jnp.int32, (sub, sub), 0) < lax.broadcasted_iota(jnp.int32, (sub, sub), 1)
    )
    above = jnp.where(above, 1.0, 0.0).astype(BF16)

    def step(k, carry):
        base = pl.multiple_of(k * chunk, chunk)
        here = pl.ds(base, chunk)
        boxes = box_ref[:, here]
        pieces = []
        for s in range(chunk // sub):
            mine = boxes[:, s * sub : (s + 1) * sub]
            chosen = lax.broadcasted_iota(jnp.int32, (devices, sub), 0) == mine
            ones = jnp.where(chosen, 1.0, 0.0)
            earlier = lax.dot_general(ones.astype(BF16), above, NN, preferred_element_type=F32) + carry
            pieces.append(jnp.sum(jnp.where(chosen, earlier, 0.0), axis=0, keepdims=True))
            carry = carry + jnp.sum(ones, axis=1, keepdims=True)
        ranks = jnp.concatenate(pieces, axis=1).astype(jnp.int32)
        rank_ref[:, here] = ranks
        hot_rank = rank_hot(ranks, slots)
        pos = pos_ref[:, here]
        motion = motion_ref[:, here]
        push = TIME_STEP * STIFFNESS * pos - TIME_STEP * DAMPING_RATE * motion[0:3]
        spin = -TIME_STEP * ROTATION_DRAG * motion[3:6]
        heat = -TIME_STEP * CONDUCTION * temp_ref[:, here]
        first = jnp.concatenate([push, spin, heat, jnp.ones((1, chunk), F32)], axis=0)
        second = jnp.concatenate([pos, radius_ref[:, here]], axis=0)
        first = jnp.concatenate(split(first), axis=0)
        second = jnp.concatenate(split(second), axis=0)
        box16 = jnp.broadcast_to(boxes, (16, chunk)).astype(F32).astype(BF16)
        first_parts = []
        second_parts = []
        for o in range(devices):
            mine = box16 == box_of[o].astype(F32).astype(BF16)
            first_parts.append(jnp.where(mine, first, jnp.zeros_like(first)))
            second_parts.append(jnp.where(mine[0:8], second, jnp.zeros_like(second)))
        first_acc[...] += lax.dot_general(
            jnp.concatenate(first_parts, axis=0), hot_rank, NT, preferred_element_type=F32
        )
        second_acc[...] += lax.dot_general(
            jnp.concatenate(second_parts, axis=0), hot_rank, NT, preferred_element_type=F32
        )
        return carry

    lax.fori_loop(0, particles // chunk, step, jnp.zeros((devices, 1), F32))

    def finish(o, _):
        first = first_acc[pl.ds(pl.multiple_of(16 * o, 16), 8), :] + first_acc[pl.ds(pl.multiple_of(16 * o + 8, 8), 8), :]
        second = second_acc[pl.ds(pl.multiple_of(8 * o, 8), 8), :]
        second = second[0:4] + second[4:8]
        for q in range(layers):
            lanes = slice(q * BLOCK, (q + 1) * BLOCK)
            out_ref[o, 8 * q : 8 * q + 8, :] = first[:, lanes]
            out_ref[o, 8 * layers + 4 * q : 8 * layers + 4 * q + 4, :] = second[:, lanes]
        return 0

    lax.fori_loop(0, devices, finish, 0)


def place(box_owner, boxes, pos, motion, radius, temp, slots):
    devices = box_owner.shape[0]
    particles = pos.shape[1]
    layers = slots // BLOCK
    vmem = pl.BlockSpec(memory_space=VMEM)
    return pl.pallas_call(
        functools.partial(place_kernel, chunk=1024),
        out_shape=(
            jax.ShapeDtypeStruct((devices, 12 * layers, BLOCK), F32),
            jax.ShapeDtypeStruct((1, particles), jnp.int32),
        ),
        in_specs=[pl.BlockSpec(memory_space=pltpu.SMEM)] + [vmem] * 5,
        out_specs=(vmem, vmem),
        scratch_shapes=[
            pltpu.SMEM((devices,), jnp.int32),
            VMEM((16 * devices, slots), F32),
            VMEM((8 * devices, slots), F32),
        ],
        compiler_params=pltpu.CompilerParams(vmem_limit_bytes=40 << 20),
        cost_estimate=pl.CostEstimate(
            flops=2 * 24 * devices * slots * particles, bytes_accessed=1 << 20, transcendentals=0
        ),
        name="place_slots",
    )(box_owner, boxes, pos, motion, radius, temp)


def contact_kernel(slot_ref, mask_ref, out_ref):
    homes, rows, _ = slot_ref.shape
    layers = rows // 12
    sign = lax.broadcasted_iota(jnp.int32, (8, 1), 0)
    sign = jnp.where((sign >= 3) & (sign < 6), 1.0, -1.0)
    for s in range(homes):
        for q in range(layers):
            mixed = slot_ref[s, 8 * q : 8 * q + 8, :]
            near = slot_ref[s, 8 * layers + 4 * q : 8 * layers + 4 * q + 4, :]
            near_i = jnp.transpose(jnp.concatenate([near, near], axis=0))
            distance = None
            for axis in range(3):
                offset = near_i[:, axis : axis + 1] - near[axis : axis + 1, :]
                distance = offset * offset if distance is None else distance + offset * offset
            reach = near_i[:, 3:4] + near[3:4, :]
            reach = reach * reach + 1.0
            inverse = pl.reciprocal(reach, approx=True)
            inverse = inverse * (2.0 - reach * inverse)
            weight = mask_ref[s * layers + q].astype(F32) * jnp.exp(-distance * inverse)
            weight_high, weight_low = split(weight)
            mixed_high, mixed_low = split(mixed)
            both = jnp.concatenate([mixed_high, mixed_low], axis=0)
            sums = lax.dot_general(both, weight_high, NT, preferred_element_type=F32)
            more = lax.dot_general(both, weight_low, NT, preferred_element_type=F32)
            sums = sums + more
            sums = sums[0:8] + sums[8:16]
            out_ref[s, 8 * q : 8 * q + 8, :] = mixed * sums[7:8] + sign * sums


def contact(arrived, mask):
    devices, rows, _ = arrived.shape
    layers = rows // 12
    blocks = mask.shape[0]
    step = 2 if layers > 1 else 8
    return pl.pallas_call(
        contact_kernel,
        grid=(devices // step,),
        out_shape=jax.ShapeDtypeStruct((devices, 8 * layers, BLOCK), F32),
        in_specs=[
            pl.BlockSpec((step, rows, BLOCK), lambda h: (h, 0, 0)),
            pl.BlockSpec((step * layers, BLOCK, BLOCK), lambda h: (h, 0, 0)),
        ],
        out_specs=pl.BlockSpec((step, 8 * layers, BLOCK), lambda h: (h, 0, 0)),
        compiler_params=pltpu.CompilerParams(vmem_limit_bytes=40 << 20),
        cost_estimate=pl.CostEstimate(
            flops=64 * blocks * BLOCK * BLOCK, bytes_accessed=blocks * BLOCK * BLOCK * 4, transcendentals=0
        ),
        name="contact_blocks",
    )(arrived, mask)


def smoothed(centre, y_first, y_last, x_first, x_last):
    layers, rows, cols = centre.shape
    zero = jnp.zeros((1, rows, cols), F32)
    up = jnp.concatenate([centre[1:], zero], axis=0)
    down = jnp.concatenate([zero, centre[:-1]], axis=0)
    row = lax.broadcasted_iota(jnp.int32, (1, rows, cols), 1)
    col = lax.broadcasted_iota(jnp.int32, (1, rows, cols), 2)
    back = jnp.where(row == 0, y_first, pltpu.roll(centre, 1, 1))
    front = jnp.where(row == rows - 1, y_last, pltpu.roll(centre, rows - 1, 1))
    left = jnp.where(col == 0, x_first, pltpu.roll(centre, 1, 2))
    right = jnp.where(col == cols - 1, x_last, pltpu.roll(centre, cols - 1, 2))
    return CENTRE_WEIGHT * centre + SIDE_WEIGHT * ((up + down) + (back + front) + (left + right))


def columns(edge, layers, rows):
    count = edge.shape[0]
    if count < 8:
        edge = jnp.concatenate([edge] * (8 // count), axis=0)
    turned = jnp.transpose(edge)
    parts = [turned[:, a : a + 1] for a in range(count)]
    return jnp.concatenate(parts, axis=0).reshape(layers, rows, 1)


def smooth_field(field_ref, y0_ref, y1_ref, x0_ref, x1_ref, k):
    _, layers, rows, cols = field_ref.shape
    per = layers * rows // BLOCK
    x0 = columns(x0_ref[k * per : (k + 1) * per, :], layers, rows)
    x1 = columns(x1_ref[k * per : (k + 1) * per, :], layers, rows)
    y0 = y0_ref[k].reshape(layers, 1, cols)
    y1 = y1_ref[k].reshape(layers, 1, cols)
    return smoothed(field_ref[k], y0, y1, x0, x1)


def write_edges(field, k, y0_ref, y1_ref, x0_ref, x1_ref):
    layers, rows, cols = field.shape
    y0_ref[k] = field[:, 0, :]
    y1_ref[k] = field[:, rows - 1, :]
    flat = field.reshape(layers * rows, cols)
    for a in range(layers * rows // BLOCK):
        turned = jnp.transpose(flat[a * BLOCK : (a + 1) * BLOCK, :])
        at = k * (layers * rows // BLOCK) + a
        x0_ref[at : at + 1, :] = turned[0:1, :]
        x1_ref[at : at + 1, :] = turned[cols - 1 : cols, :]


def paired_rows(pairs, layers, rows, scratch):
    half = pairs.shape[0]
    cols = pairs.shape[1] // 2
    scratch[pl.ds(0, half, stride=2), :] = pairs[:, :cols]
    scratch[pl.ds(1, half, stride=2), :] = pairs[:, cols:]
    return scratch[...].reshape(layers, rows, cols)


def fluid_kernel(
    fluid_ref, y0_ref, y1_ref, x0_ref, x1_ref, cell_ref, motion_ref, radius_ref, temp_ref,
    base_ref, dep_ref, dy0_ref, dy1_ref, dx0_ref, dx1_ref,
    table, rows_scratch, acc, *, chunk
):
    fields, layers, rows, cols = fluid_ref.shape
    half = layers * rows // 2
    wide = 2 * cols
    particles = cell_ref.shape[1]
    for k in range(fields):
        rows_scratch[...] = smooth_field(fluid_ref, y0_ref, y1_ref, x0_ref, x1_ref, k).reshape(layers * rows, cols)
        here = slice(k * half, (k + 1) * half)
        for part in range(2):
            high, low = split(rows_scratch[pl.ds(part, half, stride=2), :])
            table[0, here, part * cols : (part + 1) * cols] = high
            table[1, here, part * cols : (part + 1) * cols] = low
    acc[...] = jnp.zeros_like(acc)

    def step(i, _):
        here = pl.ds(pl.multiple_of(i * chunk, chunk), chunk)
        cells = cell_ref[:, here]
        hot_low = hot(wide, cells % wide)
        place_high = cells // wide
        hot_high = hot(half, place_high)
        found = lax.dot_general(table[0], hot_low, NN, preferred_element_type=F32)
        found = found + lax.dot_general(table[1], hot_low, NN, preferred_element_type=F32)
        mine = lax.broadcasted_iota(jnp.int32, (half, chunk), 0) == place_high
        seen = [
            jnp.sum(jnp.where(mine, found[k * half : (k + 1) * half], 0.0), axis=0, keepdims=True)
            for k in range(fields)
        ]
        motion = motion_ref[:, here]
        radius = radius_ref[:, here]
        temp = temp_ref[:, here]
        fluid_vel = jnp.concatenate(seen[0:3], axis=0)
        drag = DRAG_COEFF / (radius * radius + 0.25) * (fluid_vel - motion[0:3])
        upward = lax.broadcasted_iota(jnp.int32, (3, 1), 0) == 2
        moved = motion[0:3] + TIME_STEP * drag - jnp.where(upward, TIME_STEP * GRAVITY, 0.0)
        warmed = temp + TIME_STEP * HEAT_TRANSFER * (seen[3] - temp)
        base_ref[:, here] = jnp.concatenate([moved, motion[3:6], warmed, seen[3]], axis=0)
        volume = radius * radius * radius
        terms = jnp.concatenate([volume, -volume * drag], axis=0)
        high, low = split(terms)
        parts = []
        for piece in (high, low):
            parts.append(jnp.concatenate([hot_high * piece[k : k + 1] for k in range(4)], axis=0))
        total = lax.dot_general(parts[0], hot_low, NT, preferred_element_type=F32)
        acc[...] += total + lax.dot_general(parts[1], hot_low, NT, preferred_element_type=F32)
        return 0

    lax.fori_loop(0, particles // chunk, step, 0)
    for k in range(fields):
        field = paired_rows(acc[k * half : (k + 1) * half, :], layers, rows, rows_scratch)
        dep_ref[k] = field
        write_edges(field, k, dy0_ref, dy1_ref, dx0_ref, dx1_ref)


def edge_shapes(fields, layers, rows, cols):
    y_edge = jax.ShapeDtypeStruct((fields, layers, cols), F32)
    x_edge = jax.ShapeDtypeStruct((fields * layers * rows // BLOCK, BLOCK), F32)
    return (y_edge, y_edge, x_edge, x_edge)


def see_and_deposit(fluid, halo, cells, motion, radius, temp):
    fields, layers, rows, cols = fluid.shape
    particles = cells.shape[1]
    vmem = pl.BlockSpec(memory_space=VMEM)
    return pl.pallas_call(
        functools.partial(fluid_kernel, chunk=512),
        out_shape=(
            jax.ShapeDtypeStruct((8, particles), F32),
            jax.ShapeDtypeStruct(fluid.shape, F32),
        ) + edge_shapes(fields, layers, rows, cols),
        in_specs=[vmem] * 9,
        out_specs=(vmem,) * 6,
        scratch_shapes=[
            VMEM((2, fields * layers * rows // 2, 2 * cols), BF16),
            VMEM((layers * rows, cols), F32),
            VMEM((fields * layers * rows // 2, 2 * cols), F32),
        ],
        compiler_params=pltpu.CompilerParams(vmem_limit_bytes=40 << 20),
        cost_estimate=pl.CostEstimate(
            flops=16 * fields * layers * rows * cols * particles, bytes_accessed=2 << 20, transcendentals=0
        ),
        name="see_and_deposit",
    )(fluid, *halo, cells, motion, radius, temp)


def fetch_kernel(
    owner_ref, back_ref, box_ref, rank_ref, cell_ref, radius_ref, base_ref,
    next_ref, dep_ref, dy0_ref, dy1_ref, dx0_ref, dx1_ref,
    box_of, table, acc, rows_scratch, *, chunk, rows
):
    devices, tall, _ = back_ref.shape
    layers = tall // 8
    slots = layers * BLOCK
    particles = box_ref.shape[1]
    half, wide = acc.shape

    def invert(b, _):
        box_of[owner_ref[b]] = b
        return 0

    lax.fori_loop(0, devices, invert, 0)
    for o in range(0, devices, 2):
        for q in range(layers):
            pair = jnp.concatenate(
                [back_ref[o, 8 * q : 8 * q + 8, :], back_ref[o + 1, 8 * q : 8 * q + 8, :]], axis=0
            )
            high, low = split(pair)
            table[0, 8 * o : 8 * o + 16, q * BLOCK : (q + 1) * BLOCK] = high
            table[1, 8 * o : 8 * o + 16, q * BLOCK : (q + 1) * BLOCK] = low
    acc[...] = jnp.zeros_like(acc)

    def step(i, _):
        here = pl.ds(pl.multiple_of(i * chunk, chunk), chunk)
        hot_rank = rank_hot(rank_ref[:, here], slots)
        found = lax.dot_general(table[0], hot_rank, NN, preferred_element_type=F32)
        found = found + lax.dot_general(table[1], hot_rank, NN, preferred_element_type=F32)
        boxes = jnp.broadcast_to(box_ref[:, here], (8, chunk))
        gained = jnp.zeros((8, chunk), F32)
        for o in range(devices):
            gained = jnp.where(boxes == box_of[o], found[8 * o : 8 * o + 8], gained)
        base = base_ref[:, here]
        total = base[0:7] + gained[0:7]
        next_ref[:, here] = total
        radius = radius_ref[:, here]
        term = radius * radius * radius * (total[6:7] - base[7:8])
        high, low = split(term)
        cells = cell_ref[:, here]
        hot_low = hot(wide, cells % wide)
        hot_high = hot(half, cells // wide)
        added = lax.dot_general(hot_high * high, hot_low, NT, preferred_element_type=F32)
        acc[...] += added + lax.dot_general(hot_high * low, hot_low, NT, preferred_element_type=F32)
        return 0

    lax.fori_loop(0, particles // chunk, step, 0)
    field = paired_rows(acc[...], 2 * half // rows, rows, rows_scratch)
    dep_ref[0] = field
    write_edges(field, 0, dy0_ref, dy1_ref, dx0_ref, dx1_ref)


def fetch(box_owner, back, boxes, ranks, cells, radius, base, grid):
    devices, tall, _ = back.shape
    layers, rows, cols = grid
    particles = boxes.shape[1]
    slots = tall // 8 * BLOCK
    half = layers * rows // 2
    vmem = pl.BlockSpec(memory_space=VMEM)
    return pl.pallas_call(
        functools.partial(fetch_kernel, chunk=1024, rows=rows),
        out_shape=(
            jax.ShapeDtypeStruct((7, particles), F32),
            jax.ShapeDtypeStruct((1,) + grid, F32),
        ) + edge_shapes(1, layers, rows, cols),
        in_specs=[pl.BlockSpec(memory_space=pltpu.SMEM)] + [vmem] * 6,
        out_specs=(vmem,) * 6,
        scratch_shapes=[
            pltpu.SMEM((devices,), jnp.int32),
            VMEM((2, 8 * devices, slots), BF16),
            VMEM((half, 2 * cols), F32),
            VMEM((layers * rows, cols), F32),
        ],
        compiler_params=pltpu.CompilerParams(vmem_limit_bytes=40 << 20),
        cost_estimate=pl.CostEstimate(
            flops=32 * devices * slots * particles, bytes_accessed=2 << 20, transcendentals=0
        ),
        name="fetch_and_deposit",
    )(box_owner, back, boxes, ranks, cells, radius, base)


def spread_kernel(
    dep_ref, y0_ref, y1_ref, x0_ref, x1_ref, fluid_ref, next_ref, void_ref, crowd_ref
):
    crowding = 1.0 + COUPLING * smooth_field(dep_ref, y0_ref, y1_ref, x0_ref, x1_ref, 0)
    crowd_ref[...] = crowding
    void_ref[...] = 1.0 / crowding
    for k in range(3):
        spread = smooth_field(dep_ref, y0_ref, y1_ref, x0_ref, x1_ref, k + 1)
        next_ref[k] = fluid_ref[k] + TIME_STEP * COUPLING * spread * crowding


def spread_velocity(dep, halo, fluid):
    vmem = pl.BlockSpec(memory_space=VMEM)
    grid = jax.ShapeDtypeStruct(fluid.shape[1:], F32)
    return pl.pallas_call(
        spread_kernel,
        out_shape=(jax.ShapeDtypeStruct(fluid.shape, F32), grid, grid),
        in_specs=[vmem] * 6,
        out_specs=(vmem,) * 3,
        compiler_params=pltpu.CompilerParams(vmem_limit_bytes=40 << 20),
        cost_estimate=pl.CostEstimate(flops=16 * fluid.size, bytes_accessed=2 << 20, transcendentals=0),
        name="spread_velocity",
    )(dep, *halo, fluid)


def heat_kernel(next_in, dep_ref, y0_ref, y1_ref, x0_ref, x1_ref, fluid_ref, crowd_ref, next_ref):
    spread = smooth_field(dep_ref, y0_ref, y1_ref, x0_ref, x1_ref, 0)
    next_ref[0] = fluid_ref[0] + TIME_STEP * COUPLING * spread * crowd_ref[...]


def spread_heat(fluid_next, dep, halo, fluid, crowding):
    layers, rows, cols = crowding.shape
    whole = [pl.BlockSpec(a.shape, functools.partial(lambda n, i: (0,) * n, a.ndim)) for a in (dep,) + tuple(halo)]
    last = pl.BlockSpec((1, layers, rows, cols), lambda i: (3, 0, 0, 0))
    return pl.pallas_call(
        heat_kernel,
        grid=(1,),
        out_shape=jax.ShapeDtypeStruct(fluid_next.shape, F32),
        in_specs=[pl.BlockSpec(memory_space=pl.ANY)] + whole + [last, pl.BlockSpec((layers, rows, cols), lambda i: (0, 0, 0))],
        out_specs=last,
        input_output_aliases={0: 0},
        compiler_params=pltpu.CompilerParams(vmem_limit_bytes=40 << 20),
        cost_estimate=pl.CostEstimate(flops=16 * crowding.size, bytes_accessed=1 << 20, transcendentals=0),
        name="spread_heat",
    )(fluid_next, dep, *halo, fluid, crowding)


def halo_of(y_first, y_last, x_first, x_last):
    def moved(value, axis, step):
        size = lax.axis_size(axis)
        pairs = [(i, i + step) for i in range(size) if 0 <= i + step < size]
        return lax.ppermute(value, axis, pairs)

    return (
        moved(y_last, "gy", 1),
        moved(y_first, "gy", -1),
        moved(x_last, "gx", 1),
        moved(x_first, "gx", -1),
    )


def shards(
    fluid_state, particle_pos, particle_motion, particle_radius, particle_temp,
    particle_cell, particle_box, box_owner, contact_mask,
):
    devices = lax.axis_size(("gx", "gy"))
    particles = particle_pos.shape[1]
    slots = 2 * particles // devices
    fields, layers, rows, cols = fluid_state.shape
    boxes = particle_box.reshape(1, particles)
    radius = particle_radius.reshape(1, particles)
    temp = particle_temp.reshape(1, particles)
    cells = particle_cell.reshape(1, particles)

    outgoing, ranks = place(box_owner, boxes, particle_pos, particle_motion, radius, temp, slots)
    arrived = lax.all_to_all(outgoing, ("gx", "gy"), split_axis=0, concat_axis=0, tiled=True)
    result = contact(arrived, contact_mask)
    back = lax.all_to_all(result, ("gx", "gy"), split_axis=0, concat_axis=0, tiled=True)

    fluid_halo = halo_of(
        fluid_state[:, :, 0, :],
        fluid_state[:, :, rows - 1, :],
        fluid_state[:, :, :, 0].reshape(-1, BLOCK),
        fluid_state[:, :, :, cols - 1].reshape(-1, BLOCK),
    )
    seen = see_and_deposit(fluid_state, fluid_halo, cells, particle_motion, radius, temp)
    base, deposits = seen[0:2]
    fluid_next, void_fraction, crowding = spread_velocity(deposits, halo_of(*seen[2:6]), fluid_state)

    fetched = fetch(box_owner, back, boxes, ranks, cells, radius, base, (layers, rows, cols))
    particle_next, heat = fetched[0:2]
    fluid_next = spread_heat(fluid_next, heat, halo_of(*fetched[2:6]), fluid_state, crowding)
    return (fluid_next, void_fraction, particle_next)


def solution(mesh):
    in_specs = (
        P(None, None, "gy", "gx"),
        P(None, ("gx", "gy")),
        P(None, ("gx", "gy")),
        P(("gx", "gy")),
        P(("gx", "gy")),
        P(("gx", "gy")),
        P(("gx", "gy"), None),
        P(),
        P(("gx", "gy"), None, None),
    )
    out_specs = (P(None, None, "gy", "gx"), P(None, "gy", "gx"), P(None, ("gx", "gy")))
    return jax.shard_map(shards, mesh=mesh, in_specs=in_specs, out_specs=out_specs, check_vma=False)
```

```python
import functools

import jax
import jax.numpy as jnp
from jax import lax
from jax.experimental import pallas as pl
from jax.experimental.pallas import tpu as pltpu
from jax.sharding import PartitionSpec as P

BLOCK = 128
TIME_STEP = 0.1
STIFFNESS = 0.5
DAMPING_RATE = 0.2
ROTATION_DRAG = 0.1
DRAG_COEFF = 4.0
CONDUCTION = 0.3
HEAT_TRANSFER = 4.0
GRAVITY = 0.3
COUPLING = 4.0
CENTRE_WEIGHT = 0.25
SIDE_WEIGHT = 0.125

F32 = jnp.float32
BF16 = jnp.bfloat16
VMEM = pltpu.VMEM
NT = (((1,), (1,)), ((), ()))
NN = (((1,), (0,)), ((), ()))


def split(value):
    high = value.astype(BF16)
    return high, (value - high.astype(F32)).astype(BF16)


def hot(count, row):
    places = lax.broadcasted_iota(jnp.int32, (count, row.shape[1]), 0)
    return jnp.where(places == row, 1.0, 0.0).astype(BF16)


def invert(owner_ref, box_of):
    def step(b, _):
        box_of[owner_ref[b]] = b
        return 0

    lax.fori_loop(0, owner_ref.shape[0], step, 0)


WINDOW = 256
CHUNK = 1024


def place_kernel(
    owner_ref, box_ref, pos_ref, motion_ref, radius_ref, temp_ref,
    out_ref, slot_ref, spot_ref, tile_ref,
    box_of, tile_of, acc, done
):
    devices, rows, _ = out_ref.shape
    layers = rows // 12
    slots = layers * BLOCK
    particles = box_ref.shape[1]
    sub = 256
    invert(owner_ref, box_of)
    acc[...] = jnp.zeros_like(acc)

    box_row = lax.broadcasted_iota(jnp.int32, (devices, 1), 0)
    owner_column = jnp.zeros((devices, 1), F32)
    for b in range(devices):
        owner_column = jnp.where(box_row == b, owner_ref[b].astype(F32), owner_column)
    above = (
        lax.broadcasted_iota(jnp.int32, (sub, sub), 0) < lax.broadcasted_iota(jnp.int32, (sub, sub), 1)
    )
    above = jnp.where(above, 1.0, 0.0).astype(BF16)
    lane = lax.broadcasted_iota(jnp.int32, (devices, BLOCK), 1)
    tiles = jnp.zeros((devices, BLOCK), F32)
    spans = jnp.zeros((8, BLOCK), F32)
    carry = jnp.zeros((devices, 1), F32)
    per_chunk = CHUNK // sub
    for c in range(particles // CHUNK):
        chosen = []
        for s in range(per_chunk):
            at = c * CHUNK + s * sub
            chosen.append(
                lax.broadcasted_iota(jnp.int32, (devices, sub), 0) == box_ref[:, at : at + sub]
            )
        ones = [jnp.where(mine, 1.0, 0.0) for mine in chosen]
        earlier = lax.dot_general(
            jnp.concatenate(ones, axis=0).astype(BF16), above, NN, preferred_element_type=F32
        )
        tile = jnp.minimum(jnp.floor(carry * (1.0 / BLOCK)), layers - 1.0)
        tiles = jnp.where(lane == c, tile, tiles)
        highest = jnp.zeros((1, 1), F32)
        for s in range(per_chunk):
            at = c * CHUNK + s * sub
            rank = earlier[s * devices : (s + 1) * devices] + carry
            spot = jnp.where(chosen[s], rank - BLOCK * tile, 0.0)
            spot = jnp.sum(spot, axis=0, keepdims=True)
            slot = jnp.where(chosen[s], rank + slots * owner_column, 0.0)
            slot = jnp.sum(slot, axis=0, keepdims=True)
            spot_ref[:, at : at + sub] = spot.astype(jnp.int32)
            slot_ref[:, at : at + sub] = slot.astype(jnp.int32)
            highest = jnp.maximum(highest, jnp.max(spot, axis=1, keepdims=True))
            carry = carry + jnp.sum(ones[s], axis=1, keepdims=True)
        windows = jnp.floor(highest * (1.0 / WINDOW)) + 1.0
        spans = jnp.where(lane[0:8] == c, windows, spans)
    tile_ref[0:devices, :] = tiles.astype(jnp.int32)
    tile_ref[devices : devices + 8, :] = spans.astype(jnp.int32)
    copy = pltpu.make_async_copy(tile_ref, tile_of, done)
    copy.start()
    copy.wait()

    def step(c, _):
        here = pl.ds(pl.multiple_of(c * CHUNK, CHUNK), CHUNK)
        boxes = box_ref[:, here]
        pos = pos_ref[:, here]
        motion = motion_ref[:, here]
        push = TIME_STEP * STIFFNESS * pos - TIME_STEP * DAMPING_RATE * motion[0:3]
        spin = -TIME_STEP * ROTATION_DRAG * motion[3:6]
        heat = -TIME_STEP * CONDUCTION * temp_ref[:, here]
        first = jnp.concatenate([push, spin, heat, jnp.ones((1, CHUNK), F32)], axis=0)
        second = jnp.concatenate([pos, radius_ref[:, here]], axis=0)
        first = jnp.concatenate(split(first), axis=0)
        second = jnp.concatenate(split(second), axis=0)
        box16 = jnp.broadcast_to(boxes, (16, CHUNK)).astype(F32).astype(BF16)
        first_parts = []
        second_parts = []
        for o in range(devices):
            mine = box16 == box_of[o].astype(F32).astype(BF16)
            first_parts.append(jnp.where(mine, first, jnp.zeros_like(first)))
            second_parts.append(jnp.where(mine[0:8], second, jnp.zeros_like(second)))
        parts = jnp.concatenate(first_parts + second_parts, axis=0)

        def window(w, _):
            hot_spot = hot(WINDOW, spot_ref[:, here] - WINDOW * w)
            placed = lax.dot_general(parts, hot_spot, NT, preferred_element_type=F32)
            for o in range(devices):
                tile = tile_of[box_of[o], c] + 2 * w
                one = placed[16 * o : 16 * o + 8] + placed[16 * o + 8 : 16 * o + 16]
                two = placed[16 * devices + 8 * o : 16 * devices + 8 * o + 8]
                two = two + pltpu.roll(two, 4, 0)
                acc[o, tile, 0:8, :] += one[:, :BLOCK]
                acc[o, tile + 1, 0:8, :] += one[:, BLOCK:]
                acc[o, tile, 8:16, :] += two[:, :BLOCK]
                acc[o, tile + 1, 8:16, :] += two[:, BLOCK:]
            return 0

        return lax.fori_loop(0, tile_of[devices, c], window, 0)

    lax.fori_loop(0, particles // CHUNK, step, 0)

    def finish(o, _):
        for q in range(layers):
            out_ref[o, 8 * q : 8 * q + 8, :] = acc[o, q, 0:8, :]
            out_ref[o, 8 * layers + 4 * q : 8 * layers + 4 * q + 4, :] = acc[o, q, 8:12, :]
        return 0

    lax.fori_loop(0, devices, finish, 0)


def place(box_owner, boxes, pos, motion, radius, temp, slots):
    devices = box_owner.shape[0]
    particles = pos.shape[1]
    layers = slots // BLOCK
    vmem = pl.BlockSpec(memory_space=VMEM)
    row = jax.ShapeDtypeStruct((1, particles), jnp.int32)
    table = (devices + 8, BLOCK)
    return pl.pallas_call(
        place_kernel,
        out_shape=(
            jax.ShapeDtypeStruct((devices, 12 * layers, BLOCK), F32), row, row,
            jax.ShapeDtypeStruct(table, jnp.int32),
        ),
        in_specs=[pl.BlockSpec(memory_space=pltpu.SMEM)] + [vmem] * 5,
        out_specs=(vmem,) * 4,
        scratch_shapes=[
            pltpu.SMEM((devices,), jnp.int32),
            pltpu.SMEM(table, jnp.int32),
            VMEM((devices, layers + 3, 16, BLOCK), F32),
            pltpu.SemaphoreType.DMA,
        ],
        compiler_params=pltpu.CompilerParams(vmem_limit_bytes=60 << 20),
        cost_estimate=pl.CostEstimate(
            flops=2 * 24 * devices * WINDOW * particles, bytes_accessed=1 << 20, transcendentals=0
        ),
        name="place_slots",
    )(box_owner, boxes, pos, motion, radius, temp)


def pair_terms(near):
    twice = jnp.concatenate([near, near], axis=0)
    high = twice.astype(BF16).astype(F32)
    low = (twice - high).astype(BF16).astype(F32)
    row = lax.broadcasted_iota(jnp.int32, (8, 1), 0)
    kept = high + low
    squares = kept * kept
    norm = -(squares[0:1] + squares[1:2] + squares[2:3])
    total = jnp.where(row < 3, norm, squares[3:4] + 0.5)
    one = total.astype(BF16).astype(F32)
    rest = total - one
    two = rest.astype(BF16).astype(F32)
    three = (rest - two).astype(BF16).astype(F32)
    third = jnp.where((row == 0) | (row == 3), one, jnp.where((row == 1) | (row == 4), two, three))
    third = jnp.where(row < 6, third, 0.0)
    crossed = 2.0 * jnp.where(row < 4, high, low)
    is_radius = (row == 3) | (row == 7)
    cross_d = jnp.where(is_radius, 0.0, crossed)
    cross_r = jnp.where(is_radius, crossed, 0.0)
    ones = jnp.ones_like(third)
    left = jnp.concatenate([high, low, third, jnp.where(row < 6, ones, 0.0)], axis=0)
    ones_d = jnp.where(row < 3, ones, 0.0)
    ones_r = jnp.where((row >= 3) & (row < 6), ones, 0.0)
    for_d = jnp.concatenate([cross_d, cross_d, ones_d, jnp.where(row < 3, third, 0.0)], axis=0)
    for_r = jnp.concatenate([cross_r, cross_r, ones_r, jnp.where((row >= 3) & (row < 6), third, 0.0)], axis=0)
    right = jnp.concatenate([for_d, for_r], axis=1)
    return left.astype(BF16), right.astype(BF16)


def contact_kernel(slot_ref, mask_ref, out_ref, heat_ref):
    homes, rows, _ = slot_ref.shape
    layers = rows // 12
    sign = lax.broadcasted_iota(jnp.int32, (8, 1), 0)
    sign = jnp.where((sign >= 3) & (sign < 6), 1.0, -1.0)
    for s in range(homes):
        for q in range(layers):
            mixed = slot_ref[s, 8 * q : 8 * q + 8, :]
            near = slot_ref[s, 8 * layers + 4 * q : 8 * layers + 4 * q + 4, :]
            left, right = pair_terms(near)
            pair = lax.dot_general(left, right, (((0,), (0,)), ((), ())), preferred_element_type=F32)
            reach = pair[:, BLOCK:]
            inverse = pl.reciprocal(reach, approx=True)
            inverse = inverse * (2.0 - reach * inverse)
            weight = mask_ref[s * layers + q].astype(F32) * jnp.exp(pair[:, :BLOCK] * inverse)
            weight_high, weight_low = split(weight)
            mixed_high, mixed_low = split(mixed)
            both = jnp.concatenate([mixed_high, mixed_low], axis=0)
            sums = lax.dot_general(both, weight_high, NT, preferred_element_type=F32)
            sums = sums + lax.dot_general(both, weight_low, NT, preferred_element_type=F32)
            sums = sums[0:8] + sums[8:16]
            result = mixed * sums[7:8] + sign * sums
            out_ref[s, 6 * q : 6 * q + 6, :] = result[0:6]
            heat_ref[s, q : q + 1, :] = result[6:7]


def contact(arrived, mask):
    devices, rows, _ = arrived.shape
    layers = rows // 12
    blocks = mask.shape[0]
    step = 2 if layers > 1 else 8
    return pl.pallas_call(
        contact_kernel,
        grid=(devices // step,),
        out_shape=(
            jax.ShapeDtypeStruct((devices, 6 * layers, BLOCK), F32),
            jax.ShapeDtypeStruct((devices, layers, BLOCK), F32),
        ),
        in_specs=[
            pl.BlockSpec((step, rows, BLOCK), lambda h: (h, 0, 0)),
            pl.BlockSpec((step * layers, BLOCK, BLOCK), lambda h: (h, 0, 0)),
        ],
        out_specs=(
            pl.BlockSpec((step, 6 * layers, BLOCK), lambda h: (h, 0, 0)),
            pl.BlockSpec((step, layers, BLOCK), lambda h: (h, 0, 0)),
        ),
        compiler_params=pltpu.CompilerParams(vmem_limit_bytes=60 << 20),
        cost_estimate=pl.CostEstimate(
            flops=64 * blocks * BLOCK * BLOCK, bytes_accessed=blocks * BLOCK * BLOCK * 4, transcendentals=0
        ),
        name="contact_blocks",
    )(arrived, mask)


def smoothed(centre, y_first, y_last, x_first, x_last):
    layers, rows, cols = centre.shape
    zero = jnp.zeros((1, rows, cols), F32)
    up = jnp.concatenate([centre[1:], zero], axis=0)
    down = jnp.concatenate([zero, centre[:-1]], axis=0)
    row = lax.broadcasted_iota(jnp.int32, (1, rows, cols), 1)
    col = lax.broadcasted_iota(jnp.int32, (1, rows, cols), 2)
    back = jnp.where(row == 0, y_first, pltpu.roll(centre, 1, 1))
    front = jnp.where(row == rows - 1, y_last, pltpu.roll(centre, rows - 1, 1))
    left = jnp.where(col == 0, x_first, pltpu.roll(centre, 1, 2))
    right = jnp.where(col == cols - 1, x_last, pltpu.roll(centre, cols - 1, 2))
    return CENTRE_WEIGHT * centre + SIDE_WEIGHT * ((up + down) + (back + front) + (left + right))


def columns(edge, layers, rows):
    count = edge.shape[0]
    if count < 8:
        edge = jnp.concatenate([edge] * (8 // count), axis=0)
    turned = jnp.transpose(edge)
    parts = [turned[:, a : a + 1] for a in range(count)]
    return jnp.concatenate(parts, axis=0).reshape(layers, rows, 1)


def smooth_field(field_ref, y0_ref, y1_ref, x0_ref, x1_ref, k, edge=None):
    at = k if edge is None else edge
    _, layers, rows, cols = field_ref.shape
    per = layers * rows // BLOCK
    x0 = columns(x0_ref[at * per : (at + 1) * per, :], layers, rows)
    x1 = columns(x1_ref[at * per : (at + 1) * per, :], layers, rows)
    y0 = y0_ref[at].reshape(layers, 1, cols)
    y1 = y1_ref[at].reshape(layers, 1, cols)
    return smoothed(field_ref[k], y0, y1, x0, x1)


def write_edges(field, k, y0_ref, y1_ref, x0_ref, x1_ref):
    layers, rows, cols = field.shape
    y0_ref[k] = field[:, 0, :]
    y1_ref[k] = field[:, rows - 1, :]
    flat = field.reshape(layers * rows, cols)
    for a in range(layers * rows // BLOCK):
        turned = jnp.transpose(flat[a * BLOCK : (a + 1) * BLOCK, :])
        at = k * (layers * rows // BLOCK) + a
        x0_ref[at : at + 1, :] = turned[0:1, :]
        x1_ref[at : at + 1, :] = turned[cols - 1 : cols, :]


def paired_rows(pairs, layers, rows, scratch):
    half = pairs.shape[0]
    cols = pairs.shape[1] // 2
    scratch[pl.ds(0, half, stride=2), :] = pairs[:, :cols]
    scratch[pl.ds(1, half, stride=2), :] = pairs[:, cols:]
    return scratch[...].reshape(layers, rows, cols)


def gathered(tables, rows, lanes):
    group = rows // 8
    found = [None] * len(tables)
    for g in range(len(tables[0])):
        mine = group == g
        for k, table in enumerate(tables):
            value = jnp.take_along_axis(table[g], lanes, axis=1, mode="promise_in_bounds")
            found[k] = value if g == 0 else jnp.where(mine, value, found[k])
    mine = lax.broadcasted_iota(jnp.int32, (8, BLOCK), 0) == rows % 8
    return [jnp.sum(jnp.where(mine, value, 0.0), axis=0, keepdims=True) for value in found]


def fluid_kernel(
    fluid_ref, y0_ref, y1_ref, x0_ref, x1_ref, cell_ref, motion_ref, radius_ref, temp_ref,
    base_ref, dep_ref, dy0_ref, dy1_ref, dx0_ref, dx1_ref,
    table, rows_scratch, acc, *, chunk
):
    fields, layers, rows, cols = fluid_ref.shape
    half = layers * rows // 2
    wide = 2 * cols
    particles = cell_ref.shape[1]
    for k in range(fields):
        table[k] = smooth_field(fluid_ref, y0_ref, y1_ref, x0_ref, x1_ref, k)
    acc[...] = jnp.zeros_like(acc)

    def step(i, _):
        here = pl.ds(pl.multiple_of(i * chunk, chunk), chunk)
        cells = cell_ref[:, here]
        hot_low = hot(wide, cells % wide)
        hot_high = hot(half, cells // wide)
        seen = [[] for _ in range(fields)]
        for s in range(chunk // BLOCK):
            wanted = jnp.broadcast_to(cells[:, s * BLOCK : (s + 1) * BLOCK], (8, BLOCK))
            values = gathered(
                [[table[k, z] for z in range(layers)] for k in range(fields)], wanted // cols, wanted % cols
            )
            for k in range(fields):
                seen[k].append(values[k])
        seen = [jnp.concatenate(parts, axis=1) for parts in seen]
        motion = motion_ref[:, here]
        radius = radius_ref[:, here]
        temp = temp_ref[:, here]
        fluid_vel = jnp.concatenate(seen[0:3], axis=0)
        drag = DRAG_COEFF / (radius * radius + 0.25) * (fluid_vel - motion[0:3])
        upward = lax.broadcasted_iota(jnp.int32, (3, 1), 0) == 2
        moved = motion[0:3] + TIME_STEP * drag - jnp.where(upward, TIME_STEP * GRAVITY, 0.0)
        warmed = temp + TIME_STEP * HEAT_TRANSFER * (seen[3] - temp)
        base_ref[:, here] = jnp.concatenate([moved, motion[3:6], warmed, seen[3]], axis=0)
        volume = radius * radius * radius
        terms = jnp.concatenate([volume, -volume * drag], axis=0)
        high, low = split(terms)
        parts = []
        for piece in (high, low):
            parts.append(jnp.concatenate([hot_high * piece[k : k + 1] for k in range(4)], axis=0))
        total = lax.dot_general(parts[0], hot_low, NT, preferred_element_type=F32)
        acc[...] += total + lax.dot_general(parts[1], hot_low, NT, preferred_element_type=F32)
        return 0

    lax.fori_loop(0, particles // chunk, step, 0)
    for k in range(fields):
        field = paired_rows(acc[k * half : (k + 1) * half, :], layers, rows, rows_scratch)
        dep_ref[k] = field
        write_edges(field, k, dy0_ref, dy1_ref, dx0_ref, dx1_ref)


def edge_shapes(fields, layers, rows, cols):
    y_edge = jax.ShapeDtypeStruct((fields, layers, cols), F32)
    x_edge = jax.ShapeDtypeStruct((fields * layers * rows // BLOCK, BLOCK), F32)
    return (y_edge, y_edge, x_edge, x_edge)


def see_and_deposit(fluid, halo, cells, motion, radius, temp):
    fields, layers, rows, cols = fluid.shape
    particles = cells.shape[1]
    vmem = pl.BlockSpec(memory_space=VMEM)
    return pl.pallas_call(
        functools.partial(fluid_kernel, chunk=512),
        out_shape=(
            jax.ShapeDtypeStruct((8, particles), F32),
            jax.ShapeDtypeStruct(fluid.shape, F32),
        ) + edge_shapes(fields, layers, rows, cols),
        in_specs=[vmem] * 9,
        out_specs=(vmem,) * 6,
        scratch_shapes=[
            VMEM(fluid.shape, F32),
            VMEM((layers * rows, cols), F32),
            VMEM((fields * layers * rows // 2, 2 * cols), F32),
        ],
        compiler_params=pltpu.CompilerParams(vmem_limit_bytes=40 << 20),
        cost_estimate=pl.CostEstimate(
            flops=16 * fields * layers * rows * cols * particles, bytes_accessed=2 << 20, transcendentals=0
        ),
        name="see_and_deposit",
    )(fluid, *halo, cells, motion, radius, temp)


def heat_kernel(
    back_ref, slot_ref, cell_ref, radius_ref, base_ref, ey0_ref, ey1_ref, ex0_ref, ex1_ref,
    next_ref, dep_ref, dy0_ref, dy1_ref, dx0_ref, dx1_ref,
    table, acc, rows_scratch, *, chunk, rows
):
    devices, layers, _ = back_ref.shape
    particles = slot_ref.shape[1]
    half, wide = acc.shape
    for o in range(devices):
        table[o * layers : (o + 1) * layers, :] = back_ref[o]
    acc[...] = jnp.zeros_like(acc)

    def step(i, _):
        here = pl.ds(pl.multiple_of(i * chunk, chunk), chunk)
        slots = slot_ref[:, here]
        gained = []
        for s in range(chunk // BLOCK):
            wanted = jnp.broadcast_to(slots[:, s * BLOCK : (s + 1) * BLOCK], (8, BLOCK))
            tiles = [table[8 * g : 8 * g + 8, :] for g in range(devices * layers // 8)]
            gained.append(gathered([tiles], wanted // BLOCK, wanted % BLOCK)[0])
        base = base_ref[6:8, here]
        total = base[0:1] + jnp.concatenate(gained, axis=1)
        next_ref[:, here] = total
        radius = radius_ref[:, here]
        high, low = split(radius * radius * radius * (total - base[1:2]))
        cells = cell_ref[:, here]
        hot_low = hot(wide, cells % wide)
        hot_high = hot(half, cells // wide)
        added = lax.dot_general(hot_high * high, hot_low, NT, preferred_element_type=F32)
        acc[...] += added + lax.dot_general(hot_high * low, hot_low, NT, preferred_element_type=F32)
        return 0

    lax.fori_loop(0, particles // chunk, step, 0)
    field = paired_rows(acc[...], 2 * half // rows, rows, rows_scratch)
    dep_ref[0] = field
    for edge, out in ((ey0_ref, dy0_ref), (ey1_ref, dy1_ref), (ex0_ref, dx0_ref), (ex1_ref, dx1_ref)):
        out[0 : edge.shape[0]] = edge[...]
    write_edges(field, ey0_ref.shape[0], dy0_ref, dy1_ref, dx0_ref, dx1_ref)


def heat_deposit(back, slot_of, cells, radius, base, edges, grid):
    devices = back.shape[0]
    layers, rows, cols = grid
    particles = cells.shape[1]
    half = layers * rows // 2
    fields = edges[0].shape[0] + 1
    vmem = pl.BlockSpec(memory_space=VMEM)
    return pl.pallas_call(
        functools.partial(heat_kernel, chunk=1024, rows=rows),
        out_shape=(
            jax.ShapeDtypeStruct((1, particles), F32),
            jax.ShapeDtypeStruct((1,) + grid, F32),
        ) + edge_shapes(fields, layers, rows, cols),
        in_specs=[vmem] * 9,
        out_specs=(vmem,) * 6,
        scratch_shapes=[
            VMEM((devices * back.shape[1], BLOCK), F32),
            VMEM((half, 2 * cols), F32),
            VMEM((layers * rows, cols), F32),
        ],
        compiler_params=pltpu.CompilerParams(vmem_limit_bytes=40 << 20),
        cost_estimate=pl.CostEstimate(
            flops=4 * half * 2 * cols * particles, bytes_accessed=1 << 20, transcendentals=0
        ),
        name="heat_deposit",
    )(back, slot_of, cells, radius, base, *edges)


def fetch_kernel(
    owner_ref, tile_ref, back_ref, box_ref, spot_ref, base_ref, warm_ref, next_ref, box_of, table, wanted
):
    devices, tall, _ = back_ref.shape
    layers = tall // 6
    particles = box_ref.shape[1]
    invert(owner_ref, box_of)
    blank = jnp.zeros((2, BLOCK), F32)
    for o in range(devices):
        for q in range(layers):
            piece = jnp.concatenate([back_ref[o, 6 * q : 6 * q + 6, :], blank], axis=0)
            high, low = split(piece)
            table[o, q] = jnp.concatenate([high, low], axis=0)
        for q in range(layers, layers + 3):
            table[o, q] = jnp.zeros((16, BLOCK), BF16)

    def step(c, _):
        here = pl.ds(pl.multiple_of(c * CHUNK, CHUNK), CHUNK)
        boxes = jnp.broadcast_to(box_ref[:, here], (8, CHUNK))

        def window(w, total):
            for o in range(devices):
                tile = tile_ref[box_of[o], c] + 2 * w
                wanted[16 * o : 16 * o + 16, 0:BLOCK] = table[o, tile]
                wanted[16 * o : 16 * o + 16, BLOCK:] = table[o, tile + 1]
            hot_spot = hot(WINDOW, spot_ref[:, here] - WINDOW * w)
            found = lax.dot_general(wanted[...], hot_spot, NN, preferred_element_type=F32)
            gained = jnp.zeros((8, CHUNK), F32)
            for o in range(devices):
                value = found[16 * o : 16 * o + 8] + found[16 * o + 8 : 16 * o + 16]
                gained = jnp.where(boxes == box_of[o], value, gained)
            return total + gained

        gained = lax.fori_loop(0, tile_ref[devices, c], window, jnp.zeros((8, CHUNK), F32))
        next_ref[:, here] = jnp.concatenate(
            [base_ref[0:6, here] + gained[0:6], warm_ref[:, here]], axis=0
        )
        return 0

    lax.fori_loop(0, particles // CHUNK, step, 0)


def fetch(box_owner, tiles, back, boxes, spots, base, warm):
    devices, tall, _ = back.shape
    particles = boxes.shape[1]
    layers = tall // 6
    vmem = pl.BlockSpec(memory_space=VMEM)
    smem = pl.BlockSpec(memory_space=pltpu.SMEM)
    return pl.pallas_call(
        fetch_kernel,
        out_shape=jax.ShapeDtypeStruct((7, particles), F32),
        in_specs=[smem, smem] + [vmem] * 5,
        out_specs=vmem,
        scratch_shapes=[
            pltpu.SMEM((devices,), jnp.int32),
            VMEM((devices, layers + 3, 16, BLOCK), BF16),
            VMEM((16 * devices, WINDOW), BF16),
        ],
        compiler_params=pltpu.CompilerParams(vmem_limit_bytes=40 << 20),
        cost_estimate=pl.CostEstimate(
            flops=32 * devices * WINDOW * particles, bytes_accessed=1 << 20, transcendentals=0
        ),
        name="fetch_slots",
    )(box_owner, tiles, back, boxes, spots, base, warm)


def spread_kernel(dep_ref, heat_ref, y0_ref, y1_ref, x0_ref, x1_ref, fluid_ref, next_ref, void_ref):
    halo = (y0_ref, y1_ref, x0_ref, x1_ref)
    crowding = 1.0 + COUPLING * smooth_field(dep_ref, *halo, 0)
    void_ref[...] = 1.0 / crowding
    for k in range(3):
        next_ref[k] = fluid_ref[k] + TIME_STEP * COUPLING * smooth_field(dep_ref, *halo, k + 1) * crowding
    warmth = smooth_field(heat_ref, *halo, 0, 4)
    next_ref[3] = fluid_ref[3] + TIME_STEP * COUPLING * warmth * crowding


def spread(dep, heat, halo, fluid):
    vmem = pl.BlockSpec(memory_space=VMEM)
    return pl.pallas_call(
        spread_kernel,
        out_shape=(jax.ShapeDtypeStruct(fluid.shape, F32), jax.ShapeDtypeStruct(fluid.shape[1:], F32)),
        in_specs=[vmem] * 7,
        out_specs=(vmem,) * 2,
        compiler_params=pltpu.CompilerParams(vmem_limit_bytes=40 << 20),
        cost_estimate=pl.CostEstimate(flops=20 * fluid.size, bytes_accessed=2 << 20, transcendentals=0),
        name="spread_fields",
    )(dep, heat, *halo, fluid)


def halo_of(y_first, y_last, x_first, x_last):
    def moved(value, axis, step):
        size = lax.axis_size(axis)
        pairs = [(i, i + step) for i in range(size) if 0 <= i + step < size]
        return lax.ppermute(value, axis, pairs)

    return (
        moved(y_last, "gy", 1),
        moved(y_first, "gy", -1),
        moved(x_last, "gx", 1),
        moved(x_first, "gx", -1),
    )


def shards(
    fluid_state, particle_pos, particle_motion, particle_radius, particle_temp,
    particle_cell, particle_box, box_owner, contact_mask,
):
    devices = lax.axis_size(("gx", "gy"))
    particles = particle_pos.shape[1]
    slots = 2 * particles // devices
    fields, layers, rows, cols = fluid_state.shape
    boxes = particle_box.reshape(1, particles)
    radius = particle_radius.reshape(1, particles)
    temp = particle_temp.reshape(1, particles)
    cells = particle_cell.reshape(1, particles)

    outgoing, slot_of, spots, tiles = place(
        box_owner, boxes, particle_pos, particle_motion, radius, temp, slots
    )
    arrived = lax.all_to_all(outgoing, ("gx", "gy"), split_axis=0, concat_axis=0, tiled=True)

    fluid_halo = halo_of(
        fluid_state[:, :, 0, :],
        fluid_state[:, :, rows - 1, :],
        fluid_state[:, :, :, 0].reshape(-1, BLOCK),
        fluid_state[:, :, :, cols - 1].reshape(-1, BLOCK),
    )
    seen = see_and_deposit(fluid_state, fluid_halo, cells, particle_motion, radius, temp)
    arrived, base, deposits, *edges = lax.optimization_barrier((arrived,) + tuple(seen))

    result, heat = contact(arrived, contact_mask)
    heat_back = lax.all_to_all(heat, ("gx", "gy"), split_axis=0, concat_axis=0, tiled=True)
    back = lax.all_to_all(result, ("gx", "gy"), split_axis=0, concat_axis=0, tiled=True)

    warm, heat_field, *edges = heat_deposit(
        heat_back, slot_of, cells, radius, base, edges, (layers, rows, cols)
    )
    fluid_next, void_fraction = spread(deposits, heat_field, halo_of(*edges), fluid_state)
    back, void_fraction = lax.optimization_barrier((back, void_fraction))
    particle_next = fetch(box_owner, tiles, back, boxes, spots, base, warm)
    return (fluid_next, void_fraction, particle_next)


def solution(mesh):
    in_specs = (
        P(None, None, "gy", "gx"),
        P(None, ("gx", "gy")),
        P(None, ("gx", "gy")),
        P(("gx", "gy")),
        P(("gx", "gy")),
        P(("gx", "gy")),
        P(("gx", "gy"), None),
        P(),
        P(("gx", "gy"), None, None),
    )
    out_specs = (P(None, None, "gy", "gx"), P(None, "gy", "gx"), P(None, ("gx", "gy")))
    return jax.shard_map(shards, mesh=mesh, in_specs=in_specs, out_specs=out_specs, check_vma=False)
```

```python
import functools

import jax
import jax.numpy as jnp
from jax import lax
from jax.experimental import pallas as pl
from jax.experimental.pallas import tpu as pltpu
from jax.sharding import PartitionSpec as P

BLOCK = 128
TIME_STEP = 0.1
STIFFNESS = 0.5
DAMPING_RATE = 0.2
ROTATION_DRAG = 0.1
DRAG_COEFF = 4.0
CONDUCTION = 0.3
HEAT_TRANSFER = 4.0
GRAVITY = 0.3
COUPLING = 4.0
CENTRE_WEIGHT = 0.25
SIDE_WEIGHT = 0.125

F32 = jnp.float32
BF16 = jnp.bfloat16
VMEM = pltpu.VMEM
NN = (((1,), (0,)), ((), ()))


def split(value):
    high = value.astype(BF16)
    return high, (value - high.astype(F32)).astype(BF16)


def hot(count, row):
    places = lax.broadcasted_iota(jnp.int32, (count, row.shape[1]), 0)
    return jnp.where(places == row, 1.0, 0.0).astype(BF16)


def hot_columns(count, row):
    n = row.shape[1] // BLOCK
    tiles = [row[:, a * BLOCK : (a + 1) * BLOCK] for a in range(n)]
    turned = jnp.transpose(jnp.concatenate(tiles * (8 // n), axis=0).astype(F32))
    places = lax.broadcasted_iota(jnp.int32, (BLOCK, count), 1).astype(F32)
    return jnp.concatenate(
        [jnp.where(places == turned[:, a : a + 1], 1.0, 0.0).astype(BF16) for a in range(n)], axis=0
    )


def invert(owner_ref, box_of):
    def step(b, _):
        box_of[owner_ref[b]] = b
        return 0

    lax.fori_loop(0, owner_ref.shape[0], step, 0)


WINDOW = 256
CHUNK = 1024


def place_kernel(
    owner_ref, box_ref, pos_ref, motion_ref, radius_ref, temp_ref,
    out_ref, slot_ref, spot_ref, tile_ref,
    box_of, tile_of, acc, done
):
    devices, _, layers, _ = out_ref.shape
    slots = layers * BLOCK
    particles = box_ref.shape[1]
    sub = 256
    invert(owner_ref, box_of)
    acc[...] = jnp.zeros_like(acc)

    box_row = lax.broadcasted_iota(jnp.int32, (devices, 1), 0)
    owner_column = jnp.zeros((devices, 1), F32)
    for b in range(devices):
        owner_column = jnp.where(box_row == b, owner_ref[b].astype(F32), owner_column)
    above = (
        lax.broadcasted_iota(jnp.int32, (sub, sub), 0) < lax.broadcasted_iota(jnp.int32, (sub, sub), 1)
    )
    above = jnp.where(above, 1.0, 0.0).astype(BF16)
    lane = lax.broadcasted_iota(jnp.int32, (devices, BLOCK), 1)
    tiles = jnp.zeros((devices, BLOCK), F32)
    spans = jnp.zeros((8, BLOCK), F32)
    carry = jnp.zeros((devices, 1), F32)
    per_chunk = CHUNK // sub
    for c in range(particles // CHUNK):
        chosen = []
        for s in range(per_chunk):
            at = c * CHUNK + s * sub
            chosen.append(
                lax.broadcasted_iota(jnp.int32, (devices, sub), 0) == box_ref[:, at : at + sub]
            )
        ones = [jnp.where(mine, 1.0, 0.0) for mine in chosen]
        earlier = lax.dot_general(
            jnp.concatenate(ones, axis=0).astype(BF16), above, NN, preferred_element_type=F32
        )
        tile = jnp.minimum(jnp.floor(carry * (1.0 / BLOCK)), layers - 1.0)
        tiles = jnp.where(lane == c, tile, tiles)
        highest = jnp.zeros((1, 1), F32)
        for s in range(per_chunk):
            at = c * CHUNK + s * sub
            rank = earlier[s * devices : (s + 1) * devices] + carry
            spot = jnp.where(chosen[s], rank - BLOCK * tile, 0.0)
            spot = jnp.sum(spot, axis=0, keepdims=True)
            slot = jnp.where(chosen[s], rank + slots * owner_column, 0.0)
            slot = jnp.sum(slot, axis=0, keepdims=True)
            spot_ref[:, at : at + sub] = spot.astype(jnp.int32)
            slot_ref[:, at : at + sub] = slot.astype(jnp.int32)
            highest = jnp.maximum(highest, jnp.max(spot, axis=1, keepdims=True))
            carry = carry + jnp.sum(ones[s], axis=1, keepdims=True)
        windows = jnp.floor(highest * (1.0 / WINDOW)) + 1.0
        spans = jnp.where(lane[0:8] == c, windows, spans)
    tile_ref[0:devices, :] = tiles.astype(jnp.int32)
    tile_ref[devices : devices + 8, :] = spans.astype(jnp.int32)
    copy = pltpu.make_async_copy(tile_ref, tile_of, done)
    copy.start()
    copy.wait()

    def step(c, _):
        here = pl.ds(pl.multiple_of(c * CHUNK, CHUNK), CHUNK)
        boxes = box_ref[:, here]
        pos = pos_ref[:, here]
        motion = motion_ref[:, here]
        push = TIME_STEP * STIFFNESS * pos - TIME_STEP * DAMPING_RATE * motion[0:3]
        spin = -TIME_STEP * ROTATION_DRAG * motion[3:6]
        heat = -TIME_STEP * CONDUCTION * temp_ref[:, here]
        first = jnp.concatenate([push, spin, heat, jnp.zeros((1, CHUNK), F32)], axis=0)
        second = jnp.concatenate([pos, radius_ref[:, here]], axis=0)
        first = jnp.concatenate(split(first), axis=0)
        second = jnp.concatenate(split(second), axis=0)
        box16 = jnp.broadcast_to(boxes, (16, CHUNK)).astype(F32).astype(BF16)
        first_parts = []
        second_parts = []
        for o in range(devices):
            mine = box16 == box_of[o].astype(F32).astype(BF16)
            first_parts.append(jnp.where(mine, first, jnp.zeros_like(first)))
            second_parts.append(jnp.where(mine[0:8], second, jnp.zeros_like(second)))
        parts = jnp.concatenate(first_parts + second_parts, axis=0)

        def window(w, _):
            hot_spot = hot_columns(WINDOW, spot_ref[:, here] - WINDOW * w)
            placed = lax.dot_general(parts, hot_spot, NN, preferred_element_type=F32)
            for o in range(devices):
                tile = tile_of[box_of[o], c] + 2 * w
                one = placed[16 * o : 16 * o + 8] + placed[16 * o + 8 : 16 * o + 16]
                two = placed[16 * devices + 8 * o : 16 * devices + 8 * o + 8]
                two = two + pltpu.roll(two, 4, 0)
                acc[o, tile, 0:8, :] += one[:, :BLOCK]
                acc[o, tile + 1, 0:8, :] += one[:, BLOCK:]
                acc[o, tile, 8:16, :] += two[:, :BLOCK]
                acc[o, tile + 1, 8:16, :] += two[:, BLOCK:]
            return 0

        return lax.fori_loop(0, tile_of[devices, c], window, 0)

    lax.fori_loop(0, particles // CHUNK, step, 0)

    def finish(o, _):
        for q in range(layers):
            out_ref[o, 0:7, q, :] = acc[o, q, 0:7, :]
            out_ref[o, 7:11, q, :] = acc[o, q, 8:12, :]
        return 0

    lax.fori_loop(0, devices, finish, 0)


def place(box_owner, boxes, pos, motion, radius, temp, slots):
    devices = box_owner.shape[0]
    particles = pos.shape[1]
    layers = slots // BLOCK
    vmem = pl.BlockSpec(memory_space=VMEM)
    row = jax.ShapeDtypeStruct((1, particles), jnp.int32)
    table = (devices + 8, BLOCK)
    return pl.pallas_call(
        place_kernel,
        out_shape=(
            jax.ShapeDtypeStruct((devices, 11, layers, BLOCK), F32), row, row,
            jax.ShapeDtypeStruct(table, jnp.int32),
        ),
        in_specs=[pl.BlockSpec(memory_space=pltpu.SMEM)] + [vmem] * 5,
        out_specs=(vmem,) * 4,
        scratch_shapes=[
            pltpu.SMEM((devices,), jnp.int32),
            pltpu.SMEM(table, jnp.int32),
            VMEM((devices, layers + 3, 16, BLOCK), F32),
            pltpu.SemaphoreType.DMA,
        ],
        compiler_params=pltpu.CompilerParams(vmem_limit_bytes=60 << 20),
        cost_estimate=pl.CostEstimate(
            flops=2 * 24 * devices * WINDOW * particles, bytes_accessed=1 << 20, transcendentals=0
        ),
        name="place_slots",
    )(box_owner, boxes, pos, motion, radius, temp)


def pair_terms(near):
    twice = jnp.concatenate([near, near], axis=0)
    high = twice.astype(BF16).astype(F32)
    low = (twice - high).astype(BF16).astype(F32)
    row = lax.broadcasted_iota(jnp.int32, (8, 1), 0)
    kept = high + low
    squares = kept * kept
    norm = -(squares[0:1] + squares[1:2] + squares[2:3])
    total = jnp.where(row < 3, norm, squares[3:4] + 0.5)
    one = total.astype(BF16).astype(F32)
    rest = total - one
    two = rest.astype(BF16).astype(F32)
    three = (rest - two).astype(BF16).astype(F32)
    third = jnp.where((row == 0) | (row == 3), one, jnp.where((row == 1) | (row == 4), two, three))
    third = jnp.where(row < 6, third, 0.0)
    crossed = 2.0 * jnp.where(row < 4, high, low)
    is_radius = (row == 3) | (row == 7)
    cross_d = jnp.where(is_radius, 0.0, crossed)
    cross_r = jnp.where(is_radius, crossed, 0.0)
    ones = jnp.ones_like(third)
    left = jnp.concatenate([high, low, third, jnp.where(row < 6, ones, 0.0)], axis=0)
    ones_d = jnp.where(row < 3, ones, 0.0)
    ones_r = jnp.where((row >= 3) & (row < 6), ones, 0.0)
    for_d = jnp.concatenate([cross_d, cross_d, ones_d, jnp.where(row < 3, third, 0.0)], axis=0)
    for_r = jnp.concatenate([cross_r, cross_r, ones_r, jnp.where((row >= 3) & (row < 6), third, 0.0)], axis=0)
    right = jnp.concatenate([for_d, for_r], axis=1)
    return left, right.astype(BF16)


def contact_kernel(slot_ref, mask_ref, out_ref):
    homes, _, layers, _ = slot_ref.shape
    blocks = [(s, q) for s in range(homes) for q in range(layers)]
    row = lax.broadcasted_iota(jnp.int32, (8, 1), 0)
    sign = jnp.where((row >= 3) & (row < 6), 1.0, -1.0)
    mixed = []
    stacked = []
    pairs = []
    for first in range(0, len(blocks), 4):
        lefts = []
        rights = []
        for g, (s, q) in enumerate(blocks[first : first + 4]):
            near = slot_ref[s, 7:11, q, :]
            occupied = jnp.where(near[3:4] > 0.0, 1.0, 0.0)
            mine = jnp.concatenate([slot_ref[s, 0:7, q, :], occupied], axis=0)
            mixed.append(mine)
            high = mine.astype(BF16).astype(F32)
            stacked += [high, mine - high]
            left, right = pair_terms(near)
            lefts.append(left)
            spots = [jnp.zeros_like(right)] * 4
            spots[g] = right
            rights.append(jnp.concatenate(spots, axis=0))
        turned = jnp.transpose(jnp.concatenate(lefts, axis=0)).astype(BF16)
        pairs.append(
            lax.dot_general(turned, jnp.concatenate(rights, axis=1), NN, preferred_element_type=F32)
        )
    columns = jnp.transpose(jnp.concatenate(stacked, axis=0)).astype(BF16)
    lane = lax.broadcasted_iota(jnp.int32, (BLOCK, BLOCK), 1) // 16
    highs = []
    lows = []
    right = []
    for b in range(len(blocks)):
        at = 2 * BLOCK * (b % 4)
        pair = pairs[b // 4]
        reach = pair[:, at + BLOCK : at + 2 * BLOCK]
        inverse = pl.reciprocal(reach, approx=True)
        inverse = inverse * (2.0 - reach * inverse)
        weight = mask_ref[b].astype(F32) * jnp.exp(pair[:, at : at + BLOCK] * inverse)
        high, low = split(weight)
        highs.append(high)
        lows.append(low)
        right.append(jnp.where(lane == b, columns, jnp.zeros_like(columns)))
    sums = lax.dot_general(
        jnp.concatenate(highs + lows, axis=1), jnp.concatenate(right + right, axis=0), NN,
        preferred_element_type=F32,
    )
    sums = jnp.transpose(sums)
    for b, (s, q) in enumerate(blocks):
        total = sums[16 * b : 16 * b + 8] + sums[16 * b + 8 : 16 * b + 16]
        result = mixed[b] * total[7:8] + sign * total
        out_ref[s, :, q, :] = result[0:7]


def contact(arrived, mask):
    devices, values, layers, _ = arrived.shape
    blocks = mask.shape[0]
    step = 8 // layers
    return pl.pallas_call(
        contact_kernel,
        grid=(devices // step,),
        out_shape=jax.ShapeDtypeStruct((devices, 7, layers, BLOCK), F32),
        in_specs=[
            pl.BlockSpec((step, values, layers, BLOCK), lambda h: (h, 0, 0, 0)),
            pl.BlockSpec((step * layers, BLOCK, BLOCK), lambda h: (h, 0, 0)),
        ],
        out_specs=pl.BlockSpec((step, 7, layers, BLOCK), lambda h: (h, 0, 0, 0)),
        compiler_params=pltpu.CompilerParams(vmem_limit_bytes=60 << 20),
        cost_estimate=pl.CostEstimate(
            flops=64 * blocks * BLOCK * BLOCK, bytes_accessed=blocks * BLOCK * BLOCK * 4, transcendentals=0
        ),
        name="contact_blocks",
    )(arrived, mask)


def smoothed(centre, y_first, y_last, x_first, x_last):
    layers, rows, cols = centre.shape
    zero = jnp.zeros((1, rows, cols), F32)
    up = jnp.concatenate([centre[1:], zero], axis=0)
    down = jnp.concatenate([zero, centre[:-1]], axis=0)
    row = lax.broadcasted_iota(jnp.int32, (1, rows, cols), 1)
    col = lax.broadcasted_iota(jnp.int32, (1, rows, cols), 2)
    back = jnp.where(row == 0, y_first, pltpu.roll(centre, 1, 1))
    front = jnp.where(row == rows - 1, y_last, pltpu.roll(centre, rows - 1, 1))
    left = jnp.where(col == 0, x_first, pltpu.roll(centre, 1, 2))
    right = jnp.where(col == cols - 1, x_last, pltpu.roll(centre, cols - 1, 2))
    return CENTRE_WEIGHT * centre + SIDE_WEIGHT * ((up + down) + (back + front) + (left + right))


def columns(edge, layers, rows):
    count = edge.shape[0]
    if count < 8:
        edge = jnp.concatenate([edge] * (8 // count), axis=0)
    turned = jnp.transpose(edge)
    parts = [turned[:, a : a + 1] for a in range(count)]
    return jnp.concatenate(parts, axis=0).reshape(layers, rows, 1)


def smooth_field(field_ref, y0_ref, y1_ref, x0_ref, x1_ref, k, edge=None):
    at = k if edge is None else edge
    _, layers, rows, cols = field_ref.shape
    per = layers * rows // BLOCK
    x0 = columns(x0_ref[at * per : (at + 1) * per, :], layers, rows)
    x1 = columns(x1_ref[at * per : (at + 1) * per, :], layers, rows)
    y0 = y0_ref[at].reshape(layers, 1, cols)
    y1 = y1_ref[at].reshape(layers, 1, cols)
    return smoothed(field_ref[k], y0, y1, x0, x1)


def write_edges(field, k, y0_ref, y1_ref, x0_ref, x1_ref):
    layers, rows, cols = field.shape
    y0_ref[k] = field[:, 0, :]
    y1_ref[k] = field[:, rows - 1, :]
    flat = field.reshape(layers * rows, cols)
    for a in range(layers * rows // BLOCK):
        turned = jnp.transpose(flat[a * BLOCK : (a + 1) * BLOCK, :])
        at = k * (layers * rows // BLOCK) + a
        x0_ref[at : at + 1, :] = turned[0:1, :]
        x1_ref[at : at + 1, :] = turned[cols - 1 : cols, :]


def paired_rows(pairs, layers, rows, scratch):
    half = pairs.shape[0]
    cols = pairs.shape[1] // 2
    scratch[pl.ds(0, half, stride=2), :] = pairs[:, :cols]
    scratch[pl.ds(1, half, stride=2), :] = pairs[:, cols:]
    return scratch[...].reshape(layers, rows, cols)


def gathered(tables, rows, lanes):
    group = rows // 8
    found = [None] * len(tables)
    for g in range(len(tables[0])):
        mine = group == g
        for k, table in enumerate(tables):
            value = jnp.take_along_axis(table[g], lanes, axis=1, mode="promise_in_bounds")
            found[k] = value if g == 0 else jnp.where(mine, value, found[k])
    mine = lax.broadcasted_iota(jnp.int32, (8, BLOCK), 0) == rows % 8
    return [jnp.sum(jnp.where(mine, value, 0.0), axis=0, keepdims=True) for value in found]


def fluid_kernel(
    fluid_ref, y0_ref, y1_ref, x0_ref, x1_ref, cell_ref, motion_ref, radius_ref, temp_ref,
    base_ref, dep_ref, dy0_ref, dy1_ref, dx0_ref, dx1_ref,
    table, rows_scratch, acc, *, chunk
):
    fields, layers, rows, cols = fluid_ref.shape
    half = layers * rows // 2
    wide = 2 * cols
    particles = cell_ref.shape[1]
    for k in range(fields):
        table[k] = smooth_field(fluid_ref, y0_ref, y1_ref, x0_ref, x1_ref, k)
    acc[...] = jnp.zeros_like(acc)

    def step(i, _):
        here = pl.ds(pl.multiple_of(i * chunk, chunk), chunk)
        cells = cell_ref[:, here]
        hot_low = hot_columns(wide, cells % wide)
        hot_high = hot(half, cells // wide)
        seen = [[] for _ in range(fields)]
        for s in range(chunk // BLOCK):
            wanted = jnp.broadcast_to(cells[:, s * BLOCK : (s + 1) * BLOCK], (8, BLOCK))
            values = gathered(
                [[table[k, z] for z in range(layers)] for k in range(fields)], wanted // cols, wanted % cols
            )
            for k in range(fields):
                seen[k].append(values[k])
        seen = [jnp.concatenate(parts, axis=1) for parts in seen]
        motion = motion_ref[:, here]
        radius = radius_ref[:, here]
        temp = temp_ref[:, here]
        fluid_vel = jnp.concatenate(seen[0:3], axis=0)
        drag = DRAG_COEFF / (radius * radius + 0.25) * (fluid_vel - motion[0:3])
        upward = lax.broadcasted_iota(jnp.int32, (3, 1), 0) == 2
        moved = motion[0:3] + TIME_STEP * drag - jnp.where(upward, TIME_STEP * GRAVITY, 0.0)
        warmed = temp + TIME_STEP * HEAT_TRANSFER * (seen[3] - temp)
        base_ref[:, here] = jnp.concatenate([moved, motion[3:6], warmed, seen[3]], axis=0)
        volume = radius * radius * radius
        terms = jnp.concatenate([volume, -volume * drag], axis=0)
        high, low = split(terms)
        parts = []
        for piece in (high, low):
            parts.append(jnp.concatenate([hot_high * piece[k : k + 1] for k in range(4)], axis=0))
        total = lax.dot_general(parts[0], hot_low, NN, preferred_element_type=F32)
        acc[...] += total + lax.dot_general(parts[1], hot_low, NN, preferred_element_type=F32)
        return 0

    lax.fori_loop(0, particles // chunk, step, 0)
    for k in range(fields):
        field = paired_rows(acc[k * half : (k + 1) * half, :], layers, rows, rows_scratch)
        dep_ref[k] = field
        write_edges(field, k, dy0_ref, dy1_ref, dx0_ref, dx1_ref)


def edge_shapes(fields, layers, rows, cols):
    y_edge = jax.ShapeDtypeStruct((fields, layers, cols), F32)
    x_edge = jax.ShapeDtypeStruct((fields * layers * rows // BLOCK, BLOCK), F32)
    return (y_edge, y_edge, x_edge, x_edge)


def see_and_deposit(fluid, halo, cells, motion, radius, temp):
    fields, layers, rows, cols = fluid.shape
    particles = cells.shape[1]
    vmem = pl.BlockSpec(memory_space=VMEM)
    return pl.pallas_call(
        functools.partial(fluid_kernel, chunk=512),
        out_shape=(
            jax.ShapeDtypeStruct((8, particles), F32),
            jax.ShapeDtypeStruct(fluid.shape, F32),
        ) + edge_shapes(fields, layers, rows, cols),
        in_specs=[vmem] * 9,
        out_specs=(vmem,) * 6,
        scratch_shapes=[
            VMEM(fluid.shape, F32),
            VMEM((layers * rows, cols), F32),
            VMEM((fields * layers * rows // 2, 2 * cols), F32),
        ],
        compiler_params=pltpu.CompilerParams(vmem_limit_bytes=40 << 20),
        cost_estimate=pl.CostEstimate(
            flops=16 * fields * layers * rows * cols * particles, bytes_accessed=2 << 20, transcendentals=0
        ),
        name="see_and_deposit",
    )(fluid, *halo, cells, motion, radius, temp)


def heat_kernel(
    back_ref, slot_ref, cell_ref, radius_ref, base_ref, ey0_ref, ey1_ref, ex0_ref, ex1_ref,
    next_ref, dep_ref, dy0_ref, dy1_ref, dx0_ref, dx1_ref,
    table, acc, rows_scratch, *, chunk, rows
):
    devices, _, layers, _ = back_ref.shape
    particles = slot_ref.shape[1]
    half, wide = acc.shape
    for o in range(devices):
        table[o * layers : (o + 1) * layers, :] = back_ref[o, 6]
    acc[...] = jnp.zeros_like(acc)

    def step(i, _):
        here = pl.ds(pl.multiple_of(i * chunk, chunk), chunk)
        slots = slot_ref[:, here]
        gained = []
        for s in range(chunk // BLOCK):
            wanted = jnp.broadcast_to(slots[:, s * BLOCK : (s + 1) * BLOCK], (8, BLOCK))
            tiles = [table[8 * g : 8 * g + 8, :] for g in range(devices * layers // 8)]
            gained.append(gathered([tiles], wanted // BLOCK, wanted % BLOCK)[0])
        base = base_ref[6:8, here]
        total = base[0:1] + jnp.concatenate(gained, axis=1)
        next_ref[:, here] = total
        radius = radius_ref[:, here]
        high, low = split(radius * radius * radius * (total - base[1:2]))
        cells = cell_ref[:, here]
        hot_low = hot_columns(wide, cells % wide)
        hot_high = hot(half, cells // wide)
        added = lax.dot_general(hot_high * high, hot_low, NN, preferred_element_type=F32)
        acc[...] += added + lax.dot_general(hot_high * low, hot_low, NN, preferred_element_type=F32)
        return 0

    lax.fori_loop(0, particles // chunk, step, 0)
    field = paired_rows(acc[...], 2 * half // rows, rows, rows_scratch)
    dep_ref[0] = field
    for edge, out in ((ey0_ref, dy0_ref), (ey1_ref, dy1_ref), (ex0_ref, dx0_ref), (ex1_ref, dx1_ref)):
        out[0 : edge.shape[0]] = edge[...]
    write_edges(field, ey0_ref.shape[0], dy0_ref, dy1_ref, dx0_ref, dx1_ref)


def heat_deposit(back, slot_of, cells, radius, base, edges, grid):
    devices = back.shape[0]
    layers, rows, cols = grid
    particles = cells.shape[1]
    half = layers * rows // 2
    fields = edges[0].shape[0] + 1
    vmem = pl.BlockSpec(memory_space=VMEM)
    return pl.pallas_call(
        functools.partial(heat_kernel, chunk=1024, rows=rows),
        out_shape=(
            jax.ShapeDtypeStruct((1, particles), F32),
            jax.ShapeDtypeStruct((1,) + grid, F32),
        ) + edge_shapes(fields, layers, rows, cols),
        in_specs=[vmem] * 9,
        out_specs=(vmem,) * 6,
        scratch_shapes=[
            VMEM((devices * back.shape[2], BLOCK), F32),
            VMEM((half, 2 * cols), F32),
            VMEM((layers * rows, cols), F32),
        ],
        compiler_params=pltpu.CompilerParams(vmem_limit_bytes=40 << 20),
        cost_estimate=pl.CostEstimate(
            flops=4 * half * 2 * cols * particles, bytes_accessed=1 << 20, transcendentals=0
        ),
        name="heat_deposit",
    )(back, slot_of, cells, radius, base, *edges)


def fetch_kernel(
    owner_ref, tile_ref, back_ref, box_ref, spot_ref, base_ref, warm_ref, next_ref, box_of, table, wanted
):
    devices, _, layers, _ = back_ref.shape
    particles = box_ref.shape[1]
    invert(owner_ref, box_of)
    blank = jnp.zeros((2, BLOCK), F32)
    for o in range(devices):
        for q in range(layers):
            piece = jnp.concatenate([back_ref[o, 0:6, q, :], blank], axis=0)
            high, low = split(piece)
            table[o, q] = jnp.concatenate([high, low], axis=0)
        for q in range(layers, layers + 3):
            table[o, q] = jnp.zeros((16, BLOCK), BF16)

    def step(c, _):
        here = pl.ds(pl.multiple_of(c * CHUNK, CHUNK), CHUNK)
        boxes = jnp.broadcast_to(box_ref[:, here], (8, CHUNK))

        def window(w, total):
            for o in range(devices):
                tile = tile_ref[box_of[o], c] + 2 * w
                wanted[16 * o : 16 * o + 16, 0:BLOCK] = table[o, tile]
                wanted[16 * o : 16 * o + 16, BLOCK:] = table[o, tile + 1]
            hot_spot = hot(WINDOW, spot_ref[:, here] - WINDOW * w)
            found = lax.dot_general(wanted[...], hot_spot, NN, preferred_element_type=F32)
            gained = jnp.zeros((8, CHUNK), F32)
            for o in range(devices):
                value = found[16 * o : 16 * o + 8] + found[16 * o + 8 : 16 * o + 16]
                gained = jnp.where(boxes == box_of[o], value, gained)
            return total + gained

        gained = lax.fori_loop(0, tile_ref[devices, c], window, jnp.zeros((8, CHUNK), F32))
        next_ref[:, here] = jnp.concatenate(
            [base_ref[0:6, here] + gained[0:6], warm_ref[:, here]], axis=0
        )
        return 0

    lax.fori_loop(0, particles // CHUNK, step, 0)


def fetch(box_owner, tiles, back, boxes, spots, base, warm):
    devices, _, layers, _ = back.shape
    particles = boxes.shape[1]
    vmem = pl.BlockSpec(memory_space=VMEM)
    smem = pl.BlockSpec(memory_space=pltpu.SMEM)
    return pl.pallas_call(
        fetch_kernel,
        out_shape=jax.ShapeDtypeStruct((7, particles), F32),
        in_specs=[smem, smem] + [vmem] * 5,
        out_specs=vmem,
        scratch_shapes=[
            pltpu.SMEM((devices,), jnp.int32),
            VMEM((devices, layers + 3, 16, BLOCK), BF16),
            VMEM((16 * devices, WINDOW), BF16),
        ],
        compiler_params=pltpu.CompilerParams(vmem_limit_bytes=40 << 20),
        cost_estimate=pl.CostEstimate(
            flops=32 * devices * WINDOW * particles, bytes_accessed=1 << 20, transcendentals=0
        ),
        name="fetch_slots",
    )(box_owner, tiles, back, boxes, spots, base, warm)


def spread_kernel(dep_ref, heat_ref, y0_ref, y1_ref, x0_ref, x1_ref, fluid_ref, next_ref, void_ref):
    halo = (y0_ref, y1_ref, x0_ref, x1_ref)
    crowding = 1.0 + COUPLING * smooth_field(dep_ref, *halo, 0)
    void_ref[...] = 1.0 / crowding
    for k in range(3):
        next_ref[k] = fluid_ref[k] + TIME_STEP * COUPLING * smooth_field(dep_ref, *halo, k + 1) * crowding
    warmth = smooth_field(heat_ref, *halo, 0, 4)
    next_ref[3] = fluid_ref[3] + TIME_STEP * COUPLING * warmth * crowding


def spread(dep, heat, halo, fluid):
    vmem = pl.BlockSpec(memory_space=VMEM)
    return pl.pallas_call(
        spread_kernel,
        out_shape=(jax.ShapeDtypeStruct(fluid.shape, F32), jax.ShapeDtypeStruct(fluid.shape[1:], F32)),
        in_specs=[vmem] * 7,
        out_specs=(vmem,) * 2,
        compiler_params=pltpu.CompilerParams(vmem_limit_bytes=40 << 20),
        cost_estimate=pl.CostEstimate(flops=20 * fluid.size, bytes_accessed=2 << 20, transcendentals=0),
        name="spread_fields",
    )(dep, heat, *halo, fluid)


def halo_of(y_first, y_last, x_first, x_last):
    def moved(value, axis, step):
        size = lax.axis_size(axis)
        pairs = [(i, i + step) for i in range(size) if 0 <= i + step < size]
        return lax.ppermute(value, axis, pairs)

    return (
        moved(y_last, "gy", 1),
        moved(y_first, "gy", -1),
        moved(x_last, "gx", 1),
        moved(x_first, "gx", -1),
    )


def shards(
    fluid_state, particle_pos, particle_motion, particle_radius, particle_temp,
    particle_cell, particle_box, box_owner, contact_mask,
):
    devices = lax.axis_size(("gx", "gy"))
    particles = particle_pos.shape[1]
    slots = 2 * particles // devices
    fields, layers, rows, cols = fluid_state.shape
    boxes = particle_box.reshape(1, particles)
    radius = particle_radius.reshape(1, particles)
    temp = particle_temp.reshape(1, particles)
    cells = particle_cell.reshape(1, particles)

    outgoing, slot_of, spots, tiles = place(
        box_owner, boxes, particle_pos, particle_motion, radius, temp, slots
    )
    arrived = lax.all_to_all(outgoing, ("gx", "gy"), split_axis=0, concat_axis=0, tiled=True)

    spots, fluid = lax.optimization_barrier((spots, fluid_state))
    fluid_halo = halo_of(
        fluid[:, :, 0, :],
        fluid[:, :, rows - 1, :],
        fluid[:, :, :, 0].reshape(-1, BLOCK),
        fluid[:, :, :, cols - 1].reshape(-1, BLOCK),
    )
    seen = see_and_deposit(fluid_state, fluid_halo, cells, particle_motion, radius, temp)
    arrived, base, deposits, *edges = lax.optimization_barrier((arrived,) + tuple(seen))

    result = contact(arrived, contact_mask)
    back = lax.all_to_all(result, ("gx", "gy"), split_axis=0, concat_axis=0, tiled=True)
    warm, heat_field, *edges = heat_deposit(
        back, slot_of, cells, radius, base, edges, (layers, rows, cols)
    )
    halo = halo_of(*edges)
    particle_next = fetch(box_owner, tiles, back, boxes, spots, base, warm)
    fluid_next, void_fraction = spread(deposits, heat_field, halo, fluid_state)
    return (fluid_next, void_fraction, particle_next)


def solution(mesh):
    in_specs = (
        P(None, None, "gy", "gx"),
        P(None, ("gx", "gy")),
        P(None, ("gx", "gy")),
        P(("gx", "gy")),
        P(("gx", "gy")),
        P(("gx", "gy")),
        P(("gx", "gy"), None),
        P(),
        P(("gx", "gy"), None, None),
    )
    out_specs = (P(None, None, "gy", "gx"), P(None, "gy", "gx"), P(None, ("gx", "gy")))
    return jax.shard_map(shards, mesh=mesh, in_specs=in_specs, out_specs=out_specs, check_vma=False)
```

```python
import functools

import jax
import jax.numpy as jnp
from jax import lax
from jax.experimental import pallas as pl
from jax.experimental.pallas import tpu as pltpu
from jax.sharding import PartitionSpec as P

BLOCK = 128
TIME_STEP = 0.1
STIFFNESS = 0.5
DAMPING_RATE = 0.2
ROTATION_DRAG = 0.1
DRAG_COEFF = 4.0
CONDUCTION = 0.3
HEAT_TRANSFER = 4.0
GRAVITY = 0.3
COUPLING = 4.0
CENTRE_WEIGHT = 0.25
SIDE_WEIGHT = 0.125

F32 = jnp.float32
BF16 = jnp.bfloat16
VMEM = pltpu.VMEM
NN = (((1,), (0,)), ((), ()))
NT = (((1,), (1,)), ((), ()))


def split(value):
    high = value.astype(BF16)
    return high, (value - high.astype(F32)).astype(BF16)


def hot(count, row):
    places = lax.broadcasted_iota(jnp.int32, (count, row.shape[1]), 0)
    return jnp.where(places == row, 1.0, 0.0).astype(BF16)


def hot_columns(count, row):
    n = row.shape[1] // BLOCK
    tiles = [row[:, a * BLOCK : (a + 1) * BLOCK] for a in range(n)]
    turned = jnp.transpose(jnp.concatenate(tiles * (8 // n), axis=0).astype(F32))
    places = lax.broadcasted_iota(jnp.int32, (BLOCK, count), 1).astype(F32)
    return jnp.concatenate(
        [jnp.where(places == turned[:, a : a + 1], 1.0, 0.0).astype(BF16) for a in range(n)], axis=0
    )


def invert(owner_ref, box_of):
    def step(b, _):
        box_of[owner_ref[b]] = b
        return 0

    lax.fori_loop(0, owner_ref.shape[0], step, 0)


WINDOW = 256
CHUNK = 1024


def place_kernel(
    owner_ref, box_ref, pos_ref, motion_ref, radius_ref, temp_ref,
    out_ref, slot_ref, spot_ref, tile_ref,
    box_of, tile_of, acc, done
):
    devices, rows, _ = out_ref.shape
    layers = rows // 12
    slots = layers * BLOCK
    particles = box_ref.shape[1]
    sub = 256
    invert(owner_ref, box_of)
    acc[...] = jnp.zeros_like(acc)

    box_row = lax.broadcasted_iota(jnp.int32, (devices, 1), 0)
    owner_column = jnp.zeros((devices, 1), F32)
    for b in range(devices):
        owner_column = jnp.where(box_row == b, owner_ref[b].astype(F32), owner_column)
    above = (
        lax.broadcasted_iota(jnp.int32, (sub, sub), 0) < lax.broadcasted_iota(jnp.int32, (sub, sub), 1)
    )
    above = jnp.where(above, 1.0, 0.0).astype(BF16)
    lane = lax.broadcasted_iota(jnp.int32, (devices, BLOCK), 1)
    tiles = jnp.zeros((devices, BLOCK), F32)
    spans = jnp.zeros((8, BLOCK), F32)
    carry = jnp.zeros((devices, 1), F32)
    per_chunk = CHUNK // sub
    for c in range(particles // CHUNK):
        chosen = []
        for s in range(per_chunk):
            at = c * CHUNK + s * sub
            chosen.append(
                lax.broadcasted_iota(jnp.int32, (devices, sub), 0) == box_ref[:, at : at + sub]
            )
        ones = [jnp.where(mine, 1.0, 0.0) for mine in chosen]
        earlier = lax.dot_general(
            jnp.concatenate(ones, axis=0).astype(BF16), above, NN, preferred_element_type=F32
        )
        tile = jnp.minimum(jnp.floor(carry * (1.0 / BLOCK)), layers - 1.0)
        tiles = jnp.where(lane == c, tile, tiles)
        highest = jnp.zeros((1, 1), F32)
        for s in range(per_chunk):
            at = c * CHUNK + s * sub
            rank = earlier[s * devices : (s + 1) * devices] + carry
            spot = jnp.where(chosen[s], rank - BLOCK * tile, 0.0)
            spot = jnp.sum(spot, axis=0, keepdims=True)
            slot = jnp.where(chosen[s], rank + slots * owner_column, 0.0)
            slot = jnp.sum(slot, axis=0, keepdims=True)
            spot_ref[:, at : at + sub] = spot.astype(jnp.int32)
            slot_ref[:, at : at + sub] = slot.astype(jnp.int32)
            highest = jnp.maximum(highest, jnp.max(spot, axis=1, keepdims=True))
            carry = carry + jnp.sum(ones[s], axis=1, keepdims=True)
        windows = jnp.floor(highest * (1.0 / WINDOW)) + 1.0
        spans = jnp.where(lane[0:8] == c, windows, spans)
    tile_ref[0:devices, :] = tiles.astype(jnp.int32)
    tile_ref[devices : devices + 8, :] = spans.astype(jnp.int32)
    copy = pltpu.make_async_copy(tile_ref, tile_of, done)
    copy.start()
    copy.wait()

    def step(c, _):
        here = pl.ds(pl.multiple_of(c * CHUNK, CHUNK), CHUNK)
        boxes = box_ref[:, here]
        pos = pos_ref[:, here]
        motion = motion_ref[:, here]
        push = TIME_STEP * STIFFNESS * pos - TIME_STEP * DAMPING_RATE * motion[0:3]
        spin = -TIME_STEP * ROTATION_DRAG * motion[3:6]
        heat = -TIME_STEP * CONDUCTION * temp_ref[:, here]
        first = jnp.concatenate([push, spin, heat, jnp.ones((1, CHUNK), F32)], axis=0)
        second = jnp.concatenate([pos, radius_ref[:, here]], axis=0)
        first = jnp.concatenate(split(first), axis=0)
        second = jnp.concatenate(split(second) * 2, axis=0)
        lower = lax.broadcasted_iota(jnp.int32, (16, 1), 0) < 8
        box16 = jnp.broadcast_to(boxes, (16, CHUNK)).astype(F32).astype(BF16)
        first_parts = []
        second_parts = []
        for o in range(devices):
            mine = box16 == box_of[o].astype(F32).astype(BF16)
            first_parts.append(jnp.where(mine, first, jnp.zeros_like(first)))
            if o % 2 == 0:
                either = jnp.where(lower, box_of[o].astype(F32), box_of[o + 1].astype(F32)).astype(BF16)
                second_parts.append(jnp.where(box16 == either, second, jnp.zeros_like(second)))
        parts = jnp.concatenate(first_parts + second_parts, axis=0)

        def window(w, _):
            hot_spot = hot(WINDOW, spot_ref[:, here] - WINDOW * w)
            placed = lax.dot_general(parts, hot_spot, NT, preferred_element_type=F32)
            for o in range(devices):
                tile = tile_of[box_of[o], c] + 2 * w
                one = placed[16 * o : 16 * o + 8] + placed[16 * o + 8 : 16 * o + 16]
                two = placed[16 * devices + 8 * o : 16 * devices + 8 * o + 8]
                two = two + pltpu.roll(two, 4, 0)
                acc[o, tile, 0:8, :] += one[:, :BLOCK]
                acc[o, tile + 1, 0:8, :] += one[:, BLOCK:]
                acc[o, tile, 8:16, :] += two[:, :BLOCK]
                acc[o, tile + 1, 8:16, :] += two[:, BLOCK:]
            return 0

        return lax.fori_loop(0, tile_of[devices, c], window, 0)

    lax.fori_loop(0, particles // CHUNK, step, 0)

    def finish(o, _):
        for q in range(layers):
            out_ref[o, 8 * q : 8 * q + 8, :] = acc[o, q, 0:8, :]
            out_ref[o, 8 * layers + 4 * q : 8 * layers + 4 * q + 4, :] = acc[o, q, 8:12, :]
        return 0

    lax.fori_loop(0, devices, finish, 0)


def place(box_owner, boxes, pos, motion, radius, temp, slots):
    devices = box_owner.shape[0]
    particles = pos.shape[1]
    layers = slots // BLOCK
    vmem = pl.BlockSpec(memory_space=VMEM)
    row = jax.ShapeDtypeStruct((1, particles), jnp.int32)
    table = (devices + 8, BLOCK)
    return pl.pallas_call(
        place_kernel,
        out_shape=(
            jax.ShapeDtypeStruct((devices, 12 * layers, BLOCK), F32), row, row,
            jax.ShapeDtypeStruct(table, jnp.int32),
        ),
        in_specs=[pl.BlockSpec(memory_space=pltpu.SMEM)] + [vmem] * 5,
        out_specs=(vmem,) * 4,
        scratch_shapes=[
            pltpu.SMEM((devices,), jnp.int32),
            pltpu.SMEM(table, jnp.int32),
            VMEM((devices, layers + 3, 16, BLOCK), F32),
            pltpu.SemaphoreType.DMA,
        ],
        compiler_params=pltpu.CompilerParams(vmem_limit_bytes=60 << 20),
        cost_estimate=pl.CostEstimate(
            flops=2 * 24 * devices * WINDOW * particles, bytes_accessed=1 << 20, transcendentals=0
        ),
        name="place_slots",
    )(box_owner, boxes, pos, motion, radius, temp)


def pair_terms(near):
    twice = jnp.concatenate([near, near], axis=0)
    high = twice.astype(BF16).astype(F32)
    low = (twice - high).astype(BF16).astype(F32)
    row = lax.broadcasted_iota(jnp.int32, (8, 1), 0)
    kept = high + low
    squares = kept * kept
    norm = -(squares[0:1] + squares[1:2] + squares[2:3])
    total = jnp.where(row < 3, norm, squares[3:4] + 0.5)
    one = total.astype(BF16).astype(F32)
    rest = total - one
    two = rest.astype(BF16).astype(F32)
    three = (rest - two).astype(BF16).astype(F32)
    third = jnp.where((row == 0) | (row == 3), one, jnp.where((row == 1) | (row == 4), two, three))
    third = jnp.where(row < 6, third, 0.0)
    crossed = 2.0 * jnp.where(row < 4, high, low)
    is_radius = (row == 3) | (row == 7)
    cross_d = jnp.where(is_radius, 0.0, crossed)
    cross_r = jnp.where(is_radius, crossed, 0.0)
    ones = jnp.ones_like(third)
    left = jnp.concatenate([high, low, third, jnp.where(row < 6, ones, 0.0)], axis=0)
    ones_d = jnp.where(row < 3, ones, 0.0)
    ones_r = jnp.where((row >= 3) & (row < 6), ones, 0.0)
    for_d = jnp.concatenate([cross_d, cross_d, ones_d, jnp.where(row < 3, third, 0.0)], axis=0)
    for_r = jnp.concatenate([cross_r, cross_r, ones_r, jnp.where((row >= 3) & (row < 6), third, 0.0)], axis=0)
    right = jnp.concatenate([for_d, for_r], axis=1)
    return left, right.astype(BF16)


def contact_kernel(slot_ref, mask_ref, out_ref):
    homes, rows, _ = slot_ref.shape
    layers = rows // 12
    blocks = [(s, q) for s in range(homes) for q in range(layers)]
    row = lax.broadcasted_iota(jnp.int32, (8, 1), 0)
    sign = jnp.where((row >= 3) & (row < 6), 1.0, -1.0)
    lane = lax.broadcasted_iota(jnp.int32, (BLOCK, BLOCK), 1) // 16

    def pairs_of(group):
        pairs = []
        for first in range(0, 8, 4):
            lefts = []
            rights = []
            for g, (s, q) in enumerate(group[first : first + 4]):
                left, right = pair_terms(slot_ref[s, 8 * layers + 4 * q : 8 * layers + 4 * q + 4, :])
                lefts.append(left)
                spots = [jnp.zeros_like(right)] * 4
                spots[g] = right
                rights.append(jnp.concatenate(spots, axis=0))
            turned = jnp.transpose(jnp.concatenate(lefts, axis=0)).astype(BF16)
            pairs.append(
                lax.dot_general(turned, jnp.concatenate(rights, axis=1), NN, preferred_element_type=F32)
            )
        return pairs

    def sums_of(number, group, pairs):
        stacked = []
        for s, q in group:
            mine = slot_ref[s, 8 * q : 8 * q + 8, :]
            high = mine.astype(BF16).astype(F32)
            stacked += [high, mine - high]
        columns = jnp.transpose(jnp.concatenate(stacked, axis=0)).astype(BF16)
        highs = []
        lows = []
        right = []
        for b in range(8):
            at = 2 * BLOCK * (b % 4)
            pair = pairs[b // 4]
            reach = pair[:, at + BLOCK : at + 2 * BLOCK]
            inverse = pl.reciprocal(reach, approx=True)
            inverse = inverse * (2.0 - reach * inverse)
            weight = mask_ref[8 * number + b].astype(F32) * jnp.exp(pair[:, at : at + BLOCK] * inverse)
            high, low = split(weight)
            highs.append(high)
            lows.append(low)
            right.append(jnp.where(lane == b, columns, jnp.zeros_like(columns)))
        return lax.dot_general(
            jnp.concatenate(highs + lows, axis=1), jnp.concatenate(right + right, axis=0), NN,
            preferred_element_type=F32,
        )

    def finish(group, sums):
        sums = jnp.transpose(sums)
        for b, (s, q) in enumerate(group):
            total = sums[16 * b : 16 * b + 8] + sums[16 * b + 8 : 16 * b + 16]
            out_ref[s, 8 * q : 8 * q + 8, :] = slot_ref[s, 8 * q : 8 * q + 8, :] * total[7:8] + sign * total

    groups = [blocks[i : i + 8] for i in range(0, len(blocks), 8)]
    pairs = pairs_of(groups[0])
    before = None
    for number, group in enumerate(groups):
        later = pairs_of(groups[number + 1]) if number + 1 < len(groups) else None
        sums = sums_of(number, group, pairs)
        if before is not None:
            finish(*before)
        before = (group, sums)
        pairs = later
    finish(*before)


def contact(arrived, mask):
    devices, rows, _ = arrived.shape
    layers = rows // 12
    blocks = mask.shape[0]
    step = 32 // layers
    return pl.pallas_call(
        contact_kernel,
        grid=(devices // step,),
        out_shape=jax.ShapeDtypeStruct((devices, 8 * layers, BLOCK), F32),
        in_specs=[
            pl.BlockSpec((step, rows, BLOCK), lambda h: (h, 0, 0)),
            pl.BlockSpec((step * layers, BLOCK, BLOCK), lambda h: (h, 0, 0)),
        ],
        out_specs=pl.BlockSpec((step, 8 * layers, BLOCK), lambda h: (h, 0, 0)),
        compiler_params=pltpu.CompilerParams(vmem_limit_bytes=60 << 20),
        cost_estimate=pl.CostEstimate(
            flops=64 * blocks * BLOCK * BLOCK, bytes_accessed=blocks * BLOCK * BLOCK * 4, transcendentals=0
        ),
        name="contact_blocks",
    )(arrived, mask)


def smoothed(centre, y_first, y_last, x_first, x_last):
    layers, rows, cols = centre.shape
    zero = jnp.zeros((1, rows, cols), F32)
    up = jnp.concatenate([centre[1:], zero], axis=0)
    down = jnp.concatenate([zero, centre[:-1]], axis=0)
    row = lax.broadcasted_iota(jnp.int32, (1, rows, cols), 1)
    col = lax.broadcasted_iota(jnp.int32, (1, rows, cols), 2)
    back = jnp.where(row == 0, y_first, pltpu.roll(centre, 1, 1))
    front = jnp.where(row == rows - 1, y_last, pltpu.roll(centre, rows - 1, 1))
    left = jnp.where(col == 0, x_first, pltpu.roll(centre, 1, 2))
    right = jnp.where(col == cols - 1, x_last, pltpu.roll(centre, cols - 1, 2))
    return CENTRE_WEIGHT * centre + SIDE_WEIGHT * ((up + down) + (back + front) + (left + right))


def columns(edge, layers, rows):
    count = edge.shape[0]
    if count < 8:
        edge = jnp.concatenate([edge] * (8 // count), axis=0)
    turned = jnp.transpose(edge)
    parts = [turned[:, a : a + 1] for a in range(count)]
    return jnp.concatenate(parts, axis=0).reshape(layers, rows, 1)


def smooth_field(field_ref, y0_ref, y1_ref, x0_ref, x1_ref, k, edge=None):
    at = k if edge is None else edge
    _, layers, rows, cols = field_ref.shape
    per = layers * rows // BLOCK
    x0 = columns(x0_ref[at * per : (at + 1) * per, :], layers, rows)
    x1 = columns(x1_ref[at * per : (at + 1) * per, :], layers, rows)
    y0 = y0_ref[at].reshape(layers, 1, cols)
    y1 = y1_ref[at].reshape(layers, 1, cols)
    return smoothed(field_ref[k], y0, y1, x0, x1)


def write_edges(field, k, y0_ref, y1_ref, x0_ref, x1_ref):
    layers, rows, cols = field.shape
    y0_ref[k] = field[:, 0, :]
    y1_ref[k] = field[:, rows - 1, :]
    flat = field.reshape(layers * rows, cols)
    for a in range(layers * rows // BLOCK):
        turned = jnp.transpose(flat[a * BLOCK : (a + 1) * BLOCK, :])
        at = k * (layers * rows // BLOCK) + a
        x0_ref[at : at + 1, :] = turned[0:1, :]
        x1_ref[at : at + 1, :] = turned[cols - 1 : cols, :]


def paired_rows(pairs, layers, rows, scratch):
    half = pairs.shape[0]
    cols = pairs.shape[1] // 2
    scratch[pl.ds(0, half, stride=2), :] = pairs[:, :cols]
    scratch[pl.ds(1, half, stride=2), :] = pairs[:, cols:]
    return scratch[...].reshape(layers, rows, cols)


def gathered(tables, rows, lanes):
    group = rows // 8
    found = [None] * len(tables)
    for g in range(len(tables[0])):
        mine = group == g
        for k, table in enumerate(tables):
            value = jnp.take_along_axis(table[g], lanes, axis=1, mode="promise_in_bounds")
            found[k] = value if g == 0 else jnp.where(mine, value, found[k])
    mine = lax.broadcasted_iota(jnp.int32, (8, BLOCK), 0) == rows % 8
    return [jnp.sum(jnp.where(mine, value, 0.0), axis=0, keepdims=True) for value in found]


def look_kernel(
    fluid_ref, y0_ref, y1_ref, x0_ref, x1_ref, cell_ref, motion_ref, radius_ref, temp_ref,
    base_ref, term_ref, table, *, chunk
):
    fields, layers, rows, cols = fluid_ref.shape
    particles = cell_ref.shape[1]
    for k in range(fields):
        table[k] = smooth_field(fluid_ref, y0_ref, y1_ref, x0_ref, x1_ref, k)

    def step(i, _):
        here = pl.ds(pl.multiple_of(i * chunk, chunk), chunk)
        cells = cell_ref[:, here]
        seen = [[] for _ in range(fields)]
        for s in range(chunk // BLOCK):
            wanted = jnp.broadcast_to(cells[:, s * BLOCK : (s + 1) * BLOCK], (8, BLOCK))
            values = gathered(
                [[table[k, z] for z in range(layers)] for k in range(fields)], wanted // cols, wanted % cols
            )
            for k in range(fields):
                seen[k].append(values[k])
        seen = [jnp.concatenate(parts, axis=1) for parts in seen]
        motion = motion_ref[:, here]
        radius = radius_ref[:, here]
        temp = temp_ref[:, here]
        fluid_vel = jnp.concatenate(seen[0:3], axis=0)
        drag = DRAG_COEFF / (radius * radius + 0.25) * (fluid_vel - motion[0:3])
        upward = lax.broadcasted_iota(jnp.int32, (3, 1), 0) == 2
        moved = motion[0:3] + TIME_STEP * drag - jnp.where(upward, TIME_STEP * GRAVITY, 0.0)
        warmed = temp + TIME_STEP * HEAT_TRANSFER * (seen[3] - temp)
        base_ref[:, here] = jnp.concatenate([moved, motion[3:6], warmed, seen[3]], axis=0)
        volume = radius * radius * radius
        term_ref[:, here] = jnp.concatenate([volume, -volume * drag], axis=0)
        return 0

    lax.fori_loop(0, particles // chunk, step, 0)


def look_up(fluid, halo, cells, motion, radius, temp):
    particles = cells.shape[1]
    vmem = pl.BlockSpec(memory_space=VMEM)
    return pl.pallas_call(
        functools.partial(look_kernel, chunk=512),
        out_shape=(
            jax.ShapeDtypeStruct((8, particles), F32),
            jax.ShapeDtypeStruct((4, particles), F32),
        ),
        in_specs=[vmem] * 9,
        out_specs=(vmem,) * 2,
        scratch_shapes=[VMEM(fluid.shape, F32)],
        compiler_params=pltpu.CompilerParams(vmem_limit_bytes=40 << 20),
        cost_estimate=pl.CostEstimate(flops=1 << 33, bytes_accessed=2 << 20, transcendentals=0),
        name="look_up",
    )(fluid, *halo, cells, motion, radius, temp)


def deposit_kernel(
    cell_ref, term_ref, dep_ref, dy0_ref, dy1_ref, dx0_ref, dx1_ref, rows_scratch, acc, *, chunk
):
    fields, layers, rows, cols = dep_ref.shape
    half = layers * rows // 2
    wide = 2 * cols
    particles = cell_ref.shape[1]
    acc[...] = jnp.zeros_like(acc)

    def step(i, _):
        here = pl.ds(pl.multiple_of(i * chunk, chunk), chunk)
        cells = cell_ref[:, here]
        hot_low = hot(wide, cells % wide)
        hot_high = hot(half, cells // wide)
        high, low = split(term_ref[:, here])
        parts = [hot_high * piece[k : k + 1] for piece in (high, low) for k in range(fields)]
        total = lax.dot_general(jnp.concatenate(parts, axis=0), hot_low, NT, preferred_element_type=F32)
        acc[...] += total[: fields * half] + total[fields * half :]
        return 0

    lax.fori_loop(0, particles // chunk, step, 0)
    for k in range(fields):
        field = paired_rows(acc[k * half : (k + 1) * half, :], layers, rows, rows_scratch)
        dep_ref[k] = field
        write_edges(field, k, dy0_ref, dy1_ref, dx0_ref, dx1_ref)


def edge_shapes(fields, layers, rows, cols):
    y_edge = jax.ShapeDtypeStruct((fields, layers, cols), F32)
    x_edge = jax.ShapeDtypeStruct((fields * layers * rows // BLOCK, BLOCK), F32)
    return (y_edge, y_edge, x_edge, x_edge)


def deposit(cells, terms, grid):
    layers, rows, cols = grid
    fields = terms.shape[0]
    particles = cells.shape[1]
    vmem = pl.BlockSpec(memory_space=VMEM)
    return pl.pallas_call(
        functools.partial(deposit_kernel, chunk=1024),
        out_shape=(jax.ShapeDtypeStruct((fields,) + grid, F32),) + edge_shapes(fields, layers, rows, cols),
        in_specs=[vmem] * 2,
        out_specs=(vmem,) * 5,
        scratch_shapes=[
            VMEM((layers * rows, cols), F32),
            VMEM((fields * layers * rows // 2, 2 * cols), F32),
        ],
        compiler_params=pltpu.CompilerParams(vmem_limit_bytes=40 << 20),
        cost_estimate=pl.CostEstimate(
            flops=4 * fields * layers * rows * cols * particles, bytes_accessed=2 << 20, transcendentals=0
        ),
        name="deposit_fields",
    )(cells, terms)


def heat_kernel(
    back_ref, slot_ref, cell_ref, radius_ref, base_ref, ey0_ref, ey1_ref, ex0_ref, ex1_ref,
    next_ref, dep_ref, dy0_ref, dy1_ref, dx0_ref, dx1_ref,
    table, acc, rows_scratch, *, chunk, rows
):
    devices, tall, _ = back_ref.shape
    layers = tall // 8
    particles = slot_ref.shape[1]
    half, wide = acc.shape
    for o in range(devices):
        for q in range(layers):
            table[o * layers + q : o * layers + q + 1, :] = back_ref[o, 8 * q + 6 : 8 * q + 7, :]
    acc[...] = jnp.zeros_like(acc)

    def step(i, _):
        here = pl.ds(pl.multiple_of(i * chunk, chunk), chunk)
        slots = slot_ref[:, here]
        gained = []
        for s in range(chunk // BLOCK):
            wanted = jnp.broadcast_to(slots[:, s * BLOCK : (s + 1) * BLOCK], (8, BLOCK))
            tiles = [table[8 * g : 8 * g + 8, :] for g in range(devices * layers // 8)]
            gained.append(gathered([tiles], wanted // BLOCK, wanted % BLOCK)[0])
        base = base_ref[6:8, here]
        total = base[0:1] + jnp.concatenate(gained, axis=1)
        next_ref[:, here] = total
        radius = radius_ref[:, here]
        high, low = split(radius * radius * radius * (total - base[1:2]))
        cells = cell_ref[:, here]
        hot_low = hot_columns(wide, cells % wide)
        hot_high = hot(half, cells // wide)
        added = lax.dot_general(hot_high * high, hot_low, NN, preferred_element_type=F32)
        acc[...] += added + lax.dot_general(hot_high * low, hot_low, NN, preferred_element_type=F32)
        return 0

    lax.fori_loop(0, particles // chunk, step, 0)
    field = paired_rows(acc[...], 2 * half // rows, rows, rows_scratch)
    dep_ref[0] = field
    for edge, out in ((ey0_ref, dy0_ref), (ey1_ref, dy1_ref), (ex0_ref, dx0_ref), (ex1_ref, dx1_ref)):
        out[0 : edge.shape[0]] = edge[...]
    write_edges(field, ey0_ref.shape[0], dy0_ref, dy1_ref, dx0_ref, dx1_ref)


def heat_deposit(back, slot_of, cells, radius, base, edges, grid):
    devices = back.shape[0]
    layers, rows, cols = grid
    particles = cells.shape[1]
    half = layers * rows // 2
    fields = edges[0].shape[0] + 1
    vmem = pl.BlockSpec(memory_space=VMEM)
    return pl.pallas_call(
        functools.partial(heat_kernel, chunk=1024, rows=rows),
        out_shape=(
            jax.ShapeDtypeStruct((1, particles), F32),
            jax.ShapeDtypeStruct((1,) + grid, F32),
        ) + edge_shapes(fields, layers, rows, cols),
        in_specs=[vmem] * 9,
        out_specs=(vmem,) * 6,
        scratch_shapes=[
            VMEM((devices * back.shape[1] // 8, BLOCK), F32),
            VMEM((half, 2 * cols), F32),
            VMEM((layers * rows, cols), F32),
        ],
        compiler_params=pltpu.CompilerParams(vmem_limit_bytes=40 << 20),
        cost_estimate=pl.CostEstimate(
            flops=4 * half * 2 * cols * particles, bytes_accessed=1 << 20, transcendentals=0
        ),
        name="heat_deposit",
    )(back, slot_of, cells, radius, base, *edges)


def fetch_kernel(
    owner_ref, tile_ref, back_ref, box_ref, spot_ref, base_ref, warm_ref, next_ref, box_of, table, wanted
):
    devices, tall, _ = back_ref.shape
    layers = tall // 8
    particles = box_ref.shape[1]
    invert(owner_ref, box_of)
    for o in range(devices):
        for q in range(layers):
            high, low = split(back_ref[o, 8 * q : 8 * q + 8, :])
            table[o, q] = jnp.concatenate([high, low], axis=0)
        for q in range(layers, layers + 3):
            table[o, q] = jnp.zeros((16, BLOCK), BF16)

    def step(c, _):
        here = pl.ds(pl.multiple_of(c * CHUNK, CHUNK), CHUNK)
        boxes = jnp.broadcast_to(box_ref[:, here], (8, CHUNK))

        def window(w, total):
            for o in range(devices):
                tile = tile_ref[box_of[o], c] + 2 * w
                wanted[16 * o : 16 * o + 16, 0:BLOCK] = table[o, tile]
                wanted[16 * o : 16 * o + 16, BLOCK:] = table[o, tile + 1]
            hot_spot = hot(WINDOW, spot_ref[:, here] - WINDOW * w)
            found = lax.dot_general(wanted[...], hot_spot, NN, preferred_element_type=F32)
            gained = jnp.zeros((8, CHUNK), F32)
            for o in range(devices):
                value = found[16 * o : 16 * o + 8] + found[16 * o + 8 : 16 * o + 16]
                gained = jnp.where(boxes == box_of[o], value, gained)
            return total + gained

        gained = lax.fori_loop(0, tile_ref[devices, c], window, jnp.zeros((8, CHUNK), F32))
        next_ref[:, here] = jnp.concatenate(
            [base_ref[0:6, here] + gained[0:6], warm_ref[:, here]], axis=0
        )
        return 0

    lax.fori_loop(0, particles // CHUNK, step, 0)


def fetch(box_owner, tiles, back, boxes, spots, base, warm):
    devices, tall, _ = back.shape
    layers = tall // 8
    particles = boxes.shape[1]
    vmem = pl.BlockSpec(memory_space=VMEM)
    smem = pl.BlockSpec(memory_space=pltpu.SMEM)
    return pl.pallas_call(
        fetch_kernel,
        out_shape=jax.ShapeDtypeStruct((7, particles), F32),
        in_specs=[smem, smem] + [vmem] * 5,
        out_specs=vmem,
        scratch_shapes=[
            pltpu.SMEM((devices,), jnp.int32),
            VMEM((devices, layers + 3, 16, BLOCK), BF16),
            VMEM((16 * devices, WINDOW), BF16),
        ],
        compiler_params=pltpu.CompilerParams(vmem_limit_bytes=40 << 20),
        cost_estimate=pl.CostEstimate(
            flops=32 * devices * WINDOW * particles, bytes_accessed=1 << 20, transcendentals=0
        ),
        name="fetch_slots",
    )(box_owner, tiles, back, boxes, spots, base, warm)


def spread_kernel(dep_ref, heat_ref, y0_ref, y1_ref, x0_ref, x1_ref, fluid_ref, next_ref, void_ref):
    halo = (y0_ref, y1_ref, x0_ref, x1_ref)
    crowding = 1.0 + COUPLING * smooth_field(dep_ref, *halo, 0)
    void_ref[...] = 1.0 / crowding
    for k in range(3):
        next_ref[k] = fluid_ref[k] + TIME_STEP * COUPLING * smooth_field(dep_ref, *halo, k + 1) * crowding
    warmth = smooth_field(heat_ref, *halo, 0, 4)
    next_ref[3] = fluid_ref[3] + TIME_STEP * COUPLING * warmth * crowding


def spread(dep, heat, halo, fluid):
    vmem = pl.BlockSpec(memory_space=VMEM)
    return pl.pallas_call(
        spread_kernel,
        out_shape=(jax.ShapeDtypeStruct(fluid.shape, F32), jax.ShapeDtypeStruct(fluid.shape[1:], F32)),
        in_specs=[vmem] * 7,
        out_specs=(vmem,) * 2,
        compiler_params=pltpu.CompilerParams(vmem_limit_bytes=40 << 20),
        cost_estimate=pl.CostEstimate(flops=20 * fluid.size, bytes_accessed=2 << 20, transcendentals=0),
        name="spread_fields",
    )(dep, heat, *halo, fluid)


def halo_of(y_first, y_last, x_first, x_last):
    def moved(value, axis, step):
        size = lax.axis_size(axis)
        pairs = [(i, i + step) for i in range(size) if 0 <= i + step < size]
        return lax.ppermute(value, axis, pairs)

    return (
        moved(y_last, "gy", 1),
        moved(y_first, "gy", -1),
        moved(x_last, "gx", 1),
        moved(x_first, "gx", -1),
    )


def shards(
    fluid_state, particle_pos, particle_motion, particle_radius, particle_temp,
    particle_cell, particle_box, box_owner, contact_mask,
):
    devices = lax.axis_size(("gx", "gy"))
    particles = particle_pos.shape[1]
    slots = 2 * particles // devices
    fields, layers, rows, cols = fluid_state.shape
    boxes = particle_box.reshape(1, particles)
    radius = particle_radius.reshape(1, particles)
    temp = particle_temp.reshape(1, particles)
    cells = particle_cell.reshape(1, particles)

    outgoing, slot_of, spots, tiles = place(
        box_owner, boxes, particle_pos, particle_motion, radius, temp, slots
    )
    arrived = lax.all_to_all(outgoing, ("gx", "gy"), split_axis=0, concat_axis=0, tiled=True)

    spots, fluid = lax.optimization_barrier((spots, fluid_state))
    fluid_halo = halo_of(
        fluid[:, :, 0, :],
        fluid[:, :, rows - 1, :],
        fluid[:, :, :, 0].reshape(-1, BLOCK),
        fluid[:, :, :, cols - 1].reshape(-1, BLOCK),
    )
    base, terms = look_up(fluid_state, fluid_halo, cells, particle_motion, radius, temp)
    arrived, base, terms = lax.optimization_barrier((arrived, base, terms))

    result = contact(arrived, contact_mask)
    result, terms = lax.optimization_barrier((result, terms))
    deposits, *edges = deposit(cells, terms, (layers, rows, cols))
    back = lax.all_to_all(result, ("gx", "gy"), split_axis=0, concat_axis=0, tiled=True)
    warm, heat_field, *edges = heat_deposit(
        back, slot_of, cells, radius, base, edges, (layers, rows, cols)
    )
    halo = halo_of(*edges)
    particle_next = fetch(box_owner, tiles, back, boxes, spots, base, warm)
    fluid_next, void_fraction = spread(deposits, heat_field, halo, fluid_state)
    return (fluid_next, void_fraction, particle_next)


def solution(mesh):
    in_specs = (
        P(None, None, "gy", "gx"),
        P(None, ("gx", "gy")),
        P(None, ("gx", "gy")),
        P(("gx", "gy")),
        P(("gx", "gy")),
        P(("gx", "gy")),
        P(("gx", "gy"), None),
        P(),
        P(("gx", "gy"), None, None),
    )
    out_specs = (P(None, None, "gy", "gx"), P(None, "gy", "gx"), P(None, ("gx", "gy")))
    return jax.shard_map(shards, mesh=mesh, in_specs=in_specs, out_specs=out_specs, check_vma=False)
```

```python
import functools

import jax
import jax.numpy as jnp
from jax import lax
from jax.experimental import pallas as pl
from jax.experimental.pallas import tpu as pltpu
from jax.sharding import PartitionSpec as P

BLOCK = 128
TIME_STEP = 0.1
STIFFNESS = 0.5
DAMPING_RATE = 0.2
ROTATION_DRAG = 0.1
DRAG_COEFF = 4.0
CONDUCTION = 0.3
HEAT_TRANSFER = 4.0
GRAVITY = 0.3
COUPLING = 4.0
CENTRE_WEIGHT = 0.25
SIDE_WEIGHT = 0.125

F32 = jnp.float32
BF16 = jnp.bfloat16
VMEM = pltpu.VMEM
NN = (((1,), (0,)), ((), ()))
NT = (((1,), (1,)), ((), ()))


def split(value):
    high = value.astype(BF16)
    return high, (value - high.astype(F32)).astype(BF16)


def hot(count, row):
    places = lax.broadcasted_iota(jnp.int32, (count, row.shape[1]), 0)
    return jnp.where(places == row, 1.0, 0.0).astype(BF16)


def hot_columns(count, row):
    n = row.shape[1] // BLOCK
    tiles = [row[:, a * BLOCK : (a + 1) * BLOCK] for a in range(n)]
    turned = jnp.transpose(jnp.concatenate(tiles * (8 // n), axis=0).astype(F32))
    places = lax.broadcasted_iota(jnp.int32, (BLOCK, count), 1).astype(F32)
    return jnp.concatenate(
        [jnp.where(places == turned[:, a : a + 1], 1.0, 0.0).astype(BF16) for a in range(n)], axis=0
    )


def invert(owner_ref, box_of):
    def step(b, _):
        box_of[owner_ref[b]] = b
        return 0

    lax.fori_loop(0, owner_ref.shape[0], step, 0)


WINDOW = 256
CHUNK = 1024


def place_kernel(
    owner_ref, box_ref, pos_ref, motion_ref, radius_ref, temp_ref,
    out_ref, slot_ref, spot_ref, tile_ref,
    box_of, tile_of, acc, done
):
    devices, rows, _ = out_ref.shape
    layers = rows // 12
    slots = layers * BLOCK
    particles = box_ref.shape[1]
    sub = 256
    invert(owner_ref, box_of)
    acc[...] = jnp.zeros_like(acc)

    box_row = lax.broadcasted_iota(jnp.int32, (devices, 1), 0)
    owner_column = jnp.zeros((devices, 1), F32)
    for b in range(devices):
        owner_column = jnp.where(box_row == b, owner_ref[b].astype(F32), owner_column)
    above = (
        lax.broadcasted_iota(jnp.int32, (sub, sub), 0) < lax.broadcasted_iota(jnp.int32, (sub, sub), 1)
    )
    above = jnp.where(above, 1.0, 0.0).astype(BF16)
    lane = lax.broadcasted_iota(jnp.int32, (devices, BLOCK), 1)
    tiles = jnp.zeros((devices, BLOCK), F32)
    spans = jnp.zeros((8, BLOCK), F32)
    carry = jnp.zeros((devices, 1), F32)
    per_chunk = CHUNK // sub
    for c in range(particles // CHUNK):
        chosen = []
        for s in range(per_chunk):
            at = c * CHUNK + s * sub
            chosen.append(
                lax.broadcasted_iota(jnp.int32, (devices, sub), 0) == box_ref[:, at : at + sub]
            )
        ones = [jnp.where(mine, 1.0, 0.0) for mine in chosen]
        earlier = lax.dot_general(
            jnp.concatenate(ones, axis=0).astype(BF16), above, NN, preferred_element_type=F32
        )
        tile = jnp.minimum(jnp.floor(carry * (1.0 / BLOCK)), layers - 1.0)
        tiles = jnp.where(lane == c, tile, tiles)
        highest = jnp.zeros((1, 1), F32)
        for s in range(per_chunk):
            at = c * CHUNK + s * sub
            rank = earlier[s * devices : (s + 1) * devices] + carry
            spot = jnp.where(chosen[s], rank - BLOCK * tile, 0.0)
            spot = jnp.sum(spot, axis=0, keepdims=True)
            slot = jnp.where(chosen[s], rank + slots * owner_column, 0.0)
            slot = jnp.sum(slot, axis=0, keepdims=True)
            spot_ref[:, at : at + sub] = spot.astype(jnp.int32)
            slot_ref[:, at : at + sub] = slot.astype(jnp.int32)
            highest = jnp.maximum(highest, jnp.max(spot, axis=1, keepdims=True))
            carry = carry + jnp.sum(ones[s], axis=1, keepdims=True)
        windows = jnp.floor(highest * (1.0 / WINDOW)) + 1.0
        spans = jnp.where(lane[0:8] == c, windows, spans)
    if devices < BLOCK:
        tiles = jnp.concatenate([tiles, jnp.zeros((BLOCK - devices, BLOCK), F32)], axis=0)
    count = tile_ref.shape[0] - 8
    tile_ref[0:count, :] = jnp.transpose(tiles)[0:count].astype(jnp.int32)
    tile_ref[count : count + 8, :] = spans.astype(jnp.int32)
    copy = pltpu.make_async_copy(tile_ref, tile_of, done)
    copy.start()
    copy.wait()

    def step(c, _):
        here = pl.ds(pl.multiple_of(c * CHUNK, CHUNK), CHUNK)
        boxes = box_ref[:, here]
        pos = pos_ref[:, here]
        motion = motion_ref[:, here]
        push = TIME_STEP * STIFFNESS * pos - TIME_STEP * DAMPING_RATE * motion[0:3]
        spin = -TIME_STEP * ROTATION_DRAG * motion[3:6]
        heat = -TIME_STEP * CONDUCTION * temp_ref[:, here]
        first = jnp.concatenate([push, spin, heat, jnp.ones((1, CHUNK), F32)], axis=0)
        second = jnp.concatenate([pos, radius_ref[:, here]], axis=0)
        first = jnp.concatenate(split(first), axis=0)
        second = jnp.concatenate(split(second) * 2, axis=0)
        lower = lax.broadcasted_iota(jnp.int32, (16, 1), 0) < 8
        box16 = jnp.broadcast_to(boxes, (16, CHUNK)).astype(F32).astype(BF16)
        first_parts = []
        second_parts = []
        for o in range(devices):
            mine = box16 == box_of[o].astype(F32).astype(BF16)
            first_parts.append(jnp.where(mine, first, jnp.zeros_like(first)))
            if o % 2 == 0:
                either = jnp.where(lower, box_of[o].astype(F32), box_of[o + 1].astype(F32)).astype(BF16)
                second_parts.append(jnp.where(box16 == either, second, jnp.zeros_like(second)))
        parts = jnp.concatenate(first_parts + second_parts, axis=0)

        def window(w, _):
            hot_spot = hot(WINDOW, spot_ref[:, here] - WINDOW * w)
            placed = lax.dot_general(parts, hot_spot, NT, preferred_element_type=F32)
            for o in range(devices):
                tile = tile_of[c, box_of[o]] + 2 * w
                one = placed[16 * o : 16 * o + 8] + placed[16 * o + 8 : 16 * o + 16]
                two = placed[16 * devices + 8 * o : 16 * devices + 8 * o + 8]
                two = two + pltpu.roll(two, 4, 0)
                acc[o, tile, 0:8, :] += one[:, :BLOCK]
                acc[o, tile + 1, 0:8, :] += one[:, BLOCK:]
                acc[o, tile, 8:16, :] += two[:, :BLOCK]
                acc[o, tile + 1, 8:16, :] += two[:, BLOCK:]
            return 0

        return lax.fori_loop(0, tile_of[tile_ref.shape[0] - 8, c], window, 0)

    lax.fori_loop(0, particles // CHUNK, step, 0)

    def finish(o, _):
        for q in range(layers):
            out_ref[o, 8 * q : 8 * q + 8, :] = acc[o, q, 0:8, :]
            out_ref[o, 8 * layers + 4 * q : 8 * layers + 4 * q + 4, :] = acc[o, q, 8:12, :]
        return 0

    lax.fori_loop(0, devices, finish, 0)


def place(box_owner, boxes, pos, motion, radius, temp, slots):
    devices = box_owner.shape[0]
    particles = pos.shape[1]
    layers = slots // BLOCK
    vmem = pl.BlockSpec(memory_space=VMEM)
    row = jax.ShapeDtypeStruct((1, particles), jnp.int32)
    table = (-(-particles // (8 * CHUNK)) * 8 + 8, BLOCK)
    return pl.pallas_call(
        place_kernel,
        out_shape=(
            jax.ShapeDtypeStruct((devices, 12 * layers, BLOCK), F32), row, row,
            jax.ShapeDtypeStruct(table, jnp.int32),
        ),
        in_specs=[pl.BlockSpec(memory_space=pltpu.SMEM)] + [vmem] * 5,
        out_specs=(vmem,) * 4,
        scratch_shapes=[
            pltpu.SMEM((devices,), jnp.int32),
            pltpu.SMEM(table, jnp.int32),
            VMEM((devices, layers + 3, 16, BLOCK), F32),
            pltpu.SemaphoreType.DMA,
        ],
        compiler_params=pltpu.CompilerParams(vmem_limit_bytes=60 << 20),
        cost_estimate=pl.CostEstimate(
            flops=2 * 24 * devices * WINDOW * particles, bytes_accessed=1 << 20, transcendentals=0
        ),
        name="place_slots",
    )(box_owner, boxes, pos, motion, radius, temp)


def pair_terms(near):
    twice = jnp.concatenate([near, near], axis=0)
    high = twice.astype(BF16).astype(F32)
    low = (twice - high).astype(BF16).astype(F32)
    row = lax.broadcasted_iota(jnp.int32, (8, 1), 0)
    kept = high + low
    squares = kept * kept
    norm = -(squares[0:1] + squares[1:2] + squares[2:3])
    total = jnp.where(row < 3, norm, squares[3:4] + 0.5)
    one = total.astype(BF16).astype(F32)
    rest = total - one
    two = rest.astype(BF16).astype(F32)
    three = (rest - two).astype(BF16).astype(F32)
    third = jnp.where((row == 0) | (row == 3), one, jnp.where((row == 1) | (row == 4), two, three))
    third = jnp.where(row < 6, third, 0.0)
    crossed = 2.0 * jnp.where(row < 4, high, low)
    is_radius = (row == 3) | (row == 7)
    cross_d = jnp.where(is_radius, 0.0, crossed)
    cross_r = jnp.where(is_radius, crossed, 0.0)
    ones = jnp.ones_like(third)
    left = jnp.concatenate([high, low, third, jnp.where(row < 6, ones, 0.0)], axis=0)
    ones_d = jnp.where(row < 3, ones, 0.0)
    ones_r = jnp.where((row >= 3) & (row < 6), ones, 0.0)
    for_d = jnp.concatenate([cross_d, cross_d, ones_d, jnp.where(row < 3, third, 0.0)], axis=0)
    for_r = jnp.concatenate([cross_r, cross_r, ones_r, jnp.where((row >= 3) & (row < 6), third, 0.0)], axis=0)
    right = jnp.concatenate([for_d, for_r], axis=1)
    return left, right.astype(BF16)


def contact_kernel(slot_ref, mask_ref, out_ref):
    homes, rows, _ = slot_ref.shape
    layers = rows // 12
    blocks = [(s, q) for s in range(homes) for q in range(layers)]
    row = lax.broadcasted_iota(jnp.int32, (8, 1), 0)
    sign = jnp.where((row >= 3) & (row < 6), 1.0, -1.0)
    lane = lax.broadcasted_iota(jnp.int32, (BLOCK, BLOCK), 1) // 16

    def pairs_of(group):
        pairs = []
        for first in range(0, 8, 4):
            lefts = []
            rights = []
            for g, (s, q) in enumerate(group[first : first + 4]):
                left, right = pair_terms(slot_ref[s, 8 * layers + 4 * q : 8 * layers + 4 * q + 4, :])
                lefts.append(left)
                spots = [jnp.zeros_like(right)] * 4
                spots[g] = right
                rights.append(jnp.concatenate(spots, axis=0))
            turned = jnp.transpose(jnp.concatenate(lefts, axis=0)).astype(BF16)
            pairs.append(
                lax.dot_general(turned, jnp.concatenate(rights, axis=1), NN, preferred_element_type=F32)
            )
        return pairs

    def sums_of(number, group, pairs):
        stacked = []
        for s, q in group:
            mine = slot_ref[s, 8 * q : 8 * q + 8, :]
            high = mine.astype(BF16).astype(F32)
            stacked += [high, mine - high]
        columns = jnp.transpose(jnp.concatenate(stacked, axis=0)).astype(BF16)
        highs = []
        lows = []
        right = []
        for b in range(8):
            at = 2 * BLOCK * (b % 4)
            pair = pairs[b // 4]
            reach = pair[:, at + BLOCK : at + 2 * BLOCK]
            inverse = pl.reciprocal(reach, approx=True)
            inverse = inverse * (2.0 - reach * inverse)
            weight = mask_ref[8 * number + b].astype(F32) * jnp.exp(pair[:, at : at + BLOCK] * inverse)
            high, low = split(weight)
            highs.append(high)
            lows.append(low)
            right.append(jnp.where(lane == b, columns, jnp.zeros_like(columns)))
        return lax.dot_general(
            jnp.concatenate(highs + lows, axis=1), jnp.concatenate(right + right, axis=0), NN,
            preferred_element_type=F32,
        )

    def finish(group, sums):
        sums = jnp.transpose(sums)
        for b, (s, q) in enumerate(group):
            total = sums[16 * b : 16 * b + 8] + sums[16 * b + 8 : 16 * b + 16]
            out_ref[s, 8 * q : 8 * q + 8, :] = slot_ref[s, 8 * q : 8 * q + 8, :] * total[7:8] + sign * total

    groups = [blocks[i : i + 8] for i in range(0, len(blocks), 8)]
    pairs = pairs_of(groups[0])
    before = None
    for number, group in enumerate(groups):
        later = pairs_of(groups[number + 1]) if number + 1 < len(groups) else None
        sums = sums_of(number, group, pairs)
        if before is not None:
            finish(*before)
        before = (group, sums)
        pairs = later
    finish(*before)


def contact(arrived, mask):
    devices, rows, _ = arrived.shape
    layers = rows // 12
    blocks = mask.shape[0]
    step = 32 // layers
    return pl.pallas_call(
        contact_kernel,
        grid=(devices // step,),
        out_shape=jax.ShapeDtypeStruct((devices, 8 * layers, BLOCK), F32),
        in_specs=[
            pl.BlockSpec((step, rows, BLOCK), lambda h: (h, 0, 0)),
            pl.BlockSpec((step * layers, BLOCK, BLOCK), lambda h: (h, 0, 0)),
        ],
        out_specs=pl.BlockSpec((step, 8 * layers, BLOCK), lambda h: (h, 0, 0)),
        compiler_params=pltpu.CompilerParams(vmem_limit_bytes=60 << 20),
        cost_estimate=pl.CostEstimate(
            flops=64 * blocks * BLOCK * BLOCK, bytes_accessed=blocks * BLOCK * BLOCK * 4, transcendentals=0
        ),
        name="contact_blocks",
    )(arrived, mask)


def smoothed(centre, y_first, y_last, x_first, x_last):
    layers, rows, cols = centre.shape
    zero = jnp.zeros((1, rows, cols), F32)
    up = jnp.concatenate([centre[1:], zero], axis=0)
    down = jnp.concatenate([zero, centre[:-1]], axis=0)
    row = lax.broadcasted_iota(jnp.int32, (1, rows, cols), 1)
    col = lax.broadcasted_iota(jnp.int32, (1, rows, cols), 2)
    back = jnp.where(row == 0, y_first, pltpu.roll(centre, 1, 1))
    front = jnp.where(row == rows - 1, y_last, pltpu.roll(centre, rows - 1, 1))
    left = jnp.where(col == 0, x_first, pltpu.roll(centre, 1, 2))
    right = jnp.where(col == cols - 1, x_last, pltpu.roll(centre, cols - 1, 2))
    return CENTRE_WEIGHT * centre + SIDE_WEIGHT * ((up + down) + (back + front) + (left + right))


def columns(edge, layers, rows):
    count = edge.shape[0]
    if count < 8:
        edge = jnp.concatenate([edge] * (8 // count), axis=0)
    turned = jnp.transpose(edge)
    parts = [turned[:, a : a + 1] for a in range(count)]
    return jnp.concatenate(parts, axis=0).reshape(layers, rows, 1)


def smooth_field(field_ref, y0_ref, y1_ref, x0_ref, x1_ref, k, edge=None):
    at = k if edge is None else edge
    _, layers, rows, cols = field_ref.shape
    per = layers * rows // BLOCK
    x0 = columns(x0_ref[at * per : (at + 1) * per, :], layers, rows)
    x1 = columns(x1_ref[at * per : (at + 1) * per, :], layers, rows)
    y0 = y0_ref[at].reshape(layers, 1, cols)
    y1 = y1_ref[at].reshape(layers, 1, cols)
    return smoothed(field_ref[k], y0, y1, x0, x1)


def write_edges(field, k, y0_ref, y1_ref, x0_ref, x1_ref):
    layers, rows, cols = field.shape
    y0_ref[k] = field[:, 0, :]
    y1_ref[k] = field[:, rows - 1, :]
    flat = field.reshape(layers * rows, cols)
    for a in range(layers * rows // BLOCK):
        turned = jnp.transpose(flat[a * BLOCK : (a + 1) * BLOCK, :])
        at = k * (layers * rows // BLOCK) + a
        x0_ref[at : at + 1, :] = turned[0:1, :]
        x1_ref[at : at + 1, :] = turned[cols - 1 : cols, :]


def paired_rows(pairs, layers, rows, scratch):
    half = pairs.shape[0]
    cols = pairs.shape[1] // 2
    scratch[pl.ds(0, half, stride=2), :] = pairs[:, :cols]
    scratch[pl.ds(1, half, stride=2), :] = pairs[:, cols:]
    return scratch[...].reshape(layers, rows, cols)


def gathered(tables, rows, lanes):
    group = rows // 8
    found = [None] * len(tables)
    for g in range(len(tables[0])):
        mine = group == g
        for k, table in enumerate(tables):
            value = jnp.take_along_axis(table[g], lanes, axis=1, mode="promise_in_bounds")
            found[k] = value if g == 0 else jnp.where(mine, value, found[k])
    mine = lax.broadcasted_iota(jnp.int32, (8, BLOCK), 0) == rows % 8
    return [jnp.sum(jnp.where(mine, value, 0.0), axis=0, keepdims=True) for value in found]


def look_kernel(
    fluid_ref, y0_ref, y1_ref, x0_ref, x1_ref, cell_ref, motion_ref, radius_ref, temp_ref,
    base_ref, term_ref, table, rows_scratch, *, chunk
):
    fields, layers, rows, cols = fluid_ref.shape
    particles = cell_ref.shape[1]
    half = layers * rows // 2
    wide = 2 * cols
    for k in range(fields):
        rows_scratch[...] = smooth_field(fluid_ref, y0_ref, y1_ref, x0_ref, x1_ref, k).reshape(layers * rows, cols)
        here = slice(k * half, (k + 1) * half)
        for part in range(2):
            high, low = split(rows_scratch[pl.ds(part, half, stride=2), :])
            table[here, part * cols : (part + 1) * cols] = high
            table[here, wide + part * cols : wide + (part + 1) * cols] = low

    def step(i, _):
        here = pl.ds(pl.multiple_of(i * chunk, chunk), chunk)
        cells = cell_ref[:, here]
        hot_low = hot(wide, cells % wide)
        found = lax.dot_general(
            table[...], jnp.concatenate([hot_low, hot_low], axis=0), NN, preferred_element_type=F32
        )
        mine = lax.broadcasted_iota(jnp.int32, (half, chunk), 0) == cells // wide
        seen = [
            jnp.sum(jnp.where(mine, found[k * half : (k + 1) * half], 0.0), axis=0, keepdims=True)
            for k in range(fields)
        ]
        motion = motion_ref[:, here]
        radius = radius_ref[:, here]
        temp = temp_ref[:, here]
        fluid_vel = jnp.concatenate(seen[0:3], axis=0)
        drag = DRAG_COEFF / (radius * radius + 0.25) * (fluid_vel - motion[0:3])
        upward = lax.broadcasted_iota(jnp.int32, (3, 1), 0) == 2
        moved = motion[0:3] + TIME_STEP * drag - jnp.where(upward, TIME_STEP * GRAVITY, 0.0)
        warmed = temp + TIME_STEP * HEAT_TRANSFER * (seen[3] - temp)
        base_ref[:, here] = jnp.concatenate([moved, motion[3:6], warmed, seen[3]], axis=0)
        volume = radius * radius * radius
        term_ref[:, here] = jnp.concatenate([volume, -volume * drag], axis=0)
        return 0

    lax.fori_loop(0, particles // chunk, step, 0)


def look_up(fluid, halo, cells, motion, radius, temp):
    fields, layers, rows, cols = fluid.shape
    particles = cells.shape[1]
    vmem = pl.BlockSpec(memory_space=VMEM)
    return pl.pallas_call(
        functools.partial(look_kernel, chunk=512),
        out_shape=(
            jax.ShapeDtypeStruct((8, particles), F32),
            jax.ShapeDtypeStruct((4, particles), F32),
        ),
        in_specs=[vmem] * 9,
        out_specs=(vmem,) * 2,
        scratch_shapes=[
            VMEM((fields * layers * rows // 2, 4 * cols), BF16),
            VMEM((layers * rows, cols), F32),
        ],
        compiler_params=pltpu.CompilerParams(vmem_limit_bytes=40 << 20),
        cost_estimate=pl.CostEstimate(flops=1 << 33, bytes_accessed=2 << 20, transcendentals=0),
        name="look_up",
    )(fluid, *halo, cells, motion, radius, temp)


def deposit_kernel(
    cell_ref, term_ref, dep_ref, dy0_ref, dy1_ref, dx0_ref, dx1_ref, rows_scratch, acc, *, chunk
):
    fields, layers, rows, cols = dep_ref.shape
    half = layers * rows // 2
    wide = 2 * cols
    particles = cell_ref.shape[1]
    acc[...] = jnp.zeros_like(acc)

    def step(i, _):
        here = pl.ds(pl.multiple_of(i * chunk, chunk), chunk)
        cells = cell_ref[:, here]
        hot_low = hot(wide, cells % wide)
        hot_high = hot(half, cells // wide)
        high, low = split(term_ref[:, here])
        parts = [hot_high * piece[k : k + 1] for piece in (high, low) for k in range(fields)]
        total = lax.dot_general(jnp.concatenate(parts, axis=0), hot_low, NT, preferred_element_type=F32)
        acc[...] += total[: fields * half] + total[fields * half :]
        return 0

    lax.fori_loop(0, particles // chunk, step, 0)
    for k in range(fields):
        field = paired_rows(acc[k * half : (k + 1) * half, :], layers, rows, rows_scratch)
        dep_ref[k] = field
        write_edges(field, k, dy0_ref, dy1_ref, dx0_ref, dx1_ref)


def edge_shapes(fields, layers, rows, cols):
    y_edge = jax.ShapeDtypeStruct((fields, layers, cols), F32)
    x_edge = jax.ShapeDtypeStruct((fields * layers * rows // BLOCK, BLOCK), F32)
    return (y_edge, y_edge, x_edge, x_edge)


def deposit(cells, terms, grid):
    layers, rows, cols = grid
    fields = terms.shape[0]
    particles = cells.shape[1]
    vmem = pl.BlockSpec(memory_space=VMEM)
    return pl.pallas_call(
        functools.partial(deposit_kernel, chunk=1024),
        out_shape=(jax.ShapeDtypeStruct((fields,) + grid, F32),) + edge_shapes(fields, layers, rows, cols),
        in_specs=[vmem] * 2,
        out_specs=(vmem,) * 5,
        scratch_shapes=[
            VMEM((layers * rows, cols), F32),
            VMEM((fields * layers * rows // 2, 2 * cols), F32),
        ],
        compiler_params=pltpu.CompilerParams(vmem_limit_bytes=40 << 20),
        cost_estimate=pl.CostEstimate(
            flops=4 * fields * layers * rows * cols * particles, bytes_accessed=2 << 20, transcendentals=0
        ),
        name="deposit_fields",
    )(cells, terms)


def heat_kernel(
    back_ref, slot_ref, cell_ref, radius_ref, base_ref, ey0_ref, ey1_ref, ex0_ref, ex1_ref,
    next_ref, dep_ref, dy0_ref, dy1_ref, dx0_ref, dx1_ref,
    table, acc, rows_scratch, *, chunk, rows
):
    devices, tall, _ = back_ref.shape
    layers = tall // 8
    particles = slot_ref.shape[1]
    half, wide = acc.shape
    for o in range(devices):
        for q in range(layers):
            table[o * layers + q : o * layers + q + 1, :] = back_ref[o, 8 * q + 6 : 8 * q + 7, :]
    acc[...] = jnp.zeros_like(acc)

    def step(i, _):
        here = pl.ds(pl.multiple_of(i * chunk, chunk), chunk)
        slots = slot_ref[:, here]
        gained = []
        for s in range(chunk // BLOCK):
            wanted = jnp.broadcast_to(slots[:, s * BLOCK : (s + 1) * BLOCK], (8, BLOCK))
            tiles = [table[8 * g : 8 * g + 8, :] for g in range(devices * layers // 8)]
            gained.append(gathered([tiles], wanted // BLOCK, wanted % BLOCK)[0])
        base = base_ref[6:8, here]
        total = base[0:1] + jnp.concatenate(gained, axis=1)
        next_ref[:, here] = total
        radius = radius_ref[:, here]
        high, low = split(radius * radius * radius * (total - base[1:2]))
        cells = cell_ref[:, here]
        hot_low = hot_columns(wide, cells % wide)
        hot_high = hot(half, cells // wide)
        added = lax.dot_general(hot_high * high, hot_low, NN, preferred_element_type=F32)
        acc[...] += added + lax.dot_general(hot_high * low, hot_low, NN, preferred_element_type=F32)
        return 0

    lax.fori_loop(0, particles // chunk, step, 0)
    field = paired_rows(acc[...], 2 * half // rows, rows, rows_scratch)
    dep_ref[0] = field
    for edge, out in ((ey0_ref, dy0_ref), (ey1_ref, dy1_ref), (ex0_ref, dx0_ref), (ex1_ref, dx1_ref)):
        out[0 : edge.shape[0]] = edge[...]
    write_edges(field, ey0_ref.shape[0], dy0_ref, dy1_ref, dx0_ref, dx1_ref)


def heat_deposit(back, slot_of, cells, radius, base, edges, grid):
    devices = back.shape[0]
    layers, rows, cols = grid
    particles = cells.shape[1]
    half = layers * rows // 2
    fields = edges[0].shape[0] + 1
    vmem = pl.BlockSpec(memory_space=VMEM)
    return pl.pallas_call(
        functools.partial(heat_kernel, chunk=1024, rows=rows),
        out_shape=(
            jax.ShapeDtypeStruct((1, particles), F32),
            jax.ShapeDtypeStruct((1,) + grid, F32),
        ) + edge_shapes(fields, layers, rows, cols),
        in_specs=[vmem] * 9,
        out_specs=(vmem,) * 6,
        scratch_shapes=[
            VMEM((devices * back.shape[1] // 8, BLOCK), F32),
            VMEM((half, 2 * cols), F32),
            VMEM((layers * rows, cols), F32),
        ],
        compiler_params=pltpu.CompilerParams(vmem_limit_bytes=40 << 20),
        cost_estimate=pl.CostEstimate(
            flops=4 * half * 2 * cols * particles, bytes_accessed=1 << 20, transcendentals=0
        ),
        name="heat_deposit",
    )(back, slot_of, cells, radius, base, *edges)


def fetch_kernel(
    owner_ref, tile_ref, back_ref, box_ref, spot_ref, base_ref, warm_ref, next_ref, box_of, table, wanted
):
    devices, tall, _ = back_ref.shape
    layers = tall // 8
    particles = box_ref.shape[1]
    invert(owner_ref, box_of)
    for o in range(devices):
        for q in range(layers):
            high, low = split(back_ref[o, 8 * q : 8 * q + 8, :])
            table[o, q] = jnp.concatenate([high, low], axis=0)
        for q in range(layers, layers + 3):
            table[o, q] = jnp.zeros((16, BLOCK), BF16)

    def step(c, _):
        here = pl.ds(pl.multiple_of(c * CHUNK, CHUNK), CHUNK)
        boxes = jnp.broadcast_to(box_ref[:, here], (8, CHUNK))

        def window(w, total):
            for o in range(devices):
                tile = tile_ref[c, box_of[o]] + 2 * w
                wanted[16 * o : 16 * o + 16, 0:BLOCK] = table[o, tile]
                wanted[16 * o : 16 * o + 16, BLOCK:] = table[o, tile + 1]
            hot_spot = hot(WINDOW, spot_ref[:, here] - WINDOW * w)
            found = lax.dot_general(wanted[...], hot_spot, NN, preferred_element_type=F32)
            gained = jnp.zeros((8, CHUNK), F32)
            for o in range(devices):
                value = found[16 * o : 16 * o + 8] + found[16 * o + 8 : 16 * o + 16]
                gained = jnp.where(boxes == box_of[o], value, gained)
            return total + gained

        gained = lax.fori_loop(
            0, tile_ref[tile_ref.shape[0] - 8, c], window, jnp.zeros((8, CHUNK), F32)
        )
        next_ref[:, here] = jnp.concatenate(
            [base_ref[0:6, here] + gained[0:6], warm_ref[:, here]], axis=0
        )
        return 0

    lax.fori_loop(0, particles // CHUNK, step, 0)


def fetch(box_owner, tiles, back, boxes, spots, base, warm):
    devices, tall, _ = back.shape
    layers = tall // 8
    particles = boxes.shape[1]
    vmem = pl.BlockSpec(memory_space=VMEM)
    smem = pl.BlockSpec(memory_space=pltpu.SMEM)
    return pl.pallas_call(
        fetch_kernel,
        out_shape=jax.ShapeDtypeStruct((7, particles), F32),
        in_specs=[smem, smem] + [vmem] * 5,
        out_specs=vmem,
        scratch_shapes=[
            pltpu.SMEM((devices,), jnp.int32),
            VMEM((devices, layers + 3, 16, BLOCK), BF16),
            VMEM((16 * devices, WINDOW), BF16),
        ],
        compiler_params=pltpu.CompilerParams(vmem_limit_bytes=40 << 20),
        cost_estimate=pl.CostEstimate(
            flops=32 * devices * WINDOW * particles, bytes_accessed=1 << 20, transcendentals=0
        ),
        name="fetch_slots",
    )(box_owner, tiles, back, boxes, spots, base, warm)


def spread_kernel(dep_ref, heat_ref, y0_ref, y1_ref, x0_ref, x1_ref, fluid_ref, next_ref, void_ref):
    halo = (y0_ref, y1_ref, x0_ref, x1_ref)
    crowding = 1.0 + COUPLING * smooth_field(dep_ref, *halo, 0)
    void_ref[...] = 1.0 / crowding
    for k in range(3):
        next_ref[k] = fluid_ref[k] + TIME_STEP * COUPLING * smooth_field(dep_ref, *halo, k + 1) * crowding
    warmth = smooth_field(heat_ref, *halo, 0, 4)
    next_ref[3] = fluid_ref[3] + TIME_STEP * COUPLING * warmth * crowding


def spread(dep, heat, halo, fluid):
    vmem = pl.BlockSpec(memory_space=VMEM)
    return pl.pallas_call(
        spread_kernel,
        out_shape=(jax.ShapeDtypeStruct(fluid.shape, F32), jax.ShapeDtypeStruct(fluid.shape[1:], F32)),
        in_specs=[vmem] * 7,
        out_specs=(vmem,) * 2,
        compiler_params=pltpu.CompilerParams(vmem_limit_bytes=40 << 20),
        cost_estimate=pl.CostEstimate(flops=20 * fluid.size, bytes_accessed=2 << 20, transcendentals=0),
        name="spread_fields",
    )(dep, heat, *halo, fluid)


def halo_of(y_first, y_last, x_first, x_last):
    def moved(value, axis, step):
        size = lax.axis_size(axis)
        pairs = [(i, i + step) for i in range(size) if 0 <= i + step < size]
        return lax.ppermute(value, axis, pairs)

    return (
        moved(y_last, "gy", 1),
        moved(y_first, "gy", -1),
        moved(x_last, "gx", 1),
        moved(x_first, "gx", -1),
    )


def shards(
    fluid_state, particle_pos, particle_motion, particle_radius, particle_temp,
    particle_cell, particle_box, box_owner, contact_mask,
):
    devices = lax.axis_size(("gx", "gy"))
    particles = particle_pos.shape[1]
    slots = 2 * particles // devices
    fields, layers, rows, cols = fluid_state.shape
    boxes = particle_box.reshape(1, particles)
    radius = particle_radius.reshape(1, particles)
    temp = particle_temp.reshape(1, particles)
    cells = particle_cell.reshape(1, particles)

    outgoing, slot_of, spots, tiles = place(
        box_owner, boxes, particle_pos, particle_motion, radius, temp, slots
    )
    arrived = lax.all_to_all(outgoing, ("gx", "gy"), split_axis=0, concat_axis=0, tiled=True)

    spots, fluid = lax.optimization_barrier((spots, fluid_state))
    fluid_halo = halo_of(
        fluid[:, :, 0, :],
        fluid[:, :, rows - 1, :],
        fluid[:, :, :, 0].reshape(-1, BLOCK),
        fluid[:, :, :, cols - 1].reshape(-1, BLOCK),
    )
    result = contact(arrived, contact_mask)
    result, *fluid_halo = lax.optimization_barrier((result,) + tuple(fluid_halo))
    base, terms = look_up(fluid_state, fluid_halo, cells, particle_motion, radius, temp)
    deposits, *edges = deposit(cells, terms, (layers, rows, cols))
    back = lax.all_to_all(result, ("gx", "gy"), split_axis=0, concat_axis=0, tiled=True)
    warm, heat_field, *edges = heat_deposit(
        back, slot_of, cells, radius, base, edges, (layers, rows, cols)
    )
    halo = halo_of(*edges)
    particle_next = fetch(box_owner, tiles, back, boxes, spots, base, warm)
    fluid_next, void_fraction = spread(deposits, heat_field, halo, fluid_state)
    return (fluid_next, void_fraction, particle_next)


def solution(mesh):
    in_specs = (
        P(None, None, "gy", "gx"),
        P(None, ("gx", "gy")),
        P(None, ("gx", "gy")),
        P(("gx", "gy")),
        P(("gx", "gy")),
        P(("gx", "gy")),
        P(("gx", "gy"), None),
        P(),
        P(("gx", "gy"), None, None),
    )
    out_specs = (P(None, None, "gy", "gx"), P(None, "gy", "gx"), P(None, ("gx", "gy")))
    return jax.shard_map(shards, mesh=mesh, in_specs=in_specs, out_specs=out_specs, check_vma=False)
```

```python
import functools

import jax
import jax.numpy as jnp
from jax import lax
from jax.experimental import pallas as pl
from jax.experimental.pallas import tpu as pltpu
from jax.sharding import PartitionSpec as P

BLOCK = 128
TIME_STEP = 0.1
STIFFNESS = 0.5
DAMPING_RATE = 0.2
ROTATION_DRAG = 0.1
DRAG_COEFF = 4.0
CONDUCTION = 0.3
HEAT_TRANSFER = 4.0
GRAVITY = 0.3
COUPLING = 4.0
CENTRE_WEIGHT = 0.25
SIDE_WEIGHT = 0.125

F32 = jnp.float32
BF16 = jnp.bfloat16
VMEM = pltpu.VMEM
NN = (((1,), (0,)), ((), ()))
NT = (((1,), (1,)), ((), ()))


def split(value):
    high = value.astype(BF16)
    return high, (value - high.astype(F32)).astype(BF16)


def hot(count, row):
    places = lax.broadcasted_iota(jnp.int32, (count, row.shape[1]), 0)
    return jnp.where(places == row, 1.0, 0.0).astype(BF16)


def invert(owner_ref, box_of):
    def step(b, _):
        box_of[owner_ref[b]] = b
        return 0

    lax.fori_loop(0, owner_ref.shape[0], step, 0)


WINDOW = 256
CHUNK = 1024


def place_kernel(
    owner_ref, box_ref, pos_ref, motion_ref, radius_ref, temp_ref,
    out_ref, slot_ref, spot_ref, tile_ref,
    box_of, tile_of, acc, done
):
    devices, rows, _ = out_ref.shape
    layers = rows // 12
    slots = layers * BLOCK
    particles = box_ref.shape[1]
    sub = 256
    invert(owner_ref, box_of)
    acc[...] = jnp.zeros_like(acc)

    box_row = lax.broadcasted_iota(jnp.int32, (devices, 1), 0)
    owner_column = jnp.zeros((devices, 1), F32)
    for b in range(devices):
        owner_column = jnp.where(box_row == b, owner_ref[b].astype(F32), owner_column)
    above = (
        lax.broadcasted_iota(jnp.int32, (sub, sub), 0) < lax.broadcasted_iota(jnp.int32, (sub, sub), 1)
    )
    above = jnp.where(above, 1.0, 0.0).astype(BF16)
    lane = lax.broadcasted_iota(jnp.int32, (devices, BLOCK), 1)
    tiles = jnp.zeros((devices, BLOCK), F32)
    spans = jnp.zeros((8, BLOCK), F32)
    carry = jnp.zeros((devices, 1), F32)
    per_chunk = CHUNK // sub
    for c in range(particles // CHUNK):
        chosen = []
        for s in range(per_chunk):
            at = c * CHUNK + s * sub
            chosen.append(
                lax.broadcasted_iota(jnp.int32, (devices, sub), 0) == box_ref[:, at : at + sub]
            )
        ones = [jnp.where(mine, 1.0, 0.0) for mine in chosen]
        earlier = lax.dot_general(
            jnp.concatenate(ones, axis=0).astype(BF16), above, NN, preferred_element_type=F32
        )
        tile = jnp.minimum(jnp.floor(carry * (1.0 / BLOCK)), layers - 1.0)
        tiles = jnp.where(lane == c, tile, tiles)
        highest = jnp.zeros((1, 1), F32)
        for s in range(per_chunk):
            at = c * CHUNK + s * sub
            rank = earlier[s * devices : (s + 1) * devices] + carry
            spot = jnp.where(chosen[s], rank - BLOCK * tile, 0.0)
            spot = jnp.sum(spot, axis=0, keepdims=True)
            slot = jnp.where(chosen[s], rank + slots * owner_column, 0.0)
            slot = jnp.sum(slot, axis=0, keepdims=True)
            spot_ref[:, at : at + sub] = spot.astype(jnp.int32)
            slot_ref[:, at : at + sub] = slot.astype(jnp.int32)
            highest = jnp.maximum(highest, jnp.max(spot, axis=1, keepdims=True))
            carry = carry + jnp.sum(ones[s], axis=1, keepdims=True)
        windows = jnp.floor(highest * (1.0 / WINDOW)) + 1.0
        spans = jnp.where(lane[0:8] == c, windows, spans)
    if devices < BLOCK:
        tiles = jnp.concatenate([tiles, jnp.zeros((BLOCK - devices, BLOCK), F32)], axis=0)
    count = tile_ref.shape[0] - 8
    tile_ref[0:count, :] = jnp.transpose(tiles)[0:count].astype(jnp.int32)
    tile_ref[count : count + 8, :] = spans.astype(jnp.int32)
    copy = pltpu.make_async_copy(tile_ref, tile_of, done)
    copy.start()
    copy.wait()

    def step(c, _):
        here = pl.ds(pl.multiple_of(c * CHUNK, CHUNK), CHUNK)
        boxes = box_ref[:, here]
        pos = pos_ref[:, here]
        motion = motion_ref[:, here]
        push = TIME_STEP * STIFFNESS * pos - TIME_STEP * DAMPING_RATE * motion[0:3]
        spin = -TIME_STEP * ROTATION_DRAG * motion[3:6]
        heat = -TIME_STEP * CONDUCTION * temp_ref[:, here]
        first = jnp.concatenate([push, spin, heat, jnp.ones((1, CHUNK), F32)], axis=0)
        second = jnp.concatenate([pos, radius_ref[:, here]], axis=0)
        first = jnp.concatenate(split(first), axis=0)
        second = jnp.concatenate(split(second) * 2, axis=0)
        lower = lax.broadcasted_iota(jnp.int32, (16, 1), 0) < 8
        box16 = jnp.broadcast_to(boxes, (16, CHUNK)).astype(F32).astype(BF16)
        first_parts = []
        second_parts = []
        for o in range(devices):
            mine = box16 == box_of[o].astype(F32).astype(BF16)
            first_parts.append(jnp.where(mine, first, jnp.zeros_like(first)))
            if o % 2 == 0:
                either = jnp.where(lower, box_of[o].astype(F32), box_of[o + 1].astype(F32)).astype(BF16)
                second_parts.append(jnp.where(box16 == either, second, jnp.zeros_like(second)))
        parts = jnp.concatenate(first_parts + second_parts, axis=0)

        def window(w, _):
            hot_spot = hot(WINDOW, spot_ref[:, here] - WINDOW * w)
            placed = lax.dot_general(parts, hot_spot, NT, preferred_element_type=F32)
            for o in range(devices):
                tile = tile_of[c, box_of[o]] + 2 * w
                one = placed[16 * o : 16 * o + 8] + placed[16 * o + 8 : 16 * o + 16]
                two = placed[16 * devices + 8 * o : 16 * devices + 8 * o + 8]
                two = two + pltpu.roll(two, 4, 0)
                acc[o, tile, 0:8, :] += one[:, :BLOCK]
                acc[o, tile + 1, 0:8, :] += one[:, BLOCK:]
                acc[o, tile, 8:16, :] += two[:, :BLOCK]
                acc[o, tile + 1, 8:16, :] += two[:, BLOCK:]
            return 0

        return lax.fori_loop(0, tile_of[tile_ref.shape[0] - 8, c], window, 0)

    lax.fori_loop(0, particles // CHUNK, step, 0)

    def finish(o, _):
        for q in range(layers):
            out_ref[o, 8 * q : 8 * q + 8, :] = acc[o, q, 0:8, :]
            out_ref[o, 8 * layers + 4 * q : 8 * layers + 4 * q + 4, :] = acc[o, q, 8:12, :]
        return 0

    lax.fori_loop(0, devices, finish, 0)


def place(box_owner, boxes, pos, motion, radius, temp, slots):
    devices = box_owner.shape[0]
    particles = pos.shape[1]
    layers = slots // BLOCK
    vmem = pl.BlockSpec(memory_space=VMEM)
    row = jax.ShapeDtypeStruct((1, particles), jnp.int32)
    table = (-(-particles // (8 * CHUNK)) * 8 + 8, BLOCK)
    return pl.pallas_call(
        place_kernel,
        out_shape=(
            jax.ShapeDtypeStruct((devices, 12 * layers, BLOCK), F32), row, row,
            jax.ShapeDtypeStruct(table, jnp.int32),
        ),
        in_specs=[pl.BlockSpec(memory_space=pltpu.SMEM)] + [vmem] * 5,
        out_specs=(vmem,) * 4,
        scratch_shapes=[
            pltpu.SMEM((devices,), jnp.int32),
            pltpu.SMEM(table, jnp.int32),
            VMEM((devices, layers + 3, 16, BLOCK), F32),
            pltpu.SemaphoreType.DMA,
        ],
        compiler_params=pltpu.CompilerParams(vmem_limit_bytes=60 << 20),
        cost_estimate=pl.CostEstimate(
            flops=2 * 24 * devices * WINDOW * particles, bytes_accessed=1 << 20, transcendentals=0
        ),
        name="place_slots",
    )(box_owner, boxes, pos, motion, radius, temp)


def pair_terms(near):
    twice = jnp.concatenate([near, near], axis=0)
    high = twice.astype(BF16).astype(F32)
    low = (twice - high).astype(BF16).astype(F32)
    row = lax.broadcasted_iota(jnp.int32, (8, 1), 0)
    kept = high + low
    squares = kept * kept
    norm = -(squares[0:1] + squares[1:2] + squares[2:3])
    total = jnp.where(row < 3, norm, squares[3:4] + 0.5)
    one = total.astype(BF16).astype(F32)
    rest = total - one
    two = rest.astype(BF16).astype(F32)
    three = (rest - two).astype(BF16).astype(F32)
    third = jnp.where((row == 0) | (row == 3), one, jnp.where((row == 1) | (row == 4), two, three))
    third = jnp.where(row < 6, third, 0.0)
    crossed = 2.0 * jnp.where(row < 4, high, low)
    is_radius = (row == 3) | (row == 7)
    cross_d = jnp.where(is_radius, 0.0, crossed)
    cross_r = jnp.where(is_radius, crossed, 0.0)
    ones = jnp.ones_like(third)
    left = jnp.concatenate([high, low, third, jnp.where(row < 6, ones, 0.0)], axis=0)
    ones_d = jnp.where(row < 3, ones, 0.0)
    ones_r = jnp.where((row >= 3) & (row < 6), ones, 0.0)
    for_d = jnp.concatenate([cross_d, cross_d, ones_d, jnp.where(row < 3, third, 0.0)], axis=0)
    for_r = jnp.concatenate([cross_r, cross_r, ones_r, jnp.where((row >= 3) & (row < 6), third, 0.0)], axis=0)
    right = jnp.concatenate([for_d, for_r], axis=1)
    return left, right.astype(BF16)


def contact_kernel(slot_ref, mask_ref, out_ref):
    homes, rows, _ = slot_ref.shape
    layers = rows // 12
    blocks = [(s, q) for s in range(homes) for q in range(layers)]
    row = lax.broadcasted_iota(jnp.int32, (8, 1), 0)
    sign = jnp.where((row >= 3) & (row < 6), 1.0, -1.0)
    lane = lax.broadcasted_iota(jnp.int32, (BLOCK, BLOCK), 1) // 16

    def pairs_of(group):
        pairs = []
        for first in range(0, 8, 4):
            lefts = []
            rights = []
            for g, (s, q) in enumerate(group[first : first + 4]):
                left, right = pair_terms(slot_ref[s, 8 * layers + 4 * q : 8 * layers + 4 * q + 4, :])
                lefts.append(left)
                spots = [jnp.zeros_like(right)] * 4
                spots[g] = right
                rights.append(jnp.concatenate(spots, axis=0))
            turned = jnp.transpose(jnp.concatenate(lefts, axis=0)).astype(BF16)
            pairs.append(
                lax.dot_general(turned, jnp.concatenate(rights, axis=1), NN, preferred_element_type=F32)
            )
        return pairs

    def sums_of(number, group, pairs):
        stacked = []
        for s, q in group:
            mine = slot_ref[s, 8 * q : 8 * q + 8, :]
            high = mine.astype(BF16).astype(F32)
            stacked += [high, mine - high]
        columns = jnp.transpose(jnp.concatenate(stacked, axis=0)).astype(BF16)
        highs = []
        lows = []
        right = []
        for b in range(8):
            at = 2 * BLOCK * (b % 4)
            pair = pairs[b // 4]
            reach = pair[:, at + BLOCK : at + 2 * BLOCK]
            inverse = pl.reciprocal(reach, approx=True)
            inverse = inverse * (2.0 - reach * inverse)
            weight = mask_ref[8 * number + b].astype(F32) * jnp.exp(pair[:, at : at + BLOCK] * inverse)
            high, low = split(weight)
            highs.append(high)
            lows.append(low)
            right.append(jnp.where(lane == b, columns, jnp.zeros_like(columns)))
        return lax.dot_general(
            jnp.concatenate(highs + lows, axis=1), jnp.concatenate(right + right, axis=0), NN,
            preferred_element_type=F32,
        )

    def finish(group, sums):
        sums = jnp.transpose(sums)
        for b, (s, q) in enumerate(group):
            total = sums[16 * b : 16 * b + 8] + sums[16 * b + 8 : 16 * b + 16]
            out_ref[s, 8 * q : 8 * q + 8, :] = slot_ref[s, 8 * q : 8 * q + 8, :] * total[7:8] + sign * total

    groups = [blocks[i : i + 8] for i in range(0, len(blocks), 8)]
    pairs = pairs_of(groups[0])
    before = None
    for number, group in enumerate(groups):
        later = pairs_of(groups[number + 1]) if number + 1 < len(groups) else None
        sums = sums_of(number, group, pairs)
        if before is not None:
            finish(*before)
        before = (group, sums)
        pairs = later
    finish(*before)


def contact(arrived, mask):
    devices, rows, _ = arrived.shape
    layers = rows // 12
    blocks = mask.shape[0]
    step = 32 // layers
    return pl.pallas_call(
        contact_kernel,
        grid=(devices // step,),
        out_shape=jax.ShapeDtypeStruct((devices, 8 * layers, BLOCK), F32),
        in_specs=[
            pl.BlockSpec((step, rows, BLOCK), lambda h: (h, 0, 0)),
            pl.BlockSpec((step * layers, BLOCK, BLOCK), lambda h: (h, 0, 0)),
        ],
        out_specs=pl.BlockSpec((step, 8 * layers, BLOCK), lambda h: (h, 0, 0)),
        compiler_params=pltpu.CompilerParams(vmem_limit_bytes=60 << 20),
        cost_estimate=pl.CostEstimate(
            flops=64 * blocks * BLOCK * BLOCK, bytes_accessed=blocks * BLOCK * BLOCK * 4, transcendentals=0
        ),
        name="contact_blocks",
    )(arrived, mask)


def smoothed(centre, y_first, y_last, x_first, x_last):
    layers, rows, cols = centre.shape
    zero = jnp.zeros((1, rows, cols), F32)
    up = jnp.concatenate([centre[1:], zero], axis=0)
    down = jnp.concatenate([zero, centre[:-1]], axis=0)
    row = lax.broadcasted_iota(jnp.int32, (1, rows, cols), 1)
    col = lax.broadcasted_iota(jnp.int32, (1, rows, cols), 2)
    back = jnp.where(row == 0, y_first, pltpu.roll(centre, 1, 1))
    front = jnp.where(row == rows - 1, y_last, pltpu.roll(centre, rows - 1, 1))
    left = jnp.where(col == 0, x_first, pltpu.roll(centre, 1, 2))
    right = jnp.where(col == cols - 1, x_last, pltpu.roll(centre, cols - 1, 2))
    return CENTRE_WEIGHT * centre + SIDE_WEIGHT * ((up + down) + (back + front) + (left + right))


def columns(edge, layers, rows):
    count = edge.shape[0]
    if count < 8:
        edge = jnp.concatenate([edge] * (8 // count), axis=0)
    turned = jnp.transpose(edge)
    parts = [turned[:, a : a + 1] for a in range(count)]
    return jnp.concatenate(parts, axis=0).reshape(layers, rows, 1)


def smooth_field(field_ref, y0_ref, y1_ref, x0_ref, x1_ref, k, edge=None):
    at = k if edge is None else edge
    _, layers, rows, cols = field_ref.shape
    per = layers * rows // BLOCK
    x0 = columns(x0_ref[at * per : (at + 1) * per, :], layers, rows)
    x1 = columns(x1_ref[at * per : (at + 1) * per, :], layers, rows)
    y0 = y0_ref[at].reshape(layers, 1, cols)
    y1 = y1_ref[at].reshape(layers, 1, cols)
    return smoothed(field_ref[k], y0, y1, x0, x1)


def write_edges(field, k, y0_ref, y1_ref, x0_ref, x1_ref):
    layers, rows, cols = field.shape
    y0_ref[k] = field[:, 0, :]
    y1_ref[k] = field[:, rows - 1, :]
    flat = field.reshape(layers * rows, cols)
    for a in range(layers * rows // BLOCK):
        turned = jnp.transpose(flat[a * BLOCK : (a + 1) * BLOCK, :])
        at = k * (layers * rows // BLOCK) + a
        x0_ref[at : at + 1, :] = turned[0:1, :]
        x1_ref[at : at + 1, :] = turned[cols - 1 : cols, :]


def paired_rows(pairs, layers, rows, scratch):
    half = pairs.shape[0]
    cols = pairs.shape[1] // 2
    scratch[pl.ds(0, half, stride=2), :] = pairs[:, :cols]
    scratch[pl.ds(1, half, stride=2), :] = pairs[:, cols:]
    return scratch[...].reshape(layers, rows, cols)


def gathered(tables, rows, lanes):
    group = rows // 8
    found = [None] * len(tables)
    for g in range(len(tables[0])):
        mine = group == g
        for k, table in enumerate(tables):
            value = jnp.take_along_axis(table[g], lanes, axis=1, mode="promise_in_bounds")
            found[k] = value if g == 0 else jnp.where(mine, value, found[k])
    mine = lax.broadcasted_iota(jnp.int32, (8, BLOCK), 0) == rows % 8
    return [jnp.sum(jnp.where(mine, value, 0.0), axis=0, keepdims=True) for value in found]


def look_kernel(fluid_ref, cell_ref, seen_ref, table, rows_scratch, *, chunk):
    fields, layers, rows, cols = fluid_ref.shape
    particles = cell_ref.shape[1]
    half = layers * rows // 2
    wide = 2 * cols
    for k in range(fields):
        rows_scratch[...] = smoothed(fluid_ref[k], 0.0, 0.0, 0.0, 0.0).reshape(layers * rows, cols)
        here = slice(k * half, (k + 1) * half)
        for part in range(2):
            high, low = split(rows_scratch[pl.ds(part, half, stride=2), :])
            table[here, part * cols : (part + 1) * cols] = high
            table[here, wide + part * cols : wide + (part + 1) * cols] = low

    def step(i, _):
        here = pl.ds(pl.multiple_of(i * chunk, chunk), chunk)
        cells = cell_ref[:, here]
        hot_low = hot(wide, cells % wide)
        found = lax.dot_general(
            table[...], jnp.concatenate([hot_low, hot_low], axis=0), NN, preferred_element_type=F32
        )
        mine = lax.broadcasted_iota(jnp.int32, (half, chunk), 0) == cells // wide
        seen = [
            jnp.sum(jnp.where(mine, found[k * half : (k + 1) * half], 0.0), axis=0, keepdims=True)
            for k in range(fields)
        ]
        seen_ref[:, here] = jnp.concatenate(seen, axis=0)
        return 0

    lax.fori_loop(0, particles // chunk, step, 0)


def look_up(fluid, cells):
    fields, layers, rows, cols = fluid.shape
    particles = cells.shape[1]
    vmem = pl.BlockSpec(memory_space=VMEM)
    return pl.pallas_call(
        functools.partial(look_kernel, chunk=512),
        out_shape=jax.ShapeDtypeStruct((fields, particles), F32),
        in_specs=[vmem] * 2,
        out_specs=vmem,
        scratch_shapes=[
            VMEM((fields * layers * rows // 2, 4 * cols), BF16),
            VMEM((layers * rows, cols), F32),
        ],
        compiler_params=pltpu.CompilerParams(vmem_limit_bytes=40 << 20),
        cost_estimate=pl.CostEstimate(
            flops=8 * fields * layers * rows * cols * particles // 4, bytes_accessed=1 << 20, transcendentals=0
        ),
        name="look_up",
    )(fluid, cells)


def deposit_kernel(
    y0_ref, y1_ref, x0_ref, x1_ref, cell_ref, seen_ref, motion_ref, radius_ref, temp_ref,
    base_ref, dep_ref, dy0_ref, dy1_ref, dx0_ref, dx1_ref, x_table, rows_scratch, acc, *, chunk
):
    fields, layers, rows, cols = dep_ref.shape
    half = layers * rows // 2
    wide = 2 * cols
    particles = cell_ref.shape[1]
    per = layers * rows // BLOCK
    for k in range(fields):
        x_table[k] = jnp.zeros_like(x_table[k])
        x_table[k, 0:per, :] = x0_ref[k * per : (k + 1) * per, :]
        x_table[k, per : 2 * per, :] = x1_ref[k * per : (k + 1) * per, :]
    acc[...] = jnp.zeros_like(acc)

    def step(i, _):
        here = pl.ds(pl.multiple_of(i * chunk, chunk), chunk)
        cells = cell_ref[:, here]
        beside = [[] for _ in range(fields)]
        for s in range(chunk // BLOCK):
            cell = jnp.broadcast_to(cells[:, s * BLOCK : (s + 1) * BLOCK], (8, BLOCK))
            high = cell // cols
            low = cell % cols
            y = high % rows
            from_y = gathered(
                [
                    [ref[k, 8 * g : 8 * g + 8, :] for ref in (y0_ref, y1_ref) for g in range(layers // 8)]
                    for k in range(fields)
                ],
                high // rows + jnp.where(y == 0, 0, layers),
                low,
            )
            from_x = gathered(
                [[x_table[k, 8 * g : 8 * g + 8, :] for g in range(x_table.shape[1] // 8)] for k in range(fields)],
                high // BLOCK + jnp.where(low == 0, 0, per),
                high % BLOCK,
            )
            on_y = (y[0:1] == 0) | (y[0:1] == rows - 1)
            on_x = (low[0:1] == 0) | (low[0:1] == cols - 1)
            for k in range(fields):
                beside[k].append(jnp.where(on_y, from_y[k], 0.0) + jnp.where(on_x, from_x[k], 0.0))
        beside = jnp.concatenate([jnp.concatenate(parts, axis=1) for parts in beside], axis=0)
        seen = seen_ref[:, here] + SIDE_WEIGHT * beside
        motion = motion_ref[:, here]
        radius = radius_ref[:, here]
        temp = temp_ref[:, here]
        drag = DRAG_COEFF / (radius * radius + 0.25) * (seen[0:3] - motion[0:3])
        upward = lax.broadcasted_iota(jnp.int32, (3, 1), 0) == 2
        moved = motion[0:3] + TIME_STEP * drag - jnp.where(upward, TIME_STEP * GRAVITY, 0.0)
        warmed = temp + TIME_STEP * HEAT_TRANSFER * (seen[3:4] - temp)
        base_ref[:, here] = jnp.concatenate([moved, motion[3:6], warmed, seen[3:4]], axis=0)
        volume = radius * radius * radius
        high, low = split(jnp.concatenate([volume, -volume * drag], axis=0))
        hot_low = hot(wide, cells % wide)
        hot_high = hot(half, cells // wide)
        parts = [hot_high * piece[k : k + 1] for piece in (high, low) for k in range(fields)]
        total = lax.dot_general(jnp.concatenate(parts, axis=0), hot_low, NT, preferred_element_type=F32)
        acc[...] += total[: fields * half] + total[fields * half :]
        return 0

    lax.fori_loop(0, particles // chunk, step, 0)
    for k in range(fields):
        field = paired_rows(acc[k * half : (k + 1) * half, :], layers, rows, rows_scratch)
        dep_ref[k] = field
        write_edges(field, k, dy0_ref, dy1_ref, dx0_ref, dx1_ref)


def edge_shapes(fields, layers, rows, cols):
    y_edge = jax.ShapeDtypeStruct((fields, layers, cols), F32)
    x_edge = jax.ShapeDtypeStruct((fields * layers * rows // BLOCK, BLOCK), F32)
    return (y_edge, y_edge, x_edge, x_edge)


def deposit(halo, cells, seen, motion, radius, temp, grid):
    layers, rows, cols = grid
    fields, particles = seen.shape
    tall = -(-2 * layers * rows // (8 * BLOCK)) * 8
    vmem = pl.BlockSpec(memory_space=VMEM)
    return pl.pallas_call(
        functools.partial(deposit_kernel, chunk=1024),
        out_shape=(
            jax.ShapeDtypeStruct((8, particles), F32),
            jax.ShapeDtypeStruct((fields,) + grid, F32),
        ) + edge_shapes(fields, layers, rows, cols),
        in_specs=[vmem] * 9,
        out_specs=(vmem,) * 6,
        scratch_shapes=[
            VMEM((fields, tall, BLOCK), F32),
            VMEM((layers * rows, cols), F32),
            VMEM((fields * layers * rows // 2, 2 * cols), F32),
        ],
        compiler_params=pltpu.CompilerParams(vmem_limit_bytes=40 << 20),
        cost_estimate=pl.CostEstimate(
            flops=4 * fields * layers * rows * cols * particles, bytes_accessed=2 << 20, transcendentals=0
        ),
        name="deposit_fields",
    )(*halo, cells, seen, motion, radius, temp)


def heat_kernel(
    back_ref, slot_ref, cell_ref, radius_ref, base_ref, ey0_ref, ey1_ref, ex0_ref, ex1_ref,
    next_ref, dep_ref, dy0_ref, dy1_ref, dx0_ref, dx1_ref,
    table, acc, rows_scratch, *, chunk, rows
):
    devices, tall, _ = back_ref.shape
    layers = tall // 8
    particles = slot_ref.shape[1]
    half, wide = acc.shape
    for o in range(devices):
        for q in range(layers):
            table[o * layers + q : o * layers + q + 1, :] = back_ref[o, 8 * q + 6 : 8 * q + 7, :]
    acc[...] = jnp.zeros_like(acc)

    def step(i, _):
        here = pl.ds(pl.multiple_of(i * chunk, chunk), chunk)
        slots = slot_ref[:, here]
        gained = []
        for s in range(chunk // BLOCK):
            wanted = jnp.broadcast_to(slots[:, s * BLOCK : (s + 1) * BLOCK], (8, BLOCK))
            tiles = [table[8 * g : 8 * g + 8, :] for g in range(devices * layers // 8)]
            gained.append(gathered([tiles], wanted // BLOCK, wanted % BLOCK)[0])
        base = base_ref[6:8, here]
        total = base[0:1] + jnp.concatenate(gained, axis=1)
        next_ref[:, here] = total
        radius = radius_ref[:, here]
        high, low = split(radius * radius * radius * (total - base[1:2]))
        cells = cell_ref[:, here]
        hot_low = hot(wide, cells % wide)
        hot_high = hot(half, cells // wide)
        parts = jnp.concatenate([hot_high * high, hot_high * low], axis=0)
        added = lax.dot_general(parts, hot_low, NT, preferred_element_type=F32)
        acc[...] += added[:half] + added[half:]
        return 0

    lax.fori_loop(0, particles // chunk, step, 0)
    field = paired_rows(acc[...], 2 * half // rows, rows, rows_scratch)
    dep_ref[0] = field
    for edge, out in ((ey0_ref, dy0_ref), (ey1_ref, dy1_ref), (ex0_ref, dx0_ref), (ex1_ref, dx1_ref)):
        out[0 : edge.shape[0]] = edge[...]
    write_edges(field, ey0_ref.shape[0], dy0_ref, dy1_ref, dx0_ref, dx1_ref)


def heat_deposit(back, slot_of, cells, radius, base, edges, grid):
    devices = back.shape[0]
    layers, rows, cols = grid
    particles = cells.shape[1]
    half = layers * rows // 2
    fields = edges[0].shape[0] + 1
    vmem = pl.BlockSpec(memory_space=VMEM)
    return pl.pallas_call(
        functools.partial(heat_kernel, chunk=1024, rows=rows),
        out_shape=(
            jax.ShapeDtypeStruct((1, particles), F32),
            jax.ShapeDtypeStruct((1,) + grid, F32),
        ) + edge_shapes(fields, layers, rows, cols),
        in_specs=[vmem] * 9,
        out_specs=(vmem,) * 6,
        scratch_shapes=[
            VMEM((devices * back.shape[1] // 8, BLOCK), F32),
            VMEM((half, 2 * cols), F32),
            VMEM((layers * rows, cols), F32),
        ],
        compiler_params=pltpu.CompilerParams(vmem_limit_bytes=40 << 20),
        cost_estimate=pl.CostEstimate(
            flops=4 * half * 2 * cols * particles, bytes_accessed=1 << 20, transcendentals=0
        ),
        name="heat_deposit",
    )(back, slot_of, cells, radius, base, *edges)


def fetch_kernel(
    owner_ref, tile_ref, back_ref, box_ref, spot_ref, base_ref, warm_ref, next_ref, box_of, table, wanted
):
    devices, tall, _ = back_ref.shape
    layers = tall // 8
    particles = box_ref.shape[1]
    invert(owner_ref, box_of)
    for o in range(devices):
        for q in range(layers):
            high, low = split(back_ref[o, 8 * q : 8 * q + 8, :])
            table[o, q] = jnp.concatenate([high, low], axis=0)
        for q in range(layers, layers + 3):
            table[o, q] = jnp.zeros((16, BLOCK), BF16)

    def step(c, _):
        here = pl.ds(pl.multiple_of(c * CHUNK, CHUNK), CHUNK)
        boxes = jnp.broadcast_to(box_ref[:, here], (8, CHUNK))

        def window(w, total):
            for o in range(devices):
                tile = tile_ref[c, box_of[o]] + 2 * w
                wanted[16 * o : 16 * o + 16, 0:BLOCK] = table[o, tile]
                wanted[16 * o : 16 * o + 16, BLOCK:] = table[o, tile + 1]
            hot_spot = hot(WINDOW, spot_ref[:, here] - WINDOW * w)
            found = lax.dot_general(wanted[...], hot_spot, NN, preferred_element_type=F32)
            gained = jnp.zeros((8, CHUNK), F32)
            for o in range(devices):
                value = found[16 * o : 16 * o + 8] + found[16 * o + 8 : 16 * o + 16]
                gained = jnp.where(boxes == box_of[o], value, gained)
            return total + gained

        gained = lax.fori_loop(
            0, tile_ref[tile_ref.shape[0] - 8, c], window, jnp.zeros((8, CHUNK), F32)
        )
        next_ref[:, here] = jnp.concatenate(
            [base_ref[0:6, here] + gained[0:6], warm_ref[:, here]], axis=0
        )
        return 0

    lax.fori_loop(0, particles // CHUNK, step, 0)


def fetch(box_owner, tiles, back, boxes, spots, base, warm):
    devices, tall, _ = back.shape
    layers = tall // 8
    particles = boxes.shape[1]
    vmem = pl.BlockSpec(memory_space=VMEM)
    smem = pl.BlockSpec(memory_space=pltpu.SMEM)
    return pl.pallas_call(
        fetch_kernel,
        out_shape=jax.ShapeDtypeStruct((7, particles), F32),
        in_specs=[smem, smem] + [vmem] * 5,
        out_specs=vmem,
        scratch_shapes=[
            pltpu.SMEM((devices,), jnp.int32),
            VMEM((devices, layers + 3, 16, BLOCK), BF16),
            VMEM((16 * devices, WINDOW), BF16),
        ],
        compiler_params=pltpu.CompilerParams(vmem_limit_bytes=40 << 20),
        cost_estimate=pl.CostEstimate(
            flops=32 * devices * WINDOW * particles, bytes_accessed=1 << 20, transcendentals=0
        ),
        name="fetch_slots",
    )(box_owner, tiles, back, boxes, spots, base, warm)


def spread_kernel(dep_ref, heat_ref, y0_ref, y1_ref, x0_ref, x1_ref, fluid_ref, next_ref, void_ref):
    halo = (y0_ref, y1_ref, x0_ref, x1_ref)
    crowding = 1.0 + COUPLING * smooth_field(dep_ref, *halo, 0)
    void_ref[...] = 1.0 / crowding
    for k in range(3):
        next_ref[k] = fluid_ref[k] + TIME_STEP * COUPLING * smooth_field(dep_ref, *halo, k + 1) * crowding
    warmth = smooth_field(heat_ref, *halo, 0, 4)
    next_ref[3] = fluid_ref[3] + TIME_STEP * COUPLING * warmth * crowding


def spread(dep, heat, halo, fluid):
    vmem = pl.BlockSpec(memory_space=VMEM)
    return pl.pallas_call(
        spread_kernel,
        out_shape=(jax.ShapeDtypeStruct(fluid.shape, F32), jax.ShapeDtypeStruct(fluid.shape[1:], F32)),
        in_specs=[vmem] * 7,
        out_specs=(vmem,) * 2,
        compiler_params=pltpu.CompilerParams(vmem_limit_bytes=40 << 20),
        cost_estimate=pl.CostEstimate(flops=20 * fluid.size, bytes_accessed=2 << 20, transcendentals=0),
        name="spread_fields",
    )(dep, heat, *halo, fluid)


def halo_of(y_first, y_last, x_first, x_last):
    def moved(value, axis, step):
        size = lax.axis_size(axis)
        pairs = [(i, i + step) for i in range(size) if 0 <= i + step < size]
        return lax.ppermute(value, axis, pairs)

    return (
        moved(y_last, "gy", 1),
        moved(y_first, "gy", -1),
        moved(x_last, "gx", 1),
        moved(x_first, "gx", -1),
    )


def shards(
    fluid_state, particle_pos, particle_motion, particle_radius, particle_temp,
    particle_cell, particle_box, box_owner, contact_mask,
):
    devices = lax.axis_size(("gx", "gy"))
    particles = particle_pos.shape[1]
    slots = 2 * particles // devices
    fields, layers, rows, cols = fluid_state.shape
    boxes = particle_box.reshape(1, particles)
    radius = particle_radius.reshape(1, particles)
    temp = particle_temp.reshape(1, particles)
    cells = particle_cell.reshape(1, particles)

    outgoing, slot_of, spots, tiles = place(
        box_owner, boxes, particle_pos, particle_motion, radius, temp, slots
    )
    arrived = lax.all_to_all(outgoing, ("gx", "gy"), split_axis=0, concat_axis=0, tiled=True)

    spots, fluid = lax.optimization_barrier((spots, fluid_state))
    fluid_halo = halo_of(
        fluid[:, :, 0, :],
        fluid[:, :, rows - 1, :],
        fluid[:, :, :, 0].reshape(-1, BLOCK),
        fluid[:, :, :, cols - 1].reshape(-1, BLOCK),
    )
    seen = look_up(fluid, cells)
    arrived, seen = lax.optimization_barrier((arrived, seen))
    result = contact(arrived, contact_mask)

    result, *fluid_halo = lax.optimization_barrier((result,) + tuple(fluid_halo))
    base, deposits, *edges = deposit(
        fluid_halo, cells, seen, particle_motion, radius, temp, (layers, rows, cols)
    )
    back = lax.all_to_all(result, ("gx", "gy"), split_axis=0, concat_axis=0, tiled=True)
    warm, heat_field, *edges = heat_deposit(
        back, slot_of, cells, radius, base, edges, (layers, rows, cols)
    )
    halo = halo_of(*edges)
    particle_next = fetch(box_owner, tiles, back, boxes, spots, base, warm)
    fluid_next, void_fraction = spread(deposits, heat_field, halo, fluid_state)
    return (fluid_next, void_fraction, particle_next)


def solution(mesh):
    in_specs = (
        P(None, None, "gy", "gx"),
        P(None, ("gx", "gy")),
        P(None, ("gx", "gy")),
        P(("gx", "gy")),
        P(("gx", "gy")),
        P(("gx", "gy")),
        P(("gx", "gy"), None),
        P(),
        P(("gx", "gy"), None, None),
    )
    out_specs = (P(None, None, "gy", "gx"), P(None, "gy", "gx"), P(None, ("gx", "gy")))
    return jax.shard_map(shards, mesh=mesh, in_specs=in_specs, out_specs=out_specs, check_vma=False)
```

```python
import functools

import jax
import jax.numpy as jnp
from jax import lax
from jax.experimental import pallas as pl
from jax.experimental.pallas import tpu as pltpu
from jax.sharding import PartitionSpec as P

BLOCK = 128
TIME_STEP = 0.1
STIFFNESS = 0.5
DAMPING_RATE = 0.2
ROTATION_DRAG = 0.1
DRAG_COEFF = 4.0
CONDUCTION = 0.3
HEAT_TRANSFER = 4.0
GRAVITY = 0.3
COUPLING = 4.0
CENTRE_WEIGHT = 0.25
SIDE_WEIGHT = 0.125

F32 = jnp.float32
BF16 = jnp.bfloat16
VMEM = pltpu.VMEM
NN = (((1,), (0,)), ((), ()))
NT = (((1,), (1,)), ((), ()))


def split(value):
    high = value.astype(BF16)
    return high, (value - high.astype(F32)).astype(BF16)


def hot(count, row):
    places = lax.broadcasted_iota(jnp.int32, (count, row.shape[1]), 0)
    return jnp.where(places == row, 1.0, 0.0).astype(BF16)


def hot_columns(count, row):
    n = row.shape[1] // BLOCK
    tiles = [row[:, a * BLOCK : (a + 1) * BLOCK] for a in range(n)]
    turned = jnp.transpose(jnp.concatenate(tiles * (8 // n), axis=0).astype(F32))
    places = lax.broadcasted_iota(jnp.int32, (BLOCK, count), 1).astype(F32)
    return jnp.concatenate(
        [jnp.where(places == turned[:, a : a + 1], 1.0, 0.0).astype(BF16) for a in range(n)], axis=0
    )


def invert(owner_ref, box_of):
    def step(b, _):
        box_of[owner_ref[b]] = b
        return 0

    lax.fori_loop(0, owner_ref.shape[0], step, 0)


WINDOW = 256
CHUNK = 1024


def place_kernel(
    owner_ref, box_ref, pos_ref, motion_ref, radius_ref, temp_ref,
    out_ref, slot_ref, spot_ref, tile_ref,
    box_of, tile_of, acc, done
):
    devices, rows, _ = out_ref.shape
    layers = rows // 12
    slots = layers * BLOCK
    particles = box_ref.shape[1]
    sub = 256
    invert(owner_ref, box_of)
    acc[...] = jnp.zeros_like(acc)

    box_row = lax.broadcasted_iota(jnp.int32, (devices, 1), 0)
    owner_column = jnp.zeros((devices, 1), F32)
    for b in range(devices):
        owner_column = jnp.where(box_row == b, owner_ref[b].astype(F32), owner_column)
    above = (
        lax.broadcasted_iota(jnp.int32, (sub, sub), 0) < lax.broadcasted_iota(jnp.int32, (sub, sub), 1)
    )
    above = jnp.where(above, 1.0, 0.0).astype(BF16)
    lane = lax.broadcasted_iota(jnp.int32, (devices, BLOCK), 1)
    tiles = jnp.zeros((devices, BLOCK), F32)
    highest = jnp.zeros((1, sub), F32)
    carry = jnp.zeros((devices, 1), F32)
    per_chunk = CHUNK // sub
    for c in range(particles // CHUNK):
        chosen = []
        for s in range(per_chunk):
            at = c * CHUNK + s * sub
            chosen.append(
                lax.broadcasted_iota(jnp.int32, (devices, sub), 0) == box_ref[:, at : at + sub]
            )
        ones = [jnp.where(mine, 1.0, 0.0) for mine in chosen]
        earlier = lax.dot_general(
            jnp.concatenate(ones, axis=0).astype(BF16), above, NN, preferred_element_type=F32
        )
        tile = jnp.minimum(jnp.floor(carry * (1.0 / BLOCK)), layers - 1.0)
        tiles = jnp.where(lane == c, tile, tiles)
        for s in range(per_chunk):
            at = c * CHUNK + s * sub
            rank = earlier[s * devices : (s + 1) * devices] + carry
            spot = jnp.where(chosen[s], rank - BLOCK * tile, 0.0)
            spot = jnp.sum(spot, axis=0, keepdims=True)
            slot = jnp.where(chosen[s], rank + slots * owner_column, 0.0)
            slot = jnp.sum(slot, axis=0, keepdims=True)
            spot_ref[:, at : at + sub] = spot.astype(jnp.int32)
            slot_ref[:, at : at + sub] = slot.astype(jnp.int32)
            highest = jnp.maximum(highest, spot)
            carry = carry + jnp.sum(ones[s], axis=1, keepdims=True)
    if devices < BLOCK:
        tiles = jnp.concatenate([tiles, jnp.zeros((BLOCK - devices, BLOCK), F32)], axis=0)
    count = tile_ref.shape[0] - 8
    tile_ref[0:count, :] = jnp.transpose(tiles)[0:count].astype(jnp.int32)
    windows = jnp.floor(jnp.max(highest, axis=1, keepdims=True) * (1.0 / WINDOW)) + 1.0
    tile_ref[count : count + 8, :] = jnp.broadcast_to(windows, (8, BLOCK)).astype(jnp.int32)
    copy = pltpu.make_async_copy(tile_ref, tile_of, done)
    copy.start()
    copy.wait()

    def step(w, c, _):
        here = pl.ds(pl.multiple_of(c * CHUNK, CHUNK), CHUNK)
        boxes = box_ref[:, here]
        pos = pos_ref[:, here]
        motion = motion_ref[:, here]
        push = TIME_STEP * STIFFNESS * pos - TIME_STEP * DAMPING_RATE * motion[0:3]
        spin = -TIME_STEP * ROTATION_DRAG * motion[3:6]
        heat = -TIME_STEP * CONDUCTION * temp_ref[:, here]
        first = jnp.concatenate([push, spin, heat, jnp.ones((1, CHUNK), F32)], axis=0)
        second = jnp.concatenate([pos, radius_ref[:, here]], axis=0)
        first = jnp.concatenate(split(first), axis=0)
        second = jnp.concatenate(split(second) * 2, axis=0)
        lower = lax.broadcasted_iota(jnp.int32, (16, 1), 0) < 8
        box16 = jnp.broadcast_to(boxes, (16, CHUNK)).astype(F32).astype(BF16)
        first_parts = []
        second_parts = []
        for o in range(devices):
            mine = box16 == box_of[o].astype(F32).astype(BF16)
            first_parts.append(jnp.where(mine, first, jnp.zeros_like(first)))
            if o % 2 == 0:
                either = jnp.where(lower, box_of[o].astype(F32), box_of[o + 1].astype(F32)).astype(BF16)
                second_parts.append(jnp.where(box16 == either, second, jnp.zeros_like(second)))
        parts = jnp.concatenate(first_parts + second_parts, axis=0)

        hot_spot = hot(WINDOW, spot_ref[:, here] - WINDOW * w)
        placed = lax.dot_general(parts, hot_spot, NT, preferred_element_type=F32)
        for o in range(devices):
            tile = tile_of[c, box_of[o]] + 2 * w
            one = placed[16 * o : 16 * o + 8] + placed[16 * o + 8 : 16 * o + 16]
            two = placed[16 * devices + 8 * o : 16 * devices + 8 * o + 8]
            two = two + pltpu.roll(two, 4, 0)
            acc[o, tile, 0:8, :] += one[:, :BLOCK]
            acc[o, tile + 1, 0:8, :] += one[:, BLOCK:]
            acc[o, tile, 8:16, :] += two[:, :BLOCK]
            acc[o, tile + 1, 8:16, :] += two[:, BLOCK:]
        return 0

    chunks = particles // CHUNK
    lax.fori_loop(0, chunks, functools.partial(step, 0), 0, unroll=2)

    def later(w, _):
        return lax.fori_loop(0, chunks, functools.partial(step, w), 0)

    lax.fori_loop(1, tile_of[tile_ref.shape[0] - 8, 0], later, 0)

    def finish(o, _):
        for q in range(layers):
            out_ref[o, 8 * q : 8 * q + 8, :] = acc[o, q, 0:8, :]
            out_ref[o, 8 * layers + 4 * q : 8 * layers + 4 * q + 4, :] = acc[o, q, 8:12, :]
        return 0

    lax.fori_loop(0, devices, finish, 0)


def place(box_owner, boxes, pos, motion, radius, temp, slots):
    devices = box_owner.shape[0]
    particles = pos.shape[1]
    layers = slots // BLOCK
    vmem = pl.BlockSpec(memory_space=VMEM)
    row = jax.ShapeDtypeStruct((1, particles), jnp.int32)
    table = (-(-particles // (8 * CHUNK)) * 8 + 8, BLOCK)
    return pl.pallas_call(
        place_kernel,
        out_shape=(
            jax.ShapeDtypeStruct((devices, 12 * layers, BLOCK), F32), row, row,
            jax.ShapeDtypeStruct(table, jnp.int32),
        ),
        in_specs=[pl.BlockSpec(memory_space=pltpu.SMEM)] + [vmem] * 5,
        out_specs=(vmem,) * 4,
        scratch_shapes=[
            pltpu.SMEM((devices,), jnp.int32),
            pltpu.SMEM(table, jnp.int32),
            VMEM((devices, layers + 3, 16, BLOCK), F32),
            pltpu.SemaphoreType.DMA,
        ],
        compiler_params=pltpu.CompilerParams(vmem_limit_bytes=60 << 20),
        cost_estimate=pl.CostEstimate(
            flops=2 * 24 * devices * WINDOW * particles, bytes_accessed=1 << 20, transcendentals=0
        ),
        name="place_slots",
    )(box_owner, boxes, pos, motion, radius, temp)


def pair_terms(near):
    twice = jnp.concatenate([near, near], axis=0)
    high = twice.astype(BF16).astype(F32)
    low = (twice - high).astype(BF16).astype(F32)
    row = lax.broadcasted_iota(jnp.int32, (8, 1), 0)
    kept = high + low
    squares = kept * kept
    norm = -(squares[0:1] + squares[1:2] + squares[2:3])
    total = jnp.where(row < 3, norm, squares[3:4] + 0.5)
    one = total.astype(BF16).astype(F32)
    rest = total - one
    two = rest.astype(BF16).astype(F32)
    three = (rest - two).astype(BF16).astype(F32)
    third = jnp.where((row == 0) | (row == 3), one, jnp.where((row == 1) | (row == 4), two, three))
    third = jnp.where(row < 6, third, 0.0)
    crossed = 2.0 * jnp.where(row < 4, high, low)
    is_radius = (row == 3) | (row == 7)
    cross_d = jnp.where(is_radius, 0.0, crossed)
    cross_r = jnp.where(is_radius, crossed, 0.0)
    ones = jnp.ones_like(third)
    left = jnp.concatenate([high, low, third, jnp.where(row < 6, ones, 0.0)], axis=0)
    ones_d = jnp.where(row < 3, ones, 0.0)
    ones_r = jnp.where((row >= 3) & (row < 6), ones, 0.0)
    for_d = jnp.concatenate([cross_d, cross_d, ones_d, jnp.where(row < 3, third, 0.0)], axis=0)
    for_r = jnp.concatenate([cross_r, cross_r, ones_r, jnp.where((row >= 3) & (row < 6), third, 0.0)], axis=0)
    right = jnp.concatenate([for_d, for_r], axis=1)
    return left, right.astype(BF16)


def contact_kernel(slot_ref, mask_ref, out_ref):
    homes, rows, _ = slot_ref.shape
    layers = rows // 12
    blocks = [(s, q) for s in range(homes) for q in range(layers)]
    row = lax.broadcasted_iota(jnp.int32, (8, 1), 0)
    sign = jnp.where((row >= 3) & (row < 6), 1.0, -1.0)
    lane = lax.broadcasted_iota(jnp.int32, (BLOCK, BLOCK), 1) // 16

    def pairs_of(group):
        pairs = []
        for first in range(0, 8, 4):
            lefts = []
            rights = []
            for g, (s, q) in enumerate(group[first : first + 4]):
                left, right = pair_terms(slot_ref[s, 8 * layers + 4 * q : 8 * layers + 4 * q + 4, :])
                lefts.append(left)
                spots = [jnp.zeros_like(right)] * 4
                spots[g] = right
                rights.append(jnp.concatenate(spots, axis=0))
            turned = jnp.transpose(jnp.concatenate(lefts, axis=0)).astype(BF16)
            pairs.append(
                lax.dot_general(turned, jnp.concatenate(rights, axis=1), NN, preferred_element_type=F32)
            )
        return pairs

    def sums_of(number, group, pairs):
        stacked = []
        for s, q in group:
            mine = slot_ref[s, 8 * q : 8 * q + 8, :]
            high = mine.astype(BF16).astype(F32)
            stacked += [high, mine - high]
        columns = jnp.transpose(jnp.concatenate(stacked, axis=0)).astype(BF16)
        highs = []
        lows = []
        right = []
        for b in range(8):
            at = 2 * BLOCK * (b % 4)
            pair = pairs[b // 4]
            reach = pair[:, at + BLOCK : at + 2 * BLOCK]
            inverse = pl.reciprocal(reach, approx=True)
            inverse = inverse * (2.0 - reach * inverse)
            weight = mask_ref[8 * number + b].astype(F32) * jnp.exp(pair[:, at : at + BLOCK] * inverse)
            high, low = split(weight)
            highs.append(high)
            lows.append(low)
            right.append(jnp.where(lane == b, columns, jnp.zeros_like(columns)))
        return lax.dot_general(
            jnp.concatenate(highs + lows, axis=1), jnp.concatenate(right + right, axis=0), NN,
            preferred_element_type=F32,
        )

    def finish(group, sums):
        sums = jnp.transpose(sums)
        for b, (s, q) in enumerate(group):
            total = sums[16 * b : 16 * b + 8] + sums[16 * b + 8 : 16 * b + 16]
            out_ref[s, 8 * q : 8 * q + 8, :] = slot_ref[s, 8 * q : 8 * q + 8, :] * total[7:8] + sign * total

    groups = [blocks[i : i + 8] for i in range(0, len(blocks), 8)]
    pairs = pairs_of(groups[0])
    before = None
    for number, group in enumerate(groups):
        later = pairs_of(groups[number + 1]) if number + 1 < len(groups) else None
        sums = sums_of(number, group, pairs)
        if before is not None:
            finish(*before)
        before = (group, sums)
        pairs = later
    finish(*before)


def contact(arrived, mask):
    devices, rows, _ = arrived.shape
    layers = rows // 12
    blocks = mask.shape[0]
    step = 32 // layers
    return pl.pallas_call(
        contact_kernel,
        grid=(devices // step,),
        out_shape=jax.ShapeDtypeStruct((devices, 8 * layers, BLOCK), F32),
        in_specs=[
            pl.BlockSpec((step, rows, BLOCK), lambda h: (h, 0, 0)),
            pl.BlockSpec((step * layers, BLOCK, BLOCK), lambda h: (h, 0, 0)),
        ],
        out_specs=pl.BlockSpec((step, 8 * layers, BLOCK), lambda h: (h, 0, 0)),
        compiler_params=pltpu.CompilerParams(vmem_limit_bytes=54 << 20),
        cost_estimate=pl.CostEstimate(
            flops=64 * blocks * BLOCK * BLOCK, bytes_accessed=blocks * BLOCK * BLOCK * 4, transcendentals=0
        ),
        name="contact_blocks",
    )(arrived, mask)


def smoothed(centre, y_first, y_last, x_first, x_last):
    layers, rows, cols = centre.shape
    zero = jnp.zeros((1, rows, cols), F32)
    up = jnp.concatenate([centre[1:], zero], axis=0)
    down = jnp.concatenate([zero, centre[:-1]], axis=0)
    row = lax.broadcasted_iota(jnp.int32, (1, rows, cols), 1)
    col = lax.broadcasted_iota(jnp.int32, (1, rows, cols), 2)
    back = jnp.where(row == 0, y_first, pltpu.roll(centre, 1, 1))
    front = jnp.where(row == rows - 1, y_last, pltpu.roll(centre, rows - 1, 1))
    left = jnp.where(col == 0, x_first, pltpu.roll(centre, 1, 2))
    right = jnp.where(col == cols - 1, x_last, pltpu.roll(centre, cols - 1, 2))
    return CENTRE_WEIGHT * centre + SIDE_WEIGHT * ((up + down) + (back + front) + (left + right))


def columns(edge, layers, rows):
    count = edge.shape[0]
    if count < 8:
        edge = jnp.concatenate([edge] * (8 // count), axis=0)
    turned = jnp.transpose(edge)
    parts = [turned[:, a : a + 1] for a in range(count)]
    return jnp.concatenate(parts, axis=0).reshape(layers, rows, 1)


def smooth_field(field_ref, y0_ref, y1_ref, x0_ref, x1_ref, k, edge=None):
    at = k if edge is None else edge
    _, layers, rows, cols = field_ref.shape
    per = layers * rows // BLOCK
    x0 = columns(x0_ref[at * per : (at + 1) * per, :], layers, rows)
    x1 = columns(x1_ref[at * per : (at + 1) * per, :], layers, rows)
    y0 = y0_ref[at].reshape(layers, 1, cols)
    y1 = y1_ref[at].reshape(layers, 1, cols)
    return smoothed(field_ref[k], y0, y1, x0, x1)


def write_edges(field, k, y0_ref, y1_ref, x0_ref, x1_ref):
    layers, rows, cols = field.shape
    y0_ref[k] = field[:, 0, :]
    y1_ref[k] = field[:, rows - 1, :]
    flat = field.reshape(layers * rows, cols)
    for a in range(layers * rows // BLOCK):
        turned = jnp.transpose(flat[a * BLOCK : (a + 1) * BLOCK, :])
        at = k * (layers * rows // BLOCK) + a
        x0_ref[at : at + 1, :] = turned[0:1, :]
        x1_ref[at : at + 1, :] = turned[cols - 1 : cols, :]


def paired_rows(pairs, layers, rows, scratch):
    half = pairs.shape[0]
    cols = pairs.shape[1] // 2
    scratch[pl.ds(0, half, stride=2), :] = pairs[:, :cols]
    scratch[pl.ds(1, half, stride=2), :] = pairs[:, cols:]
    return scratch[...].reshape(layers, rows, cols)


def gathered(tables, rows, lanes):
    group = rows // 8
    found = [None] * len(tables)
    for g in range(len(tables[0])):
        mine = group == g
        for k, table in enumerate(tables):
            value = jnp.take_along_axis(table[g], lanes, axis=1, mode="promise_in_bounds")
            found[k] = value if g == 0 else jnp.where(mine, value, found[k])
    mine = lax.broadcasted_iota(jnp.int32, (8, BLOCK), 0) == rows % 8
    return [jnp.sum(jnp.where(mine, value, 0.0), axis=0, keepdims=True) for value in found]


def look_kernel(fluid_ref, cell_ref, seen_ref, table, rows_scratch, *, chunk):
    fields, layers, rows, cols = fluid_ref.shape
    particles = cell_ref.shape[1]
    half = layers * rows // 2
    wide = 2 * cols
    for k in range(fields):
        rows_scratch[...] = smoothed(fluid_ref[k], 0.0, 0.0, 0.0, 0.0).reshape(layers * rows, cols)
        here = slice(k * half, (k + 1) * half)
        for part in range(2):
            high, low = split(rows_scratch[pl.ds(part, half, stride=2), :])
            table[here, part * cols : (part + 1) * cols] = high
            table[here, wide + part * cols : wide + (part + 1) * cols] = low

    def step(i, _):
        here = pl.ds(pl.multiple_of(i * chunk, chunk), chunk)
        cells = cell_ref[:, here]
        hot_low = hot(wide, cells % wide)
        found = lax.dot_general(
            table[...], jnp.concatenate([hot_low, hot_low], axis=0), NN, preferred_element_type=F32
        )
        mine = lax.broadcasted_iota(jnp.int32, (half, chunk), 0) == cells // wide
        seen = [
            jnp.sum(jnp.where(mine, found[k * half : (k + 1) * half], 0.0), axis=0, keepdims=True)
            for k in range(fields)
        ]
        seen_ref[:, here] = jnp.concatenate(seen, axis=0)
        return 0

    lax.fori_loop(0, particles // chunk, step, 0)


def look_up(fluid, cells):
    fields, layers, rows, cols = fluid.shape
    particles = cells.shape[1]
    vmem = pl.BlockSpec(memory_space=VMEM)
    return pl.pallas_call(
        functools.partial(look_kernel, chunk=512),
        out_shape=jax.ShapeDtypeStruct((fields, particles), F32),
        in_specs=[vmem] * 2,
        out_specs=vmem,
        scratch_shapes=[
            VMEM((fields * layers * rows // 2, 4 * cols), BF16),
            VMEM((layers * rows, cols), F32),
        ],
        compiler_params=pltpu.CompilerParams(vmem_limit_bytes=40 << 20),
        cost_estimate=pl.CostEstimate(
            flops=8 * fields * layers * rows * cols * particles // 4, bytes_accessed=1 << 20, transcendentals=0
        ),
        name="look_up",
    )(fluid, cells)


def deposit_kernel(
    y0_ref, y1_ref, x0_ref, x1_ref, cell_ref, seen_ref, motion_ref, radius_ref, temp_ref,
    base_ref, dep_ref, dy0_ref, dy1_ref, dx0_ref, dx1_ref, x_table, rows_scratch, acc, *, chunk
):
    fields, layers, rows, cols = dep_ref.shape
    half = layers * rows // 2
    wide = 2 * cols
    particles = cell_ref.shape[1]
    per = layers * rows // BLOCK
    for k in range(fields):
        x_table[k] = jnp.zeros_like(x_table[k])
        x_table[k, 0:per, :] = x0_ref[k * per : (k + 1) * per, :]
        x_table[k, per : 2 * per, :] = x1_ref[k * per : (k + 1) * per, :]
    acc[...] = jnp.zeros_like(acc)

    def step(i, _):
        here = pl.ds(pl.multiple_of(i * chunk, chunk), chunk)
        cells = cell_ref[:, here]
        beside = [[] for _ in range(fields)]
        for s in range(chunk // BLOCK):
            cell = jnp.broadcast_to(cells[:, s * BLOCK : (s + 1) * BLOCK], (8, BLOCK))
            high = cell // cols
            low = cell % cols
            y = high % rows
            from_y = gathered(
                [
                    [ref[k, 8 * g : 8 * g + 8, :] for ref in (y0_ref, y1_ref) for g in range(layers // 8)]
                    for k in range(fields)
                ],
                high // rows + jnp.where(y == 0, 0, layers),
                low,
            )
            from_x = gathered(
                [[x_table[k, 8 * g : 8 * g + 8, :] for g in range(x_table.shape[1] // 8)] for k in range(fields)],
                high // BLOCK + jnp.where(low == 0, 0, per),
                high % BLOCK,
            )
            on_y = (y[0:1] == 0) | (y[0:1] == rows - 1)
            on_x = (low[0:1] == 0) | (low[0:1] == cols - 1)
            for k in range(fields):
                beside[k].append(jnp.where(on_y, from_y[k], 0.0) + jnp.where(on_x, from_x[k], 0.0))
        beside = jnp.concatenate([jnp.concatenate(parts, axis=1) for parts in beside], axis=0)
        seen = seen_ref[:, here] + SIDE_WEIGHT * beside
        motion = motion_ref[:, here]
        radius = radius_ref[:, here]
        temp = temp_ref[:, here]
        drag = DRAG_COEFF / (radius * radius + 0.25) * (seen[0:3] - motion[0:3])
        upward = lax.broadcasted_iota(jnp.int32, (3, 1), 0) == 2
        moved = motion[0:3] + TIME_STEP * drag - jnp.where(upward, TIME_STEP * GRAVITY, 0.0)
        warmed = temp + TIME_STEP * HEAT_TRANSFER * (seen[3:4] - temp)
        base_ref[:, here] = jnp.concatenate([moved, motion[3:6], warmed, seen[3:4]], axis=0)
        volume = radius * radius * radius
        high, low = split(jnp.concatenate([volume, -volume * drag], axis=0))
        hot_low = hot(wide, cells % wide)
        hot_high = hot(half, cells // wide)
        parts = [hot_high * piece[k : k + 1] for piece in (high, low) for k in range(fields)]
        total = lax.dot_general(jnp.concatenate(parts, axis=0), hot_low, NT, preferred_element_type=F32)
        acc[...] += total[: fields * half] + total[fields * half :]
        return 0

    lax.fori_loop(0, particles // chunk, step, 0)
    for k in range(fields):
        field = paired_rows(acc[k * half : (k + 1) * half, :], layers, rows, rows_scratch)
        dep_ref[k] = field
        write_edges(field, k, dy0_ref, dy1_ref, dx0_ref, dx1_ref)


def edge_shapes(fields, layers, rows, cols):
    y_edge = jax.ShapeDtypeStruct((fields, layers, cols), F32)
    x_edge = jax.ShapeDtypeStruct((fields * layers * rows // BLOCK, BLOCK), F32)
    return (y_edge, y_edge, x_edge, x_edge)


def deposit(halo, cells, seen, motion, radius, temp, grid):
    layers, rows, cols = grid
    fields, particles = seen.shape
    tall = -(-2 * layers * rows // (8 * BLOCK)) * 8
    vmem = pl.BlockSpec(memory_space=VMEM)
    return pl.pallas_call(
        functools.partial(deposit_kernel, chunk=1024),
        out_shape=(
            jax.ShapeDtypeStruct((8, particles), F32),
            jax.ShapeDtypeStruct((fields,) + grid, F32),
        ) + edge_shapes(fields, layers, rows, cols),
        in_specs=[vmem] * 9,
        out_specs=(vmem,) * 6,
        scratch_shapes=[
            VMEM((fields, tall, BLOCK), F32),
            VMEM((layers * rows, cols), F32),
            VMEM((fields * layers * rows // 2, 2 * cols), F32),
        ],
        compiler_params=pltpu.CompilerParams(vmem_limit_bytes=40 << 20),
        cost_estimate=pl.CostEstimate(
            flops=4 * fields * layers * rows * cols * particles, bytes_accessed=2 << 20, transcendentals=0
        ),
        name="deposit_fields",
    )(*halo, cells, seen, motion, radius, temp)


def heat_kernel(
    back_ref, slot_ref, cell_ref, radius_ref, base_ref, ey0_ref, ey1_ref, ex0_ref, ex1_ref,
    next_ref, dep_ref, dy0_ref, dy1_ref, dx0_ref, dx1_ref,
    table, acc, rows_scratch, *, chunk, rows
):
    devices, tall, _ = back_ref.shape
    layers = tall // 8
    particles = slot_ref.shape[1]
    half, wide = acc.shape
    for o in range(devices):
        for q in range(layers):
            table[o * layers + q : o * layers + q + 1, :] = back_ref[o, 8 * q + 6 : 8 * q + 7, :]
    acc[...] = jnp.zeros_like(acc)

    def step(i, _):
        here = pl.ds(pl.multiple_of(i * chunk, chunk), chunk)
        slots = slot_ref[:, here]
        gained = []
        for s in range(chunk // BLOCK):
            wanted = jnp.broadcast_to(slots[:, s * BLOCK : (s + 1) * BLOCK], (8, BLOCK))
            tiles = [table[8 * g : 8 * g + 8, :] for g in range(devices * layers // 8)]
            gained.append(gathered([tiles], wanted // BLOCK, wanted % BLOCK)[0])
        base = base_ref[6:8, here]
        total = base[0:1] + jnp.concatenate(gained, axis=1)
        next_ref[:, here] = total
        radius = radius_ref[:, here]
        high, low = split(radius * radius * radius * (total - base[1:2]))
        cells = cell_ref[:, here]
        hot_low = hot_columns(wide, cells % wide)
        hot_high = hot(half, cells // wide)
        parts = jnp.concatenate([hot_high * high, hot_high * low], axis=0)
        added = lax.dot_general(parts, hot_low, NN, preferred_element_type=F32)
        acc[...] += added[:half] + added[half:]
        return 0

    lax.fori_loop(0, particles // chunk, step, 0)
    field = paired_rows(acc[...], 2 * half // rows, rows, rows_scratch)
    dep_ref[0] = field
    for edge, out in ((ey0_ref, dy0_ref), (ey1_ref, dy1_ref), (ex0_ref, dx0_ref), (ex1_ref, dx1_ref)):
        out[0 : edge.shape[0]] = edge[...]
    write_edges(field, ey0_ref.shape[0], dy0_ref, dy1_ref, dx0_ref, dx1_ref)


def heat_deposit(back, slot_of, cells, radius, base, edges, grid):
    devices = back.shape[0]
    layers, rows, cols = grid
    particles = cells.shape[1]
    half = layers * rows // 2
    fields = edges[0].shape[0] + 1
    vmem = pl.BlockSpec(memory_space=VMEM)
    return pl.pallas_call(
        functools.partial(heat_kernel, chunk=1024, rows=rows),
        out_shape=(
            jax.ShapeDtypeStruct((1, particles), F32),
            jax.ShapeDtypeStruct((1,) + grid, F32),
        ) + edge_shapes(fields, layers, rows, cols),
        in_specs=[vmem] * 9,
        out_specs=(vmem,) * 6,
        scratch_shapes=[
            VMEM((devices * back.shape[1] // 8, BLOCK), F32),
            VMEM((half, 2 * cols), F32),
            VMEM((layers * rows, cols), F32),
        ],
        compiler_params=pltpu.CompilerParams(vmem_limit_bytes=40 << 20),
        cost_estimate=pl.CostEstimate(
            flops=4 * half * 2 * cols * particles, bytes_accessed=1 << 20, transcendentals=0
        ),
        name="heat_deposit",
    )(back, slot_of, cells, radius, base, *edges)


def fetch_kernel(
    owner_ref, tile_ref, back_ref, box_ref, spot_ref, base_ref, warm_ref, next_ref, box_of, table
):
    devices, tall, _ = back_ref.shape
    layers = tall // 8
    particles = box_ref.shape[1]
    invert(owner_ref, box_of)
    for o in range(devices):
        for q in range(layers):
            high, low = split(back_ref[o, 8 * q : 8 * q + 8, :])
            table[o, q] = jnp.concatenate([high, low], axis=0)
        for q in range(layers, layers + 3):
            table[o, q] = jnp.zeros((16, BLOCK), BF16)

    def gained_of(w, c):
        here = pl.ds(pl.multiple_of(c * CHUNK, CHUNK), CHUNK)
        boxes = jnp.broadcast_to(box_ref[:, here], (8, CHUNK))
        tile = [tile_ref[c, box_of[o]] + 2 * w for o in range(devices)]
        wanted = jnp.concatenate(
            [jnp.concatenate([table[o, tile[o]], table[o, tile[o] + 1]], axis=1) for o in range(devices)], axis=0
        )
        hot_spot = hot(WINDOW, spot_ref[:, here] - WINDOW * w)
        found = lax.dot_general(wanted, hot_spot, NN, preferred_element_type=F32)
        gained = jnp.zeros((8, CHUNK), F32)
        for o in range(devices):
            value = found[16 * o : 16 * o + 8] + found[16 * o + 8 : 16 * o + 16]
            gained = jnp.where(boxes == box_of[o], value, gained)
        return here, gained

    def step(c, _):
        here, gained = gained_of(0, c)
        next_ref[:, here] = jnp.concatenate(
            [base_ref[0:6, here] + gained[0:6], warm_ref[:, here]], axis=0
        )
        return 0

    chunks = particles // CHUNK
    lax.fori_loop(0, chunks, step, 0, unroll=2)

    def later(w, _):
        def again(c, _):
            here, gained = gained_of(w, c)
            next_ref[0:6, here] += gained[0:6]
            return 0

        return lax.fori_loop(0, chunks, again, 0)

    lax.fori_loop(1, tile_ref[tile_ref.shape[0] - 8, 0], later, 0)


def fetch(box_owner, tiles, back, boxes, spots, base, warm):
    devices, tall, _ = back.shape
    layers = tall // 8
    particles = boxes.shape[1]
    vmem = pl.BlockSpec(memory_space=VMEM)
    smem = pl.BlockSpec(memory_space=pltpu.SMEM)
    return pl.pallas_call(
        fetch_kernel,
        out_shape=jax.ShapeDtypeStruct((7, particles), F32),
        in_specs=[smem, smem] + [vmem] * 5,
        out_specs=vmem,
        scratch_shapes=[
            pltpu.SMEM((devices,), jnp.int32),
            VMEM((devices, layers + 3, 16, BLOCK), BF16),
        ],
        compiler_params=pltpu.CompilerParams(vmem_limit_bytes=40 << 20),
        cost_estimate=pl.CostEstimate(
            flops=32 * devices * WINDOW * particles, bytes_accessed=1 << 20, transcendentals=0
        ),
        name="fetch_slots",
    )(box_owner, tiles, back, boxes, spots, base, warm)


def spread_kernel(dep_ref, heat_ref, y0_ref, y1_ref, x0_ref, x1_ref, fluid_ref, next_ref, void_ref):
    halo = (y0_ref, y1_ref, x0_ref, x1_ref)
    crowding = 1.0 + COUPLING * smooth_field(dep_ref, *halo, 0)
    void_ref[...] = 1.0 / crowding
    for k in range(3):
        next_ref[k] = fluid_ref[k] + TIME_STEP * COUPLING * smooth_field(dep_ref, *halo, k + 1) * crowding
    warmth = smooth_field(heat_ref, *halo, 0, 4)
    next_ref[3] = fluid_ref[3] + TIME_STEP * COUPLING * warmth * crowding


def spread(dep, heat, halo, fluid):
    vmem = pl.BlockSpec(memory_space=VMEM)
    return pl.pallas_call(
        spread_kernel,
        out_shape=(jax.ShapeDtypeStruct(fluid.shape, F32), jax.ShapeDtypeStruct(fluid.shape[1:], F32)),
        in_specs=[vmem] * 7,
        out_specs=(vmem,) * 2,
        compiler_params=pltpu.CompilerParams(vmem_limit_bytes=40 << 20),
        cost_estimate=pl.CostEstimate(flops=20 * fluid.size, bytes_accessed=2 << 20, transcendentals=0),
        name="spread_fields",
    )(dep, heat, *halo, fluid)


def halo_of(y_first, y_last, x_first, x_last):
    def moved(value, axis, step):
        size = lax.axis_size(axis)
        pairs = [(i, i + step) for i in range(size) if 0 <= i + step < size]
        return lax.ppermute(value, axis, pairs)

    return (
        moved(y_last, "gy", 1),
        moved(y_first, "gy", -1),
        moved(x_last, "gx", 1),
        moved(x_first, "gx", -1),
    )


def shards(
    fluid_state, particle_pos, particle_motion, particle_radius, particle_temp,
    particle_cell, particle_box, box_owner, contact_mask,
):
    devices = lax.axis_size(("gx", "gy"))
    particles = particle_pos.shape[1]
    slots = 2 * particles // devices
    fields, layers, rows, cols = fluid_state.shape
    boxes = particle_box.reshape(1, particles)
    radius = particle_radius.reshape(1, particles)
    temp = particle_temp.reshape(1, particles)
    cells = particle_cell.reshape(1, particles)

    outgoing, slot_of, spots, tiles = place(
        box_owner, boxes, particle_pos, particle_motion, radius, temp, slots
    )
    arrived = lax.all_to_all(outgoing, ("gx", "gy"), split_axis=0, concat_axis=0, tiled=True)

    spots, fluid = lax.optimization_barrier((spots, fluid_state))
    fluid_halo = halo_of(
        fluid[:, :, 0, :],
        fluid[:, :, rows - 1, :],
        fluid[:, :, :, 0].reshape(-1, BLOCK),
        fluid[:, :, :, cols - 1].reshape(-1, BLOCK),
    )
    seen = look_up(fluid, cells)
    arrived, seen = lax.optimization_barrier((arrived, seen))
    result = contact(arrived, contact_mask)

    result, *fluid_halo = lax.optimization_barrier((result,) + tuple(fluid_halo))
    base, deposits, *edges = deposit(
        fluid_halo, cells, seen, particle_motion, radius, temp, (layers, rows, cols)
    )
    back = lax.all_to_all(result, ("gx", "gy"), split_axis=0, concat_axis=0, tiled=True)
    warm, heat_field, *edges = heat_deposit(
        back, slot_of, cells, radius, base, edges, (layers, rows, cols)
    )
    halo = halo_of(*edges)
    particle_next = fetch(box_owner, tiles, back, boxes, spots, base, warm)
    fluid_next, void_fraction = spread(deposits, heat_field, halo, fluid_state)
    return (fluid_next, void_fraction, particle_next)


def solution(mesh):
    in_specs = (
        P(None, None, "gy", "gx"),
        P(None, ("gx", "gy")),
        P(None, ("gx", "gy")),
        P(("gx", "gy")),
        P(("gx", "gy")),
        P(("gx", "gy")),
        P(("gx", "gy"), None),
        P(),
        P(("gx", "gy"), None, None),
    )
    out_specs = (P(None, None, "gy", "gx"), P(None, "gy", "gx"), P(None, ("gx", "gy")))
    return jax.shard_map(shards, mesh=mesh, in_specs=in_specs, out_specs=out_specs, check_vma=False)
```

```python
import functools

import jax
import jax.numpy as jnp
from jax import lax
from jax.experimental import pallas as pl
from jax.experimental.pallas import tpu as pltpu
from jax.sharding import PartitionSpec as P

BLOCK = 128
TIME_STEP = 0.1
STIFFNESS = 0.5
DAMPING_RATE = 0.2
ROTATION_DRAG = 0.1
DRAG_COEFF = 4.0
CONDUCTION = 0.3
HEAT_TRANSFER = 4.0
GRAVITY = 0.3
COUPLING = 4.0
CENTRE_WEIGHT = 0.25
SIDE_WEIGHT = 0.125

F32 = jnp.float32
BF16 = jnp.bfloat16
VMEM = pltpu.VMEM
NN = (((1,), (0,)), ((), ()))
NT = (((1,), (1,)), ((), ()))


def split(value):
    high = value.astype(BF16)
    return high, (value - high.astype(F32)).astype(BF16)


def hot(count, row):
    places = lax.broadcasted_iota(jnp.int32, (count, row.shape[1]), 0)
    return jnp.where(places == row, 1.0, 0.0).astype(BF16)


def hot_columns(count, row):
    n = row.shape[1] // BLOCK
    tiles = [row[:, a * BLOCK : (a + 1) * BLOCK] for a in range(n)]
    turned = jnp.transpose(jnp.concatenate(tiles * (8 // n), axis=0).astype(F32))
    places = lax.broadcasted_iota(jnp.int32, (BLOCK, count), 1).astype(F32)
    return jnp.concatenate(
        [jnp.where(places == turned[:, a : a + 1], 1.0, 0.0).astype(BF16) for a in range(n)], axis=0
    )


def invert(owner_ref, box_of):
    def step(b, _):
        box_of[owner_ref[b]] = b
        return 0

    lax.fori_loop(0, owner_ref.shape[0], step, 0)


WINDOW = 256
CHUNK = 1024


def place_kernel(
    owner_ref, box_ref, pos_ref, motion_ref, radius_ref, temp_ref,
    out_ref, slot_ref, spot_ref, tile_ref,
    box_of, tile_of, acc, done
):
    devices, rows, _ = out_ref.shape
    layers = rows // 12
    slots = layers * BLOCK
    particles = box_ref.shape[1]
    sub = 256
    invert(owner_ref, box_of)
    acc[...] = jnp.zeros_like(acc)

    box_row = lax.broadcasted_iota(jnp.int32, (devices, 1), 0)
    owner_column = jnp.zeros((devices, 1), F32)
    for b in range(devices):
        owner_column = jnp.where(box_row == b, owner_ref[b].astype(F32), owner_column)
    above = (
        lax.broadcasted_iota(jnp.int32, (sub, sub), 0) < lax.broadcasted_iota(jnp.int32, (sub, sub), 1)
    )
    above = jnp.where(above, 1.0, 0.0).astype(BF16)
    lane = lax.broadcasted_iota(jnp.int32, (devices, BLOCK), 1)
    tiles = jnp.zeros((devices, BLOCK), F32)
    highest = jnp.zeros((1, sub), F32)
    carry = jnp.zeros((devices, 1), F32)
    per_chunk = CHUNK // sub
    for c in range(particles // CHUNK):
        chosen = []
        for s in range(per_chunk):
            at = c * CHUNK + s * sub
            chosen.append(
                lax.broadcasted_iota(jnp.int32, (devices, sub), 0) == box_ref[:, at : at + sub]
            )
        ones = [jnp.where(mine, 1.0, 0.0) for mine in chosen]
        earlier = lax.dot_general(
            jnp.concatenate(ones, axis=0).astype(BF16), above, NN, preferred_element_type=F32
        )
        tile = jnp.minimum(jnp.floor(carry * (1.0 / BLOCK)), layers - 1.0)
        tiles = jnp.where(lane == c, tile, tiles)
        for s in range(per_chunk):
            at = c * CHUNK + s * sub
            rank = earlier[s * devices : (s + 1) * devices] + carry
            spot = jnp.where(chosen[s], rank - BLOCK * tile, 0.0)
            spot = jnp.sum(spot, axis=0, keepdims=True)
            slot = jnp.where(chosen[s], rank + slots * owner_column, 0.0)
            slot = jnp.sum(slot, axis=0, keepdims=True)
            spot_ref[:, at : at + sub] = spot.astype(jnp.int32)
            slot_ref[:, at : at + sub] = slot.astype(jnp.int32)
            highest = jnp.maximum(highest, spot)
            carry = carry + jnp.sum(ones[s], axis=1, keepdims=True)
    if devices < BLOCK:
        tiles = jnp.concatenate([tiles, jnp.zeros((BLOCK - devices, BLOCK), F32)], axis=0)
    count = tile_ref.shape[0] - 8
    tile_ref[0:count, :] = jnp.transpose(tiles)[0:count].astype(jnp.int32)
    windows = jnp.floor(jnp.max(highest, axis=1, keepdims=True) * (1.0 / WINDOW)) + 1.0
    tile_ref[count : count + 8, :] = jnp.broadcast_to(windows, (8, BLOCK)).astype(jnp.int32)
    copy = pltpu.make_async_copy(tile_ref, tile_of, done)
    copy.start()
    copy.wait()

    def step(w, c, _):
        here = pl.ds(pl.multiple_of(c * CHUNK, CHUNK), CHUNK)
        boxes = box_ref[:, here]
        pos = pos_ref[:, here]
        motion = motion_ref[:, here]
        push = TIME_STEP * STIFFNESS * pos - TIME_STEP * DAMPING_RATE * motion[0:3]
        spin = -TIME_STEP * ROTATION_DRAG * motion[3:6]
        heat = -TIME_STEP * CONDUCTION * temp_ref[:, here]
        first = jnp.concatenate([push, spin, heat, jnp.ones((1, CHUNK), F32)], axis=0)
        second = jnp.concatenate([pos, radius_ref[:, here]], axis=0)
        first = jnp.concatenate(split(first), axis=0)
        second = jnp.concatenate(split(second) * 2, axis=0)
        lower = lax.broadcasted_iota(jnp.int32, (16, 1), 0) < 8
        box16 = jnp.broadcast_to(boxes, (16, CHUNK)).astype(F32).astype(BF16)
        first_parts = []
        second_parts = []
        for o in range(devices):
            mine = box16 == box_of[o].astype(F32).astype(BF16)
            first_parts.append(jnp.where(mine, first, jnp.zeros_like(first)))
            if o % 2 == 0:
                either = jnp.where(lower, box_of[o].astype(F32), box_of[o + 1].astype(F32)).astype(BF16)
                second_parts.append(jnp.where(box16 == either, second, jnp.zeros_like(second)))
        parts = jnp.concatenate(first_parts + second_parts, axis=0)

        hot_spot = hot(WINDOW, spot_ref[:, here] - WINDOW * w)
        placed = lax.dot_general(parts, hot_spot, NT, preferred_element_type=F32)
        for o in range(devices):
            tile = tile_of[c, box_of[o]] + 2 * w
            one = placed[16 * o : 16 * o + 8] + placed[16 * o + 8 : 16 * o + 16]
            two = placed[16 * devices + 8 * o : 16 * devices + 8 * o + 8]
            two = two + pltpu.roll(two, 4, 0)
            acc[o, tile, 0:8, :] += one[:, :BLOCK]
            acc[o, tile + 1, 0:8, :] += one[:, BLOCK:]
            acc[o, tile, 8:16, :] += two[:, :BLOCK]
            acc[o, tile + 1, 8:16, :] += two[:, BLOCK:]
        return 0

    chunks = particles // CHUNK
    lax.fori_loop(0, chunks, functools.partial(step, 0), 0, unroll=2)

    def later(w, _):
        return lax.fori_loop(0, chunks, functools.partial(step, w), 0)

    lax.fori_loop(1, tile_of[tile_ref.shape[0] - 8, 0], later, 0)

    def finish(o, _):
        for q in range(layers):
            out_ref[o, 8 * q : 8 * q + 8, :] = acc[o, q, 0:8, :]
            out_ref[o, 8 * layers + 4 * q : 8 * layers + 4 * q + 4, :] = acc[o, q, 8:12, :]
        return 0

    lax.fori_loop(0, devices, finish, 0)


def place(box_owner, boxes, pos, motion, radius, temp, slots):
    devices = box_owner.shape[0]
    particles = pos.shape[1]
    layers = slots // BLOCK
    vmem = pl.BlockSpec(memory_space=VMEM)
    row = jax.ShapeDtypeStruct((1, particles), jnp.int32)
    table = (-(-particles // (8 * CHUNK)) * 8 + 8, BLOCK)
    return pl.pallas_call(
        place_kernel,
        out_shape=(
            jax.ShapeDtypeStruct((devices, 12 * layers, BLOCK), F32), row, row,
            jax.ShapeDtypeStruct(table, jnp.int32),
        ),
        in_specs=[pl.BlockSpec(memory_space=pltpu.SMEM)] + [vmem] * 5,
        out_specs=(vmem,) * 4,
        scratch_shapes=[
            pltpu.SMEM((devices,), jnp.int32),
            pltpu.SMEM(table, jnp.int32),
            VMEM((devices, layers + 3, 16, BLOCK), F32),
            pltpu.SemaphoreType.DMA,
        ],
        compiler_params=pltpu.CompilerParams(vmem_limit_bytes=60 << 20),
        cost_estimate=pl.CostEstimate(
            flops=2 * 24 * devices * WINDOW * particles, bytes_accessed=1 << 20, transcendentals=0
        ),
        name="place_slots",
    )(box_owner, boxes, pos, motion, radius, temp)


def pair_terms(near):
    twice = jnp.concatenate([near, near], axis=0)
    high = twice.astype(BF16).astype(F32)
    low = (twice - high).astype(BF16).astype(F32)
    row = lax.broadcasted_iota(jnp.int32, (8, 1), 0)
    kept = high + low
    squares = kept * kept
    norm = -(squares[0:1] + squares[1:2] + squares[2:3])
    total = jnp.where(row < 3, norm, squares[3:4] + 0.5)
    one = total.astype(BF16).astype(F32)
    rest = total - one
    two = rest.astype(BF16).astype(F32)
    three = (rest - two).astype(BF16).astype(F32)
    third = jnp.where((row == 0) | (row == 3), one, jnp.where((row == 1) | (row == 4), two, three))
    third = jnp.where(row < 6, third, 0.0)
    crossed = 2.0 * jnp.where(row < 4, high, low)
    is_radius = (row == 3) | (row == 7)
    cross_d = jnp.where(is_radius, 0.0, crossed)
    cross_r = jnp.where(is_radius, crossed, 0.0)
    ones = jnp.ones_like(third)
    left = jnp.concatenate([high, low, third, jnp.where(row < 6, ones, 0.0)], axis=0)
    ones_d = jnp.where(row < 3, ones, 0.0)
    ones_r = jnp.where((row >= 3) & (row < 6), ones, 0.0)
    for_d = jnp.concatenate([cross_d, cross_d, ones_d, jnp.where(row < 3, third, 0.0)], axis=0)
    for_r = jnp.concatenate([cross_r, cross_r, ones_r, jnp.where((row >= 3) & (row < 6), third, 0.0)], axis=0)
    right = jnp.concatenate([for_d, for_r], axis=1)
    return left, right.astype(BF16)


def contact_kernel(slot_ref, mask_ref, out_ref):
    homes, rows, _ = slot_ref.shape
    layers = rows // 12
    blocks = [(s, q) for s in range(homes) for q in range(layers)]
    row = lax.broadcasted_iota(jnp.int32, (8, 1), 0)
    sign = jnp.where((row >= 3) & (row < 6), 1.0, -1.0)
    lane = lax.broadcasted_iota(jnp.int32, (BLOCK, BLOCK), 1) // 16

    def pairs_of(group):
        pairs = []
        for first in range(0, 8, 4):
            lefts = []
            rights = []
            for g, (s, q) in enumerate(group[first : first + 4]):
                left, right = pair_terms(slot_ref[s, 8 * layers + 4 * q : 8 * layers + 4 * q + 4, :])
                lefts.append(left)
                spots = [jnp.zeros_like(right)] * 4
                spots[g] = right
                rights.append(jnp.concatenate(spots, axis=0))
            turned = jnp.transpose(jnp.concatenate(lefts, axis=0)).astype(BF16)
            pairs.append(
                lax.dot_general(turned, jnp.concatenate(rights, axis=1), NN, preferred_element_type=F32)
            )
        return pairs

    def sums_of(number, group, pairs):
        stacked = []
        for s, q in group:
            mine = slot_ref[s, 8 * q : 8 * q + 8, :]
            high = mine.astype(BF16).astype(F32)
            stacked += [high, mine - high]
        columns = jnp.transpose(jnp.concatenate(stacked, axis=0)).astype(BF16)
        highs = []
        lows = []
        right = []
        for b in range(8):
            at = 2 * BLOCK * (b % 4)
            pair = pairs[b // 4]
            reach = pair[:, at + BLOCK : at + 2 * BLOCK]
            inverse = pl.reciprocal(reach, approx=True)
            inverse = inverse * (2.0 - reach * inverse)
            weight = mask_ref[8 * number + b].astype(F32) * jnp.exp(pair[:, at : at + BLOCK] * inverse)
            high, low = split(weight)
            highs.append(high)
            lows.append(low)
            right.append(jnp.where(lane == b, columns, jnp.zeros_like(columns)))
        return lax.dot_general(
            jnp.concatenate(highs + lows, axis=1), jnp.concatenate(right + right, axis=0), NN,
            preferred_element_type=F32,
        )

    def finish(group, sums):
        sums = jnp.transpose(sums)
        for b, (s, q) in enumerate(group):
            total = sums[16 * b : 16 * b + 8] + sums[16 * b + 8 : 16 * b + 16]
            out_ref[s, 8 * q : 8 * q + 8, :] = slot_ref[s, 8 * q : 8 * q + 8, :] * total[7:8] + sign * total

    groups = [blocks[i : i + 8] for i in range(0, len(blocks), 8)]
    pairs = pairs_of(groups[0])
    before = None
    for number, group in enumerate(groups):
        later = pairs_of(groups[number + 1]) if number + 1 < len(groups) else None
        sums = sums_of(number, group, pairs)
        if before is not None:
            finish(*before)
        before = (group, sums)
        pairs = later
    finish(*before)


def contact(arrived, mask):
    devices, rows, _ = arrived.shape
    layers = rows // 12
    blocks = mask.shape[0]
    step = 32 // layers
    return pl.pallas_call(
        contact_kernel,
        grid=(devices // step,),
        out_shape=jax.ShapeDtypeStruct((devices, 8 * layers, BLOCK), F32),
        in_specs=[
            pl.BlockSpec((step, rows, BLOCK), lambda h: (h, 0, 0)),
            pl.BlockSpec((step * layers, BLOCK, BLOCK), lambda h: (h, 0, 0)),
        ],
        out_specs=pl.BlockSpec((step, 8 * layers, BLOCK), lambda h: (h, 0, 0)),
        compiler_params=pltpu.CompilerParams(vmem_limit_bytes=40 << 20),
        cost_estimate=pl.CostEstimate(
            flops=64 * blocks * BLOCK * BLOCK, bytes_accessed=blocks * BLOCK * BLOCK * 4, transcendentals=0
        ),
        name="contact_blocks",
    )(arrived, mask)


def smoothed(centre, y_first, y_last, x_first, x_last):
    layers, rows, cols = centre.shape
    zero = jnp.zeros((1, rows, cols), F32)
    up = jnp.concatenate([centre[1:], zero], axis=0)
    down = jnp.concatenate([zero, centre[:-1]], axis=0)
    row = lax.broadcasted_iota(jnp.int32, (1, rows, cols), 1)
    col = lax.broadcasted_iota(jnp.int32, (1, rows, cols), 2)
    back = jnp.where(row == 0, y_first, pltpu.roll(centre, 1, 1))
    front = jnp.where(row == rows - 1, y_last, pltpu.roll(centre, rows - 1, 1))
    left = jnp.where(col == 0, x_first, pltpu.roll(centre, 1, 2))
    right = jnp.where(col == cols - 1, x_last, pltpu.roll(centre, cols - 1, 2))
    return CENTRE_WEIGHT * centre + SIDE_WEIGHT * ((up + down) + (back + front) + (left + right))


def columns(edge, layers, rows):
    count = edge.shape[0]
    if count < 8:
        edge = jnp.concatenate([edge] * (8 // count), axis=0)
    turned = jnp.transpose(edge)
    parts = [turned[:, a : a + 1] for a in range(count)]
    return jnp.concatenate(parts, axis=0).reshape(layers, rows, 1)


def smooth_field(field_ref, y0_ref, y1_ref, x_first, x_last, k, edge=None):
    at = k if edge is None else edge
    _, layers, rows, cols = field_ref.shape
    per = layers * rows // BLOCK
    x0 = columns(x_first[at * per : (at + 1) * per, :], layers, rows)
    x1 = columns(x_last[at * per : (at + 1) * per, :], layers, rows)
    y0 = y0_ref[at].reshape(layers, 1, cols)
    y1 = y1_ref[at].reshape(layers, 1, cols)
    return smoothed(field_ref[k], y0, y1, x0, x1)


def x_beside(gathered_ref):
    at = lax.axis_index("gx")
    last = gathered_ref.shape[0] - 1
    before = gathered_ref[jnp.maximum(at - 1, 0), 1]
    after = gathered_ref[jnp.minimum(at + 1, last), 0]
    return jnp.where(at > 0, before, 0.0), jnp.where(at < last, after, 0.0)


def write_edges(field, k, y0_ref, y1_ref, x_ref):
    layers, rows, cols = field.shape
    y0_ref[k] = field[:, 0, :]
    y1_ref[k] = field[:, rows - 1, :]
    flat = field.reshape(layers * rows, cols)
    for a in range(layers * rows // BLOCK):
        turned = jnp.transpose(flat[a * BLOCK : (a + 1) * BLOCK, :])
        at = k * (layers * rows // BLOCK) + a
        x_ref[0, at : at + 1, :] = turned[0:1, :]
        x_ref[1, at : at + 1, :] = turned[cols - 1 : cols, :]


def paired_rows(pairs, layers, rows, scratch):
    half = pairs.shape[0]
    cols = pairs.shape[1] // 2
    scratch[pl.ds(0, half, stride=2), :] = pairs[:, :cols]
    scratch[pl.ds(1, half, stride=2), :] = pairs[:, cols:]
    return scratch[...].reshape(layers, rows, cols)


def gathered(tables, rows, lanes):
    group = rows // 8
    found = [None] * len(tables)
    for g in range(len(tables[0])):
        mine = group == g
        for k, table in enumerate(tables):
            value = jnp.take_along_axis(table[g], lanes, axis=1, mode="promise_in_bounds")
            found[k] = value if g == 0 else jnp.where(mine, value, found[k])
    mine = lax.broadcasted_iota(jnp.int32, (8, BLOCK), 0) == rows % 8
    return [jnp.sum(jnp.where(mine, value, 0.0), axis=0, keepdims=True) for value in found]


def look_kernel(fluid_ref, cell_ref, seen_ref, table, rows_scratch, *, chunk):
    fields, layers, rows, cols = fluid_ref.shape
    particles = cell_ref.shape[1]
    half = layers * rows // 2
    wide = 2 * cols
    for k in range(fields):
        rows_scratch[...] = smoothed(fluid_ref[k], 0.0, 0.0, 0.0, 0.0).reshape(layers * rows, cols)
        here = slice(k * half, (k + 1) * half)
        for part in range(2):
            high, low = split(rows_scratch[pl.ds(part, half, stride=2), :])
            table[here, part * cols : (part + 1) * cols] = high
            table[here, wide + part * cols : wide + (part + 1) * cols] = low

    def step(i, _):
        here = pl.ds(pl.multiple_of(i * chunk, chunk), chunk)
        cells = cell_ref[:, here]
        hot_low = hot(wide, cells % wide)
        found = lax.dot_general(
            table[...], jnp.concatenate([hot_low, hot_low], axis=0), NN, preferred_element_type=F32
        )
        mine = lax.broadcasted_iota(jnp.int32, (half, chunk), 0) == cells // wide
        seen = [
            jnp.sum(jnp.where(mine, found[k * half : (k + 1) * half], 0.0), axis=0, keepdims=True)
            for k in range(fields)
        ]
        seen_ref[:, here] = jnp.concatenate(seen, axis=0)
        return 0

    lax.fori_loop(0, particles // chunk, step, 0, unroll=2)


def look_up(fluid, cells):
    fields, layers, rows, cols = fluid.shape
    particles = cells.shape[1]
    vmem = pl.BlockSpec(memory_space=VMEM)
    return pl.pallas_call(
        functools.partial(look_kernel, chunk=512),
        out_shape=jax.ShapeDtypeStruct((fields, particles), F32),
        in_specs=[vmem] * 2,
        out_specs=vmem,
        scratch_shapes=[
            VMEM((fields * layers * rows // 2, 4 * cols), BF16),
            VMEM((layers * rows, cols), F32),
        ],
        compiler_params=pltpu.CompilerParams(vmem_limit_bytes=40 << 20),
        cost_estimate=pl.CostEstimate(
            flops=8 * fields * layers * rows * cols * particles // 4, bytes_accessed=1 << 20, transcendentals=0
        ),
        name="look_up",
    )(fluid, cells)


def deposit_kernel(
    y0_ref, y1_ref, x_ref, cell_ref, seen_ref, motion_ref, radius_ref, temp_ref,
    base_ref, dep_ref, dy0_ref, dy1_ref, dx_ref, x_table, rows_scratch, acc, *, chunk
):
    fields, layers, rows, cols = dep_ref.shape
    half = layers * rows // 2
    wide = 2 * cols
    particles = cell_ref.shape[1]
    per = layers * rows // BLOCK
    x_first, x_last = x_beside(x_ref)
    for k in range(fields):
        x_table[k] = jnp.zeros_like(x_table[k])
        x_table[k, 0:per, :] = x_first[k * per : (k + 1) * per]
        x_table[k, per : 2 * per, :] = x_last[k * per : (k + 1) * per]
    acc[...] = jnp.zeros_like(acc)

    def step(i, _):
        here = pl.ds(pl.multiple_of(i * chunk, chunk), chunk)
        cells = cell_ref[:, here]
        beside = [[] for _ in range(fields)]
        for s in range(chunk // BLOCK):
            cell = jnp.broadcast_to(cells[:, s * BLOCK : (s + 1) * BLOCK], (8, BLOCK))
            high = cell // cols
            low = cell % cols
            y = high % rows
            from_y = gathered(
                [
                    [ref[k, 8 * g : 8 * g + 8, :] for ref in (y0_ref, y1_ref) for g in range(layers // 8)]
                    for k in range(fields)
                ],
                high // rows + jnp.where(y == 0, 0, layers),
                low,
            )
            from_x = gathered(
                [[x_table[k, 8 * g : 8 * g + 8, :] for g in range(x_table.shape[1] // 8)] for k in range(fields)],
                high // BLOCK + jnp.where(low == 0, 0, per),
                high % BLOCK,
            )
            on_y = (y[0:1] == 0) | (y[0:1] == rows - 1)
            on_x = (low[0:1] == 0) | (low[0:1] == cols - 1)
            for k in range(fields):
                beside[k].append(jnp.where(on_y, from_y[k], 0.0) + jnp.where(on_x, from_x[k], 0.0))
        beside = jnp.concatenate([jnp.concatenate(parts, axis=1) for parts in beside], axis=0)
        seen = seen_ref[:, here] + SIDE_WEIGHT * beside
        motion = motion_ref[:, here]
        radius = radius_ref[:, here]
        temp = temp_ref[:, here]
        drag = DRAG_COEFF / (radius * radius + 0.25) * (seen[0:3] - motion[0:3])
        upward = lax.broadcasted_iota(jnp.int32, (3, 1), 0) == 2
        moved = motion[0:3] + TIME_STEP * drag - jnp.where(upward, TIME_STEP * GRAVITY, 0.0)
        warmed = temp + TIME_STEP * HEAT_TRANSFER * (seen[3:4] - temp)
        base_ref[:, here] = jnp.concatenate([moved, motion[3:6], warmed, seen[3:4]], axis=0)
        volume = radius * radius * radius
        high, low = split(jnp.concatenate([volume, -volume * drag], axis=0))
        hot_low = hot(wide, cells % wide)
        hot_high = hot(half, cells // wide)
        parts = [hot_high * piece[k : k + 1] for piece in (high, low) for k in range(fields)]
        total = lax.dot_general(jnp.concatenate(parts, axis=0), hot_low, NT, preferred_element_type=F32)
        acc[...] += total[: fields * half] + total[fields * half :]
        return 0

    lax.fori_loop(0, particles // chunk, step, 0)
    for k in range(fields):
        field = paired_rows(acc[k * half : (k + 1) * half, :], layers, rows, rows_scratch)
        dep_ref[k] = field
        write_edges(field, k, dy0_ref, dy1_ref, dx_ref)


def edge_shapes(fields, layers, rows, cols):
    y_edge = jax.ShapeDtypeStruct((fields, layers, cols), F32)
    x_edges = jax.ShapeDtypeStruct((2, fields * layers * rows // BLOCK, BLOCK), F32)
    return (y_edge, y_edge, x_edges)


def deposit(halo, cells, seen, motion, radius, temp, grid):
    layers, rows, cols = grid
    fields, particles = seen.shape
    tall = -(-2 * layers * rows // (8 * BLOCK)) * 8
    vmem = pl.BlockSpec(memory_space=VMEM)
    return pl.pallas_call(
        functools.partial(deposit_kernel, chunk=1024),
        out_shape=(
            jax.ShapeDtypeStruct((8, particles), F32),
            jax.ShapeDtypeStruct((fields,) + grid, F32),
        ) + edge_shapes(fields, layers, rows, cols),
        in_specs=[vmem] * 8,
        out_specs=(vmem,) * 5,
        scratch_shapes=[
            VMEM((fields, tall, BLOCK), F32),
            VMEM((layers * rows, cols), F32),
            VMEM((fields * layers * rows // 2, 2 * cols), F32),
        ],
        compiler_params=pltpu.CompilerParams(vmem_limit_bytes=40 << 20),
        cost_estimate=pl.CostEstimate(
            flops=4 * fields * layers * rows * cols * particles, bytes_accessed=2 << 20, transcendentals=0
        ),
        name="deposit_fields",
    )(*halo, cells, seen, motion, radius, temp)


def heat_kernel(
    back_ref, slot_ref, cell_ref, radius_ref, base_ref, ey0_ref, ey1_ref, ex_ref,
    next_ref, dep_ref, dy0_ref, dy1_ref, dx_ref,
    table, acc, rows_scratch, *, chunk, rows
):
    devices, tall, _ = back_ref.shape
    layers = tall // 8
    particles = slot_ref.shape[1]
    half, wide = acc.shape
    for o in range(devices):
        for q in range(layers):
            table[o * layers + q : o * layers + q + 1, :] = back_ref[o, 8 * q + 6 : 8 * q + 7, :]
    acc[...] = jnp.zeros_like(acc)

    def step(i, _):
        here = pl.ds(pl.multiple_of(i * chunk, chunk), chunk)
        slots = slot_ref[:, here]
        gained = []
        for s in range(chunk // BLOCK):
            wanted = jnp.broadcast_to(slots[:, s * BLOCK : (s + 1) * BLOCK], (8, BLOCK))
            tiles = [table[8 * g : 8 * g + 8, :] for g in range(devices * layers // 8)]
            gained.append(gathered([tiles], wanted // BLOCK, wanted % BLOCK)[0])
        base = base_ref[6:8, here]
        total = base[0:1] + jnp.concatenate(gained, axis=1)
        next_ref[:, here] = total
        radius = radius_ref[:, here]
        high, low = split(radius * radius * radius * (total - base[1:2]))
        cells = cell_ref[:, here]
        hot_low = hot_columns(wide, cells % wide)
        hot_high = hot(half, cells // wide)
        added = lax.dot_general(hot_high * high, hot_low, NN, preferred_element_type=F32)
        acc[...] += added + lax.dot_general(hot_high * low, hot_low, NN, preferred_element_type=F32)
        return 0

    lax.fori_loop(0, particles // chunk, step, 0, unroll=2)
    field = paired_rows(acc[...], 2 * half // rows, rows, rows_scratch)
    dep_ref[0] = field
    for edge, out in ((ey0_ref, dy0_ref), (ey1_ref, dy1_ref)):
        out[0 : edge.shape[0]] = edge[...]
    dx_ref[:, 0 : ex_ref.shape[1], :] = ex_ref[...]
    write_edges(field, ey0_ref.shape[0], dy0_ref, dy1_ref, dx_ref)


def heat_deposit(back, slot_of, cells, radius, base, edges, grid):
    devices = back.shape[0]
    layers, rows, cols = grid
    particles = cells.shape[1]
    half = layers * rows // 2
    fields = edges[0].shape[0] + 1
    vmem = pl.BlockSpec(memory_space=VMEM)
    return pl.pallas_call(
        functools.partial(heat_kernel, chunk=1024, rows=rows),
        out_shape=(
            jax.ShapeDtypeStruct((1, particles), F32),
            jax.ShapeDtypeStruct((1,) + grid, F32),
        ) + edge_shapes(fields, layers, rows, cols),
        in_specs=[vmem] * 8,
        out_specs=(vmem,) * 5,
        scratch_shapes=[
            VMEM((devices * back.shape[1] // 8, BLOCK), F32),
            VMEM((half, 2 * cols), F32),
            VMEM((layers * rows, cols), F32),
        ],
        compiler_params=pltpu.CompilerParams(vmem_limit_bytes=40 << 20),
        cost_estimate=pl.CostEstimate(
            flops=4 * half * 2 * cols * particles, bytes_accessed=1 << 20, transcendentals=0
        ),
        name="heat_deposit",
    )(back, slot_of, cells, radius, base, *edges)


def fetch_kernel(
    owner_ref, tile_ref, back_ref, box_ref, spot_ref, base_ref, warm_ref, next_ref, box_of, table
):
    devices, tall, _ = back_ref.shape
    layers = tall // 8
    particles = box_ref.shape[1]
    invert(owner_ref, box_of)
    for o in range(devices):
        for q in range(layers):
            high, low = split(back_ref[o, 8 * q : 8 * q + 8, :])
            table[o, q] = jnp.concatenate([high, low], axis=0)
        for q in range(layers, layers + 3):
            table[o, q] = jnp.zeros((16, BLOCK), BF16)

    def gained_of(w, c):
        here = pl.ds(pl.multiple_of(c * CHUNK, CHUNK), CHUNK)
        boxes = jnp.broadcast_to(box_ref[:, here], (8, CHUNK))
        tile = [tile_ref[c, box_of[o]] + 2 * w for o in range(devices)]
        wanted = jnp.concatenate(
            [jnp.concatenate([table[o, tile[o]], table[o, tile[o] + 1]], axis=1) for o in range(devices)], axis=0
        )
        hot_spot = hot(WINDOW, spot_ref[:, here] - WINDOW * w)
        found = lax.dot_general(wanted, hot_spot, NN, preferred_element_type=F32)
        gained = jnp.zeros((8, CHUNK), F32)
        for o in range(devices):
            value = found[16 * o : 16 * o + 8] + found[16 * o + 8 : 16 * o + 16]
            gained = jnp.where(boxes == box_of[o], value, gained)
        return here, gained

    def step(c, _):
        here, gained = gained_of(0, c)
        next_ref[:, here] = jnp.concatenate(
            [base_ref[0:6, here] + gained[0:6], warm_ref[:, here]], axis=0
        )
        return 0

    chunks = particles // CHUNK
    lax.fori_loop(0, chunks, step, 0, unroll=2)

    def later(w, _):
        def again(c, _):
            here, gained = gained_of(w, c)
            next_ref[0:6, here] += gained[0:6]
            return 0

        return lax.fori_loop(0, chunks, again, 0)

    lax.fori_loop(1, tile_ref[tile_ref.shape[0] - 8, 0], later, 0)


def fetch(box_owner, tiles, back, boxes, spots, base, warm):
    devices, tall, _ = back.shape
    layers = tall // 8
    particles = boxes.shape[1]
    vmem = pl.BlockSpec(memory_space=VMEM)
    smem = pl.BlockSpec(memory_space=pltpu.SMEM)
    return pl.pallas_call(
        fetch_kernel,
        out_shape=jax.ShapeDtypeStruct((7, particles), F32),
        in_specs=[smem, smem] + [vmem] * 5,
        out_specs=vmem,
        scratch_shapes=[
            pltpu.SMEM((devices,), jnp.int32),
            VMEM((devices, layers + 3, 16, BLOCK), BF16),
        ],
        compiler_params=pltpu.CompilerParams(vmem_limit_bytes=40 << 20),
        cost_estimate=pl.CostEstimate(
            flops=32 * devices * WINDOW * particles, bytes_accessed=1 << 20, transcendentals=0
        ),
        name="fetch_slots",
    )(box_owner, tiles, back, boxes, spots, base, warm)


def spread_kernel(dep_ref, heat_ref, y0_ref, y1_ref, x_ref, fluid_ref, next_ref, void_ref):
    halo = (y0_ref, y1_ref) + x_beside(x_ref)
    crowding = 1.0 + COUPLING * smooth_field(dep_ref, *halo, 0)
    void_ref[...] = 1.0 / crowding
    for k in range(3):
        next_ref[k] = fluid_ref[k] + TIME_STEP * COUPLING * smooth_field(dep_ref, *halo, k + 1) * crowding
    warmth = smooth_field(heat_ref, *halo, 0, 4)
    next_ref[3] = fluid_ref[3] + TIME_STEP * COUPLING * warmth * crowding


def spread(dep, heat, halo, fluid):
    vmem = pl.BlockSpec(memory_space=VMEM)
    return pl.pallas_call(
        spread_kernel,
        out_shape=(jax.ShapeDtypeStruct(fluid.shape, F32), jax.ShapeDtypeStruct(fluid.shape[1:], F32)),
        in_specs=[vmem] * 6,
        out_specs=(vmem,) * 2,
        compiler_params=pltpu.CompilerParams(vmem_limit_bytes=40 << 20),
        cost_estimate=pl.CostEstimate(flops=20 * fluid.size, bytes_accessed=2 << 20, transcendentals=0),
        name="spread_fields",
    )(dep, heat, *halo, fluid)


def halo_of(y_first, y_last, x_edges):
    def moved(value, axis, step):
        size = lax.axis_size(axis)
        pairs = [(i, i + step) for i in range(size) if 0 <= i + step < size]
        return lax.ppermute(value, axis, pairs)

    return (
        moved(y_last, "gy", 1),
        moved(y_first, "gy", -1),
        lax.all_gather(x_edges, "gx"),
    )


def shards(
    fluid_state, particle_pos, particle_motion, particle_radius, particle_temp,
    particle_cell, particle_box, box_owner, contact_mask,
):
    devices = lax.axis_size(("gx", "gy"))
    particles = particle_pos.shape[1]
    slots = 2 * particles // devices
    fields, layers, rows, cols = fluid_state.shape
    boxes = particle_box.reshape(1, particles)
    radius = particle_radius.reshape(1, particles)
    temp = particle_temp.reshape(1, particles)
    cells = particle_cell.reshape(1, particles)

    outgoing, slot_of, spots, tiles = place(
        box_owner, boxes, particle_pos, particle_motion, radius, temp, slots
    )
    arrived = lax.all_to_all(outgoing, ("gx", "gy"), split_axis=0, concat_axis=0, tiled=True)

    spots, fluid = lax.optimization_barrier((spots, fluid_state))
    fluid_halo = halo_of(
        fluid[:, :, 0, :],
        fluid[:, :, rows - 1, :],
        jnp.stack([fluid[:, :, :, 0].reshape(-1, BLOCK), fluid[:, :, :, cols - 1].reshape(-1, BLOCK)]),
    )
    seen = look_up(fluid, cells)
    arrived, seen = lax.optimization_barrier((arrived, seen))
    result = contact(arrived, contact_mask)

    result, *fluid_halo = lax.optimization_barrier((result,) + tuple(fluid_halo))
    base, deposits, *edges = deposit(
        fluid_halo, cells, seen, particle_motion, radius, temp, (layers, rows, cols)
    )
    back = lax.all_to_all(result, ("gx", "gy"), split_axis=0, concat_axis=0, tiled=True)
    warm, heat_field, *edges = heat_deposit(
        back, slot_of, cells, radius, base, edges, (layers, rows, cols)
    )
    halo = halo_of(*edges)
    particle_next = fetch(box_owner, tiles, back, boxes, spots, base, warm)
    fluid_next, void_fraction = spread(deposits, heat_field, halo, fluid_state)
    return (fluid_next, void_fraction, particle_next)


def solution(mesh):
    in_specs = (
        P(None, None, "gy", "gx"),
        P(None, ("gx", "gy")),
        P(None, ("gx", "gy")),
        P(("gx", "gy")),
        P(("gx", "gy")),
        P(("gx", "gy")),
        P(("gx", "gy"), None),
        P(),
        P(("gx", "gy"), None, None),
    )
    out_specs = (P(None, None, "gy", "gx"), P(None, "gy", "gx"), P(None, ("gx", "gy")))
    return jax.shard_map(shards, mesh=mesh, in_specs=in_specs, out_specs=out_specs, check_vma=False)
```

```python
import functools

import jax
import jax.numpy as jnp
from jax import lax
from jax.experimental import pallas as pl
from jax.experimental.pallas import tpu as pltpu
from jax.sharding import PartitionSpec as P

BLOCK = 128
TIME_STEP = 0.1
STIFFNESS = 0.5
DAMPING_RATE = 0.2
ROTATION_DRAG = 0.1
DRAG_COEFF = 4.0
CONDUCTION = 0.3
HEAT_TRANSFER = 4.0
GRAVITY = 0.3
COUPLING = 4.0
CENTRE_WEIGHT = 0.25
SIDE_WEIGHT = 0.125

F32 = jnp.float32
BF16 = jnp.bfloat16
VMEM = pltpu.VMEM
NN = (((1,), (0,)), ((), ()))
NT = (((1,), (1,)), ((), ()))


def split(value):
    high = value.astype(BF16)
    return high, (value - high.astype(F32)).astype(BF16)


def hot(count, row):
    places = lax.broadcasted_iota(jnp.int32, (count, row.shape[1]), 0)
    return jnp.where(places == row, 1.0, 0.0).astype(BF16)


def hot_columns(count, row):
    n = row.shape[1] // BLOCK
    tiles = [row[:, a * BLOCK : (a + 1) * BLOCK] for a in range(n)]
    turned = jnp.transpose(jnp.concatenate(tiles * (8 // n), axis=0).astype(F32))
    places = lax.broadcasted_iota(jnp.int32, (BLOCK, count), 1).astype(F32)
    return jnp.concatenate(
        [jnp.where(places == turned[:, a : a + 1], 1.0, 0.0).astype(BF16) for a in range(n)], axis=0
    )


def invert(owner_ref, box_of):
    def step(b, _):
        box_of[owner_ref[b]] = b
        return 0

    lax.fori_loop(0, owner_ref.shape[0], step, 0)


WINDOW = 256
CHUNK = 1024


def place_kernel(
    owner_ref, box_ref, pos_ref, motion_ref, radius_ref, temp_ref,
    out_ref, slot_ref, spot_ref, tile_ref,
    box_of, tile_of, acc, done
):
    devices, rows, _ = out_ref.shape
    layers = rows // 12
    slots = layers * BLOCK
    particles = box_ref.shape[1]
    sub = 256
    invert(owner_ref, box_of)
    acc[...] = jnp.zeros_like(acc)

    box_row = lax.broadcasted_iota(jnp.int32, (devices, 1), 0)
    owner_column = jnp.zeros((devices, 1), F32)
    for b in range(devices):
        owner_column = jnp.where(box_row == b, owner_ref[b].astype(F32), owner_column)
    above = (
        lax.broadcasted_iota(jnp.int32, (sub, sub), 0) < lax.broadcasted_iota(jnp.int32, (sub, sub), 1)
    )
    above = jnp.where(above, 1.0, 0.0).astype(BF16)
    lane = lax.broadcasted_iota(jnp.int32, (devices, BLOCK), 1)
    tiles = jnp.zeros((devices, BLOCK), F32)
    highest = jnp.zeros((1, sub), F32)
    carry = jnp.zeros((devices, 1), F32)
    per_chunk = CHUNK // sub
    for c in range(particles // CHUNK):
        chosen = []
        for s in range(per_chunk):
            at = c * CHUNK + s * sub
            chosen.append(
                lax.broadcasted_iota(jnp.int32, (devices, sub), 0) == box_ref[:, at : at + sub]
            )
        ones = [jnp.where(mine, 1.0, 0.0) for mine in chosen]
        earlier = lax.dot_general(
            jnp.concatenate(ones, axis=0).astype(BF16), above, NN, preferred_element_type=F32
        )
        tile = jnp.minimum(jnp.floor(carry * (1.0 / BLOCK)), layers - 1.0)
        tiles = jnp.where(lane == c, tile, tiles)
        for s in range(per_chunk):
            at = c * CHUNK + s * sub
            rank = earlier[s * devices : (s + 1) * devices] + carry
            spot = jnp.where(chosen[s], rank - BLOCK * tile, 0.0)
            spot = jnp.sum(spot, axis=0, keepdims=True)
            slot = jnp.where(chosen[s], rank + slots * owner_column, 0.0)
            slot = jnp.sum(slot, axis=0, keepdims=True)
            spot_ref[:, at : at + sub] = spot.astype(jnp.int32)
            slot_ref[:, at : at + sub] = slot.astype(jnp.int32)
            highest = jnp.maximum(highest, spot)
            carry = carry + jnp.sum(ones[s], axis=1, keepdims=True)
    if devices < BLOCK:
        tiles = jnp.concatenate([tiles, jnp.zeros((BLOCK - devices, BLOCK), F32)], axis=0)
    count = tile_ref.shape[0] - 8
    tile_ref[0:count, :] = jnp.transpose(tiles)[0:count].astype(jnp.int32)
    windows = jnp.floor(jnp.max(highest, axis=1, keepdims=True) * (1.0 / WINDOW)) + 1.0
    tile_ref[count : count + 8, :] = jnp.broadcast_to(windows, (8, BLOCK)).astype(jnp.int32)
    copy = pltpu.make_async_copy(tile_ref, tile_of, done)
    copy.start()
    copy.wait()

    def step(w, c, _):
        here = pl.ds(pl.multiple_of(c * CHUNK, CHUNK), CHUNK)
        boxes = box_ref[:, here]
        pos = pos_ref[:, here]
        motion = motion_ref[:, here]
        push = TIME_STEP * STIFFNESS * pos - TIME_STEP * DAMPING_RATE * motion[0:3]
        spin = -TIME_STEP * ROTATION_DRAG * motion[3:6]
        heat = -TIME_STEP * CONDUCTION * temp_ref[:, here]
        first = jnp.concatenate([push, spin, heat, jnp.ones((1, CHUNK), F32)], axis=0)
        second = jnp.concatenate([pos, radius_ref[:, here]], axis=0)
        first = jnp.concatenate(split(first), axis=0)
        second = jnp.concatenate(split(second) * 2, axis=0)
        lower = lax.broadcasted_iota(jnp.int32, (16, 1), 0) < 8
        box16 = jnp.broadcast_to(boxes, (16, CHUNK)).astype(F32).astype(BF16)
        first_parts = []
        second_parts = []
        for o in range(devices):
            mine = box16 == box_of[o].astype(F32).astype(BF16)
            first_parts.append(jnp.where(mine, first, jnp.zeros_like(first)))
            if o % 2 == 0:
                either = jnp.where(lower, box_of[o].astype(F32), box_of[o + 1].astype(F32)).astype(BF16)
                second_parts.append(jnp.where(box16 == either, second, jnp.zeros_like(second)))
        parts = jnp.concatenate(first_parts + second_parts, axis=0)

        hot_spot = hot(WINDOW, spot_ref[:, here] - WINDOW * w)
        placed = lax.dot_general(parts, hot_spot, NT, preferred_element_type=F32)
        for o in range(devices):
            tile = tile_of[c, box_of[o]] + 2 * w
            one = placed[16 * o : 16 * o + 8] + placed[16 * o + 8 : 16 * o + 16]
            two = placed[16 * devices + 8 * o : 16 * devices + 8 * o + 8]
            two = two + pltpu.roll(two, 4, 0)
            acc[o, tile, 0:8, :] += one[:, :BLOCK]
            acc[o, tile + 1, 0:8, :] += one[:, BLOCK:]
            acc[o, tile, 8:16, :] += two[:, :BLOCK]
            acc[o, tile + 1, 8:16, :] += two[:, BLOCK:]
        return 0

    chunks = particles // CHUNK
    lax.fori_loop(0, chunks, functools.partial(step, 0), 0, unroll=2)

    def later(w, _):
        return lax.fori_loop(0, chunks, functools.partial(step, w), 0)

    lax.fori_loop(1, tile_of[tile_ref.shape[0] - 8, 0], later, 0)

    def finish(o, _):
        for q in range(layers):
            out_ref[o, 8 * q : 8 * q + 8, :] = acc[o, q, 0:8, :]
            out_ref[o, 8 * layers + 4 * q : 8 * layers + 4 * q + 4, :] = acc[o, q, 8:12, :]
        return 0

    lax.fori_loop(0, devices, finish, 0)


def place(box_owner, boxes, pos, motion, radius, temp, slots):
    devices = box_owner.shape[0]
    particles = pos.shape[1]
    layers = slots // BLOCK
    vmem = pl.BlockSpec(memory_space=VMEM)
    row = jax.ShapeDtypeStruct((1, particles), jnp.int32)
    table = (-(-particles // (8 * CHUNK)) * 8 + 8, BLOCK)
    return pl.pallas_call(
        place_kernel,
        out_shape=(
            jax.ShapeDtypeStruct((devices, 12 * layers, BLOCK), F32), row, row,
            jax.ShapeDtypeStruct(table, jnp.int32),
        ),
        in_specs=[pl.BlockSpec(memory_space=pltpu.SMEM)] + [vmem] * 5,
        out_specs=(vmem,) * 4,
        scratch_shapes=[
            pltpu.SMEM((devices,), jnp.int32),
            pltpu.SMEM(table, jnp.int32),
            VMEM((devices, layers + 3, 16, BLOCK), F32),
            pltpu.SemaphoreType.DMA,
        ],
        compiler_params=pltpu.CompilerParams(vmem_limit_bytes=60 << 20),
        cost_estimate=pl.CostEstimate(
            flops=2 * 24 * devices * WINDOW * particles, bytes_accessed=1 << 20, transcendentals=0
        ),
        name="place_slots",
    )(box_owner, boxes, pos, motion, radius, temp)


def pair_terms(near):
    twice = jnp.concatenate([near, near], axis=0)
    high = twice.astype(BF16).astype(F32)
    low = (twice - high).astype(BF16).astype(F32)
    row = lax.broadcasted_iota(jnp.int32, (8, 1), 0)
    kept = high + low
    squares = kept * kept
    norm = -(squares[0:1] + squares[1:2] + squares[2:3])
    total = jnp.where(row < 3, norm, squares[3:4] + 0.5)
    one = total.astype(BF16).astype(F32)
    rest = total - one
    two = rest.astype(BF16).astype(F32)
    three = (rest - two).astype(BF16).astype(F32)
    third = jnp.where((row == 0) | (row == 3), one, jnp.where((row == 1) | (row == 4), two, three))
    third = jnp.where(row < 6, third, 0.0)
    crossed = 2.0 * jnp.where(row < 4, high, low)
    is_radius = (row == 3) | (row == 7)
    cross_d = jnp.where(is_radius, 0.0, crossed)
    cross_r = jnp.where(is_radius, crossed, 0.0)
    ones = jnp.ones_like(third)
    left = jnp.concatenate([high, low, third, jnp.where(row < 6, ones, 0.0)], axis=0)
    ones_d = jnp.where(row < 3, ones, 0.0)
    ones_r = jnp.where((row >= 3) & (row < 6), ones, 0.0)
    for_d = jnp.concatenate([cross_d, cross_d, ones_d, jnp.where(row < 3, third, 0.0)], axis=0)
    for_r = jnp.concatenate([cross_r, cross_r, ones_r, jnp.where((row >= 3) & (row < 6), third, 0.0)], axis=0)
    right = jnp.concatenate([for_d, for_r], axis=1)
    return left, right.astype(BF16)


def contact_kernel(slot_ref, mask_ref, out_ref):
    homes, rows, _ = slot_ref.shape
    layers = rows // 12
    blocks = [(s, q) for s in range(homes) for q in range(layers)]
    row = lax.broadcasted_iota(jnp.int32, (8, 1), 0)
    sign = jnp.where((row >= 3) & (row < 6), 1.0, -1.0)
    lane = lax.broadcasted_iota(jnp.int32, (BLOCK, BLOCK), 1) // 16

    def pairs_of(group):
        pairs = []
        for first in range(0, 8, 4):
            lefts = []
            rights = []
            for g, (s, q) in enumerate(group[first : first + 4]):
                left, right = pair_terms(slot_ref[s, 8 * layers + 4 * q : 8 * layers + 4 * q + 4, :])
                lefts.append(left)
                spots = [jnp.zeros_like(right)] * 4
                spots[g] = right
                rights.append(jnp.concatenate(spots, axis=0))
            turned = jnp.transpose(jnp.concatenate(lefts, axis=0)).astype(BF16)
            pairs.append(
                lax.dot_general(turned, jnp.concatenate(rights, axis=1), NN, preferred_element_type=F32)
            )
        return pairs

    def sums_of(number, group, pairs):
        stacked = []
        for s, q in group:
            mine = slot_ref[s, 8 * q : 8 * q + 8, :]
            high = mine.astype(BF16).astype(F32)
            stacked += [high, mine - high]
        columns = jnp.transpose(jnp.concatenate(stacked, axis=0)).astype(BF16)
        highs = []
        lows = []
        right = []
        for b in range(8):
            at = 2 * BLOCK * (b % 4)
            pair = pairs[b // 4]
            reach = pair[:, at + BLOCK : at + 2 * BLOCK]
            inverse = pl.reciprocal(reach, approx=True)
            inverse = inverse * (2.0 - reach * inverse)
            weight = mask_ref[8 * number + b].astype(F32) * jnp.exp(pair[:, at : at + BLOCK] * inverse)
            high, low = split(weight)
            highs.append(high)
            lows.append(low)
            right.append(jnp.where(lane == b, columns, jnp.zeros_like(columns)))
        return lax.dot_general(
            jnp.concatenate(highs + lows, axis=1), jnp.concatenate(right + right, axis=0), NN,
            preferred_element_type=F32,
        )

    def finish(group, sums):
        sums = jnp.transpose(sums)
        for b, (s, q) in enumerate(group):
            total = sums[16 * b : 16 * b + 8] + sums[16 * b + 8 : 16 * b + 16]
            out_ref[s, 8 * q : 8 * q + 8, :] = slot_ref[s, 8 * q : 8 * q + 8, :] * total[7:8] + sign * total

    groups = [blocks[i : i + 8] for i in range(0, len(blocks), 8)]
    pairs = pairs_of(groups[0])
    before = None
    for number, group in enumerate(groups):
        later = pairs_of(groups[number + 1]) if number + 1 < len(groups) else None
        sums = sums_of(number, group, pairs)
        if before is not None:
            finish(*before)
        before = (group, sums)
        pairs = later
    finish(*before)


def contact(arrived, mask):
    devices, rows, _ = arrived.shape
    layers = rows // 12
    blocks = mask.shape[0]
    step = 32 // layers
    return pl.pallas_call(
        contact_kernel,
        grid=(devices // step,),
        out_shape=jax.ShapeDtypeStruct((devices, 8 * layers, BLOCK), F32),
        in_specs=[
            pl.BlockSpec((step, rows, BLOCK), lambda h: (h, 0, 0)),
            pl.BlockSpec((step * layers, BLOCK, BLOCK), lambda h: (h, 0, 0)),
        ],
        out_specs=pl.BlockSpec((step, 8 * layers, BLOCK), lambda h: (h, 0, 0)),
        compiler_params=pltpu.CompilerParams(vmem_limit_bytes=32 << 20),
        cost_estimate=pl.CostEstimate(
            flops=64 * blocks * BLOCK * BLOCK, bytes_accessed=blocks * BLOCK * BLOCK * 4, transcendentals=0
        ),
        name="contact_blocks",
    )(arrived, mask)


def smoothed(centre, y_first, y_last, x_first, x_last):
    layers, rows, cols = centre.shape
    zero = jnp.zeros((1, rows, cols), F32)
    up = jnp.concatenate([centre[1:], zero], axis=0)
    down = jnp.concatenate([zero, centre[:-1]], axis=0)
    row = lax.broadcasted_iota(jnp.int32, (1, rows, cols), 1)
    col = lax.broadcasted_iota(jnp.int32, (1, rows, cols), 2)
    back = jnp.where(row == 0, y_first, pltpu.roll(centre, 1, 1))
    front = jnp.where(row == rows - 1, y_last, pltpu.roll(centre, rows - 1, 1))
    left = jnp.where(col == 0, x_first, pltpu.roll(centre, 1, 2))
    right = jnp.where(col == cols - 1, x_last, pltpu.roll(centre, cols - 1, 2))
    return CENTRE_WEIGHT * centre + SIDE_WEIGHT * ((up + down) + (back + front) + (left + right))


def columns(edge, layers, rows):
    count = edge.shape[0]
    if count < 8:
        edge = jnp.concatenate([edge] * (8 // count), axis=0)
    turned = jnp.transpose(edge)
    parts = [turned[:, a : a + 1] for a in range(count)]
    return jnp.concatenate(parts, axis=0).reshape(layers, rows, 1)


def smooth_field(field_ref, y0_ref, y1_ref, x0_ref, x1_ref, k, edge=None):
    at = k if edge is None else edge
    _, layers, rows, cols = field_ref.shape
    per = layers * rows // BLOCK
    x0 = columns(x0_ref[at * per : (at + 1) * per, :], layers, rows)
    x1 = columns(x1_ref[at * per : (at + 1) * per, :], layers, rows)
    y0 = y0_ref[at].reshape(layers, 1, cols)
    y1 = y1_ref[at].reshape(layers, 1, cols)
    return smoothed(field_ref[k], y0, y1, x0, x1)


def write_edges(field, k, y0_ref, y1_ref, x0_ref, x1_ref):
    layers, rows, cols = field.shape
    y0_ref[k] = field[:, 0, :]
    y1_ref[k] = field[:, rows - 1, :]
    flat = field.reshape(layers * rows, cols)
    for a in range(layers * rows // BLOCK):
        turned = jnp.transpose(flat[a * BLOCK : (a + 1) * BLOCK, :])
        at = k * (layers * rows // BLOCK) + a
        x0_ref[at : at + 1, :] = turned[0:1, :]
        x1_ref[at : at + 1, :] = turned[cols - 1 : cols, :]


def paired_rows(pairs, layers, rows, scratch):
    half = pairs.shape[0]
    cols = pairs.shape[1] // 2
    scratch[pl.ds(0, half, stride=2), :] = pairs[:, :cols]
    scratch[pl.ds(1, half, stride=2), :] = pairs[:, cols:]
    return scratch[...].reshape(layers, rows, cols)


def gathered(tables, rows, lanes):
    group = rows // 8
    found = [None] * len(tables)
    for g in range(len(tables[0])):
        mine = group == g
        for k, table in enumerate(tables):
            value = jnp.take_along_axis(table[g], lanes, axis=1, mode="promise_in_bounds")
            found[k] = value if g == 0 else jnp.where(mine, value, found[k])
    mine = lax.broadcasted_iota(jnp.int32, (8, BLOCK), 0) == rows % 8
    return [jnp.sum(jnp.where(mine, value, 0.0), axis=0, keepdims=True) for value in found]


def look_kernel(fluid_ref, cell_ref, mask_ref, seen_ref, mask_out, table, rows_scratch, done, *, chunk):
    copy = pltpu.make_async_copy(mask_ref, mask_out, done)
    copy.start()
    fields, layers, rows, cols = fluid_ref.shape
    particles = cell_ref.shape[1]
    half = layers * rows // 2
    wide = 2 * cols
    for k in range(fields):
        rows_scratch[...] = smoothed(fluid_ref[k], 0.0, 0.0, 0.0, 0.0).reshape(layers * rows, cols)
        here = slice(k * half, (k + 1) * half)
        for part in range(2):
            high, low = split(rows_scratch[pl.ds(part, half, stride=2), :])
            table[here, part * cols : (part + 1) * cols] = high
            table[here, wide + part * cols : wide + (part + 1) * cols] = low

    def step(i, _):
        here = pl.ds(pl.multiple_of(i * chunk, chunk), chunk)
        cells = cell_ref[:, here]
        hot_low = hot(wide, cells % wide)
        found = lax.dot_general(
            table[...], jnp.concatenate([hot_low, hot_low], axis=0), NN, preferred_element_type=F32
        )
        mine = lax.broadcasted_iota(jnp.int32, (half, chunk), 0) == cells // wide
        seen = [
            jnp.sum(jnp.where(mine, found[k * half : (k + 1) * half], 0.0), axis=0, keepdims=True)
            for k in range(fields)
        ]
        seen_ref[:, here] = jnp.concatenate(seen, axis=0)
        return 0

    lax.fori_loop(0, particles // chunk, step, 0, unroll=2)
    copy.wait()


def look_up(fluid, cells, mask):
    fields, layers, rows, cols = fluid.shape
    particles = cells.shape[1]
    vmem = pl.BlockSpec(memory_space=VMEM)
    anywhere = pl.BlockSpec(memory_space=pl.ANY)
    return pl.pallas_call(
        functools.partial(look_kernel, chunk=512),
        out_shape=(
            jax.ShapeDtypeStruct((fields, particles), F32),
            jax.ShapeDtypeStruct(mask.shape, mask.dtype),
        ),
        in_specs=[vmem, vmem, anywhere],
        out_specs=(vmem, anywhere),
        scratch_shapes=[
            VMEM((fields * layers * rows // 2, 4 * cols), BF16),
            VMEM((layers * rows, cols), F32),
            pltpu.SemaphoreType.DMA,
        ],
        compiler_params=pltpu.CompilerParams(vmem_limit_bytes=32 << 20),
        cost_estimate=pl.CostEstimate(
            flops=8 * fields * layers * rows * cols * particles // 4, bytes_accessed=1 << 20, transcendentals=0
        ),
        name="look_up",
    )(fluid, cells, mask)


def deposit_kernel(
    y0_ref, y1_ref, x0_ref, x1_ref, cell_ref, seen_ref, motion_ref, radius_ref, temp_ref,
    base_ref, dep_ref, dy0_ref, dy1_ref, dx0_ref, dx1_ref, x_table, rows_scratch, acc, *, chunk
):
    fields, layers, rows, cols = dep_ref.shape
    half = layers * rows // 2
    wide = 2 * cols
    particles = cell_ref.shape[1]
    per = layers * rows // BLOCK
    for k in range(fields):
        x_table[k] = jnp.zeros_like(x_table[k])
        x_table[k, 0:per, :] = x0_ref[k * per : (k + 1) * per, :]
        x_table[k, per : 2 * per, :] = x1_ref[k * per : (k + 1) * per, :]
    acc[...] = jnp.zeros_like(acc)

    def step(i, _):
        here = pl.ds(pl.multiple_of(i * chunk, chunk), chunk)
        cells = cell_ref[:, here]
        beside = [[] for _ in range(fields)]
        for s in range(chunk // BLOCK):
            cell = jnp.broadcast_to(cells[:, s * BLOCK : (s + 1) * BLOCK], (8, BLOCK))
            high = cell // cols
            low = cell % cols
            y = high % rows
            from_y = gathered(
                [
                    [ref[k, 8 * g : 8 * g + 8, :] for ref in (y0_ref, y1_ref) for g in range(layers // 8)]
                    for k in range(fields)
                ],
                high // rows + jnp.where(y == 0, 0, layers),
                low,
            )
            from_x = gathered(
                [[x_table[k, 8 * g : 8 * g + 8, :] for g in range(x_table.shape[1] // 8)] for k in range(fields)],
                high // BLOCK + jnp.where(low == 0, 0, per),
                high % BLOCK,
            )
            on_y = (y[0:1] == 0) | (y[0:1] == rows - 1)
            on_x = (low[0:1] == 0) | (low[0:1] == cols - 1)
            for k in range(fields):
                beside[k].append(jnp.where(on_y, from_y[k], 0.0) + jnp.where(on_x, from_x[k], 0.0))
        beside = jnp.concatenate([jnp.concatenate(parts, axis=1) for parts in beside], axis=0)
        seen = seen_ref[:, here] + SIDE_WEIGHT * beside
        motion = motion_ref[:, here]
        radius = radius_ref[:, here]
        temp = temp_ref[:, here]
        drag = DRAG_COEFF / (radius * radius + 0.25) * (seen[0:3] - motion[0:3])
        upward = lax.broadcasted_iota(jnp.int32, (3, 1), 0) == 2
        moved = motion[0:3] + TIME_STEP * drag - jnp.where(upward, TIME_STEP * GRAVITY, 0.0)
        warmed = temp + TIME_STEP * HEAT_TRANSFER * (seen[3:4] - temp)
        base_ref[:, here] = jnp.concatenate([moved, motion[3:6], warmed, seen[3:4]], axis=0)
        volume = radius * radius * radius
        high, low = split(jnp.concatenate([volume, -volume * drag], axis=0))
        hot_low = hot(wide, cells % wide)
        hot_high = hot(half, cells // wide)
        parts = [hot_high * piece[k : k + 1] for piece in (high, low) for k in range(fields)]
        total = lax.dot_general(jnp.concatenate(parts, axis=0), hot_low, NT, preferred_element_type=F32)
        acc[...] += total[: fields * half] + total[fields * half :]
        return 0

    lax.fori_loop(0, particles // chunk, step, 0)
    for k in range(fields):
        field = paired_rows(acc[k * half : (k + 1) * half, :], layers, rows, rows_scratch)
        dep_ref[k] = field
        write_edges(field, k, dy0_ref, dy1_ref, dx0_ref, dx1_ref)


def edge_shapes(fields, layers, rows, cols):
    y_edge = jax.ShapeDtypeStruct((fields, layers, cols), F32)
    x_edge = jax.ShapeDtypeStruct((fields * layers * rows // BLOCK, BLOCK), F32)
    return (y_edge, y_edge, x_edge, x_edge)


def deposit(halo, cells, seen, motion, radius, temp, grid):
    layers, rows, cols = grid
    fields, particles = seen.shape
    tall = -(-2 * layers * rows // (8 * BLOCK)) * 8
    vmem = pl.BlockSpec(memory_space=VMEM)
    return pl.pallas_call(
        functools.partial(deposit_kernel, chunk=1024),
        out_shape=(
            jax.ShapeDtypeStruct((8, particles), F32),
            jax.ShapeDtypeStruct((fields,) + grid, F32),
        ) + edge_shapes(fields, layers, rows, cols),
        in_specs=[vmem] * 9,
        out_specs=(vmem,) * 6,
        scratch_shapes=[
            VMEM((fields, tall, BLOCK), F32),
            VMEM((layers * rows, cols), F32),
            VMEM((fields * layers * rows // 2, 2 * cols), F32),
        ],
        compiler_params=pltpu.CompilerParams(vmem_limit_bytes=40 << 20),
        cost_estimate=pl.CostEstimate(
            flops=4 * fields * layers * rows * cols * particles, bytes_accessed=2 << 20, transcendentals=0
        ),
        name="deposit_fields",
    )(*halo, cells, seen, motion, radius, temp)


def heat_kernel(
    back_ref, slot_ref, cell_ref, radius_ref, base_ref, ey0_ref, ey1_ref, ex0_ref, ex1_ref,
    next_ref, dep_ref, dy0_ref, dy1_ref, dx0_ref, dx1_ref,
    table, acc, rows_scratch, *, chunk, rows
):
    devices, tall, _ = back_ref.shape
    layers = tall // 8
    particles = slot_ref.shape[1]
    half, wide = acc.shape
    for o in range(devices):
        for q in range(layers):
            table[o * layers + q : o * layers + q + 1, :] = back_ref[o, 8 * q + 6 : 8 * q + 7, :]
    acc[...] = jnp.zeros_like(acc)

    def step(i, _):
        here = pl.ds(pl.multiple_of(i * chunk, chunk), chunk)
        slots = slot_ref[:, here]
        gained = []
        for s in range(chunk // BLOCK):
            wanted = jnp.broadcast_to(slots[:, s * BLOCK : (s + 1) * BLOCK], (8, BLOCK))
            tiles = [table[8 * g : 8 * g + 8, :] for g in range(devices * layers // 8)]
            gained.append(gathered([tiles], wanted // BLOCK, wanted % BLOCK)[0])
        base = base_ref[6:8, here]
        total = base[0:1] + jnp.concatenate(gained, axis=1)
        next_ref[:, here] = total
        radius = radius_ref[:, here]
        high, low = split(radius * radius * radius * (total - base[1:2]))
        cells = cell_ref[:, here]
        hot_low = hot_columns(wide, cells % wide)
        hot_high = hot(half, cells // wide)
        added = lax.dot_general(hot_high * high, hot_low, NN, preferred_element_type=F32)
        acc[...] += added + lax.dot_general(hot_high * low, hot_low, NN, preferred_element_type=F32)
        return 0

    lax.fori_loop(0, particles // chunk, step, 0, unroll=2)
    field = paired_rows(acc[...], 2 * half // rows, rows, rows_scratch)
    dep_ref[0] = field
    for edge, out in ((ey0_ref, dy0_ref), (ey1_ref, dy1_ref), (ex0_ref, dx0_ref), (ex1_ref, dx1_ref)):
        out[0 : edge.shape[0]] = edge[...]
    write_edges(field, ey0_ref.shape[0], dy0_ref, dy1_ref, dx0_ref, dx1_ref)


def heat_deposit(back, slot_of, cells, radius, base, edges, grid):
    devices = back.shape[0]
    layers, rows, cols = grid
    particles = cells.shape[1]
    half = layers * rows // 2
    fields = edges[0].shape[0] + 1
    vmem = pl.BlockSpec(memory_space=VMEM)
    return pl.pallas_call(
        functools.partial(heat_kernel, chunk=1024, rows=rows),
        out_shape=(
            jax.ShapeDtypeStruct((1, particles), F32),
            jax.ShapeDtypeStruct((1,) + grid, F32),
        ) + edge_shapes(fields, layers, rows, cols),
        in_specs=[vmem] * 9,
        out_specs=(vmem,) * 6,
        scratch_shapes=[
            VMEM((devices * back.shape[1] // 8, BLOCK), F32),
            VMEM((half, 2 * cols), F32),
            VMEM((layers * rows, cols), F32),
        ],
        compiler_params=pltpu.CompilerParams(vmem_limit_bytes=40 << 20),
        cost_estimate=pl.CostEstimate(
            flops=4 * half * 2 * cols * particles, bytes_accessed=1 << 20, transcendentals=0
        ),
        name="heat_deposit",
    )(back, slot_of, cells, radius, base, *edges)


def fetch_kernel(
    owner_ref, tile_ref, back_ref, box_ref, spot_ref, base_ref, warm_ref, next_ref, box_of, table
):
    devices, tall, _ = back_ref.shape
    layers = tall // 8
    particles = box_ref.shape[1]
    invert(owner_ref, box_of)
    for o in range(devices):
        for q in range(layers):
            high, low = split(back_ref[o, 8 * q : 8 * q + 8, :])
            table[o, q] = jnp.concatenate([high, low], axis=0)
        for q in range(layers, layers + 3):
            table[o, q] = jnp.zeros((16, BLOCK), BF16)

    def gained_of(w, c):
        here = pl.ds(pl.multiple_of(c * CHUNK, CHUNK), CHUNK)
        boxes = jnp.broadcast_to(box_ref[:, here], (8, CHUNK))
        tile = [tile_ref[c, box_of[o]] + 2 * w for o in range(devices)]
        wanted = jnp.concatenate(
            [jnp.concatenate([table[o, tile[o]], table[o, tile[o] + 1]], axis=1) for o in range(devices)], axis=0
        )
        hot_spot = hot(WINDOW, spot_ref[:, here] - WINDOW * w)
        found = lax.dot_general(wanted, hot_spot, NN, preferred_element_type=F32)
        gained = jnp.zeros((8, CHUNK), F32)
        for o in range(devices):
            value = found[16 * o : 16 * o + 8] + found[16 * o + 8 : 16 * o + 16]
            gained = jnp.where(boxes == box_of[o], value, gained)
        return here, gained

    def step(c, _):
        here, gained = gained_of(0, c)
        next_ref[:, here] = jnp.concatenate(
            [base_ref[0:6, here] + gained[0:6], warm_ref[:, here]], axis=0
        )
        return 0

    chunks = particles // CHUNK
    lax.fori_loop(0, chunks, step, 0, unroll=2)

    def later(w, _):
        def again(c, _):
            here, gained = gained_of(w, c)
            next_ref[0:6, here] += gained[0:6]
            return 0

        return lax.fori_loop(0, chunks, again, 0)

    lax.fori_loop(1, tile_ref[tile_ref.shape[0] - 8, 0], later, 0)


def fetch(box_owner, tiles, back, boxes, spots, base, warm):
    devices, tall, _ = back.shape
    layers = tall // 8
    particles = boxes.shape[1]
    vmem = pl.BlockSpec(memory_space=VMEM)
    smem = pl.BlockSpec(memory_space=pltpu.SMEM)
    return pl.pallas_call(
        fetch_kernel,
        out_shape=jax.ShapeDtypeStruct((7, particles), F32),
        in_specs=[smem, smem] + [vmem] * 5,
        out_specs=vmem,
        scratch_shapes=[
            pltpu.SMEM((devices,), jnp.int32),
            VMEM((devices, layers + 3, 16, BLOCK), BF16),
        ],
        compiler_params=pltpu.CompilerParams(vmem_limit_bytes=40 << 20),
        cost_estimate=pl.CostEstimate(
            flops=32 * devices * WINDOW * particles, bytes_accessed=1 << 20, transcendentals=0
        ),
        name="fetch_slots",
    )(box_owner, tiles, back, boxes, spots, base, warm)


def spread_kernel(dep_ref, heat_ref, y0_ref, y1_ref, x0_ref, x1_ref, fluid_ref, next_ref, void_ref):
    halo = (y0_ref, y1_ref, x0_ref, x1_ref)
    crowding = 1.0 + COUPLING * smooth_field(dep_ref, *halo, 0)
    void_ref[...] = 1.0 / crowding
    for k in range(3):
        next_ref[k] = fluid_ref[k] + TIME_STEP * COUPLING * smooth_field(dep_ref, *halo, k + 1) * crowding
    warmth = smooth_field(heat_ref, *halo, 0, 4)
    next_ref[3] = fluid_ref[3] + TIME_STEP * COUPLING * warmth * crowding


def spread(dep, heat, halo, fluid):
    vmem = pl.BlockSpec(memory_space=VMEM)
    return pl.pallas_call(
        spread_kernel,
        out_shape=(jax.ShapeDtypeStruct(fluid.shape, F32), jax.ShapeDtypeStruct(fluid.shape[1:], F32)),
        in_specs=[vmem] * 7,
        out_specs=(vmem,) * 2,
        compiler_params=pltpu.CompilerParams(vmem_limit_bytes=40 << 20),
        cost_estimate=pl.CostEstimate(flops=20 * fluid.size, bytes_accessed=2 << 20, transcendentals=0),
        name="spread_fields",
    )(dep, heat, *halo, fluid)


def halo_of(y_first, y_last, x_first, x_last):
    def moved(value, axis, step):
        size = lax.axis_size(axis)
        pairs = [(i, i + step) for i in range(size) if 0 <= i + step < size]
        return lax.ppermute(value, axis, pairs)

    return (
        moved(y_last, "gy", 1),
        moved(y_first, "gy", -1),
        moved(x_last, "gx", 1),
        moved(x_first, "gx", -1),
    )


def shards(
    fluid_state, particle_pos, particle_motion, particle_radius, particle_temp,
    particle_cell, particle_box, box_owner, contact_mask,
):
    devices = lax.axis_size(("gx", "gy"))
    particles = particle_pos.shape[1]
    slots = 2 * particles // devices
    fields, layers, rows, cols = fluid_state.shape
    boxes = particle_box.reshape(1, particles)
    radius = particle_radius.reshape(1, particles)
    temp = particle_temp.reshape(1, particles)
    cells = particle_cell.reshape(1, particles)

    outgoing, slot_of, spots, tiles = place(
        box_owner, boxes, particle_pos, particle_motion, radius, temp, slots
    )
    arrived = lax.all_to_all(outgoing, ("gx", "gy"), split_axis=0, concat_axis=0, tiled=True)

    spots, fluid = lax.optimization_barrier((spots, fluid_state))
    fluid_halo = halo_of(
        fluid[:, :, 0, :],
        fluid[:, :, rows - 1, :],
        fluid[:, :, :, 0].reshape(-1, BLOCK),
        fluid[:, :, :, cols - 1].reshape(-1, BLOCK),
    )
    seen, mask = look_up(fluid, cells, contact_mask)
    arrived, seen, mask = lax.optimization_barrier((arrived, seen, mask))
    result = contact(arrived, mask)

    result, *fluid_halo = lax.optimization_barrier((result,) + tuple(fluid_halo))
    base, deposits, *edges = deposit(
        fluid_halo, cells, seen, particle_motion, radius, temp, (layers, rows, cols)
    )
    back = lax.all_to_all(result, ("gx", "gy"), split_axis=0, concat_axis=0, tiled=True)
    warm, heat_field, *edges = heat_deposit(
        back, slot_of, cells, radius, base, edges, (layers, rows, cols)
    )
    halo = halo_of(*edges)
    particle_next = fetch(box_owner, tiles, back, boxes, spots, base, warm)
    fluid_next, void_fraction = spread(deposits, heat_field, halo, fluid_state)
    return (fluid_next, void_fraction, particle_next)


def solution(mesh):
    in_specs = (
        P(None, None, "gy", "gx"),
        P(None, ("gx", "gy")),
        P(None, ("gx", "gy")),
        P(("gx", "gy")),
        P(("gx", "gy")),
        P(("gx", "gy")),
        P(("gx", "gy"), None),
        P(),
        P(("gx", "gy"), None, None),
    )
    out_specs = (P(None, None, "gy", "gx"), P(None, "gy", "gx"), P(None, ("gx", "gy")))
    return jax.shard_map(shards, mesh=mesh, in_specs=in_specs, out_specs=out_specs, check_vma=False)
```

```python
import functools

import jax
import jax.numpy as jnp
from jax import lax
from jax.experimental import pallas as pl
from jax.experimental.pallas import tpu as pltpu
from jax.sharding import PartitionSpec as P

BLOCK = 128
TIME_STEP = 0.1
STIFFNESS = 0.5
DAMPING_RATE = 0.2
ROTATION_DRAG = 0.1
DRAG_COEFF = 4.0
CONDUCTION = 0.3
HEAT_TRANSFER = 4.0
GRAVITY = 0.3
COUPLING = 4.0
CENTRE_WEIGHT = 0.25
SIDE_WEIGHT = 0.125

F32 = jnp.float32
BF16 = jnp.bfloat16
VMEM = pltpu.VMEM
NN = (((1,), (0,)), ((), ()))
NT = (((1,), (1,)), ((), ()))


def split(value):
    high = value.astype(BF16)
    return high, (value - high.astype(F32)).astype(BF16)


def hot(count, row):
    places = lax.broadcasted_iota(jnp.int32, (count, row.shape[1]), 0)
    return jnp.where(places == row, 1.0, 0.0).astype(BF16)


def hot_columns(count, row):
    n = row.shape[1] // BLOCK
    tiles = [row[:, a * BLOCK : (a + 1) * BLOCK] for a in range(n)]
    turned = jnp.transpose(jnp.concatenate(tiles * (8 // n), axis=0).astype(F32))
    places = lax.broadcasted_iota(jnp.int32, (BLOCK, count), 1).astype(F32)
    return jnp.concatenate(
        [jnp.where(places == turned[:, a : a + 1], 1.0, 0.0).astype(BF16) for a in range(n)], axis=0
    )


def invert(owner_ref, box_of):
    def step(b, _):
        box_of[owner_ref[b]] = b
        return 0

    lax.fori_loop(0, owner_ref.shape[0], step, 0)


WINDOW = 256
CHUNK = 1024


def place_kernel(
    owner_ref, box_ref, pos_ref, motion_ref, radius_ref, temp_ref,
    out_ref, slot_ref, spot_ref, tile_ref,
    box_of, tile_of, acc, done
):
    devices, rows, _ = out_ref.shape
    layers = rows // 12
    slots = layers * BLOCK
    particles = box_ref.shape[1]
    sub = 256
    invert(owner_ref, box_of)
    acc[...] = jnp.zeros_like(acc)

    box_row = lax.broadcasted_iota(jnp.int32, (devices, 1), 0)
    owner_column = jnp.zeros((devices, 1), F32)
    for b in range(devices):
        owner_column = jnp.where(box_row == b, owner_ref[b].astype(F32), owner_column)
    above = (
        lax.broadcasted_iota(jnp.int32, (sub, sub), 0) < lax.broadcasted_iota(jnp.int32, (sub, sub), 1)
    )
    above = jnp.where(above, 1.0, 0.0).astype(BF16)
    lane = lax.broadcasted_iota(jnp.int32, (devices, BLOCK), 1)
    tiles = jnp.zeros((devices, BLOCK), F32)
    highest = jnp.zeros((1, sub), F32)
    carry = jnp.zeros((devices, 1), F32)
    per_chunk = CHUNK // sub
    for c in range(particles // CHUNK):
        chosen = []
        for s in range(per_chunk):
            at = c * CHUNK + s * sub
            chosen.append(
                lax.broadcasted_iota(jnp.int32, (devices, sub), 0) == box_ref[:, at : at + sub]
            )
        ones = [jnp.where(mine, 1.0, 0.0) for mine in chosen]
        earlier = lax.dot_general(
            jnp.concatenate(ones, axis=0).astype(BF16), above, NN, preferred_element_type=F32
        )
        tile = jnp.minimum(jnp.floor(carry * (1.0 / BLOCK)), layers - 1.0)
        tiles = jnp.where(lane == c, tile, tiles)
        for s in range(per_chunk):
            at = c * CHUNK + s * sub
            rank = earlier[s * devices : (s + 1) * devices] + carry
            spot = jnp.where(chosen[s], rank - BLOCK * tile, 0.0)
            spot = jnp.sum(spot, axis=0, keepdims=True)
            slot = jnp.where(chosen[s], rank + slots * owner_column, 0.0)
            slot = jnp.sum(slot, axis=0, keepdims=True)
            spot_ref[:, at : at + sub] = spot.astype(jnp.int32)
            slot_ref[:, at : at + sub] = slot.astype(jnp.int32)
            highest = jnp.maximum(highest, spot)
            carry = carry + jnp.sum(ones[s], axis=1, keepdims=True)
    if devices < BLOCK:
        tiles = jnp.concatenate([tiles, jnp.zeros((BLOCK - devices, BLOCK), F32)], axis=0)
    count = tile_ref.shape[0] - 8
    tile_ref[0:count, :] = jnp.transpose(tiles)[0:count].astype(jnp.int32)
    windows = jnp.floor(jnp.max(highest, axis=1, keepdims=True) * (1.0 / WINDOW)) + 1.0
    tile_ref[count : count + 8, :] = jnp.broadcast_to(windows, (8, BLOCK)).astype(jnp.int32)
    copy = pltpu.make_async_copy(tile_ref, tile_of, done)
    copy.start()
    copy.wait()

    def step(w, c, _):
        here = pl.ds(pl.multiple_of(c * CHUNK, CHUNK), CHUNK)
        boxes = box_ref[:, here]
        pos = pos_ref[:, here]
        motion = motion_ref[:, here]
        push = TIME_STEP * STIFFNESS * pos - TIME_STEP * DAMPING_RATE * motion[0:3]
        spin = -TIME_STEP * ROTATION_DRAG * motion[3:6]
        heat = -TIME_STEP * CONDUCTION * temp_ref[:, here]
        first = jnp.concatenate([push, spin, heat, jnp.ones((1, CHUNK), F32)], axis=0)
        second = jnp.concatenate([pos, radius_ref[:, here]], axis=0)
        first = jnp.concatenate(split(first), axis=0)
        second = jnp.concatenate(split(second) * 2, axis=0)
        lower = lax.broadcasted_iota(jnp.int32, (16, 1), 0) < 8
        box16 = jnp.broadcast_to(boxes, (16, CHUNK)).astype(F32).astype(BF16)
        first_parts = []
        second_parts = []
        for o in range(devices):
            mine = box16 == box_of[o].astype(F32).astype(BF16)
            first_parts.append(jnp.where(mine, first, jnp.zeros_like(first)))
            if o % 2 == 0:
                either = jnp.where(lower, box_of[o].astype(F32), box_of[o + 1].astype(F32)).astype(BF16)
                second_parts.append(jnp.where(box16 == either, second, jnp.zeros_like(second)))
        parts = jnp.concatenate(first_parts + second_parts, axis=0)

        hot_spot = hot(WINDOW, spot_ref[:, here] - WINDOW * w)
        placed = lax.dot_general(parts, hot_spot, NT, preferred_element_type=F32)
        for o in range(devices):
            tile = tile_of[c, box_of[o]] + 2 * w
            one = placed[16 * o : 16 * o + 8] + placed[16 * o + 8 : 16 * o + 16]
            two = placed[16 * devices + 8 * o : 16 * devices + 8 * o + 8]
            two = two + pltpu.roll(two, 4, 0)
            acc[o, tile, 0:8, :] += one[:, :BLOCK]
            acc[o, tile + 1, 0:8, :] += one[:, BLOCK:]
            acc[o, tile, 8:16, :] += two[:, :BLOCK]
            acc[o, tile + 1, 8:16, :] += two[:, BLOCK:]
        return 0

    chunks = particles // CHUNK
    lax.fori_loop(0, chunks, functools.partial(step, 0), 0, unroll=2)

    def later(w, _):
        return lax.fori_loop(0, chunks, functools.partial(step, w), 0)

    lax.fori_loop(1, tile_of[tile_ref.shape[0] - 8, 0], later, 0)

    def finish(o, _):
        for q in range(layers):
            out_ref[o, 8 * q : 8 * q + 8, :] = acc[o, q, 0:8, :]
            out_ref[o, 8 * layers + 4 * q : 8 * layers + 4 * q + 4, :] = acc[o, q, 8:12, :]
        return 0

    lax.fori_loop(0, devices, finish, 0)


def place(box_owner, boxes, pos, motion, radius, temp, slots):
    devices = box_owner.shape[0]
    particles = pos.shape[1]
    layers = slots // BLOCK
    vmem = pl.BlockSpec(memory_space=VMEM)
    row = jax.ShapeDtypeStruct((1, particles), jnp.int32)
    table = (-(-particles // (8 * CHUNK)) * 8 + 8, BLOCK)
    return pl.pallas_call(
        place_kernel,
        out_shape=(
            jax.ShapeDtypeStruct((devices, 12 * layers, BLOCK), F32), row, row,
            jax.ShapeDtypeStruct(table, jnp.int32),
        ),
        in_specs=[pl.BlockSpec(memory_space=pltpu.SMEM)] + [vmem] * 5,
        out_specs=(vmem,) * 4,
        scratch_shapes=[
            pltpu.SMEM((devices,), jnp.int32),
            pltpu.SMEM(table, jnp.int32),
            VMEM((devices, layers + 3, 16, BLOCK), F32),
            pltpu.SemaphoreType.DMA,
        ],
        compiler_params=pltpu.CompilerParams(vmem_limit_bytes=60 << 20),
        cost_estimate=pl.CostEstimate(
            flops=2 * 24 * devices * WINDOW * particles, bytes_accessed=1 << 20, transcendentals=0
        ),
        name="place_slots",
    )(box_owner, boxes, pos, motion, radius, temp)


def pair_terms(near):
    twice = jnp.concatenate([near, near], axis=0)
    high = twice.astype(BF16).astype(F32)
    low = (twice - high).astype(BF16).astype(F32)
    row = lax.broadcasted_iota(jnp.int32, (8, 1), 0)
    kept = high + low
    squares = kept * kept
    norm = -(squares[0:1] + squares[1:2] + squares[2:3])
    total = jnp.where(row < 3, norm, squares[3:4] + 0.5)
    one = total.astype(BF16).astype(F32)
    rest = total - one
    two = rest.astype(BF16).astype(F32)
    three = (rest - two).astype(BF16).astype(F32)
    third = jnp.where((row == 0) | (row == 3), one, jnp.where((row == 1) | (row == 4), two, three))
    third = jnp.where(row < 6, third, 0.0)
    crossed = 2.0 * jnp.where(row < 4, high, low)
    is_radius = (row == 3) | (row == 7)
    cross_d = jnp.where(is_radius, 0.0, crossed)
    cross_r = jnp.where(is_radius, crossed, 0.0)
    ones = jnp.ones_like(third)
    left = jnp.concatenate([high, low, third, jnp.where(row < 6, ones, 0.0)], axis=0)
    ones_d = jnp.where(row < 3, ones, 0.0)
    ones_r = jnp.where((row >= 3) & (row < 6), ones, 0.0)
    for_d = jnp.concatenate([cross_d, cross_d, ones_d, jnp.where(row < 3, third, 0.0)], axis=0)
    for_r = jnp.concatenate([cross_r, cross_r, ones_r, jnp.where((row >= 3) & (row < 6), third, 0.0)], axis=0)
    right = jnp.concatenate([for_d, for_r], axis=1)
    return left, right.astype(BF16)


def contact_kernel(slot_ref, mask_ref, out_ref):
    homes, rows, _ = slot_ref.shape
    layers = rows // 12
    blocks = [(s, q) for s in range(homes) for q in range(layers)]
    row = lax.broadcasted_iota(jnp.int32, (8, 1), 0)
    sign = jnp.where((row >= 3) & (row < 6), 1.0, -1.0)
    lane = lax.broadcasted_iota(jnp.int32, (BLOCK, BLOCK), 1) // 16

    def pairs_of(group):
        pairs = []
        for first in range(0, 8, 4):
            lefts = []
            rights = []
            for g, (s, q) in enumerate(group[first : first + 4]):
                left, right = pair_terms(slot_ref[s, 8 * layers + 4 * q : 8 * layers + 4 * q + 4, :])
                lefts.append(left)
                spots = [jnp.zeros_like(right)] * 4
                spots[g] = right
                rights.append(jnp.concatenate(spots, axis=0))
            turned = jnp.transpose(jnp.concatenate(lefts, axis=0)).astype(BF16)
            pairs.append(
                lax.dot_general(turned, jnp.concatenate(rights, axis=1), NN, preferred_element_type=F32)
            )
        return pairs

    def sums_of(number, group, pairs):
        stacked = []
        for s, q in group:
            mine = slot_ref[s, 8 * q : 8 * q + 8, :]
            high = mine.astype(BF16).astype(F32)
            stacked += [high, mine - high]
        columns = jnp.transpose(jnp.concatenate(stacked, axis=0)).astype(BF16)
        highs = []
        lows = []
        right = []
        for b in range(8):
            at = 2 * BLOCK * (b % 4)
            pair = pairs[b // 4]
            reach = pair[:, at + BLOCK : at + 2 * BLOCK]
            inverse = pl.reciprocal(reach, approx=True)
            inverse = inverse * (2.0 - reach * inverse)
            weight = mask_ref[8 * number + b].astype(F32) * jnp.exp(pair[:, at : at + BLOCK] * inverse)
            high, low = split(weight)
            highs.append(high)
            lows.append(low)
            right.append(jnp.where(lane == b, columns, jnp.zeros_like(columns)))
        return lax.dot_general(
            jnp.concatenate(highs + lows, axis=1), jnp.concatenate(right + right, axis=0), NN,
            preferred_element_type=F32,
        )

    def finish(group, sums):
        sums = jnp.transpose(sums)
        for b, (s, q) in enumerate(group):
            total = sums[16 * b : 16 * b + 8] + sums[16 * b + 8 : 16 * b + 16]
            out_ref[s, 8 * q : 8 * q + 8, :] = slot_ref[s, 8 * q : 8 * q + 8, :] * total[7:8] + sign * total

    groups = [blocks[i : i + 8] for i in range(0, len(blocks), 8)]
    pairs = pairs_of(groups[0])
    before = None
    for number, group in enumerate(groups):
        later = pairs_of(groups[number + 1]) if number + 1 < len(groups) else None
        sums = sums_of(number, group, pairs)
        if before is not None:
            finish(*before)
        before = (group, sums)
        pairs = later
    finish(*before)


def contact(arrived, mask):
    devices, rows, _ = arrived.shape
    layers = rows // 12
    blocks = mask.shape[0]
    step = 32 // layers
    return pl.pallas_call(
        contact_kernel,
        grid=(devices // step,),
        out_shape=jax.ShapeDtypeStruct((devices, 8 * layers, BLOCK), F32),
        in_specs=[
            pl.BlockSpec((step, rows, BLOCK), lambda h: (h, 0, 0)),
            pl.BlockSpec((step * layers, BLOCK, BLOCK), lambda h: (h, 0, 0)),
        ],
        out_specs=pl.BlockSpec((step, 8 * layers, BLOCK), lambda h: (h, 0, 0)),
        compiler_params=pltpu.CompilerParams(vmem_limit_bytes=54 << 20),
        cost_estimate=pl.CostEstimate(
            flops=64 * blocks * BLOCK * BLOCK, bytes_accessed=blocks * BLOCK * BLOCK * 4, transcendentals=0
        ),
        name="contact_blocks",
    )(arrived, mask)


def smoothed(centre, y_first, y_last, x_first, x_last):
    layers, rows, cols = centre.shape
    zero = jnp.zeros((1, rows, cols), F32)
    up = jnp.concatenate([centre[1:], zero], axis=0)
    down = jnp.concatenate([zero, centre[:-1]], axis=0)
    row = lax.broadcasted_iota(jnp.int32, (1, rows, cols), 1)
    col = lax.broadcasted_iota(jnp.int32, (1, rows, cols), 2)
    back = jnp.where(row == 0, y_first, pltpu.roll(centre, 1, 1))
    front = jnp.where(row == rows - 1, y_last, pltpu.roll(centre, rows - 1, 1))
    left = jnp.where(col == 0, x_first, pltpu.roll(centre, 1, 2))
    right = jnp.where(col == cols - 1, x_last, pltpu.roll(centre, cols - 1, 2))
    return CENTRE_WEIGHT * centre + SIDE_WEIGHT * ((up + down) + (back + front) + (left + right))


def columns(edge, layers, rows):
    count = edge.shape[0]
    if count < 8:
        edge = jnp.concatenate([edge] * (8 // count), axis=0)
    turned = jnp.transpose(edge)
    parts = [turned[:, a : a + 1] for a in range(count)]
    return jnp.concatenate(parts, axis=0).reshape(layers, rows, 1)


def smooth_field(field_ref, y0_ref, y1_ref, x0_ref, x1_ref, k, edge=None):
    at = k if edge is None else edge
    _, layers, rows, cols = field_ref.shape
    per = layers * rows // BLOCK
    x0 = columns(x0_ref[at * per : (at + 1) * per, :], layers, rows)
    x1 = columns(x1_ref[at * per : (at + 1) * per, :], layers, rows)
    y0 = y0_ref[at].reshape(layers, 1, cols)
    y1 = y1_ref[at].reshape(layers, 1, cols)
    return smoothed(field_ref[k], y0, y1, x0, x1)


def write_edges(field, k, y0_ref, y1_ref, x0_ref, x1_ref):
    layers, rows, cols = field.shape
    y0_ref[k] = field[:, 0, :]
    y1_ref[k] = field[:, rows - 1, :]
    flat = field.reshape(layers * rows, cols)
    for a in range(layers * rows // BLOCK):
        turned = jnp.transpose(flat[a * BLOCK : (a + 1) * BLOCK, :])
        at = k * (layers * rows // BLOCK) + a
        x0_ref[at : at + 1, :] = turned[0:1, :]
        x1_ref[at : at + 1, :] = turned[cols - 1 : cols, :]


def paired_rows(pairs, layers, rows, scratch):
    half = pairs.shape[0]
    cols = pairs.shape[1] // 2
    scratch[pl.ds(0, half, stride=2), :] = pairs[:, :cols]
    scratch[pl.ds(1, half, stride=2), :] = pairs[:, cols:]
    return scratch[...].reshape(layers, rows, cols)


def gathered(tables, rows, lanes):
    group = rows // 8
    found = [None] * len(tables)
    for g in range(len(tables[0])):
        mine = group == g
        for k, table in enumerate(tables):
            value = jnp.take_along_axis(table[g], lanes, axis=1, mode="promise_in_bounds")
            found[k] = value if g == 0 else jnp.where(mine, value, found[k])
    mine = lax.broadcasted_iota(jnp.int32, (8, BLOCK), 0) == rows % 8
    return [jnp.sum(jnp.where(mine, value, 0.0), axis=0, keepdims=True) for value in found]


def look_kernel(fluid_ref, cell_ref, seen_ref, table, rows_scratch, *, chunk):
    fields, layers, rows, cols = fluid_ref.shape
    particles = cell_ref.shape[1]
    half = layers * rows // 2
    wide = 2 * cols
    for k in range(fields):
        rows_scratch[...] = smoothed(fluid_ref[k], 0.0, 0.0, 0.0, 0.0).reshape(layers * rows, cols)
        here = slice(k * half, (k + 1) * half)
        for part in range(2):
            high, low = split(rows_scratch[pl.ds(part, half, stride=2), :])
            table[here, part * cols : (part + 1) * cols] = high
            table[here, wide + part * cols : wide + (part + 1) * cols] = low

    def step(i, _):
        here = pl.ds(pl.multiple_of(i * chunk, chunk), chunk)
        cells = cell_ref[:, here]
        hot_low = hot(wide, cells % wide)
        found = lax.dot_general(
            table[...], jnp.concatenate([hot_low, hot_low], axis=0), NN, preferred_element_type=F32
        )
        mine = lax.broadcasted_iota(jnp.int32, (half, chunk), 0) == cells // wide
        seen = [
            jnp.sum(jnp.where(mine, found[k * half : (k + 1) * half], 0.0), axis=0, keepdims=True)
            for k in range(fields)
        ]
        seen_ref[:, here] = jnp.concatenate(seen, axis=0)
        return 0

    lax.fori_loop(0, particles // chunk, step, 0, unroll=2)


def look_up(fluid, cells):
    fields, layers, rows, cols = fluid.shape
    particles = cells.shape[1]
    vmem = pl.BlockSpec(memory_space=VMEM)
    return pl.pallas_call(
        functools.partial(look_kernel, chunk=512),
        out_shape=jax.ShapeDtypeStruct((fields, particles), F32),
        in_specs=[vmem] * 2,
        out_specs=vmem,
        scratch_shapes=[
            VMEM((fields * layers * rows // 2, 4 * cols), BF16),
            VMEM((layers * rows, cols), F32),
        ],
        compiler_params=pltpu.CompilerParams(vmem_limit_bytes=40 << 20),
        cost_estimate=pl.CostEstimate(
            flops=8 * fields * layers * rows * cols * particles // 4, bytes_accessed=1 << 20, transcendentals=0
        ),
        name="look_up",
    )(fluid, cells)


def deposit_kernel(
    y0_ref, y1_ref, x0_ref, x1_ref, cell_ref, seen_ref, motion_ref, radius_ref, temp_ref,
    base_ref, dep_ref, dy0_ref, dy1_ref, dx0_ref, dx1_ref, x_table, rows_scratch, acc, *, chunk
):
    fields, layers, rows, cols = dep_ref.shape
    half = layers * rows // 2
    wide = 2 * cols
    particles = cell_ref.shape[1]
    per = layers * rows // BLOCK
    for k in range(fields):
        x_table[k] = jnp.zeros_like(x_table[k])
        x_table[k, 0:per, :] = x0_ref[k * per : (k + 1) * per, :]
        x_table[k, per : 2 * per, :] = x1_ref[k * per : (k + 1) * per, :]
    acc[...] = jnp.zeros_like(acc)

    def step(i, _):
        here = pl.ds(pl.multiple_of(i * chunk, chunk), chunk)
        cells = cell_ref[:, here]
        beside = [[] for _ in range(fields)]
        for s in range(chunk // BLOCK):
            cell = jnp.broadcast_to(cells[:, s * BLOCK : (s + 1) * BLOCK], (8, BLOCK))
            high = cell // cols
            low = cell % cols
            y = high % rows
            from_y = gathered(
                [
                    [ref[k, 8 * g : 8 * g + 8, :] for ref in (y0_ref, y1_ref) for g in range(layers // 8)]
                    for k in range(fields)
                ],
                high // rows + jnp.where(y == 0, 0, layers),
                low,
            )
            from_x = gathered(
                [[x_table[k, 8 * g : 8 * g + 8, :] for g in range(x_table.shape[1] // 8)] for k in range(fields)],
                high // BLOCK + jnp.where(low == 0, 0, per),
                high % BLOCK,
            )
            on_y = (y[0:1] == 0) | (y[0:1] == rows - 1)
            on_x = (low[0:1] == 0) | (low[0:1] == cols - 1)
            for k in range(fields):
                beside[k].append(jnp.where(on_y, from_y[k], 0.0) + jnp.where(on_x, from_x[k], 0.0))
        beside = jnp.concatenate([jnp.concatenate(parts, axis=1) for parts in beside], axis=0)
        seen = seen_ref[:, here] + SIDE_WEIGHT * beside
        motion = motion_ref[:, here]
        radius = radius_ref[:, here]
        temp = temp_ref[:, here]
        drag = DRAG_COEFF / (radius * radius + 0.25) * (seen[0:3] - motion[0:3])
        upward = lax.broadcasted_iota(jnp.int32, (3, 1), 0) == 2
        moved = motion[0:3] + TIME_STEP * drag - jnp.where(upward, TIME_STEP * GRAVITY, 0.0)
        warmed = temp + TIME_STEP * HEAT_TRANSFER * (seen[3:4] - temp)
        base_ref[:, here] = jnp.concatenate([moved, motion[3:6], warmed, seen[3:4]], axis=0)
        volume = radius * radius * radius
        high, low = split(jnp.concatenate([volume, -volume * drag], axis=0))
        hot_low = hot(wide, cells % wide)
        hot_high = hot(half, cells // wide)
        parts = [hot_high * piece[k : k + 1] for piece in (high, low) for k in range(fields)]
        total = lax.dot_general(jnp.concatenate(parts, axis=0), hot_low, NT, preferred_element_type=F32)
        acc[...] += total[: fields * half] + total[fields * half :]
        return 0

    lax.fori_loop(0, particles // chunk, step, 0)
    for k in range(fields):
        field = paired_rows(acc[k * half : (k + 1) * half, :], layers, rows, rows_scratch)
        dep_ref[k] = field
        write_edges(field, k, dy0_ref, dy1_ref, dx0_ref, dx1_ref)


def edge_shapes(fields, layers, rows, cols):
    y_edge = jax.ShapeDtypeStruct((fields, layers, cols), F32)
    x_edge = jax.ShapeDtypeStruct((fields * layers * rows // BLOCK, BLOCK), F32)
    return (y_edge, y_edge, x_edge, x_edge)


def deposit(halo, cells, seen, motion, radius, temp, grid):
    layers, rows, cols = grid
    fields, particles = seen.shape
    tall = -(-2 * layers * rows // (8 * BLOCK)) * 8
    vmem = pl.BlockSpec(memory_space=VMEM)
    return pl.pallas_call(
        functools.partial(deposit_kernel, chunk=1024),
        out_shape=(
            jax.ShapeDtypeStruct((8, particles), F32),
            jax.ShapeDtypeStruct((fields,) + grid, F32),
        ) + edge_shapes(fields, layers, rows, cols),
        in_specs=[vmem] * 9,
        out_specs=(vmem,) * 6,
        scratch_shapes=[
            VMEM((fields, tall, BLOCK), F32),
            VMEM((layers * rows, cols), F32),
            VMEM((fields * layers * rows // 2, 2 * cols), F32),
        ],
        compiler_params=pltpu.CompilerParams(vmem_limit_bytes=40 << 20),
        cost_estimate=pl.CostEstimate(
            flops=4 * fields * layers * rows * cols * particles, bytes_accessed=2 << 20, transcendentals=0
        ),
        name="deposit_fields",
    )(*halo, cells, seen, motion, radius, temp)


def heat_kernel(
    back_ref, slot_ref, cell_ref, radius_ref, base_ref, ey0_ref, ey1_ref, ex0_ref, ex1_ref,
    next_ref, dep_ref, dy0_ref, dy1_ref, dx0_ref, dx1_ref,
    table, acc, rows_scratch, *, chunk, rows
):
    devices, tall, _ = back_ref.shape
    layers = tall // 8
    particles = slot_ref.shape[1]
    half, wide = acc.shape
    for o in range(devices):
        for q in range(layers):
            table[o * layers + q : o * layers + q + 1, :] = back_ref[o, 8 * q + 6 : 8 * q + 7, :]
    acc[...] = jnp.zeros_like(acc)

    def step(i, _):
        here = pl.ds(pl.multiple_of(i * chunk, chunk), chunk)
        slots = slot_ref[:, here]
        gained = []
        for s in range(chunk // BLOCK):
            wanted = jnp.broadcast_to(slots[:, s * BLOCK : (s + 1) * BLOCK], (8, BLOCK))
            tiles = [table[8 * g : 8 * g + 8, :] for g in range(devices * layers // 8)]
            gained.append(gathered([tiles], wanted // BLOCK, wanted % BLOCK)[0])
        base = base_ref[6:8, here]
        total = base[0:1] + jnp.concatenate(gained, axis=1)
        next_ref[:, here] = total
        radius = radius_ref[:, here]
        high, low = split(radius * radius * radius * (total - base[1:2]))
        cells = cell_ref[:, here]
        hot_low = hot_columns(wide, cells % wide)
        hot_high = hot(half, cells // wide)
        added = lax.dot_general(hot_high * high, hot_low, NN, preferred_element_type=F32)
        acc[...] += added + lax.dot_general(hot_high * low, hot_low, NN, preferred_element_type=F32)
        return 0

    lax.fori_loop(0, particles // chunk, step, 0, unroll=2)
    field = paired_rows(acc[...], 2 * half // rows, rows, rows_scratch)
    dep_ref[0] = field
    for edge, out in ((ey0_ref, dy0_ref), (ey1_ref, dy1_ref), (ex0_ref, dx0_ref), (ex1_ref, dx1_ref)):
        out[0 : edge.shape[0]] = edge[...]
    write_edges(field, ey0_ref.shape[0], dy0_ref, dy1_ref, dx0_ref, dx1_ref)


def heat_deposit(back, slot_of, cells, radius, base, edges, grid):
    devices = back.shape[0]
    layers, rows, cols = grid
    particles = cells.shape[1]
    half = layers * rows // 2
    fields = edges[0].shape[0] + 1
    vmem = pl.BlockSpec(memory_space=VMEM)
    return pl.pallas_call(
        functools.partial(heat_kernel, chunk=1024, rows=rows),
        out_shape=(
            jax.ShapeDtypeStruct((1, particles), F32),
            jax.ShapeDtypeStruct((1,) + grid, F32),
        ) + edge_shapes(fields, layers, rows, cols),
        in_specs=[vmem] * 9,
        out_specs=(vmem,) * 6,
        scratch_shapes=[
            VMEM((devices * back.shape[1] // 8, BLOCK), F32),
            VMEM((half, 2 * cols), F32),
            VMEM((layers * rows, cols), F32),
        ],
        compiler_params=pltpu.CompilerParams(vmem_limit_bytes=40 << 20),
        cost_estimate=pl.CostEstimate(
            flops=4 * half * 2 * cols * particles, bytes_accessed=1 << 20, transcendentals=0
        ),
        name="heat_deposit",
    )(back, slot_of, cells, radius, base, *edges)


def fetch_kernel(
    owner_ref, tile_ref, back_ref, box_ref, spot_ref, base_ref, warm_ref, next_ref, box_of, table
):
    devices, tall, _ = back_ref.shape
    layers = tall // 8
    particles = box_ref.shape[1]
    invert(owner_ref, box_of)
    for o in range(devices):
        for q in range(layers):
            high, low = split(back_ref[o, 8 * q : 8 * q + 8, :])
            table[o, q] = jnp.concatenate([high, low], axis=0)
        for q in range(layers, layers + 3):
            table[o, q] = jnp.zeros((16, BLOCK), BF16)

    def gained_of(w, c):
        here = pl.ds(pl.multiple_of(c * CHUNK, CHUNK), CHUNK)
        boxes = jnp.broadcast_to(box_ref[:, here], (8, CHUNK))
        tile = [tile_ref[c, box_of[o]] + 2 * w for o in range(devices)]
        wanted = jnp.concatenate(
            [jnp.concatenate([table[o, tile[o]], table[o, tile[o] + 1]], axis=1) for o in range(devices)], axis=0
        )
        hot_spot = hot(WINDOW, spot_ref[:, here] - WINDOW * w)
        found = lax.dot_general(wanted, hot_spot, NN, preferred_element_type=F32)
        gained = jnp.zeros((8, CHUNK), F32)
        for o in range(devices):
            value = found[16 * o : 16 * o + 8] + found[16 * o + 8 : 16 * o + 16]
            gained = jnp.where(boxes == box_of[o], value, gained)
        return here, gained

    def step(c, _):
        here, gained = gained_of(0, c)
        next_ref[:, here] = jnp.concatenate(
            [base_ref[0:6, here] + gained[0:6], warm_ref[:, here]], axis=0
        )
        return 0

    chunks = particles // CHUNK
    lax.fori_loop(0, chunks, step, 0, unroll=2)

    def later(w, _):
        def again(c, _):
            here, gained = gained_of(w, c)
            next_ref[0:6, here] += gained[0:6]
            return 0

        return lax.fori_loop(0, chunks, again, 0)

    lax.fori_loop(1, tile_ref[tile_ref.shape[0] - 8, 0], later, 0)


def fetch(box_owner, tiles, back, boxes, spots, base, warm):
    devices, tall, _ = back.shape
    layers = tall // 8
    particles = boxes.shape[1]
    vmem = pl.BlockSpec(memory_space=VMEM)
    smem = pl.BlockSpec(memory_space=pltpu.SMEM)
    return pl.pallas_call(
        fetch_kernel,
        out_shape=jax.ShapeDtypeStruct((7, particles), F32),
        in_specs=[smem, smem] + [vmem] * 5,
        out_specs=vmem,
        scratch_shapes=[
            pltpu.SMEM((devices,), jnp.int32),
            VMEM((devices, layers + 3, 16, BLOCK), BF16),
        ],
        compiler_params=pltpu.CompilerParams(vmem_limit_bytes=40 << 20),
        cost_estimate=pl.CostEstimate(
            flops=32 * devices * WINDOW * particles, bytes_accessed=1 << 20, transcendentals=0
        ),
        name="fetch_slots",
    )(box_owner, tiles, back, boxes, spots, base, warm)


def spread_kernel(dep_ref, heat_ref, y0_ref, y1_ref, x0_ref, x1_ref, fluid_ref, next_ref, void_ref):
    halo = (y0_ref, y1_ref, x0_ref, x1_ref)
    crowding = 1.0 + COUPLING * smooth_field(dep_ref, *halo, 0)
    void_ref[...] = 1.0 / crowding
    for k in range(3):
        next_ref[k] = fluid_ref[k] + TIME_STEP * COUPLING * smooth_field(dep_ref, *halo, k + 1) * crowding
    warmth = smooth_field(heat_ref, *halo, 0, 4)
    next_ref[3] = fluid_ref[3] + TIME_STEP * COUPLING * warmth * crowding


def spread(dep, heat, halo, fluid):
    vmem = pl.BlockSpec(memory_space=VMEM)
    return pl.pallas_call(
        spread_kernel,
        out_shape=(jax.ShapeDtypeStruct(fluid.shape, F32), jax.ShapeDtypeStruct(fluid.shape[1:], F32)),
        in_specs=[vmem] * 7,
        out_specs=(vmem,) * 2,
        compiler_params=pltpu.CompilerParams(vmem_limit_bytes=40 << 20),
        cost_estimate=pl.CostEstimate(flops=20 * fluid.size, bytes_accessed=2 << 20, transcendentals=0),
        name="spread_fields",
    )(dep, heat, *halo, fluid)


def halo_of(y_first, y_last, x_first, x_last):
    def moved(value, axis, step):
        size = lax.axis_size(axis)
        pairs = [(i, i + step) for i in range(size) if 0 <= i + step < size]
        return lax.ppermute(value, axis, pairs)

    return (
        moved(y_last, "gy", 1),
        moved(y_first, "gy", -1),
        moved(x_last, "gx", 1),
        moved(x_first, "gx", -1),
    )


def shards(
    fluid_state, particle_pos, particle_motion, particle_radius, particle_temp,
    particle_cell, particle_box, box_owner, contact_mask,
):
    devices = lax.axis_size(("gx", "gy"))
    particles = particle_pos.shape[1]
    slots = 2 * particles // devices
    fields, layers, rows, cols = fluid_state.shape
    boxes = particle_box.reshape(1, particles)
    radius = particle_radius.reshape(1, particles)
    temp = particle_temp.reshape(1, particles)
    cells = particle_cell.reshape(1, particles)

    outgoing, slot_of, spots, tiles = place(
        box_owner, boxes, particle_pos, particle_motion, radius, temp, slots
    )
    arrived = lax.all_to_all(outgoing, ("gx", "gy"), split_axis=0, concat_axis=0, tiled=True)

    spots, fluid = lax.optimization_barrier((spots, fluid_state))
    fluid_halo = halo_of(
        fluid[:, :, 0, :],
        fluid[:, :, rows - 1, :],
        fluid[:, :, :, 0].reshape(-1, BLOCK),
        fluid[:, :, :, cols - 1].reshape(-1, BLOCK),
    )
    seen = look_up(fluid, cells)
    arrived, seen = lax.optimization_barrier((arrived, seen))
    result = contact(arrived, contact_mask)

    result, *fluid_halo = lax.optimization_barrier((result,) + tuple(fluid_halo))
    base, deposits, *edges = deposit(
        fluid_halo, cells, seen, particle_motion, radius, temp, (layers, rows, cols)
    )
    back = lax.all_to_all(result, ("gx", "gy"), split_axis=0, concat_axis=0, tiled=True)
    warm, heat_field, *edges = heat_deposit(
        back, slot_of, cells, radius, base, edges, (layers, rows, cols)
    )
    halo = halo_of(*edges)
    particle_next = fetch(box_owner, tiles, back, boxes, spots, base, warm)
    fluid_next, void_fraction = spread(deposits, heat_field, halo, fluid_state)
    return (fluid_next, void_fraction, particle_next)


def solution(mesh):
    in_specs = (
        P(None, None, "gy", "gx"),
        P(None, ("gx", "gy")),
        P(None, ("gx", "gy")),
        P(("gx", "gy")),
        P(("gx", "gy")),
        P(("gx", "gy")),
        P(("gx", "gy"), None),
        P(),
        P(("gx", "gy"), None, None),
    )
    out_specs = (P(None, None, "gy", "gx"), P(None, "gy", "gx"), P(None, ("gx", "gy")))
    return jax.shard_map(shards, mesh=mesh, in_specs=in_specs, out_specs=out_specs, check_vma=False)
```

```python
import functools

import jax
import jax.numpy as jnp
from jax import lax
from jax.experimental import pallas as pl
from jax.experimental.pallas import tpu as pltpu
from jax.sharding import PartitionSpec as P

BLOCK = 128
TIME_STEP = 0.1
STIFFNESS = 0.5
DAMPING_RATE = 0.2
ROTATION_DRAG = 0.1
DRAG_COEFF = 4.0
CONDUCTION = 0.3
HEAT_TRANSFER = 4.0
GRAVITY = 0.3
COUPLING = 4.0
CENTRE_WEIGHT = 0.25
SIDE_WEIGHT = 0.125

F32 = jnp.float32
BF16 = jnp.bfloat16
VMEM = pltpu.VMEM
NN = (((1,), (0,)), ((), ()))
NT = (((1,), (1,)), ((), ()))


def split(value):
    high = value.astype(BF16)
    return high, (value - high.astype(F32)).astype(BF16)


def hot(count, row):
    places = lax.broadcasted_iota(jnp.int32, (count, row.shape[1]), 0)
    return jnp.where(places == row, 1.0, 0.0).astype(BF16)


def hot_columns(count, row):
    n = row.shape[1] // BLOCK
    tiles = [row[:, a * BLOCK : (a + 1) * BLOCK] for a in range(n)]
    turned = jnp.transpose(jnp.concatenate(tiles * (8 // n), axis=0).astype(F32))
    places = lax.broadcasted_iota(jnp.int32, (BLOCK, count), 1).astype(F32)
    return jnp.concatenate(
        [jnp.where(places == turned[:, a : a + 1], 1.0, 0.0).astype(BF16) for a in range(n)], axis=0
    )


def invert(owner_ref, box_of):
    def step(b, _):
        box_of[owner_ref[b]] = b
        return 0

    lax.fori_loop(0, owner_ref.shape[0], step, 0)


WINDOW = 256
CHUNK = 1024


def place_kernel(
    owner_ref, box_ref, pos_ref, motion_ref, radius_ref, temp_ref,
    out_ref, slot_ref, spot_ref, tile_ref,
    box_of, tile_of, acc, done
):
    devices, rows, _ = out_ref.shape
    layers = rows // 12
    slots = layers * BLOCK
    particles = box_ref.shape[1]
    sub = 256
    invert(owner_ref, box_of)
    acc[...] = jnp.zeros_like(acc)

    box_row = lax.broadcasted_iota(jnp.int32, (devices, 1), 0)
    owner_column = jnp.zeros((devices, 1), F32)
    for b in range(devices):
        owner_column = jnp.where(box_row == b, owner_ref[b].astype(F32), owner_column)
    above = (
        lax.broadcasted_iota(jnp.int32, (sub, sub), 0) < lax.broadcasted_iota(jnp.int32, (sub, sub), 1)
    )
    above = jnp.where(above, 1.0, 0.0).astype(BF16)
    lane = lax.broadcasted_iota(jnp.int32, (devices, BLOCK), 1)
    tiles = jnp.zeros((devices, BLOCK), F32)
    highest = jnp.zeros((1, sub), F32)
    carry = jnp.zeros((devices, 1), F32)
    per_chunk = CHUNK // sub
    for c in range(particles // CHUNK):
        chosen = []
        for s in range(per_chunk):
            at = c * CHUNK + s * sub
            chosen.append(
                lax.broadcasted_iota(jnp.int32, (devices, sub), 0) == box_ref[:, at : at + sub]
            )
        ones = [jnp.where(mine, 1.0, 0.0) for mine in chosen]
        earlier = lax.dot_general(
            jnp.concatenate(ones, axis=0).astype(BF16), above, NN, preferred_element_type=F32
        )
        tile = jnp.minimum(jnp.floor(carry * (1.0 / BLOCK)), layers - 1.0)
        tiles = jnp.where(lane == c, tile, tiles)
        for s in range(per_chunk):
            at = c * CHUNK + s * sub
            rank = earlier[s * devices : (s + 1) * devices] + carry
            spot = jnp.where(chosen[s], rank - BLOCK * tile, 0.0)
            spot = jnp.sum(spot, axis=0, keepdims=True)
            slot = jnp.where(chosen[s], rank + slots * owner_column, 0.0)
            slot = jnp.sum(slot, axis=0, keepdims=True)
            spot_ref[:, at : at + sub] = spot.astype(jnp.int32)
            slot_ref[:, at : at + sub] = slot.astype(jnp.int32)
            highest = jnp.maximum(highest, spot)
            carry = carry + jnp.sum(ones[s], axis=1, keepdims=True)
    if devices < BLOCK:
        tiles = jnp.concatenate([tiles, jnp.zeros((BLOCK - devices, BLOCK), F32)], axis=0)
    count = tile_ref.shape[0] - 8
    tile_ref[0:count, :] = jnp.transpose(tiles)[0:count].astype(jnp.int32)
    windows = jnp.floor(jnp.max(highest, axis=1, keepdims=True) * (1.0 / WINDOW)) + 1.0
    tile_ref[count : count + 8, :] = jnp.broadcast_to(windows, (8, BLOCK)).astype(jnp.int32)
    copy = pltpu.make_async_copy(tile_ref, tile_of, done)
    copy.start()
    copy.wait()

    def step(w, c, _):
        here = pl.ds(pl.multiple_of(c * CHUNK, CHUNK), CHUNK)
        boxes = box_ref[:, here]
        pos = pos_ref[:, here]
        motion = motion_ref[:, here]
        push = TIME_STEP * STIFFNESS * pos - TIME_STEP * DAMPING_RATE * motion[0:3]
        spin = -TIME_STEP * ROTATION_DRAG * motion[3:6]
        heat = -TIME_STEP * CONDUCTION * temp_ref[:, here]
        first = jnp.concatenate([push, spin, heat, jnp.ones((1, CHUNK), F32)], axis=0)
        second = jnp.concatenate([pos, radius_ref[:, here]], axis=0)
        first = jnp.concatenate(split(first), axis=0)
        second = jnp.concatenate(split(second) * 2, axis=0)
        lower = lax.broadcasted_iota(jnp.int32, (16, 1), 0) < 8
        box16 = jnp.broadcast_to(boxes, (16, CHUNK)).astype(F32).astype(BF16)
        first_parts = []
        second_parts = []
        for o in range(devices):
            mine = box16 == box_of[o].astype(F32).astype(BF16)
            first_parts.append(jnp.where(mine, first, jnp.zeros_like(first)))
            if o % 2 == 0:
                either = jnp.where(lower, box_of[o].astype(F32), box_of[o + 1].astype(F32)).astype(BF16)
                second_parts.append(jnp.where(box16 == either, second, jnp.zeros_like(second)))
        parts = jnp.concatenate(first_parts + second_parts, axis=0)

        hot_spot = hot(WINDOW, spot_ref[:, here] - WINDOW * w)
        placed = lax.dot_general(parts, hot_spot, NT, preferred_element_type=F32)
        for o in range(devices):
            tile = tile_of[c, box_of[o]] + 2 * w
            one = placed[16 * o : 16 * o + 8] + placed[16 * o + 8 : 16 * o + 16]
            two = placed[16 * devices + 8 * o : 16 * devices + 8 * o + 8]
            two = two + pltpu.roll(two, 4, 0)
            acc[o, tile, 0:8, :] += one[:, :BLOCK]
            acc[o, tile + 1, 0:8, :] += one[:, BLOCK:]
            acc[o, tile, 8:16, :] += two[:, :BLOCK]
            acc[o, tile + 1, 8:16, :] += two[:, BLOCK:]
        return 0

    chunks = particles // CHUNK
    lax.fori_loop(0, chunks, functools.partial(step, 0), 0, unroll=2)

    def later(w, _):
        return lax.fori_loop(0, chunks, functools.partial(step, w), 0)

    lax.fori_loop(1, tile_of[tile_ref.shape[0] - 8, 0], later, 0)

    def finish(o, _):
        for q in range(layers):
            out_ref[o, 8 * q : 8 * q + 8, :] = acc[o, q, 0:8, :]
            out_ref[o, 8 * layers + 4 * q : 8 * layers + 4 * q + 4, :] = acc[o, q, 8:12, :]
        return 0

    lax.fori_loop(0, devices, finish, 0)


def place(box_owner, boxes, pos, motion, radius, temp, slots):
    devices = box_owner.shape[0]
    particles = pos.shape[1]
    layers = slots // BLOCK
    vmem = pl.BlockSpec(memory_space=VMEM)
    row = jax.ShapeDtypeStruct((1, particles), jnp.int32)
    table = (-(-particles // (8 * CHUNK)) * 8 + 8, BLOCK)
    return pl.pallas_call(
        place_kernel,
        out_shape=(
            jax.ShapeDtypeStruct((devices, 12 * layers, BLOCK), F32), row, row,
            jax.ShapeDtypeStruct(table, jnp.int32),
        ),
        in_specs=[pl.BlockSpec(memory_space=pltpu.SMEM)] + [vmem] * 5,
        out_specs=(vmem,) * 4,
        scratch_shapes=[
            pltpu.SMEM((devices,), jnp.int32),
            pltpu.SMEM(table, jnp.int32),
            VMEM((devices, layers + 3, 16, BLOCK), F32),
            pltpu.SemaphoreType.DMA,
        ],
        compiler_params=pltpu.CompilerParams(vmem_limit_bytes=60 << 20),
        cost_estimate=pl.CostEstimate(
            flops=2 * 24 * devices * WINDOW * particles, bytes_accessed=1 << 20, transcendentals=0
        ),
        name="place_slots",
    )(box_owner, boxes, pos, motion, radius, temp)


def pair_terms(near):
    twice = jnp.concatenate([near, near], axis=0)
    high = twice.astype(BF16).astype(F32)
    low = (twice - high).astype(BF16).astype(F32)
    row = lax.broadcasted_iota(jnp.int32, (8, 1), 0)
    kept = high + low
    squares = kept * kept
    norm = -(squares[0:1] + squares[1:2] + squares[2:3])
    total = jnp.where(row < 3, norm, squares[3:4] + 0.5)
    one = total.astype(BF16).astype(F32)
    rest = total - one
    two = rest.astype(BF16).astype(F32)
    three = (rest - two).astype(BF16).astype(F32)
    third = jnp.where((row == 0) | (row == 3), one, jnp.where((row == 1) | (row == 4), two, three))
    third = jnp.where(row < 6, third, 0.0)
    crossed = 2.0 * jnp.where(row < 4, high, low)
    is_radius = (row == 3) | (row == 7)
    cross_d = jnp.where(is_radius, 0.0, crossed)
    cross_r = jnp.where(is_radius, crossed, 0.0)
    ones = jnp.ones_like(third)
    left = jnp.concatenate([high, low, third, jnp.where(row < 6, ones, 0.0)], axis=0)
    ones_d = jnp.where(row < 3, ones, 0.0)
    ones_r = jnp.where((row >= 3) & (row < 6), ones, 0.0)
    for_d = jnp.concatenate([cross_d, cross_d, ones_d, jnp.where(row < 3, third, 0.0)], axis=0)
    for_r = jnp.concatenate([cross_r, cross_r, ones_r, jnp.where((row >= 3) & (row < 6), third, 0.0)], axis=0)
    right = jnp.concatenate([for_d, for_r], axis=1)
    return left, right.astype(BF16)


def contact_kernel(slot_ref, mask_hbm, out_ref, mask_ref, arrived):
    homes, rows, _ = slot_ref.shape
    layers = rows // 12
    blocks = [(s, q) for s in range(homes) for q in range(layers)]
    row = lax.broadcasted_iota(jnp.int32, (8, 1), 0)
    sign = jnp.where((row >= 3) & (row < 6), 1.0, -1.0)
    lane = lax.broadcasted_iota(jnp.int32, (BLOCK, BLOCK), 1) // 16
    at_step = pl.program_id(0)

    def mask_copy(number):
        part = pl.ds(8 * number, 8)
        return pltpu.make_async_copy(mask_hbm.at[part], mask_ref.at[part], arrived.at[number])

    @pl.when(at_step == 0)
    def _():
        for number in range(mask_hbm.shape[0] // 8):
            mask_copy(number).start()

    def pairs_of(group):
        pairs = []
        for first in range(0, 8, 4):
            lefts = []
            rights = []
            for g, (s, q) in enumerate(group[first : first + 4]):
                left, right = pair_terms(slot_ref[s, 8 * layers + 4 * q : 8 * layers + 4 * q + 4, :])
                lefts.append(left)
                spots = [jnp.zeros_like(right)] * 4
                spots[g] = right
                rights.append(jnp.concatenate(spots, axis=0))
            turned = jnp.transpose(jnp.concatenate(lefts, axis=0)).astype(BF16)
            pairs.append(
                lax.dot_general(turned, jnp.concatenate(rights, axis=1), NN, preferred_element_type=F32)
            )
        return pairs

    def sums_of(number, group, pairs):
        stacked = []
        for s, q in group:
            mine = slot_ref[s, 8 * q : 8 * q + 8, :]
            high = mine.astype(BF16).astype(F32)
            stacked += [high, mine - high]
        columns = jnp.transpose(jnp.concatenate(stacked, axis=0)).astype(BF16)
        highs = []
        lows = []
        right = []
        for b in range(8):
            at = 2 * BLOCK * (b % 4)
            pair = pairs[b // 4]
            reach = pair[:, at + BLOCK : at + 2 * BLOCK]
            inverse = pl.reciprocal(reach, approx=True)
            inverse = inverse * (2.0 - reach * inverse)
            weight = mask_ref[at_step * len(blocks) + 8 * number + b].astype(F32) * jnp.exp(pair[:, at : at + BLOCK] * inverse)
            high, low = split(weight)
            highs.append(high)
            lows.append(low)
            right.append(jnp.where(lane == b, columns, jnp.zeros_like(columns)))
        return lax.dot_general(
            jnp.concatenate(highs + lows, axis=1), jnp.concatenate(right + right, axis=0), NN,
            preferred_element_type=F32,
        )

    def finish(group, sums):
        sums = jnp.transpose(sums)
        for b, (s, q) in enumerate(group):
            total = sums[16 * b : 16 * b + 8] + sums[16 * b + 8 : 16 * b + 16]
            out_ref[s, 8 * q : 8 * q + 8, :] = slot_ref[s, 8 * q : 8 * q + 8, :] * total[7:8] + sign * total

    groups = [blocks[i : i + 8] for i in range(0, len(blocks), 8)]
    pairs = pairs_of(groups[0])
    before = None
    for number, group in enumerate(groups):
        later = pairs_of(groups[number + 1]) if number + 1 < len(groups) else None
        mask_copy(at_step * len(groups) + number).wait()
        sums = sums_of(number, group, pairs)
        if before is not None:
            finish(*before)
        before = (group, sums)
        pairs = later
    finish(*before)


def contact(arrived, mask):
    devices, rows, _ = arrived.shape
    layers = rows // 12
    blocks = mask.shape[0]
    step = 32 // layers
    return pl.pallas_call(
        contact_kernel,
        grid=(devices // step,),
        out_shape=jax.ShapeDtypeStruct((devices, 8 * layers, BLOCK), F32),
        in_specs=[
            pl.BlockSpec((step, rows, BLOCK), lambda h: (h, 0, 0)),
            pl.BlockSpec(memory_space=pltpu.HBM),
        ],
        out_specs=pl.BlockSpec((step, 8 * layers, BLOCK), lambda h: (h, 0, 0)),
        scratch_shapes=[VMEM(mask.shape, mask.dtype), pltpu.SemaphoreType.DMA((blocks // 8,))],
        compiler_params=pltpu.CompilerParams(vmem_limit_bytes=60 << 20),
        cost_estimate=pl.CostEstimate(
            flops=64 * blocks * BLOCK * BLOCK, bytes_accessed=blocks * BLOCK * BLOCK * 4, transcendentals=0
        ),
        name="contact_blocks",
    )(arrived, mask)


def smoothed(centre, y_first, y_last, x_first, x_last):
    layers, rows, cols = centre.shape
    zero = jnp.zeros((1, rows, cols), F32)
    up = jnp.concatenate([centre[1:], zero], axis=0)
    down = jnp.concatenate([zero, centre[:-1]], axis=0)
    row = lax.broadcasted_iota(jnp.int32, (1, rows, cols), 1)
    col = lax.broadcasted_iota(jnp.int32, (1, rows, cols), 2)
    back = jnp.where(row == 0, y_first, pltpu.roll(centre, 1, 1))
    front = jnp.where(row == rows - 1, y_last, pltpu.roll(centre, rows - 1, 1))
    left = jnp.where(col == 0, x_first, pltpu.roll(centre, 1, 2))
    right = jnp.where(col == cols - 1, x_last, pltpu.roll(centre, cols - 1, 2))
    return CENTRE_WEIGHT * centre + SIDE_WEIGHT * ((up + down) + (back + front) + (left + right))


def columns(edge, layers, rows):
    count = edge.shape[0]
    if count < 8:
        edge = jnp.concatenate([edge] * (8 // count), axis=0)
    turned = jnp.transpose(edge)
    parts = [turned[:, a : a + 1] for a in range(count)]
    return jnp.concatenate(parts, axis=0).reshape(layers, rows, 1)


def smooth_field(field_ref, y0_ref, y1_ref, x0_ref, x1_ref, k, edge=None):
    at = k if edge is None else edge
    _, layers, rows, cols = field_ref.shape
    per = layers * rows // BLOCK
    x0 = columns(x0_ref[at * per : (at + 1) * per, :], layers, rows)
    x1 = columns(x1_ref[at * per : (at + 1) * per, :], layers, rows)
    y0 = y0_ref[at].reshape(layers, 1, cols)
    y1 = y1_ref[at].reshape(layers, 1, cols)
    return smoothed(field_ref[k], y0, y1, x0, x1)


def write_edges(field, k, y0_ref, y1_ref, x0_ref, x1_ref):
    layers, rows, cols = field.shape
    y0_ref[k] = field[:, 0, :]
    y1_ref[k] = field[:, rows - 1, :]
    flat = field.reshape(layers * rows, cols)
    for a in range(layers * rows // BLOCK):
        turned = jnp.transpose(flat[a * BLOCK : (a + 1) * BLOCK, :])
        at = k * (layers * rows // BLOCK) + a
        x0_ref[at : at + 1, :] = turned[0:1, :]
        x1_ref[at : at + 1, :] = turned[cols - 1 : cols, :]


def paired_rows(pairs, layers, rows, scratch):
    half = pairs.shape[0]
    cols = pairs.shape[1] // 2
    scratch[pl.ds(0, half, stride=2), :] = pairs[:, :cols]
    scratch[pl.ds(1, half, stride=2), :] = pairs[:, cols:]
    return scratch[...].reshape(layers, rows, cols)


def gathered(tables, rows, lanes):
    group = rows // 8
    found = [None] * len(tables)
    for g in range(len(tables[0])):
        mine = group == g
        for k, table in enumerate(tables):
            value = jnp.take_along_axis(table[g], lanes, axis=1, mode="promise_in_bounds")
            found[k] = value if g == 0 else jnp.where(mine, value, found[k])
    mine = lax.broadcasted_iota(jnp.int32, (8, BLOCK), 0) == rows % 8
    return [jnp.sum(jnp.where(mine, value, 0.0), axis=0, keepdims=True) for value in found]


def look_kernel(fluid_ref, cell_ref, seen_ref, table, rows_scratch, *, chunk):
    fields, layers, rows, cols = fluid_ref.shape
    particles = cell_ref.shape[1]
    half = layers * rows // 2
    wide = 2 * cols
    for k in range(fields):
        rows_scratch[...] = smoothed(fluid_ref[k], 0.0, 0.0, 0.0, 0.0).reshape(layers * rows, cols)
        here = slice(k * half, (k + 1) * half)
        for part in range(2):
            high, low = split(rows_scratch[pl.ds(part, half, stride=2), :])
            table[here, part * cols : (part + 1) * cols] = high
            table[here, wide + part * cols : wide + (part + 1) * cols] = low

    def step(i, _):
        here = pl.ds(pl.multiple_of(i * chunk, chunk), chunk)
        cells = cell_ref[:, here]
        hot_low = hot(wide, cells % wide)
        found = lax.dot_general(
            table[...], jnp.concatenate([hot_low, hot_low], axis=0), NN, preferred_element_type=F32
        )
        mine = lax.broadcasted_iota(jnp.int32, (half, chunk), 0) == cells // wide
        seen = [
            jnp.sum(jnp.where(mine, found[k * half : (k + 1) * half], 0.0), axis=0, keepdims=True)
            for k in range(fields)
        ]
        seen_ref[:, here] = jnp.concatenate(seen, axis=0)
        return 0

    lax.fori_loop(0, particles // chunk, step, 0, unroll=2)


def look_up(fluid, cells):
    fields, layers, rows, cols = fluid.shape
    particles = cells.shape[1]
    vmem = pl.BlockSpec(memory_space=VMEM)
    return pl.pallas_call(
        functools.partial(look_kernel, chunk=512),
        out_shape=jax.ShapeDtypeStruct((fields, particles), F32),
        in_specs=[vmem] * 2,
        out_specs=vmem,
        scratch_shapes=[
            VMEM((fields * layers * rows // 2, 4 * cols), BF16),
            VMEM((layers * rows, cols), F32),
        ],
        compiler_params=pltpu.CompilerParams(vmem_limit_bytes=40 << 20),
        cost_estimate=pl.CostEstimate(
            flops=8 * fields * layers * rows * cols * particles // 4, bytes_accessed=1 << 20, transcendentals=0
        ),
        name="look_up",
    )(fluid, cells)


def deposit_kernel(
    y0_ref, y1_ref, x0_ref, x1_ref, cell_ref, seen_ref, motion_ref, radius_ref, temp_ref,
    base_ref, dep_ref, dy0_ref, dy1_ref, dx0_ref, dx1_ref, x_table, rows_scratch, acc, *, chunk
):
    fields, layers, rows, cols = dep_ref.shape
    half = layers * rows // 2
    wide = 2 * cols
    particles = cell_ref.shape[1]
    per = layers * rows // BLOCK
    for k in range(fields):
        x_table[k] = jnp.zeros_like(x_table[k])
        x_table[k, 0:per, :] = x0_ref[k * per : (k + 1) * per, :]
        x_table[k, per : 2 * per, :] = x1_ref[k * per : (k + 1) * per, :]
    acc[...] = jnp.zeros_like(acc)

    def step(i, _):
        here = pl.ds(pl.multiple_of(i * chunk, chunk), chunk)
        cells = cell_ref[:, here]
        beside = [[] for _ in range(fields)]
        for s in range(chunk // BLOCK):
            cell = jnp.broadcast_to(cells[:, s * BLOCK : (s + 1) * BLOCK], (8, BLOCK))
            high = cell // cols
            low = cell % cols
            y = high % rows
            from_y = gathered(
                [
                    [ref[k, 8 * g : 8 * g + 8, :] for ref in (y0_ref, y1_ref) for g in range(layers // 8)]
                    for k in range(fields)
                ],
                high // rows + jnp.where(y == 0, 0, layers),
                low,
            )
            from_x = gathered(
                [[x_table[k, 8 * g : 8 * g + 8, :] for g in range(x_table.shape[1] // 8)] for k in range(fields)],
                high // BLOCK + jnp.where(low == 0, 0, per),
                high % BLOCK,
            )
            on_y = (y[0:1] == 0) | (y[0:1] == rows - 1)
            on_x = (low[0:1] == 0) | (low[0:1] == cols - 1)
            for k in range(fields):
                beside[k].append(jnp.where(on_y, from_y[k], 0.0) + jnp.where(on_x, from_x[k], 0.0))
        beside = jnp.concatenate([jnp.concatenate(parts, axis=1) for parts in beside], axis=0)
        seen = seen_ref[:, here] + SIDE_WEIGHT * beside
        motion = motion_ref[:, here]
        radius = radius_ref[:, here]
        temp = temp_ref[:, here]
        drag = DRAG_COEFF / (radius * radius + 0.25) * (seen[0:3] - motion[0:3])
        upward = lax.broadcasted_iota(jnp.int32, (3, 1), 0) == 2
        moved = motion[0:3] + TIME_STEP * drag - jnp.where(upward, TIME_STEP * GRAVITY, 0.0)
        warmed = temp + TIME_STEP * HEAT_TRANSFER * (seen[3:4] - temp)
        base_ref[:, here] = jnp.concatenate([moved, motion[3:6], warmed, seen[3:4]], axis=0)
        volume = radius * radius * radius
        high, low = split(jnp.concatenate([volume, -volume * drag], axis=0))
        hot_low = hot(wide, cells % wide)
        hot_high = hot(half, cells // wide)
        parts = [hot_high * piece[k : k + 1] for piece in (high, low) for k in range(fields)]
        total = lax.dot_general(jnp.concatenate(parts, axis=0), hot_low, NT, preferred_element_type=F32)
        acc[...] += total[: fields * half] + total[fields * half :]
        return 0

    lax.fori_loop(0, particles // chunk, step, 0)
    for k in range(fields):
        field = paired_rows(acc[k * half : (k + 1) * half, :], layers, rows, rows_scratch)
        dep_ref[k] = field
        write_edges(field, k, dy0_ref, dy1_ref, dx0_ref, dx1_ref)


def edge_shapes(fields, layers, rows, cols):
    y_edge = jax.ShapeDtypeStruct((fields, layers, cols), F32)
    x_edge = jax.ShapeDtypeStruct((fields * layers * rows // BLOCK, BLOCK), F32)
    return (y_edge, y_edge, x_edge, x_edge)


def deposit(halo, cells, seen, motion, radius, temp, grid):
    layers, rows, cols = grid
    fields, particles = seen.shape
    tall = -(-2 * layers * rows // (8 * BLOCK)) * 8
    vmem = pl.BlockSpec(memory_space=VMEM)
    return pl.pallas_call(
        functools.partial(deposit_kernel, chunk=1024),
        out_shape=(
            jax.ShapeDtypeStruct((8, particles), F32),
            jax.ShapeDtypeStruct((fields,) + grid, F32),
        ) + edge_shapes(fields, layers, rows, cols),
        in_specs=[vmem] * 9,
        out_specs=(vmem,) * 6,
        scratch_shapes=[
            VMEM((fields, tall, BLOCK), F32),
            VMEM((layers * rows, cols), F32),
            VMEM((fields * layers * rows // 2, 2 * cols), F32),
        ],
        compiler_params=pltpu.CompilerParams(vmem_limit_bytes=40 << 20),
        cost_estimate=pl.CostEstimate(
            flops=4 * fields * layers * rows * cols * particles, bytes_accessed=2 << 20, transcendentals=0
        ),
        name="deposit_fields",
    )(*halo, cells, seen, motion, radius, temp)


def heat_kernel(
    back_ref, slot_ref, cell_ref, radius_ref, base_ref, ey0_ref, ey1_ref, ex0_ref, ex1_ref,
    next_ref, dep_ref, dy0_ref, dy1_ref, dx0_ref, dx1_ref,
    table, acc, rows_scratch, *, chunk, rows
):
    devices, tall, _ = back_ref.shape
    layers = tall // 8
    particles = slot_ref.shape[1]
    half, wide = acc.shape
    for o in range(devices):
        for q in range(layers):
            table[o * layers + q : o * layers + q + 1, :] = back_ref[o, 8 * q + 6 : 8 * q + 7, :]
    acc[...] = jnp.zeros_like(acc)

    def step(i, _):
        here = pl.ds(pl.multiple_of(i * chunk, chunk), chunk)
        slots = slot_ref[:, here]
        gained = []
        for s in range(chunk // BLOCK):
            wanted = jnp.broadcast_to(slots[:, s * BLOCK : (s + 1) * BLOCK], (8, BLOCK))
            tiles = [table[8 * g : 8 * g + 8, :] for g in range(devices * layers // 8)]
            gained.append(gathered([tiles], wanted // BLOCK, wanted % BLOCK)[0])
        base = base_ref[6:8, here]
        total = base[0:1] + jnp.concatenate(gained, axis=1)
        next_ref[:, here] = total
        radius = radius_ref[:, here]
        high, low = split(radius * radius * radius * (total - base[1:2]))
        cells = cell_ref[:, here]
        hot_low = hot_columns(wide, cells % wide)
        hot_high = hot(half, cells // wide)
        added = lax.dot_general(hot_high * high, hot_low, NN, preferred_element_type=F32)
        acc[...] += added + lax.dot_general(hot_high * low, hot_low, NN, preferred_element_type=F32)
        return 0

    lax.fori_loop(0, particles // chunk, step, 0, unroll=2)
    field = paired_rows(acc[...], 2 * half // rows, rows, rows_scratch)
    dep_ref[0] = field
    for edge, out in ((ey0_ref, dy0_ref), (ey1_ref, dy1_ref), (ex0_ref, dx0_ref), (ex1_ref, dx1_ref)):
        out[0 : edge.shape[0]] = edge[...]
    write_edges(field, ey0_ref.shape[0], dy0_ref, dy1_ref, dx0_ref, dx1_ref)


def heat_deposit(back, slot_of, cells, radius, base, edges, grid):
    devices = back.shape[0]
    layers, rows, cols = grid
    particles = cells.shape[1]
    half = layers * rows // 2
    fields = edges[0].shape[0] + 1
    vmem = pl.BlockSpec(memory_space=VMEM)
    return pl.pallas_call(
        functools.partial(heat_kernel, chunk=1024, rows=rows),
        out_shape=(
            jax.ShapeDtypeStruct((1, particles), F32),
            jax.ShapeDtypeStruct((1,) + grid, F32),
        ) + edge_shapes(fields, layers, rows, cols),
        in_specs=[vmem] * 9,
        out_specs=(vmem,) * 6,
        scratch_shapes=[
            VMEM((devices * back.shape[1] // 8, BLOCK), F32),
            VMEM((half, 2 * cols), F32),
            VMEM((layers * rows, cols), F32),
        ],
        compiler_params=pltpu.CompilerParams(vmem_limit_bytes=40 << 20),
        cost_estimate=pl.CostEstimate(
            flops=4 * half * 2 * cols * particles, bytes_accessed=1 << 20, transcendentals=0
        ),
        name="heat_deposit",
    )(back, slot_of, cells, radius, base, *edges)


def fetch_kernel(
    owner_ref, tile_ref, back_ref, box_ref, spot_ref, base_ref, warm_ref, next_ref, box_of, table
):
    devices, tall, _ = back_ref.shape
    layers = tall // 8
    particles = box_ref.shape[1]
    invert(owner_ref, box_of)
    for o in range(devices):
        for q in range(layers):
            high, low = split(back_ref[o, 8 * q : 8 * q + 8, :])
            table[o, q] = jnp.concatenate([high, low], axis=0)
        for q in range(layers, layers + 3):
            table[o, q] = jnp.zeros((16, BLOCK), BF16)

    def gained_of(w, c):
        here = pl.ds(pl.multiple_of(c * CHUNK, CHUNK), CHUNK)
        boxes = jnp.broadcast_to(box_ref[:, here], (8, CHUNK))
        tile = [tile_ref[c, box_of[o]] + 2 * w for o in range(devices)]
        wanted = jnp.concatenate(
            [jnp.concatenate([table[o, tile[o]], table[o, tile[o] + 1]], axis=1) for o in range(devices)], axis=0
        )
        hot_spot = hot(WINDOW, spot_ref[:, here] - WINDOW * w)
        found = lax.dot_general(wanted, hot_spot, NN, preferred_element_type=F32)
        gained = jnp.zeros((8, CHUNK), F32)
        for o in range(devices):
            value = found[16 * o : 16 * o + 8] + found[16 * o + 8 : 16 * o + 16]
            gained = jnp.where(boxes == box_of[o], value, gained)
        return here, gained

    def step(c, _):
        here, gained = gained_of(0, c)
        next_ref[:, here] = jnp.concatenate(
            [base_ref[0:6, here] + gained[0:6], warm_ref[:, here]], axis=0
        )
        return 0

    chunks = particles // CHUNK
    lax.fori_loop(0, chunks, step, 0, unroll=2)

    def later(w, _):
        def again(c, _):
            here, gained = gained_of(w, c)
            next_ref[0:6, here] += gained[0:6]
            return 0

        return lax.fori_loop(0, chunks, again, 0)

    lax.fori_loop(1, tile_ref[tile_ref.shape[0] - 8, 0], later, 0)


def fetch(box_owner, tiles, back, boxes, spots, base, warm):
    devices, tall, _ = back.shape
    layers = tall // 8
    particles = boxes.shape[1]
    vmem = pl.BlockSpec(memory_space=VMEM)
    smem = pl.BlockSpec(memory_space=pltpu.SMEM)
    return pl.pallas_call(
        fetch_kernel,
        out_shape=jax.ShapeDtypeStruct((7, particles), F32),
        in_specs=[smem, smem] + [vmem] * 5,
        out_specs=vmem,
        scratch_shapes=[
            pltpu.SMEM((devices,), jnp.int32),
            VMEM((devices, layers + 3, 16, BLOCK), BF16),
        ],
        compiler_params=pltpu.CompilerParams(vmem_limit_bytes=40 << 20),
        cost_estimate=pl.CostEstimate(
            flops=32 * devices * WINDOW * particles, bytes_accessed=1 << 20, transcendentals=0
        ),
        name="fetch_slots",
    )(box_owner, tiles, back, boxes, spots, base, warm)


def spread_kernel(dep_ref, heat_ref, y0_ref, y1_ref, x0_ref, x1_ref, fluid_ref, next_ref, void_ref):
    halo = (y0_ref, y1_ref, x0_ref, x1_ref)
    crowding = 1.0 + COUPLING * smooth_field(dep_ref, *halo, 0)
    void_ref[...] = 1.0 / crowding
    for k in range(3):
        next_ref[k] = fluid_ref[k] + TIME_STEP * COUPLING * smooth_field(dep_ref, *halo, k + 1) * crowding
    warmth = smooth_field(heat_ref, *halo, 0, 4)
    next_ref[3] = fluid_ref[3] + TIME_STEP * COUPLING * warmth * crowding


def spread(dep, heat, halo, fluid):
    vmem = pl.BlockSpec(memory_space=VMEM)
    return pl.pallas_call(
        spread_kernel,
        out_shape=(jax.ShapeDtypeStruct(fluid.shape, F32), jax.ShapeDtypeStruct(fluid.shape[1:], F32)),
        in_specs=[vmem] * 7,
        out_specs=(vmem,) * 2,
        compiler_params=pltpu.CompilerParams(vmem_limit_bytes=40 << 20),
        cost_estimate=pl.CostEstimate(flops=20 * fluid.size, bytes_accessed=2 << 20, transcendentals=0),
        name="spread_fields",
    )(dep, heat, *halo, fluid)


def halo_of(y_first, y_last, x_first, x_last):
    def moved(value, axis, step):
        size = lax.axis_size(axis)
        pairs = [(i, i + step) for i in range(size) if 0 <= i + step < size]
        return lax.ppermute(value, axis, pairs)

    return (
        moved(y_last, "gy", 1),
        moved(y_first, "gy", -1),
        moved(x_last, "gx", 1),
        moved(x_first, "gx", -1),
    )


def shards(
    fluid_state, particle_pos, particle_motion, particle_radius, particle_temp,
    particle_cell, particle_box, box_owner, contact_mask,
):
    devices = lax.axis_size(("gx", "gy"))
    particles = particle_pos.shape[1]
    slots = 2 * particles // devices
    fields, layers, rows, cols = fluid_state.shape
    boxes = particle_box.reshape(1, particles)
    radius = particle_radius.reshape(1, particles)
    temp = particle_temp.reshape(1, particles)
    cells = particle_cell.reshape(1, particles)

    outgoing, slot_of, spots, tiles = place(
        box_owner, boxes, particle_pos, particle_motion, radius, temp, slots
    )
    arrived = lax.all_to_all(outgoing, ("gx", "gy"), split_axis=0, concat_axis=0, tiled=True)

    spots, fluid = lax.optimization_barrier((spots, fluid_state))
    fluid_halo = halo_of(
        fluid[:, :, 0, :],
        fluid[:, :, rows - 1, :],
        fluid[:, :, :, 0].reshape(-1, BLOCK),
        fluid[:, :, :, cols - 1].reshape(-1, BLOCK),
    )
    seen = look_up(fluid, cells)
    arrived, seen = lax.optimization_barrier((arrived, seen))
    result = contact(arrived, contact_mask)

    result, *fluid_halo = lax.optimization_barrier((result,) + tuple(fluid_halo))
    base, deposits, *edges = deposit(
        fluid_halo, cells, seen, particle_motion, radius, temp, (layers, rows, cols)
    )
    back = lax.all_to_all(result, ("gx", "gy"), split_axis=0, concat_axis=0, tiled=True)
    warm, heat_field, *edges = heat_deposit(
        back, slot_of, cells, radius, base, edges, (layers, rows, cols)
    )
    halo = halo_of(*edges)
    particle_next = fetch(box_owner, tiles, back, boxes, spots, base, warm)
    fluid_next, void_fraction = spread(deposits, heat_field, halo, fluid_state)
    return (fluid_next, void_fraction, particle_next)


def solution(mesh):
    in_specs = (
        P(None, None, "gy", "gx"),
        P(None, ("gx", "gy")),
        P(None, ("gx", "gy")),
        P(("gx", "gy")),
        P(("gx", "gy")),
        P(("gx", "gy")),
        P(("gx", "gy"), None),
        P(),
        P(("gx", "gy"), None, None),
    )
    out_specs = (P(None, None, "gy", "gx"), P(None, "gy", "gx"), P(None, ("gx", "gy")))
    return jax.shard_map(shards, mesh=mesh, in_specs=in_specs, out_specs=out_specs, check_vma=False)
```

```python
import functools

import jax
import jax.numpy as jnp
from jax import lax
from jax.experimental import pallas as pl
from jax.experimental.pallas import tpu as pltpu
from jax.sharding import PartitionSpec as P

BLOCK = 128
TIME_STEP = 0.1
STIFFNESS = 0.5
DAMPING_RATE = 0.2
ROTATION_DRAG = 0.1
DRAG_COEFF = 4.0
CONDUCTION = 0.3
HEAT_TRANSFER = 4.0
GRAVITY = 0.3
COUPLING = 4.0
CENTRE_WEIGHT = 0.25
SIDE_WEIGHT = 0.125

F32 = jnp.float32
BF16 = jnp.bfloat16
VMEM = pltpu.VMEM
NN = (((1,), (0,)), ((), ()))
NT = (((1,), (1,)), ((), ()))


def split(value):
    high = value.astype(BF16)
    return high, (value - high.astype(F32)).astype(BF16)


def hot(count, row):
    places = lax.broadcasted_iota(jnp.int32, (count, row.shape[1]), 0)
    return jnp.where(places == row, 1.0, 0.0).astype(BF16)


def hot_columns(count, row):
    n = row.shape[1] // BLOCK
    tiles = [row[:, a * BLOCK : (a + 1) * BLOCK] for a in range(n)]
    turned = jnp.transpose(jnp.concatenate(tiles * (8 // n), axis=0).astype(F32))
    places = lax.broadcasted_iota(jnp.int32, (BLOCK, count), 1).astype(F32)
    return jnp.concatenate(
        [jnp.where(places == turned[:, a : a + 1], 1.0, 0.0).astype(BF16) for a in range(n)], axis=0
    )


def invert(owner_ref, box_of):
    def step(b, _):
        box_of[owner_ref[b]] = b
        return 0

    lax.fori_loop(0, owner_ref.shape[0], step, 0)


WINDOW = 256
CHUNK = 1024


def place_kernel(
    owner_ref, box_ref, pos_ref, motion_ref, radius_ref, temp_ref,
    out_ref, slot_ref, spot_ref, tile_ref,
    box_of, tile_of, acc, done
):
    devices, rows, _ = out_ref.shape
    layers = rows // 12
    slots = layers * BLOCK
    particles = box_ref.shape[1]
    sub = 256
    invert(owner_ref, box_of)
    acc[...] = jnp.zeros_like(acc)

    box_row = lax.broadcasted_iota(jnp.int32, (devices, 1), 0)
    owner_column = jnp.zeros((devices, 1), F32)
    for b in range(devices):
        owner_column = jnp.where(box_row == b, owner_ref[b].astype(F32), owner_column)
    above = (
        lax.broadcasted_iota(jnp.int32, (sub, sub), 0) < lax.broadcasted_iota(jnp.int32, (sub, sub), 1)
    )
    above = jnp.where(above, 1.0, 0.0).astype(BF16)
    lane = lax.broadcasted_iota(jnp.int32, (devices, BLOCK), 1)
    tiles = jnp.zeros((devices, BLOCK), F32)
    highest = jnp.zeros((1, sub), F32)
    carry = jnp.zeros((devices, 1), F32)
    per_chunk = CHUNK // sub
    for c in range(particles // CHUNK):
        chosen = []
        for s in range(per_chunk):
            at = c * CHUNK + s * sub
            chosen.append(
                lax.broadcasted_iota(jnp.int32, (devices, sub), 0) == box_ref[:, at : at + sub]
            )
        ones = [jnp.where(mine, 1.0, 0.0) for mine in chosen]
        earlier = lax.dot_general(
            jnp.concatenate(ones, axis=0).astype(BF16), above, NN, preferred_element_type=F32
        )
        tile = jnp.minimum(jnp.floor(carry * (1.0 / BLOCK)), layers - 1.0)
        tiles = jnp.where(lane == c, tile, tiles)
        for s in range(per_chunk):
            at = c * CHUNK + s * sub
            rank = earlier[s * devices : (s + 1) * devices] + carry
            spot = jnp.where(chosen[s], rank - BLOCK * tile, 0.0)
            spot = jnp.sum(spot, axis=0, keepdims=True)
            slot = jnp.where(chosen[s], rank + slots * owner_column, 0.0)
            slot = jnp.sum(slot, axis=0, keepdims=True)
            spot_ref[:, at : at + sub] = spot.astype(jnp.int32)
            slot_ref[:, at : at + sub] = slot.astype(jnp.int32)
            highest = jnp.maximum(highest, spot)
            carry = carry + jnp.sum(ones[s], axis=1, keepdims=True)
    if devices < BLOCK:
        tiles = jnp.concatenate([tiles, jnp.zeros((BLOCK - devices, BLOCK), F32)], axis=0)
    count = tile_ref.shape[0] - 8
    tile_ref[0:count, :] = jnp.transpose(tiles)[0:count].astype(jnp.int32)
    windows = jnp.floor(jnp.max(highest, axis=1, keepdims=True) * (1.0 / WINDOW)) + 1.0
    tile_ref[count : count + 8, :] = jnp.broadcast_to(windows, (8, BLOCK)).astype(jnp.int32)
    copy = pltpu.make_async_copy(tile_ref, tile_of, done)
    copy.start()
    copy.wait()

    def step(w, c, _):
        here = pl.ds(pl.multiple_of(c * CHUNK, CHUNK), CHUNK)
        boxes = box_ref[:, here]
        pos = pos_ref[:, here]
        motion = motion_ref[:, here]
        push = TIME_STEP * STIFFNESS * pos - TIME_STEP * DAMPING_RATE * motion[0:3]
        spin = -TIME_STEP * ROTATION_DRAG * motion[3:6]
        heat = -TIME_STEP * CONDUCTION * temp_ref[:, here]
        first = jnp.concatenate([push, spin, heat, jnp.ones((1, CHUNK), F32)], axis=0)
        second = jnp.concatenate([pos, radius_ref[:, here]], axis=0)
        first = jnp.concatenate(split(first), axis=0)
        second = jnp.concatenate(split(second) * 2, axis=0)
        lower = lax.broadcasted_iota(jnp.int32, (16, 1), 0) < 8
        box16 = jnp.broadcast_to(boxes, (16, CHUNK)).astype(F32).astype(BF16)
        first_parts = []
        second_parts = []
        for o in range(devices):
            mine = box16 == box_of[o].astype(F32).astype(BF16)
            first_parts.append(jnp.where(mine, first, jnp.zeros_like(first)))
            if o % 2 == 0:
                either = jnp.where(lower, box_of[o].astype(F32), box_of[o + 1].astype(F32)).astype(BF16)
                second_parts.append(jnp.where(box16 == either, second, jnp.zeros_like(second)))
        parts = jnp.concatenate(first_parts + second_parts, axis=0)

        hot_spot = hot(WINDOW, spot_ref[:, here] - WINDOW * w)
        placed = lax.dot_general(parts, hot_spot, NT, preferred_element_type=F32)
        for o in range(devices):
            tile = tile_of[c, box_of[o]] + 2 * w
            one = placed[16 * o : 16 * o + 8] + placed[16 * o + 8 : 16 * o + 16]
            two = placed[16 * devices + 8 * o : 16 * devices + 8 * o + 8]
            two = two + pltpu.roll(two, 4, 0)
            acc[o, tile, 0:8, :] += one[:, :BLOCK]
            acc[o, tile + 1, 0:8, :] += one[:, BLOCK:]
            acc[o, tile, 8:16, :] += two[:, :BLOCK]
            acc[o, tile + 1, 8:16, :] += two[:, BLOCK:]
        return 0

    chunks = particles // CHUNK
    lax.fori_loop(0, chunks, functools.partial(step, 0), 0, unroll=4)

    def later(w, _):
        return lax.fori_loop(0, chunks, functools.partial(step, w), 0)

    lax.fori_loop(1, tile_of[tile_ref.shape[0] - 8, 0], later, 0)

    def finish(o, _):
        for q in range(layers):
            out_ref[o, 8 * q : 8 * q + 8, :] = acc[o, q, 0:8, :]
            out_ref[o, 8 * layers + 4 * q : 8 * layers + 4 * q + 4, :] = acc[o, q, 8:12, :]
        return 0

    lax.fori_loop(0, devices, finish, 0)


def place(box_owner, boxes, pos, motion, radius, temp, slots):
    devices = box_owner.shape[0]
    particles = pos.shape[1]
    layers = slots // BLOCK
    vmem = pl.BlockSpec(memory_space=VMEM)
    row = jax.ShapeDtypeStruct((1, particles), jnp.int32)
    table = (-(-particles // (8 * CHUNK)) * 8 + 8, BLOCK)
    return pl.pallas_call(
        place_kernel,
        out_shape=(
            jax.ShapeDtypeStruct((devices, 12 * layers, BLOCK), F32), row, row,
            jax.ShapeDtypeStruct(table, jnp.int32),
        ),
        in_specs=[pl.BlockSpec(memory_space=pltpu.SMEM)] + [vmem] * 5,
        out_specs=(vmem,) * 4,
        scratch_shapes=[
            pltpu.SMEM((devices,), jnp.int32),
            pltpu.SMEM(table, jnp.int32),
            VMEM((devices, layers + 3, 16, BLOCK), F32),
            pltpu.SemaphoreType.DMA,
        ],
        compiler_params=pltpu.CompilerParams(vmem_limit_bytes=60 << 20),
        cost_estimate=pl.CostEstimate(
            flops=2 * 24 * devices * WINDOW * particles, bytes_accessed=1 << 20, transcendentals=0
        ),
        name="place_slots",
    )(box_owner, boxes, pos, motion, radius, temp)


def pair_terms(near):
    twice = jnp.concatenate([near, near], axis=0)
    high = twice.astype(BF16).astype(F32)
    low = (twice - high).astype(BF16).astype(F32)
    row = lax.broadcasted_iota(jnp.int32, (8, 1), 0)
    kept = high + low
    squares = kept * kept
    norm = -(squares[0:1] + squares[1:2] + squares[2:3])
    total = jnp.where(row < 3, norm, squares[3:4] + 0.5)
    one = total.astype(BF16).astype(F32)
    rest = total - one
    two = rest.astype(BF16).astype(F32)
    three = (rest - two).astype(BF16).astype(F32)
    third = jnp.where((row == 0) | (row == 3), one, jnp.where((row == 1) | (row == 4), two, three))
    third = jnp.where(row < 6, third, 0.0)
    crossed = 2.0 * jnp.where(row < 4, high, low)
    is_radius = (row == 3) | (row == 7)
    cross_d = jnp.where(is_radius, 0.0, crossed)
    cross_r = jnp.where(is_radius, crossed, 0.0)
    ones = jnp.ones_like(third)
    left = jnp.concatenate([high, low, third, jnp.where(row < 6, ones, 0.0)], axis=0)
    ones_d = jnp.where(row < 3, ones, 0.0)
    ones_r = jnp.where((row >= 3) & (row < 6), ones, 0.0)
    for_d = jnp.concatenate([cross_d, cross_d, ones_d, jnp.where(row < 3, third, 0.0)], axis=0)
    for_r = jnp.concatenate([cross_r, cross_r, ones_r, jnp.where((row >= 3) & (row < 6), third, 0.0)], axis=0)
    right = jnp.concatenate([for_d, for_r], axis=1)
    return left, right.astype(BF16)


def contact_kernel(slot_ref, mask_ref, out_ref):
    homes, rows, _ = slot_ref.shape
    layers = rows // 12
    blocks = [(s, q) for s in range(homes) for q in range(layers)]
    row = lax.broadcasted_iota(jnp.int32, (8, 1), 0)
    sign = jnp.where((row >= 3) & (row < 6), 1.0, -1.0)
    lane = lax.broadcasted_iota(jnp.int32, (BLOCK, BLOCK), 1) // 16

    def pairs_of(group):
        pairs = []
        for first in range(0, 8, 4):
            lefts = []
            rights = []
            for g, (s, q) in enumerate(group[first : first + 4]):
                left, right = pair_terms(slot_ref[s, 8 * layers + 4 * q : 8 * layers + 4 * q + 4, :])
                lefts.append(left)
                spots = [jnp.zeros_like(right)] * 4
                spots[g] = right
                rights.append(jnp.concatenate(spots, axis=0))
            turned = jnp.transpose(jnp.concatenate(lefts, axis=0)).astype(BF16)
            pairs.append(
                lax.dot_general(turned, jnp.concatenate(rights, axis=1), NN, preferred_element_type=F32)
            )
        return pairs

    def sums_of(number, group, pairs):
        stacked = []
        for s, q in group:
            mine = slot_ref[s, 8 * q : 8 * q + 8, :]
            high = mine.astype(BF16).astype(F32)
            stacked += [high, mine - high]
        columns = jnp.transpose(jnp.concatenate(stacked, axis=0)).astype(BF16)
        highs = []
        lows = []
        right = []
        for b in range(8):
            at = 2 * BLOCK * (b % 4)
            pair = pairs[b // 4]
            reach = pair[:, at + BLOCK : at + 2 * BLOCK]
            inverse = pl.reciprocal(reach, approx=True)
            inverse = inverse * (2.0 - reach * inverse)
            weight = mask_ref[8 * number + b].astype(F32) * jnp.exp(pair[:, at : at + BLOCK] * inverse)
            high, low = split(weight)
            highs.append(high)
            lows.append(low)
            right.append(jnp.where(lane == b, columns, jnp.zeros_like(columns)))
        return lax.dot_general(
            jnp.concatenate(highs + lows, axis=1), jnp.concatenate(right + right, axis=0), NN,
            preferred_element_type=F32,
        )

    def finish(group, sums):
        sums = jnp.transpose(sums)
        for b, (s, q) in enumerate(group):
            total = sums[16 * b : 16 * b + 8] + sums[16 * b + 8 : 16 * b + 16]
            out_ref[s, 8 * q : 8 * q + 8, :] = slot_ref[s, 8 * q : 8 * q + 8, :] * total[7:8] + sign * total

    groups = [blocks[i : i + 8] for i in range(0, len(blocks), 8)]
    pairs = pairs_of(groups[0])
    before = None
    for number, group in enumerate(groups):
        later = pairs_of(groups[number + 1]) if number + 1 < len(groups) else None
        sums = sums_of(number, group, pairs)
        if before is not None:
            finish(*before)
        before = (group, sums)
        pairs = later
    finish(*before)


def contact(arrived, mask):
    devices, rows, _ = arrived.shape
    layers = rows // 12
    blocks = mask.shape[0]
    step = 32 // layers
    return pl.pallas_call(
        contact_kernel,
        grid=(devices // step,),
        out_shape=jax.ShapeDtypeStruct((devices, 8 * layers, BLOCK), F32),
        in_specs=[
            pl.BlockSpec((step, rows, BLOCK), lambda h: (h, 0, 0)),
            pl.BlockSpec((step * layers, BLOCK, BLOCK), lambda h: (h, 0, 0)),
        ],
        out_specs=pl.BlockSpec((step, 8 * layers, BLOCK), lambda h: (h, 0, 0)),
        compiler_params=pltpu.CompilerParams(vmem_limit_bytes=54 << 20),
        cost_estimate=pl.CostEstimate(
            flops=64 * blocks * BLOCK * BLOCK, bytes_accessed=blocks * BLOCK * BLOCK * 4, transcendentals=0
        ),
        name="contact_blocks",
    )(arrived, mask)


def smoothed(centre, y_first, y_last, x_first, x_last):
    layers, rows, cols = centre.shape
    zero = jnp.zeros((1, rows, cols), F32)
    up = jnp.concatenate([centre[1:], zero], axis=0)
    down = jnp.concatenate([zero, centre[:-1]], axis=0)
    row = lax.broadcasted_iota(jnp.int32, (1, rows, cols), 1)
    col = lax.broadcasted_iota(jnp.int32, (1, rows, cols), 2)
    back = jnp.where(row == 0, y_first, pltpu.roll(centre, 1, 1))
    front = jnp.where(row == rows - 1, y_last, pltpu.roll(centre, rows - 1, 1))
    left = jnp.where(col == 0, x_first, pltpu.roll(centre, 1, 2))
    right = jnp.where(col == cols - 1, x_last, pltpu.roll(centre, cols - 1, 2))
    return CENTRE_WEIGHT * centre + SIDE_WEIGHT * ((up + down) + (back + front) + (left + right))


def columns(edge, layers, rows):
    count = edge.shape[0]
    if count < 8:
        edge = jnp.concatenate([edge] * (8 // count), axis=0)
    turned = jnp.transpose(edge)
    parts = [turned[:, a : a + 1] for a in range(count)]
    return jnp.concatenate(parts, axis=0).reshape(layers, rows, 1)


def smooth_field(field_ref, y0_ref, y1_ref, x0_ref, x1_ref, k, edge=None):
    at = k if edge is None else edge
    _, layers, rows, cols = field_ref.shape
    per = layers * rows // BLOCK
    x0 = columns(x0_ref[at * per : (at + 1) * per, :], layers, rows)
    x1 = columns(x1_ref[at * per : (at + 1) * per, :], layers, rows)
    y0 = y0_ref[at].reshape(layers, 1, cols)
    y1 = y1_ref[at].reshape(layers, 1, cols)
    return smoothed(field_ref[k], y0, y1, x0, x1)


def write_edges(field, k, y0_ref, y1_ref, x0_ref, x1_ref):
    layers, rows, cols = field.shape
    y0_ref[k] = field[:, 0, :]
    y1_ref[k] = field[:, rows - 1, :]
    flat = field.reshape(layers * rows, cols)
    for a in range(layers * rows // BLOCK):
        turned = jnp.transpose(flat[a * BLOCK : (a + 1) * BLOCK, :])
        at = k * (layers * rows // BLOCK) + a
        x0_ref[at : at + 1, :] = turned[0:1, :]
        x1_ref[at : at + 1, :] = turned[cols - 1 : cols, :]


def paired_rows(pairs, layers, rows, scratch):
    half = pairs.shape[0]
    cols = pairs.shape[1] // 2
    scratch[pl.ds(0, half, stride=2), :] = pairs[:, :cols]
    scratch[pl.ds(1, half, stride=2), :] = pairs[:, cols:]
    return scratch[...].reshape(layers, rows, cols)


def gathered(tables, rows, lanes):
    group = rows // 8
    found = [None] * len(tables)
    for g in range(len(tables[0])):
        mine = group == g
        for k, table in enumerate(tables):
            value = jnp.take_along_axis(table[g], lanes, axis=1, mode="promise_in_bounds")
            found[k] = value if g == 0 else jnp.where(mine, value, found[k])
    mine = lax.broadcasted_iota(jnp.int32, (8, BLOCK), 0) == rows % 8
    return [jnp.sum(jnp.where(mine, value, 0.0), axis=0, keepdims=True) for value in found]


def look_kernel(fluid_ref, cell_ref, seen_ref, table, rows_scratch, *, chunk):
    fields, layers, rows, cols = fluid_ref.shape
    particles = cell_ref.shape[1]
    half = layers * rows // 2
    wide = 2 * cols
    for k in range(fields):
        rows_scratch[...] = smoothed(fluid_ref[k], 0.0, 0.0, 0.0, 0.0).reshape(layers * rows, cols)
        here = slice(k * half, (k + 1) * half)
        for part in range(2):
            high, low = split(rows_scratch[pl.ds(part, half, stride=2), :])
            table[here, part * cols : (part + 1) * cols] = high
            table[here, wide + part * cols : wide + (part + 1) * cols] = low

    def step(i, _):
        here = pl.ds(pl.multiple_of(i * chunk, chunk), chunk)
        cells = cell_ref[:, here]
        hot_low = hot(wide, cells % wide)
        found = lax.dot_general(
            table[...], jnp.concatenate([hot_low, hot_low], axis=0), NN, preferred_element_type=F32
        )
        mine = lax.broadcasted_iota(jnp.int32, (half, chunk), 0) == cells // wide
        seen = [
            jnp.sum(jnp.where(mine, found[k * half : (k + 1) * half], 0.0), axis=0, keepdims=True)
            for k in range(fields)
        ]
        seen_ref[:, here] = jnp.concatenate(seen, axis=0)
        return 0

    lax.fori_loop(0, particles // chunk, step, 0, unroll=2)


def look_up(fluid, cells):
    fields, layers, rows, cols = fluid.shape
    particles = cells.shape[1]
    vmem = pl.BlockSpec(memory_space=VMEM)
    return pl.pallas_call(
        functools.partial(look_kernel, chunk=512),
        out_shape=jax.ShapeDtypeStruct((fields, particles), F32),
        in_specs=[vmem] * 2,
        out_specs=vmem,
        scratch_shapes=[
            VMEM((fields * layers * rows // 2, 4 * cols), BF16),
            VMEM((layers * rows, cols), F32),
        ],
        compiler_params=pltpu.CompilerParams(vmem_limit_bytes=40 << 20),
        cost_estimate=pl.CostEstimate(
            flops=8 * fields * layers * rows * cols * particles // 4, bytes_accessed=1 << 20, transcendentals=0
        ),
        name="look_up",
    )(fluid, cells)


def deposit_kernel(
    y0_ref, y1_ref, x0_ref, x1_ref, cell_ref, seen_ref, motion_ref, radius_ref, temp_ref,
    base_ref, dep_ref, dy0_ref, dy1_ref, dx0_ref, dx1_ref, x_table, rows_scratch, acc, *, chunk
):
    fields, layers, rows, cols = dep_ref.shape
    half = layers * rows // 2
    wide = 2 * cols
    particles = cell_ref.shape[1]
    per = layers * rows // BLOCK
    for k in range(fields):
        x_table[k] = jnp.zeros_like(x_table[k])
        x_table[k, 0:per, :] = x0_ref[k * per : (k + 1) * per, :]
        x_table[k, per : 2 * per, :] = x1_ref[k * per : (k + 1) * per, :]
    acc[...] = jnp.zeros_like(acc)

    def step(i, _):
        here = pl.ds(pl.multiple_of(i * chunk, chunk), chunk)
        cells = cell_ref[:, here]
        beside = [[] for _ in range(fields)]
        for s in range(chunk // BLOCK):
            cell = jnp.broadcast_to(cells[:, s * BLOCK : (s + 1) * BLOCK], (8, BLOCK))
            high = cell // cols
            low = cell % cols
            y = high % rows
            from_y = gathered(
                [
                    [ref[k, 8 * g : 8 * g + 8, :] for ref in (y0_ref, y1_ref) for g in range(layers // 8)]
                    for k in range(fields)
                ],
                high // rows + jnp.where(y == 0, 0, layers),
                low,
            )
            from_x = gathered(
                [[x_table[k, 8 * g : 8 * g + 8, :] for g in range(x_table.shape[1] // 8)] for k in range(fields)],
                high // BLOCK + jnp.where(low == 0, 0, per),
                high % BLOCK,
            )
            on_y = (y[0:1] == 0) | (y[0:1] == rows - 1)
            on_x = (low[0:1] == 0) | (low[0:1] == cols - 1)
            for k in range(fields):
                beside[k].append(jnp.where(on_y, from_y[k], 0.0) + jnp.where(on_x, from_x[k], 0.0))
        beside = jnp.concatenate([jnp.concatenate(parts, axis=1) for parts in beside], axis=0)
        seen = seen_ref[:, here] + SIDE_WEIGHT * beside
        motion = motion_ref[:, here]
        radius = radius_ref[:, here]
        temp = temp_ref[:, here]
        drag = DRAG_COEFF / (radius * radius + 0.25) * (seen[0:3] - motion[0:3])
        upward = lax.broadcasted_iota(jnp.int32, (3, 1), 0) == 2
        moved = motion[0:3] + TIME_STEP * drag - jnp.where(upward, TIME_STEP * GRAVITY, 0.0)
        warmed = temp + TIME_STEP * HEAT_TRANSFER * (seen[3:4] - temp)
        base_ref[:, here] = jnp.concatenate([moved, motion[3:6], warmed, seen[3:4]], axis=0)
        volume = radius * radius * radius
        high, low = split(jnp.concatenate([volume, -volume * drag], axis=0))
        hot_low = hot(wide, cells % wide)
        hot_high = hot(half, cells // wide)
        parts = [hot_high * piece[k : k + 1] for piece in (high, low) for k in range(fields)]
        total = lax.dot_general(jnp.concatenate(parts, axis=0), hot_low, NT, preferred_element_type=F32)
        acc[...] += total[: fields * half] + total[fields * half :]
        return 0

    lax.fori_loop(0, particles // chunk, step, 0)
    for k in range(fields):
        field = paired_rows(acc[k * half : (k + 1) * half, :], layers, rows, rows_scratch)
        dep_ref[k] = field
        write_edges(field, k, dy0_ref, dy1_ref, dx0_ref, dx1_ref)


def edge_shapes(fields, layers, rows, cols):
    y_edge = jax.ShapeDtypeStruct((fields, layers, cols), F32)
    x_edge = jax.ShapeDtypeStruct((fields * layers * rows // BLOCK, BLOCK), F32)
    return (y_edge, y_edge, x_edge, x_edge)


def deposit(halo, cells, seen, motion, radius, temp, grid):
    layers, rows, cols = grid
    fields, particles = seen.shape
    tall = -(-2 * layers * rows // (8 * BLOCK)) * 8
    vmem = pl.BlockSpec(memory_space=VMEM)
    return pl.pallas_call(
        functools.partial(deposit_kernel, chunk=1024),
        out_shape=(
            jax.ShapeDtypeStruct((8, particles), F32),
            jax.ShapeDtypeStruct((fields,) + grid, F32),
        ) + edge_shapes(fields, layers, rows, cols),
        in_specs=[vmem] * 9,
        out_specs=(vmem,) * 6,
        scratch_shapes=[
            VMEM((fields, tall, BLOCK), F32),
            VMEM((layers * rows, cols), F32),
            VMEM((fields * layers * rows // 2, 2 * cols), F32),
        ],
        compiler_params=pltpu.CompilerParams(vmem_limit_bytes=40 << 20),
        cost_estimate=pl.CostEstimate(
            flops=4 * fields * layers * rows * cols * particles, bytes_accessed=2 << 20, transcendentals=0
        ),
        name="deposit_fields",
    )(*halo, cells, seen, motion, radius, temp)


def heat_kernel(
    back_ref, slot_ref, cell_ref, radius_ref, base_ref, ey0_ref, ey1_ref, ex0_ref, ex1_ref,
    next_ref, dep_ref, dy0_ref, dy1_ref, dx0_ref, dx1_ref,
    table, acc, rows_scratch, *, chunk, rows
):
    devices, tall, _ = back_ref.shape
    layers = tall // 8
    particles = slot_ref.shape[1]
    half, wide = acc.shape
    for o in range(devices):
        for q in range(layers):
            table[o * layers + q : o * layers + q + 1, :] = back_ref[o, 8 * q + 6 : 8 * q + 7, :]
    acc[...] = jnp.zeros_like(acc)

    def step(i, _):
        here = pl.ds(pl.multiple_of(i * chunk, chunk), chunk)
        slots = slot_ref[:, here]
        gained = []
        for s in range(chunk // BLOCK):
            wanted = jnp.broadcast_to(slots[:, s * BLOCK : (s + 1) * BLOCK], (8, BLOCK))
            tiles = [table[8 * g : 8 * g + 8, :] for g in range(devices * layers // 8)]
            gained.append(gathered([tiles], wanted // BLOCK, wanted % BLOCK)[0])
        base = base_ref[6:8, here]
        total = base[0:1] + jnp.concatenate(gained, axis=1)
        next_ref[:, here] = total
        radius = radius_ref[:, here]
        high, low = split(radius * radius * radius * (total - base[1:2]))
        cells = cell_ref[:, here]
        hot_low = hot_columns(wide, cells % wide)
        hot_high = hot(half, cells // wide)
        added = lax.dot_general(hot_high * high, hot_low, NN, preferred_element_type=F32)
        acc[...] += added + lax.dot_general(hot_high * low, hot_low, NN, preferred_element_type=F32)
        return 0

    lax.fori_loop(0, particles // chunk, step, 0, unroll=4)
    field = paired_rows(acc[...], 2 * half // rows, rows, rows_scratch)
    dep_ref[0] = field
    for edge, out in ((ey0_ref, dy0_ref), (ey1_ref, dy1_ref), (ex0_ref, dx0_ref), (ex1_ref, dx1_ref)):
        out[0 : edge.shape[0]] = edge[...]
    write_edges(field, ey0_ref.shape[0], dy0_ref, dy1_ref, dx0_ref, dx1_ref)


def heat_deposit(back, slot_of, cells, radius, base, edges, grid):
    devices = back.shape[0]
    layers, rows, cols = grid
    particles = cells.shape[1]
    half = layers * rows // 2
    fields = edges[0].shape[0] + 1
    vmem = pl.BlockSpec(memory_space=VMEM)
    return pl.pallas_call(
        functools.partial(heat_kernel, chunk=1024, rows=rows),
        out_shape=(
            jax.ShapeDtypeStruct((1, particles), F32),
            jax.ShapeDtypeStruct((1,) + grid, F32),
        ) + edge_shapes(fields, layers, rows, cols),
        in_specs=[vmem] * 9,
        out_specs=(vmem,) * 6,
        scratch_shapes=[
            VMEM((devices * back.shape[1] // 8, BLOCK), F32),
            VMEM((half, 2 * cols), F32),
            VMEM((layers * rows, cols), F32),
        ],
        compiler_params=pltpu.CompilerParams(vmem_limit_bytes=40 << 20),
        cost_estimate=pl.CostEstimate(
            flops=4 * half * 2 * cols * particles, bytes_accessed=1 << 20, transcendentals=0
        ),
        name="heat_deposit",
    )(back, slot_of, cells, radius, base, *edges)


def fetch_kernel(
    owner_ref, tile_ref, back_ref, box_ref, spot_ref, base_ref, warm_ref, next_ref, box_of, table
):
    devices, tall, _ = back_ref.shape
    layers = tall // 8
    particles = box_ref.shape[1]
    invert(owner_ref, box_of)
    for o in range(devices):
        for q in range(layers):
            high, low = split(back_ref[o, 8 * q : 8 * q + 8, :])
            table[o, q] = jnp.concatenate([high, low], axis=0)
        for q in range(layers, layers + 3):
            table[o, q] = jnp.zeros((16, BLOCK), BF16)

    def gained_of(w, c):
        here = pl.ds(pl.multiple_of(c * CHUNK, CHUNK), CHUNK)
        boxes = jnp.broadcast_to(box_ref[:, here], (8, CHUNK))
        tile = [tile_ref[c, box_of[o]] + 2 * w for o in range(devices)]
        wanted = jnp.concatenate(
            [jnp.concatenate([table[o, tile[o]], table[o, tile[o] + 1]], axis=1) for o in range(devices)], axis=0
        )
        hot_spot = hot(WINDOW, spot_ref[:, here] - WINDOW * w)
        found = lax.dot_general(wanted, hot_spot, NN, preferred_element_type=F32)
        gained = jnp.zeros((8, CHUNK), F32)
        for o in range(devices):
            value = found[16 * o : 16 * o + 8] + found[16 * o + 8 : 16 * o + 16]
            gained = jnp.where(boxes == box_of[o], value, gained)
        return here, gained

    def step(c, _):
        here, gained = gained_of(0, c)
        next_ref[:, here] = jnp.concatenate(
            [base_ref[0:6, here] + gained[0:6], warm_ref[:, here]], axis=0
        )
        return 0

    chunks = particles // CHUNK
    lax.fori_loop(0, chunks, step, 0, unroll=4)

    def later(w, _):
        def again(c, _):
            here, gained = gained_of(w, c)
            next_ref[0:6, here] += gained[0:6]
            return 0

        return lax.fori_loop(0, chunks, again, 0)

    lax.fori_loop(1, tile_ref[tile_ref.shape[0] - 8, 0], later, 0)


def fetch(box_owner, tiles, back, boxes, spots, base, warm):
    devices, tall, _ = back.shape
    layers = tall // 8
    particles = boxes.shape[1]
    vmem = pl.BlockSpec(memory_space=VMEM)
    smem = pl.BlockSpec(memory_space=pltpu.SMEM)
    return pl.pallas_call(
        fetch_kernel,
        out_shape=jax.ShapeDtypeStruct((7, particles), F32),
        in_specs=[smem, smem] + [vmem] * 5,
        out_specs=vmem,
        scratch_shapes=[
            pltpu.SMEM((devices,), jnp.int32),
            VMEM((devices, layers + 3, 16, BLOCK), BF16),
        ],
        compiler_params=pltpu.CompilerParams(vmem_limit_bytes=40 << 20),
        cost_estimate=pl.CostEstimate(
            flops=32 * devices * WINDOW * particles, bytes_accessed=1 << 20, transcendentals=0
        ),
        name="fetch_slots",
    )(box_owner, tiles, back, boxes, spots, base, warm)


def spread_kernel(dep_ref, heat_ref, y0_ref, y1_ref, x0_ref, x1_ref, fluid_ref, next_ref, void_ref):
    halo = (y0_ref, y1_ref, x0_ref, x1_ref)
    crowding = 1.0 + COUPLING * smooth_field(dep_ref, *halo, 0)
    void_ref[...] = 1.0 / crowding
    for k in range(3):
        next_ref[k] = fluid_ref[k] + TIME_STEP * COUPLING * smooth_field(dep_ref, *halo, k + 1) * crowding
    warmth = smooth_field(heat_ref, *halo, 0, 4)
    next_ref[3] = fluid_ref[3] + TIME_STEP * COUPLING * warmth * crowding


def spread(dep, heat, halo, fluid):
    vmem = pl.BlockSpec(memory_space=VMEM)
    return pl.pallas_call(
        spread_kernel,
        out_shape=(jax.ShapeDtypeStruct(fluid.shape, F32), jax.ShapeDtypeStruct(fluid.shape[1:], F32)),
        in_specs=[vmem] * 7,
        out_specs=(vmem,) * 2,
        compiler_params=pltpu.CompilerParams(vmem_limit_bytes=40 << 20),
        cost_estimate=pl.CostEstimate(flops=20 * fluid.size, bytes_accessed=2 << 20, transcendentals=0),
        name="spread_fields",
    )(dep, heat, *halo, fluid)


def halo_of(y_first, y_last, x_first, x_last):
    def moved(value, axis, step):
        size = lax.axis_size(axis)
        pairs = [(i, i + step) for i in range(size) if 0 <= i + step < size]
        return lax.ppermute(value, axis, pairs)

    return (
        moved(y_last, "gy", 1),
        moved(y_first, "gy", -1),
        moved(x_last, "gx", 1),
        moved(x_first, "gx", -1),
    )


def shards(
    fluid_state, particle_pos, particle_motion, particle_radius, particle_temp,
    particle_cell, particle_box, box_owner, contact_mask,
):
    devices = lax.axis_size(("gx", "gy"))
    particles = particle_pos.shape[1]
    slots = 2 * particles // devices
    fields, layers, rows, cols = fluid_state.shape
    boxes = particle_box.reshape(1, particles)
    radius = particle_radius.reshape(1, particles)
    temp = particle_temp.reshape(1, particles)
    cells = particle_cell.reshape(1, particles)

    outgoing, slot_of, spots, tiles = place(
        box_owner, boxes, particle_pos, particle_motion, radius, temp, slots
    )
    arrived = lax.all_to_all(outgoing, ("gx", "gy"), split_axis=0, concat_axis=0, tiled=True)

    spots, fluid = lax.optimization_barrier((spots, fluid_state))
    fluid_halo = halo_of(
        fluid[:, :, 0, :],
        fluid[:, :, rows - 1, :],
        fluid[:, :, :, 0].reshape(-1, BLOCK),
        fluid[:, :, :, cols - 1].reshape(-1, BLOCK),
    )
    seen = look_up(fluid, cells)
    arrived, seen = lax.optimization_barrier((arrived, seen))
    result = contact(arrived, contact_mask)

    result, *fluid_halo = lax.optimization_barrier((result,) + tuple(fluid_halo))
    base, deposits, *edges = deposit(
        fluid_halo, cells, seen, particle_motion, radius, temp, (layers, rows, cols)
    )
    back = lax.all_to_all(result, ("gx", "gy"), split_axis=0, concat_axis=0, tiled=True)
    warm, heat_field, *edges = heat_deposit(
        back, slot_of, cells, radius, base, edges, (layers, rows, cols)
    )
    halo = halo_of(*edges)
    particle_next = fetch(box_owner, tiles, back, boxes, spots, base, warm)
    fluid_next, void_fraction = spread(deposits, heat_field, halo, fluid_state)
    return (fluid_next, void_fraction, particle_next)


def solution(mesh):
    in_specs = (
        P(None, None, "gy", "gx"),
        P(None, ("gx", "gy")),
        P(None, ("gx", "gy")),
        P(("gx", "gy")),
        P(("gx", "gy")),
        P(("gx", "gy")),
        P(("gx", "gy"), None),
        P(),
        P(("gx", "gy"), None, None),
    )
    out_specs = (P(None, None, "gy", "gx"), P(None, "gy", "gx"), P(None, ("gx", "gy")))
    return jax.shard_map(shards, mesh=mesh, in_specs=in_specs, out_specs=out_specs, check_vma=False)
```
